32 devices in a mesh: dp: 16 (over z, y, x), rows: 2 (over core).
Axes of the slice: x: 2, y: 2, z: 4, core: 2. Of those that a mesh axis runs over, the one named last changes fastest.
Arguments:
- glob_in: bfloat16 [16, 28, 28, 1492], P('dp', 'rows'), may hold values from -6 to 6
- small_in: bfloat16 [80, 12, 12, 1492], P('dp', 'rows'), may hold values from -6 to 6
- small_count: int32 [16], P('dp'), may hold values from 1 to 5, as said below
- kernel_in: bfloat16 [1492, 1492], P(None, 'rows'), may hold values from -0.15625 to 0.15625
- kernel_mid: bfloat16 [3, 3, 373, 1492], P(None, None, None, 'rows'), may hold values from -0.109375 to 0.109375
- kernel_out: bfloat16 [1492, 1492], P(None, 'rows'), may hold values from -0.15625 to 0.15625
- squeeze_weight: bfloat16 [1492, 373], P('rows'), may hold values from -0.3125 to 0.3125
- squeeze_bias: bfloat16 [373], replicated, may hold values from -3 to 3
- excite_weight: bfloat16 [373, 1492], P(None, 'rows'), may hold values from -0.625 to 0.625
- excite_bias: bfloat16 [1492], P('rows'), may hold values from -3 to 3
- gain_first: bfloat16 [1492], P('rows'), may hold values from 0.099609375 to 1.8984375
- shift_first: bfloat16 [1492], P('rows'), may hold values from -3 to 3
- gain_second: bfloat16 [1492], P('rows'), may hold values from 0.099609375 to 1.8984375
- shift_second: bfloat16 [1492], P('rows'), may hold values from -3 to 3
- gain_third: bfloat16 [1492], P('rows'), may hold values from 0.099609375 to 1.8984375
- shift_third: bfloat16 [1492], P('rows'), may hold values from -3 to 3
- glob_cotangent: bfloat16 [16, 28, 28, 1492], P('dp', 'rows'), may hold values from -6 to 6
- small_cotangent: bfloat16 [80, 12, 12, 1492], P('dp', 'rows'), may hold values from -6 to 6
Outputs:
- glob_out: float32 [16, 28, 28, 1492], P('dp', 'rows')
- small_out: float32 [80, 12, 12, 1492], P('dp', 'rows')
- glob_grad: float32 [16, 28, 28, 1492], P('dp', 'rows')
- small_grad: float32 [80, 12, 12, 1492], P('dp', 'rows')
- grad_kernel_in: float32 [1492, 1492], P(None, 'rows')
- grad_kernel_mid: float32 [3, 3, 373, 1492], P(None, None, None, 'rows')
- grad_kernel_out: float32 [1492, 1492], P(None, 'rows')
- grad_squeeze_weight: float32 [1492, 373], P('rows')
- grad_squeeze_bias: float32 [373], replicated
- grad_excite_weight: float32 [373, 1492], P(None, 'rows')
- grad_excite_bias: float32 [1492], P('rows')
- grad_gain_first: float32 [1492], P('rows')
- grad_shift_first: float32 [1492], P('rows')
- grad_gain_second: float32 [1492], P('rows')
- grad_shift_second: float32 [1492], P('rows')
- grad_gain_third: float32 [1492], P('rows')
- grad_shift_third: float32 [1492], P('rows')
The draws below stay inside these ranges and needn't reach their ends.
Inputs may be any that keep to these rules, and one draw needn't show every extreme that they name: Block b's live small crops are its first small_count[b] slots; some block uses all 5.
All inputs are finite; a program needn't handle non-finite values.
Results may differ from the reference program's by a relative error of at most 0.017.
Values may be sent and summed in bfloat16 or wider, within the bound.
A program may use at most 384 MiB of HBM per device.

```python
import jax
import jax.numpy as jnp
from jax import lax

C = 1492
GW = 373
SE = 373
GSIDE = 28
SSIDE = 12
SLOTS = 5
BLOCKS = 16


def draw_small_count(key, part):
    key = jax.random.fold_in(key, 7)
    first_key, second_key = jax.random.split(key)
    counts = jax.random.randint(first_key, (BLOCKS,), 1, SLOTS + 1)
    chosen = jax.random.randint(second_key, (), 0, BLOCKS)
    return counts.at[chosen].set(SLOTS).astype(jnp.int32)


def level_of(own_key, extent, shards, least, high):
    def one(position, shards_of):
        draws = jax.random.uniform(jax.random.fold_in(jax.random.fold_in(own_key, 6), position), (shards_of,), jnp.float32, least / len(shards), high / len(shards))
        return jnp.repeat(jnp.exp(draws), extent[position] // shards_of).reshape((-1,) + (1,) * (len(extent) - position - 1))

    loudness = one(*shards[0])
    for cut in shards[1:]:
        loudness = loudness * one(*cut)
    return loudness


def scatter_about(own_key, shape, width, bound, pieces=(), dtype=jnp.bfloat16):
    values = width * jax.random.normal(own_key, shape, jnp.float32)
    if pieces:
        values = values * level_of(own_key, shape, pieces, -0.22, 0.18)
    return jnp.clip(values, -bound, bound).astype(dtype)


def setup_inputs(seed: int = 0) -> dict:
    keys = jax.random.split(jax.random.key(seed), 19)
    return {
        "glob_in": scatter_about(keys[0], (BLOCKS, GSIDE, GSIDE, C), 1.0, 6.0, ((0, 16), (1, 2))),
        "small_in": scatter_about(keys[1], (BLOCKS * SLOTS, SSIDE, SSIDE, C), 1.0, 6.0, ((0, 16), (1, 2))),
        "small_count": draw_small_count(jax.random.fold_in(keys[18], 71), 0),
        "kernel_in": scatter_about(keys[3], (C, C), C ** -0.5, 0.15625, ((1, 2),)),
        "kernel_mid": scatter_about(keys[4], (3, 3, GW, C), (9 * GW) ** -0.5, 0.109375, ((3, 2),)),
        "kernel_out": scatter_about(keys[5], (C, C), C ** -0.5, 0.15625, ((1, 2),)),
        "squeeze_weight": scatter_about(keys[6], (C, SE), (C // 4) ** -0.5, 0.3125, ((0, 2),)),
        "squeeze_bias": scatter_about(keys[7], (SE,), 0.5, 3.0),
        "excite_weight": scatter_about(keys[8], (SE, C), (SE // 4) ** -0.5, 0.625, ((1, 2),)),
        "excite_bias": scatter_about(keys[9], (C,), 0.5, 3.0, ((0, 2),)),
        "gain_first": jnp.clip(1.0 + 0.18 * jax.random.normal(keys[10], (C,), jnp.float32), 0.099609375, 1.8984375).astype(jnp.bfloat16),
        "shift_first": scatter_about(keys[11], (C,), 0.5, 3.0, ((0, 2),)),
        "gain_second": jnp.clip(1.0 + 0.18 * jax.random.normal(keys[12], (C,), jnp.float32), 0.099609375, 1.8984375).astype(jnp.bfloat16),
        "shift_second": scatter_about(keys[13], (C,), 0.5, 3.0, ((0, 2),)),
        "gain_third": jnp.clip(1.0 + 0.18 * jax.random.normal(keys[14], (C,), jnp.float32), 0.099609375, 1.8984375).astype(jnp.bfloat16),
        "shift_third": scatter_about(keys[15], (C,), 0.5, 3.0, ((0, 2),)),
        "glob_cotangent": scatter_about(keys[16], (BLOCKS, GSIDE, GSIDE, C), 1.0, 6.0, ((0, 16), (1, 2))),
        "small_cotangent": scatter_about(keys[17], (BLOCKS * SLOTS, SSIDE, SSIDE, C), 1.0, 6.0, ((0, 16), (1, 2))),
    }


EPSILON = 1e-05
HIGHEST = lax.Precision.HIGHEST

@jax.custom_vjp
def low(v):
    return lax.optimization_barrier(v.astype(jnp.bfloat16)).astype(jnp.float32)

@jax.custom_vjp
def low_back(v):
    return v

def low_keep(v):
    return (low(v), None)

def low_pass(kept, grad):
    return (grad,)

def back_keep(v):
    return (v, None)

def back_low(kept, grad):
    return (low(grad),)
low.defvjp(low_keep, low_pass)
low_back.defvjp(back_keep, back_low)

def group_conv(maps, kernel, groups):
    number, height, breadth, channels = maps.shape
    group_width = channels // groups
    padded = jnp.pad(maps, ((0, 0), (1, 1), (1, 1), (0, 0)))
    running = jnp.zeros((number, height, breadth, groups, group_width), jnp.float32)
    for row_tap in range(3):
        for col_tap in range(3):
            window = padded[:, row_tap:row_tap + height, col_tap:col_tap + breadth].reshape(number, height, breadth, groups, group_width)
            weights = kernel[row_tap, col_tap].reshape(group_width, groups, group_width)
            running = running + jnp.einsum('mhwgc,cgo->mhwgo', window, weights, precision=HIGHEST)
    return running.reshape(number, height, breadth, channels)

def batch_norm(values, pixel_mask, total_count, norm_gain, norm_offset):
    mean_value = lax.optimization_barrier(jnp.sum(values * pixel_mask, 0)) / total_count
    centered = values - mean_value
    spread = lax.optimization_barrier(jnp.sum(pixel_mask * centered * centered, 0)) / total_count
    return centered * lax.rsqrt(spread + EPSILON) * norm_gain + norm_offset

def spread_crops(per_crop, first_count, first_area, other_area):
    channels = per_crop.shape[-1]
    leading = jnp.broadcast_to(per_crop[:first_count, None, :], (first_count, first_area, channels)).reshape(-1, channels)
    remaining = per_crop[first_count:]
    trailing = jnp.broadcast_to(remaining[:, None, :], (remaining.shape[0], other_area, channels)).reshape(-1, channels)
    return jnp.concatenate([leading, trailing], 0)

def reference(glob_in, small_in, small_count, kernel_in, kernel_mid, kernel_out, squeeze_weight, squeeze_bias, excite_weight, excite_bias, gain_first, shift_first, gain_second, shift_second, gain_third, shift_third, glob_cotangent, small_cotangent):
    glob_shape = glob_in.shape
    small_shape = small_in.shape
    channels = glob_shape[-1]
    groups = channels // kernel_mid.shape[2]
    glob_maps = glob_shape[0]
    glob_area = glob_shape[1] * glob_shape[2]
    small_area = small_shape[1] * small_shape[2]
    glob_pixels = glob_maps * glob_area
    slot_index = lax.iota(jnp.int32, small_shape[0])
    live_slots = (slot_index % SLOTS < small_count[slot_index // SLOTS]).astype(jnp.float32)
    small_mask = jnp.broadcast_to(live_slots[:, None], (small_shape[0], small_area)).reshape(-1, 1)
    pixel_mask = jnp.concatenate([jnp.ones((glob_pixels, 1), jnp.float32), small_mask], 0)
    total_count = jnp.sum(pixel_mask)

    def forward(params):
        glob_value, small_value, matrix_in, matrix_mid, matrix_out, squeeze_matrix, squeeze_vector, excite_matrix, excite_vector, gain_one, offset_one, gain_two, offset_two, gain_three, offset_three = params
        inputs = jnp.concatenate([glob_value.reshape(-1, channels), small_value.reshape(-1, channels)], 0)
        pre_one = low_back(jnp.dot(inputs, matrix_in, precision=HIGHEST))
        act_one = low(jax.nn.silu(batch_norm(pre_one, pixel_mask, total_count, gain_one, offset_one)))
        glob_conv = group_conv(act_one[:glob_pixels].reshape(glob_shape), matrix_mid, groups)
        small_conv = group_conv(act_one[glob_pixels:].reshape(small_shape), matrix_mid, groups)
        pre_two = low_back(jnp.concatenate([glob_conv.reshape(-1, channels), small_conv.reshape(-1, channels)], 0))
        act_two = jax.nn.silu(batch_norm(pre_two, pixel_mask, total_count, gain_two, offset_two))
        glob_pool = lax.optimization_barrier(jnp.mean(act_two[:glob_pixels].reshape(glob_maps, glob_area, channels), 1))
        small_pool = lax.optimization_barrier(jnp.mean(act_two[glob_pixels:].reshape(-1, small_area, channels), 1))
        pooled = jnp.concatenate([glob_pool, small_pool], 0)
        squeezed = jax.nn.silu(jnp.dot(pooled, squeeze_matrix, precision=HIGHEST) + squeeze_vector)
        excite = jax.nn.sigmoid(jnp.dot(squeezed, excite_matrix, precision=HIGHEST) + excite_vector)
        act_three = low(act_two * spread_crops(excite, glob_maps, glob_area, small_area))
        pre_three = low_back(jnp.dot(act_three, matrix_out, precision=HIGHEST))
        summed = batch_norm(pre_three, pixel_mask, total_count, gain_three, offset_three) + inputs
        result = pixel_mask * jax.nn.silu(summed)
        return (result[:glob_pixels].reshape(glob_shape), result[glob_pixels:].reshape(small_shape))
    floats = tuple((array.astype(jnp.float32) for array in (glob_in, small_in, kernel_in, kernel_mid, kernel_out, squeeze_weight, squeeze_bias, excite_weight, excite_bias, gain_first, shift_first, gain_second, shift_second, gain_third, shift_third)))
    outputs, pullback = jax.vjp(forward, floats)
    grads, = pullback((glob_cotangent.astype(jnp.float32), small_cotangent.astype(jnp.float32)))
    return (outputs[0], outputs[1], grads[0], grads[1], grads[2], grads[3], grads[4], grads[5], grads[6], grads[7], grads[8], grads[9], grads[10], grads[11], grads[12], grads[13], grads[14])
```

```python
import functools

import jax
import jax.numpy as jnp
from jax import lax
from jax.experimental import pallas as pl
from jax.experimental.pallas import tpu as pltpu
from jax.sharding import PartitionSpec as P

EPSILON = 1e-05
MESH = pl.DeviceIdType.MESH
F32 = jnp.float32
BF16 = jnp.bfloat16
ANY = pl.BlockSpec(memory_space=pl.ANY)
VMEM = pl.BlockSpec(memory_space=pltpu.VMEM)
LANE = 128
TILE = 64
VMEM_BYTES = 62 * 1024 * 1024


def round_up(value, step):
    return -(-value // step) * step


class Plan:
    def __init__(self, glob_shape, small_shape, group_width, dp):
        self.glob_height, self.glob_side = glob_shape[1], glob_shape[2]
        self.slots, self.small_height, self.small_side = small_shape[:3]
        self.channels = glob_shape[3]
        self.glob_width = round_up(self.glob_side + 1, 32)
        self.small_width = round_up(self.small_side + 1, 16)
        self.glob_own = self.glob_height * self.glob_width
        self.slot_own = self.small_height * self.small_width
        self.own = self.glob_own + self.slots * self.slot_own
        self.glob_all = 2 * self.glob_own
        self.slot_all = 2 * self.slot_own
        self.all = 2 * self.own
        self.glob_base = self.glob_width
        self.small_base = self.glob_all + 2 * self.glob_width
        self.slot_conv = self.slot_all + self.small_width
        self.small_conv = self.slots * self.slot_conv
        self.conv = self.small_base + self.small_conv
        self.width = group_width
        self.group = round_up(group_width, LANE)
        self.half = 2 * self.group
        self.half_real = self.channels // 2
        self.dp = dp
        self.glob_tiles = self.glob_all // TILE
        self.slot_tiles = self.slot_all // TILE
        self.slot_rows = round_up(1 + self.slots, 8)
        self.glob_area = float(2 * self.glob_height * self.glob_side)
        self.slot_area = float(2 * self.small_height * self.small_side)

    def own_pieces(self, core):
        pieces = [(pl.multiple_of(core * self.glob_own, 16), 0, self.glob_own)]
        for slot in range(self.slots):
            place = self.glob_all + slot * self.slot_all + core * self.slot_own
            pieces.append(
                (pl.multiple_of(place, 16), self.glob_own + slot * self.slot_own, self.slot_own)
            )
        return pieces

    def sweep(self, body, carry):
        def glob_step(tile, state):
            start = pl.multiple_of(tile * TILE, TILE)
            return body(start, pl.multiple_of(self.glob_base + start, 16), 0, state)

        def slot_step(tile, state):
            slot = tile // self.slot_tiles
            start = pl.multiple_of(self.glob_all + tile * TILE, TILE)
            place = self.small_base + tile * TILE + slot * self.small_width
            return body(start, pl.multiple_of(place, 16), 1 + slot, state)

        carry = lax.fori_loop(0, self.glob_tiles, glob_step, carry)
        return lax.fori_loop(0, self.slots * self.slot_tiles, slot_step, carry)

    def segments(self):
        return (
            (self.glob_base, self.glob_all, self.glob_width),
            (self.small_base, self.small_conv - self.small_width, self.small_width),
        )


def sigmoid(value):
    return 0.5 * jnp.tanh(0.5 * value) + 0.5


def rows_down(tile):
    return jnp.sum(tile.reshape(tile.shape[0] // 8, 8, tile.shape[1]), 0)


def widen(mask, lanes):
    return jnp.concatenate([mask] * (lanes // mask.shape[1]), 1)


def dot(left, right):
    return jnp.dot(left, right, preferred_element_type=F32)


def dot_nt(left, right):
    return lax.dot_general(left, right, (((1,), (1,)), ((), ())), preferred_element_type=F32)


def dot_tn(left, right):
    return lax.dot_general(left, right, (((0,), (0,)), ((), ())), preferred_element_type=F32)


def split_dot(left, right, nt=False):
    high = left.astype(BF16)
    low = (left - high.astype(F32)).astype(BF16)
    call = dot_nt if nt else dot
    return call(high, right) + call(low, right)


def entry_barrier(n, me, core):
    barrier = pltpu.get_barrier_semaphore()

    def greet(step, carry):
        pl.semaphore_signal(
            barrier, inc=1, device_id=(lax.rem(me + step, n), core), device_id_type=MESH
        )
        return carry

    lax.fori_loop(1, n, greet, 0)
    pl.semaphore_signal(barrier, inc=1, device_id=(me, 1 - core), device_id_type=MESH)
    pl.semaphore_wait(barrier, n)


class Spread:
    def __init__(self, n, me, core, source, slots, send, recv):
        self.n, self.me, self.core = n, me, core
        self.source, self.slots, self.send, self.recv = source, slots, send, recv

    def copy(self, step):
        return pltpu.make_async_remote_copy(
            src_ref=self.source,
            dst_ref=self.slots.at[self.me],
            send_sem=self.send.at[step],
            recv_sem=self.recv.at[step],
            device_id=(lax.rem(self.me + step, self.n), self.core),
            device_id_type=MESH,
        )

    def start(self):
        def begin(step, carry):
            self.copy(step).start()
            return carry

        lax.fori_loop(1, self.n, begin, 0)
        self.slots[pl.ds(self.me, 1)] = self.source[...][None]

    def wait(self):
        def end(step, carry):
            self.copy(step).wait()
            return carry

        lax.fori_loop(1, self.n, end, 0)


def to_partner(me, core, source, target, send, recv):
    return pltpu.make_async_remote_copy(
        src_ref=source,
        dst_ref=target,
        send_sem=send,
        recv_sem=recv,
        device_id=(me, 1 - core),
        device_id_type=MESH,
    )


def merge_moments(slots, n, lanes):
    def add(step, carry):
        total, count = carry
        return (total + slots[step, :, :lanes], count + slots[step, :, 2 * lanes : 2 * lanes + LANE])

    total, count = lax.fori_loop(
        0, n, add, (jnp.zeros((1, lanes), F32), jnp.zeros((1, LANE), F32))
    )
    wide_count = widen(count, lanes)
    mean = total / wide_count

    def spread(step, carry):
        own_count = widen(slots[step, :, 2 * lanes : 2 * lanes + LANE], lanes)
        gap = slots[step, :, :lanes] / own_count - mean
        return carry + slots[step, :, lanes : 2 * lanes] + own_count * gap * gap

    squares = lax.fori_loop(0, n, spread, jnp.zeros((1, lanes), F32))
    return mean, squares / wide_count, wide_count


def local_moments(plan, values, mask, which, count):
    lanes = plan.half

    def add(start, place, crop, carry):
        row = start if which == "all" else place
        tile = values[pl.ds(row, TILE), :] * widen(mask[pl.ds(start, TILE), :], lanes)
        return carry + rows_down(tile)

    total = jnp.sum(plan.sweep(add, jnp.zeros((8, lanes), F32)), 0, keepdims=True)
    mean = total / count

    def spread(start, place, crop, carry):
        row = start if which == "all" else place
        gap = (values[pl.ds(row, TILE), :] - mean) * widen(mask[pl.ds(start, TILE), :], lanes)
        return carry + rows_down(gap * gap)

    squares = jnp.sum(plan.sweep(spread, jnp.zeros((8, lanes), F32)), 0, keepdims=True)
    return total, squares


GAIN_ONE, SHIFT_ONE, GAIN_TWO, SHIFT_TWO, EXCITE_BIAS, SQUEEZE_BIAS, COUNT = range(7)
MEAN_ONE, INVERSE_ONE, MEAN_TWO, INVERSE_TWO, TOTAL = range(5)


def forward_kernel(
    plan,
    x_own,
    w_in,
    w_mid_hbm,
    k_out,
    w_in_hbm,
    vec,
    vec_three,
    mask,
    w_squeeze,
    w_excite,
    x_out,
    pre_one_out,
    act_one_out,
    pre_two_out,
    act_three_out,
    k_out_all,
    w_in_all,
    vec_three_all,
    stats,
    pooled_out,
    excite_out,
    squeeze_pre_out,
    x_all,
    pre_one,
    shifted,
    w_mid,
    pre_two,
    act_two,
    act_three,
    pay_one,
    slots_one,
    pay_two,
    slots_two,
    squeeze_send,
    squeeze_recv,
    local_sem,
    send_sem,
    recv_sem,
    spread_send,
    spread_recv,
):
    n, half, group = plan.dp, plan.half, plan.group
    me, core = lax.axis_index("dp"), lax.axis_index("rows")
    pieces = plan.own_pieces(core)
    entry_barrier(n, me, core)

    def local(source, target, index):
        copy = pltpu.make_async_copy(source, target, local_sem.at[index])
        copy.start()
        return copy

    def partner(source, target, index):
        copy = to_partner(me, core, source, target, send_sem.at[index], recv_sem.at[index])
        copy.start()
        return copy

    x_local, x_remote = [], []
    for index, (place, start, length) in enumerate(pieces):
        source = x_own.at[:, pl.ds(start, length), :]
        target = x_all.at[:, pl.ds(place, length), :]
        x_remote.append(partner(source, target, index))
        x_local.append(local(source, target, index))
    base = len(pieces)
    mid_copy = local(w_mid_hbm, w_mid, base)
    others = [
        local(k_out, k_out_all.at[core], base + 1),
        local(w_in_hbm, w_in_all.at[core], base + 2),
        local(vec_three, vec_three_all.at[core], base + 3),
    ]
    others += [
        partner(k_out, k_out_all.at[core], base),
        partner(w_in_hbm, w_in_all.at[core], base + 1),
        partner(vec_three, vec_three_all.at[core], base + 2),
    ]
    for side in range(2):
        shifted[side, : plan.glob_base, :] = jnp.zeros((plan.glob_base, 3 * group), BF16)
        shifted[side, plan.glob_base + plan.glob_all : plan.small_base, :] = jnp.zeros(
            (plan.glob_width, 3 * group), BF16
        )
        for slot in range(plan.slots):
            low = plan.small_base + slot * plan.slot_conv + plan.slot_all
            shifted[side, low : low + plan.small_width, :] = jnp.zeros(
                (plan.small_width, 3 * group), BF16
            )

    def product(owner):
        place = pl.multiple_of(owner * plan.glob_own, 16)
        rows = pl.ds(place, plan.glob_own)
        pre_one[rows, :] = dot(x_all[0, rows, :], w_in[0]) + dot(x_all[1, rows, :], w_in[1])
        places = [spot for spot, _, _ in plan.own_pieces(owner)[1:]]
        sides = [
            jnp.concatenate([x_all[side, pl.ds(spot, plan.slot_own), :] for spot in places], 0)
            for side in range(2)
        ]
        result = dot(sides[0], w_in[0]) + dot(sides[1], w_in[1])
        for slot, spot in enumerate(places):
            pre_one[pl.ds(spot, plan.slot_own), :] = result[
                slot * plan.slot_own : (slot + 1) * plan.slot_own
            ]

    for copy in x_local:
        copy.wait()
    product(core)
    for copy in x_remote:
        copy.wait()
    product(1 - core)
    saves = [
        local(x_all, x_out, base + 4),
        local(pre_one, pre_one_out, base + 5),
    ]

    chip_count = vec[COUNT : COUNT + 1, :]

    def statistics(values, which, pay, slots, index):
        total, squares = local_moments(plan, values, mask, which, chip_count)
        pay[:, :half] = total
        pay[:, half : 2 * half] = squares
        pay[:, 2 * half :] = chip_count[:, :LANE]
        spread = Spread(n, me, core, pay, slots, spread_send.at[index], spread_recv.at[index])
        spread.start()
        spread.wait()
        mean, variance, count = merge_moments(slots, n, half)
        return mean, lax.rsqrt(variance + EPSILON), count

    mean, inverse, count = statistics(pre_one, "all", pay_one, slots_one, 0)
    stats[...] = jnp.zeros_like(stats)
    stats[MEAN_ONE : MEAN_ONE + 1, :] = mean
    stats[INVERSE_ONE : INVERSE_ONE + 1, :] = inverse
    stats[TOTAL : TOTAL + 1, :] = count
    scale = inverse * vec[GAIN_ONE : GAIN_ONE + 1, :]
    shift = vec[SHIFT_ONE : SHIFT_ONE + 1, :]

    def activate_one(start, place, crop, carry):
        norm = (pre_one[pl.ds(start, TILE), :] - mean) * scale + shift
        act = norm * sigmoid(norm) * widen(mask[pl.ds(start, TILE), :], half)
        before = pltpu.roll(act, 1, 0)
        after = pltpu.roll(act, TILE - 1, 0)
        for tap, value in enumerate((before, act, after)):
            for side in range(2):
                shifted[side, pl.ds(place, TILE), tap * group : (tap + 1) * group] = value[
                    :, side * group : (side + 1) * group
                ].astype(BF16)
        return carry

    plan.sweep(activate_one, 0)
    for side in range(2):
        saves.append(
            local(
                shifted.at[side, :, group : 2 * group],
                act_one_out.at[:, side * group : (side + 1) * group],
                base + 6 + side,
            )
        )
    mid_copy.wait()

    for low, length, width in plan.segments():
        for side in range(2):
            lanes = slice(side * group, (side + 1) * group)
            block = length // 2
            for part in range(2):
                at = low + part * block
                total = None
                for tap in range(3):
                    first = at + (tap - 1) * width
                    term = dot(shifted[side, first : first + block, :], w_mid[tap, :, lanes])
                    total = term if total is None else total + term
                pre_two[at : at + block, lanes] = total
    saves.append(local(pre_two, pre_two_out, base + 8))

    mean_two, inverse_two, _ = statistics(pre_two, "conv", pay_two, slots_two, 1)
    stats[MEAN_TWO : MEAN_TWO + 1, :] = mean_two
    stats[INVERSE_TWO : INVERSE_TWO + 1, :] = inverse_two
    scale_two = inverse_two * vec[GAIN_TWO : GAIN_TWO + 1, :]
    shift_two = vec[SHIFT_TWO : SHIFT_TWO + 1, :]
    pooled_out[...] = jnp.zeros_like(pooled_out)

    def activate_two(start, place, crop, carry):
        norm = (pre_two[pl.ds(place, TILE), :] - mean_two) * scale_two + shift_two
        act = norm * sigmoid(norm) * widen(mask[pl.ds(start, TILE), :], half)
        act_two[pl.ds(start, TILE), :] = act
        pooled_out[pl.ds(crop, 1), :] += jnp.sum(act, 0, keepdims=True)
        return carry

    plan.sweep(activate_two, 0)
    pooled_out[:1, :] = pooled_out[:1, :] * (1.0 / plan.glob_area)
    pooled_out[1:, :] = pooled_out[1:, :] * (1.0 / plan.slot_area)
    part = split_dot(pooled_out[...], w_squeeze[...])
    squeeze_send[...] = part
    swap = partner(squeeze_send, squeeze_recv, base + 3)
    swap.wait()
    squeeze_pre = part + squeeze_recv[...] + vec[SQUEEZE_BIAS : SQUEEZE_BIAS + 1, :group]
    squeeze_pre_out[...] = squeeze_pre
    squeezed = squeeze_pre * sigmoid(squeeze_pre)
    excite_out[...] = sigmoid(
        split_dot(squeezed, w_excite[...]) + vec[EXCITE_BIAS : EXCITE_BIAS + 1, :]
    )

    def activate_three(start, place, crop, carry):
        act_three[core, pl.ds(start, TILE), :] = (
            act_two[pl.ds(start, TILE), :] * excite_out[pl.ds(crop, 1), :]
        ).astype(BF16)
        return carry

    plan.sweep(activate_three, 0)
    exchange = partner(act_three.at[core], act_three.at[core], base + 4)
    exchange.wait()
    saves.append(local(act_three, act_three_out, base + 9))
    for copy in others + saves:
        copy.wait()


def forward(plan, x_own, w_in, w_mid, k_out, vec, vec_three, mask, w_squeeze, w_excite):
    n, half, group = plan.dp, plan.half, plan.group
    shape = jax.ShapeDtypeStruct
    copies = 1 + plan.slots
    pay = 2 * half + LANE
    return pl.pallas_call(
        functools.partial(forward_kernel, plan),
        out_shape=(
            shape((2, plan.all, half), BF16),
            shape((plan.all, half), F32),
            shape((plan.conv, half), BF16),
            shape((plan.conv, half), F32),
            shape((2, plan.all, half), BF16),
            shape((2,) + k_out.shape, BF16),
            shape((2,) + w_in.shape, BF16),
            shape((2,) + vec_three.shape, F32),
            shape((8, half), F32),
            shape((plan.slot_rows, half), F32),
            shape((plan.slot_rows, half), F32),
            shape((plan.slot_rows, group), F32),
        ),
        in_specs=[ANY, VMEM, ANY, ANY, ANY, VMEM, ANY, VMEM, VMEM, VMEM],
        out_specs=(ANY,) * 8 + (VMEM,) * 4,
        scratch_shapes=[
            pltpu.VMEM((2, plan.all, half), BF16),
            pltpu.VMEM((plan.all, half), F32),
            pltpu.VMEM((2, plan.conv, 3 * group), BF16),
            pltpu.VMEM(w_mid.shape, BF16),
            pltpu.VMEM((plan.conv, half), F32),
            pltpu.VMEM((plan.all, half), F32),
            pltpu.VMEM((2, plan.all, half), BF16),
            pltpu.VMEM((1, pay), F32),
            pltpu.VMEM((n, 1, pay), F32),
            pltpu.VMEM((1, pay), F32),
            pltpu.VMEM((n, 1, pay), F32),
            pltpu.VMEM((plan.slot_rows, group), F32),
            pltpu.VMEM((plan.slot_rows, group), F32),
            pltpu.SemaphoreType.DMA((copies + 10,)),
            pltpu.SemaphoreType.DMA((copies + 5,)),
            pltpu.SemaphoreType.DMA((copies + 5,)),
            pltpu.SemaphoreType.DMA((2, n)),
            pltpu.SemaphoreType.DMA((2, n)),
        ],
        compiler_params=pltpu.CompilerParams(
            collective_id=0, has_side_effects=True, vmem_limit_bytes=VMEM_BYTES
        ),
    )(x_own, w_in, w_mid, k_out, w_in, vec, vec_three, mask, w_squeeze, w_excite)


def halves(rows, plan):
    real = plan.half_real
    pad = ((0, 0), (0, plan.half - real))
    return jnp.stack([jnp.pad(rows[:, :real], pad), jnp.pad(rows[:, real:], pad)], 0)


def own_rows(glob, small, plan):
    glob = jnp.pad(glob[0], ((0, 0), (0, plan.glob_width - plan.glob_side), (0, 0)))
    small = jnp.pad(small, ((0, 0), (0, 0), (0, plan.small_width - plan.small_side), (0, 0)))
    return halves(
        jnp.concatenate(
            [glob.reshape(-1, plan.channels), small.reshape(-1, plan.channels)], 0
        ),
        plan,
    )


def group_lanes(array, plan):
    pad = ((0, 0),) * (array.ndim - 1) + ((0, plan.group - plan.width),)
    return jnp.concatenate(
        [jnp.pad(array[..., : plan.width], pad), jnp.pad(array[..., plan.width :], pad)], -1
    )


def group_rows(array, plan):
    pieces = array.reshape(-1, plan.width, array.shape[1])
    pieces = jnp.pad(pieces, ((0, 0), (0, plan.group - plan.width), (0, 0)))
    return pieces.reshape(-1, array.shape[1])


def pad_to(array, *sizes):
    return jnp.pad(array, [(0, size - have) for size, have in zip(sizes, array.shape)])


def row_masks(plan, small_count):
    glob = (lax.iota(jnp.int32, plan.glob_width) < plan.glob_side).astype(F32)
    small = (lax.iota(jnp.int32, plan.small_width) < plan.small_side).astype(F32)
    live = (lax.iota(jnp.int32, plan.slots) < small_count[0]).astype(F32)

    def build(times):
        first = jnp.tile(glob, times * plan.glob_height)
        rest = (live[:, None] * jnp.tile(small, times * plan.small_height)[None]).reshape(-1)
        return jnp.broadcast_to(jnp.concatenate([first, rest])[:, None], (first.size + rest.size, LANE))

    count = plan.glob_area + plan.slot_area * small_count[0].astype(F32)
    return build(2), build(1), count
def prepare(
    dp,
    glob_in,
    small_in,
    small_count,
    kernel_in,
    kernel_mid,
    kernel_out,
    squeeze_weight,
    squeeze_bias,
    excite_weight,
    excite_bias,
    gain_first,
    shift_first,
    gain_second,
    shift_second,
    gain_third,
    shift_third,
    glob_cotangent,
    small_cotangent,
):
    plan = Plan(glob_in.shape, small_in.shape, kernel_mid.shape[2], dp)
    half, group, real = plan.half, plan.group, plan.half_real
    x_own = own_rows(glob_in, small_in, plan)
    cot_own = own_rows(glob_cotangent, small_cotangent, plan)
    w_in = group_lanes(kernel_in, plan)
    w_in = jnp.stack([pad_to(w_in[:real], half, half), pad_to(w_in[real:], half, half)], 0)
    w_mid = pad_to(group_lanes(kernel_mid, plan), 3, 3, group, half).reshape(3, 3 * group, half)
    k_out = group_rows(pad_to(kernel_out, plan.channels, half), plan).reshape(2, half, half)
    w_squeeze = group_rows(pad_to(squeeze_weight, real, group), plan)
    w_excite = pad_to(group_lanes(excite_weight, plan), group, half)
    mask_all, mask_own, count = row_masks(plan, small_count)

    def grouped(vector):
        return group_lanes(vector.astype(F32)[None], plan)

    vec = jnp.concatenate(
        [
            grouped(gain_first),
            grouped(shift_first),
            grouped(gain_second),
            grouped(shift_second),
            grouped(excite_bias),
            pad_to(squeeze_bias.astype(F32)[None], 1, half),
            jnp.full((1, half), count, F32),
            jnp.zeros((1, half), F32),
        ],
        0,
    )
    vec_three = pad_to(jnp.stack([gain_third, shift_third], 0).astype(F32), 8, half)
    return plan, x_own, cot_own, w_in, w_mid, k_out, w_squeeze, w_excite, mask_all, mask_own, vec, vec_three
def own_steps(plan, body, carry):
    step = 32

    def run(tile, state):
        return body(pl.multiple_of(tile * step, step), step, state)

    return lax.fori_loop(0, plan.own // step, run, carry)


def merge_two(first, second, lanes):
    sums = [part[:, :lanes] for part in (first, second)]
    squares = [part[:, lanes : 2 * lanes] for part in (first, second)]
    counts = [widen(part[:, 2 * lanes :], lanes) for part in (first, second)]
    total = sums[0] + sums[1]
    count = counts[0] + counts[1]
    mean = total / count
    spread = squares[0] + squares[1]
    for index in range(2):
        gap = sums[index] / counts[index] - mean
        spread = spread + counts[index] * gap * gap
    return total, spread, count


def third_kernel(
    plan,
    act_three_hbm,
    k_out_hbm,
    x_own,
    cot_own,
    mask,
    vec,
    vec_three,
    result_out,
    grad_summed_out,
    grad_pre_three_out,
    sums_out,
    act_three,
    k_out,
    pre_three,
    grad_summed,
    grad_pre_three,
    pay,
    pair,
    chip,
    slots,
    finals,
    pay_back,
    pair_back,
    chip_back,
    slots_back,
    finals_back,
    local_sem,
    send_sem,
    recv_sem,
    spread_send,
    spread_recv,
):
    n, half = plan.dp, plan.half
    me, core = lax.axis_index("dp"), lax.axis_index("rows")
    pieces = plan.own_pieces(core)
    entry_barrier(n, me, core)

    def local(source, target, index):
        copy = pltpu.make_async_copy(source, target, local_sem.at[index])
        copy.start()
        return copy

    def partner(source, target, index):
        copy = to_partner(me, core, source, target, send_sem.at[index], recv_sem.at[index])
        copy.start()
        return copy

    loads = [
        local(
            act_three_hbm.at[:, pl.ds(place, length), :],
            act_three.at[:, pl.ds(start, length), :],
            index,
        )
        for index, (place, start, length) in enumerate(pieces)
    ]
    base = len(pieces)
    loads.append(local(k_out_hbm, k_out, base))
    for copy in loads:
        copy.wait()
    own_count = 0.5 * vec[COUNT : COUNT + 1, :]

    block = plan.own // 2
    for side in range(2):

        def product(part, carry, side=side):
            rows = pl.ds(pl.multiple_of(part * block, 16), block)
            pre_three[side, rows, :] = dot(act_three[0, rows, :], k_out[side, 0]) + dot(
                act_three[1, rows, :], k_out[side, 1]
            )
            return carry

        lax.fori_loop(0, 2, product, 0)

    for side in range(2):

        def add(row, step, carry, side=side):
            rows = pl.ds(row, step)
            return carry + rows_down(pre_three[side, rows, :] * widen(mask[rows, :], half))

        total = jnp.sum(own_steps(plan, add, jnp.zeros((8, half), F32)), 0, keepdims=True)
        mean = total / own_count

        def spread(row, step, carry, side=side, mean=mean):
            rows = pl.ds(row, step)
            gap = (pre_three[side, rows, :] - mean) * widen(mask[rows, :], half)
            return carry + rows_down(gap * gap)

        squares = jnp.sum(own_steps(plan, spread, jnp.zeros((8, half), F32)), 0, keepdims=True)
        pay[side, :, :half] = total
        pay[side, :, half : 2 * half] = squares
        pay[side, :, 2 * half :] = own_count[:, :LANE]
    partner(pay.at[1 - core], pair, 0).wait()
    total, squares, count = merge_two(pay[core], pair[...], half)
    chip[:, :half] = total
    chip[:, half : 2 * half] = squares
    chip[:, 2 * half :] = count[:, :LANE]
    exchange = Spread(n, me, core, chip, slots, spread_send.at[0], spread_recv.at[0])
    exchange.start()
    exchange.wait()
    mean, variance, full_count = merge_moments(slots, n, half)
    finals[core, :, :half] = mean
    finals[core, :, half:] = lax.rsqrt(variance + EPSILON)
    partner(finals.at[core], finals.at[core], 1).wait()

    for side in range(2):
        mean = finals[side, :, :half]
        inverse = finals[side, :, half:]
        gain = vec_three[side, :1, :]
        shift = vec_three[side, 1:2, :]

        def outer(row, step, carry, side=side, mean=mean, inverse=inverse, gain=gain, shift=shift):
            rows = pl.ds(row, step)
            seen = widen(mask[rows, :], half)
            normed = (pre_three[side, rows, :] - mean) * inverse
            summed = normed * gain + shift + x_own[side, rows, :].astype(F32)
            sigma = sigmoid(summed)
            result_out[side, rows, :] = (seen * summed * sigma).astype(BF16)
            slope = sigma * (1.0 + summed * (1.0 - sigma))
            grad = cot_own[side, rows, :].astype(F32) * seen * slope
            grad_summed[side, rows, :] = grad
            grad_summed_out[side, rows, :] = grad.astype(BF16)
            return carry[0] + rows_down(grad), carry[1] + rows_down(grad * normed)

        zero = jnp.zeros((8, half), F32)
        shift_sum, gain_sum = own_steps(plan, outer, (zero, zero))
        pay_back[side, :, :half] = jnp.sum(shift_sum, 0, keepdims=True)
        pay_back[side, :, half:] = jnp.sum(gain_sum, 0, keepdims=True)
    partner(pay_back.at[1 - core], pair_back, 2).wait()
    chip_back[...] = pay_back[core] + pair_back[...]
    exchange = Spread(n, me, core, chip_back, slots_back, spread_send.at[1], spread_recv.at[1])
    exchange.start()
    exchange.wait()

    finals_back[core] = gather_sum(slots_back, n, 2 * half)
    partner(finals_back.at[core], finals_back.at[core], 3).wait()
    copies = []
    for side in range(2):
        mean = finals[side, :, :half]
        inverse = finals[side, :, half:]
        shift_sum = finals_back[side, :, :half]
        gain_sum = finals_back[side, :, half:]
        sums_out[side] = jnp.concatenate([shift_sum, gain_sum, jnp.zeros((6, half), F32)], 0)
        scale = vec_three[side, :1, :] * inverse
        shift_mean = shift_sum / full_count
        gain_mean = gain_sum / full_count

        def inner(
            row, step, carry, side=side, mean=mean, inverse=inverse, scale=scale,
            shift_mean=shift_mean, gain_mean=gain_mean
        ):
            rows = pl.ds(row, step)
            normed = (pre_three[side, rows, :] - mean) * inverse
            grad = scale * (grad_summed[side, rows, :] - shift_mean - normed * gain_mean)
            grad_pre_three[side, rows, :] = (grad * widen(mask[rows, :], half)).astype(BF16)
            return carry

        own_steps(plan, inner, 0)
        for index, (place, start, length) in enumerate(pieces):
            source = grad_pre_three.at[side, pl.ds(start, length), :]
            target = grad_pre_three_out.at[side, pl.ds(place, length), :]
            copies.append(partner(source, target, 4 + side * base + index))
            copies.append(local(source, target, base + 1 + side * base + index))
    for copy in copies:
        copy.wait()


def gather_sum(slots, n, lanes):
    def add(step, carry):
        return carry + slots[step]

    return lax.fori_loop(0, n, add, jnp.zeros((1, lanes), F32))


def third(plan, act_three, k_out_all, x_own, cot_own, mask, vec, vec_three):
    n, half = plan.dp, plan.half
    shape = jax.ShapeDtypeStruct
    pieces = 1 + plan.slots
    pay = 2 * half + LANE
    own = (2, plan.own, half)
    return pl.pallas_call(
        functools.partial(third_kernel, plan),
        out_shape=(
            shape(own, BF16),
            shape(own, BF16),
            shape((2, plan.all, half), BF16),
            shape((2, 8, half), F32),
        ),
        in_specs=[ANY, ANY, VMEM, VMEM, VMEM, VMEM, VMEM],
        out_specs=(VMEM, VMEM, ANY, VMEM),
        scratch_shapes=[
            pltpu.VMEM(own, BF16),
            pltpu.VMEM(k_out_all.shape, BF16),
            pltpu.VMEM(own, F32),
            pltpu.VMEM(own, F32),
            pltpu.VMEM(own, BF16),
            pltpu.VMEM((2, 1, pay), F32),
            pltpu.VMEM((1, pay), F32),
            pltpu.VMEM((1, pay), F32),
            pltpu.VMEM((n, 1, pay), F32),
            pltpu.VMEM((2, 1, 2 * half), F32),
            pltpu.VMEM((2, 1, 2 * half), F32),
            pltpu.VMEM((1, 2 * half), F32),
            pltpu.VMEM((1, 2 * half), F32),
            pltpu.VMEM((n, 1, 2 * half), F32),
            pltpu.VMEM((2, 1, 2 * half), F32),
            pltpu.SemaphoreType.DMA((3 * pieces + 1,)),
            pltpu.SemaphoreType.DMA((2 * pieces + 4,)),
            pltpu.SemaphoreType.DMA((2 * pieces + 4,)),
            pltpu.SemaphoreType.DMA((2, n)),
            pltpu.SemaphoreType.DMA((2, n)),
        ],
        compiler_params=pltpu.CompilerParams(
            collective_id=1, has_side_effects=True, vmem_limit_bytes=VMEM_BYTES
        ),
    )(act_three, k_out_all, x_own, cot_own, mask, vec, vec_three)


class Steps:
    def __init__(self, n, me, core):
        bits = n.bit_length() - 1
        self.halvings = min(bits, 4)
        self.shards = 2**self.halvings
        self.doublings = bits - self.halvings
        self.bit, self.partner = [], []
        for step in range(bits):
            first, second = 2**step, 2 ** (step + 1 - 2 * (step % 2))
            if step >= 2 or bits < 2:
                second = first
            distance = first + (second - first) * core
            bit = lax.rem(me // distance, 2)
            self.bit.append(bit)
            self.partner.append((me + distance * (1 - 2 * bit), core))


class Reduction:
    def __init__(self, steps, rows, work, land, gathered, send, recv, local):
        self.steps, self.rows = steps, rows
        self.work, self.land, self.gathered = work, land, gathered
        self.send, self.recv, self.local = send, recv, local
        self.shard = rows // steps.shards
        self.step = 0
        self.at = 0
        self.pending = None
        self.sending = True

    def remote(self, source, target, step):
        return pltpu.make_async_remote_copy(
            src_ref=source,
            dst_ref=target,
            send_sem=self.send.at[self.slot],
            recv_sem=self.recv.at[self.slot],
            device_id=self.steps.partner[step],
            device_id_type=MESH,
        )

    def reduce_last(self):
        return self.steps.halvings + self.steps.doublings

    def place(self, row):
        return row if isinstance(row, int) else pl.multiple_of(row, 16)

    def begin(self):
        step = self.step
        self.slot = step
        if step < self.steps.halvings:
            length = self.rows >> (step + 1)
            bit = self.steps.bit[step]
            self.keep = self.at + bit * length
            gone = self.at + (1 - bit) * length
            low = self.rows - 2 * length
            self.now = (self.land.at[pl.ds(low, length), :], length)
            source = self.work.at[pl.ds(self.place(gone), length), :]
            self.pending = self.remote(source, self.now[0], step)
        else:
            low = self.rows - self.shard + (step - self.steps.halvings) * self.shard
            self.keep = self.at
            self.now = (self.land.at[pl.ds(low, self.shard), :], self.shard)
            source = self.work.at[pl.ds(self.place(self.at), self.shard), :]
            self.pending = self.remote(source, self.now[0], step)
        self.pending.start()

    def end(self):
        self.pending.wait()
        self.pending = None
        landed, length = self.now
        size = 48 if self.shard % 48 == 0 else 16

        def add(tile, carry):
            there = pl.ds(self.place(self.keep + tile * size), size)
            here = pl.ds(pl.multiple_of(tile * size, 16), size)
            total = self.work[there, :].astype(F32) + landed[here, :].astype(F32)
            self.work[there, :] = total.astype(BF16)
            return carry

        lax.fori_loop(0, length // size, add, 0)
        self.at = self.keep
        self.step += 1

    def advance(self):
        if self.pending is not None:
            self.end()
        if self.step < self.reduce_last():
            self.begin()

    def reduced(self):
        return self.step == self.reduce_last()


class Gathering:
    def __init__(self, steps, rows, at, shard_ref, gathered, send, recv, local):
        self.steps, self.rows = steps, rows
        self.at, self.shard_ref, self.gathered = at, shard_ref, gathered
        self.send, self.recv, self.local = send, recv, local
        self.shard = rows // steps.shards
        self.step = steps.halvings - 1
        self.length = self.shard
        self.pending = None
        self.first = None

    def advance(self):
        if self.pending is not None:
            self.pending.wait()
            self.pending = None
            self.at = self.at - self.steps.bit[self.step] * self.length
            self.length *= 2
            self.step -= 1
        if self.step >= 0:
            rows = pl.ds(pl.multiple_of(self.at, 16), self.length)
            target = self.gathered.at[rows, :]
            if self.first is None:
                self.first = pltpu.make_async_copy(self.shard_ref, target, self.local)
                self.first.start()
                self.first.wait()
                source = self.shard_ref
            else:
                source = target
            self.pending = pltpu.make_async_remote_copy(
                src_ref=source,
                dst_ref=target,
                send_sem=self.send.at[self.step],
                recv_sem=self.recv.at[self.step],
                device_id=self.steps.partner[self.step],
                device_id_type=MESH,
            )
            self.pending.start()

    def done(self):
        return self.step < 0 and self.pending is None


def shard_place(steps, rows):
    place = 0
    for step in range(steps.halvings):
        place = place + steps.bit[step] * (rows >> (step + 1))
    return place


def land_rows(n, rows):
    bits = n.bit_length() - 1
    halvings = min(bits, 4)
    shard = rows >> halvings
    return rows - shard + max(bits - halvings, 0) * shard


def silu_slope(value, sigma):
    return sigma * (1.0 + value * (1.0 - sigma))
SHIFT_TWO_SUM, GAIN_TWO_SUM, EXCITE_SUM, SQUEEZE_SUM = range(4)
SHIFT_ONE_SUM, GAIN_ONE_SUM = range(2)


def second_kernel(
    plan,
    grad_pre_three_hbm,
    act_three_hbm,
    k_out_hbm,
    pre_two_hbm,
    stats,
    vec,
    mask,
    pooled,
    excite,
    squeeze_pre,
    w_squeeze,
    w_excite,
    shard_out,
    grad_norm_out,
    grad_excite_out,
    grad_squeeze_out,
    sums_out,
    grad_pre_three,
    act_three,
    k_out,
    pre_two,
    grad_act,
    slopes,
    work,
    land,
    grad_excite,
    squeeze_send,
    squeeze_recv,
    grad_pooled,
    factors,
    factor_slots,
    pay,
    slots,
    local_sem,
    pair_send,
    pair_recv,
    spread_send,
    spread_recv,
    reduce_send,
    reduce_recv,
):
    n, half, group = plan.dp, plan.half, plan.group
    me, core = lax.axis_index("dp"), lax.axis_index("rows")
    entry_barrier(n, me, core)

    def local(source, target, index):
        copy = pltpu.make_async_copy(source, target, local_sem.at[index])
        copy.start()
        return copy

    loads = [
        local(grad_pre_three_hbm, grad_pre_three, 0),
        local(act_three_hbm, act_three, 1),
        local(k_out_hbm.at[:, core], k_out, 2),
        local(pre_two_hbm, pre_two, 3),
    ]
    loads[0].wait()
    loads[1].wait()
    for side in range(2):
        for part in range(2):
            lanes = slice(part * group, (part + 1) * group)
            low = side * half + part * group
            work[low : low + group, :] = dot_tn(
                act_three[side, :, lanes], grad_pre_three[core]
            ).astype(BF16)
    steps = Steps(n, me, core)
    reduction = Reduction(steps, 2 * half, work, land, None, reduce_send, reduce_recv, None)
    reduction.advance()
    loads[2].wait()

    block = plan.all // 4

    def product(part, carry):
        rows = pl.ds(pl.multiple_of(part * block, 16), block)
        grad_act[rows, :] = dot_nt(grad_pre_three[0, rows, :], k_out[0]) + dot_nt(
            grad_pre_three[1, rows, :], k_out[1]
        )
        return carry

    lax.fori_loop(0, 4, product, 0)
    loads[3].wait()
    reduction.advance()

    mean = stats[MEAN_TWO : MEAN_TWO + 1, :]
    inverse = stats[INVERSE_TWO : INVERSE_TWO + 1, :]
    count = stats[TOTAL : TOTAL + 1, :]
    gain = vec[GAIN_TWO : GAIN_TWO + 1, :]
    shift = vec[SHIFT_TWO : SHIFT_TWO + 1, :]
    grad_excite[...] = jnp.zeros_like(grad_excite)

    def excitation(start, place, crop, carry):
        rows = pl.ds(start, TILE)
        norm = (pre_two[pl.ds(place, TILE), :] - mean) * (inverse * gain) + shift
        sigma = sigmoid(norm)
        seen = widen(mask[rows, :], half)
        slopes[rows, :] = silu_slope(norm, sigma) * seen
        term = grad_act[rows, :] * (norm * sigma * seen)
        grad_excite[pl.ds(crop, 1), :] += jnp.sum(term, 0, keepdims=True)
        return carry

    plan.sweep(excitation, 0)
    level = excite[...]
    grad_excite_pre = grad_excite[...] * level * (1.0 - level)
    part = split_dot(grad_excite_pre, w_excite[...], nt=True)
    squeeze_send[...] = part
    swap = to_partner(me, core, squeeze_send, squeeze_recv, pair_send.at[0], pair_recv.at[0])
    swap.start()
    reduction.advance()
    swap.wait()
    before = squeeze_pre[...]
    sigma = sigmoid(before)
    squeezed = before * sigma
    grad_squeeze_pre = (part + squeeze_recv[...]) * silu_slope(before, sigma)
    back = split_dot(grad_squeeze_pre, w_squeeze[...], nt=True)
    crop_row = lax.broadcasted_iota(jnp.int32, back.shape, 0)
    area = jnp.where(crop_row == 0, 1.0 / plan.glob_area, 1.0 / plan.slot_area)
    grad_pooled[...] = back * area
    deep = plan.slot_rows
    factors[:deep, :group] = squeezed.astype(BF16)
    factors[:deep, group:] = grad_excite_pre.astype(BF16)
    factors[deep:, :group] = grad_squeeze_pre.astype(BF16)
    factors[deep:, group:] = pooled[...].astype(BF16)
    factor_spread = Spread(n, me, core, factors, factor_slots, spread_send.at[0], spread_recv.at[0])
    factor_spread.start()

    def gradient(start, place, crop, carry):
        rows = pl.ds(start, TILE)
        incoming = grad_act[rows, :] * excite[pl.ds(crop, 1), :] + grad_pooled[pl.ds(crop, 1), :]
        grad = incoming * slopes[rows, :]
        grad_act[rows, :] = grad
        normed = (pre_two[pl.ds(place, TILE), :] - mean) * inverse
        return carry[0] + rows_down(grad), carry[1] + rows_down(grad * normed)

    zero = jnp.zeros((8, half), F32)
    shift_sum, gain_sum = plan.sweep(gradient, (zero, zero))
    save = local(grad_act, grad_norm_out, 4)
    pay[:, :half] = jnp.sum(shift_sum, 0, keepdims=True)
    pay[:, half:] = jnp.sum(gain_sum, 0, keepdims=True)
    spread = Spread(n, me, core, pay, slots, spread_send.at[1], spread_recv.at[1])
    spread.start()
    while not reduction.reduced():
        reduction.advance()
    shard = reduction.shard
    store = local(work.at[pl.ds(pl.multiple_of(reduction.at, 16), shard), :], shard_out, 5)
    factor_spread.wait()
    left = factor_slots[:, :, :group].reshape(n * 2 * deep, group)
    right = factor_slots[:, :, group:].reshape(n * 2 * deep, half)
    upper = lax.broadcasted_iota(jnp.int32, left.shape, 0) % (2 * deep) < deep
    zeros = jnp.zeros_like(left)
    excite_left = jnp.where(upper, left, zeros)
    squeeze_left = jnp.where(upper, zeros, left)
    grad_excite_out[...] = dot_tn(excite_left, right)
    grad_squeeze_out[...] = dot_tn(right, squeeze_left)
    wide_upper = lax.broadcasted_iota(jnp.int32, right.shape, 0) % (2 * deep) < deep
    excite_bias = jnp.sum(jnp.where(wide_upper, right.astype(F32), 0.0), 0, keepdims=True)
    squeeze_bias = jnp.sum(squeeze_left.astype(F32), 0, keepdims=True)
    spread.wait()
    totals = gather_sum(slots, n, 2 * half)
    sums_out[...] = jnp.zeros_like(sums_out)
    sums_out[SHIFT_TWO_SUM : SHIFT_TWO_SUM + 1, :] = totals[:, :half]
    sums_out[GAIN_TWO_SUM : GAIN_TWO_SUM + 1, :] = totals[:, half:]
    sums_out[EXCITE_SUM : EXCITE_SUM + 1, :] = excite_bias
    sums_out[SQUEEZE_SUM : SQUEEZE_SUM + 1, :group] = squeeze_bias
    save.wait()
    store.wait()


def second(
    plan, grad_pre_three, act_three, k_out_all, pre_two, stats, vec, mask, pooled, excite,
    squeeze_pre, w_squeeze, w_excite
):
    n, half, group = plan.dp, plan.half, plan.group
    shape = jax.ShapeDtypeStruct
    rows = 2 * half
    shard = rows >> min(n.bit_length() - 1, 4)
    deep = plan.slot_rows
    bits = n.bit_length() - 1
    return pl.pallas_call(
        functools.partial(second_kernel, plan),
        out_shape=(
            shape((shard, half), BF16),
            shape((plan.all, half), F32),
            shape((group, half), F32),
            shape((half, group), F32),
            shape((8, half), F32),
        ),
        in_specs=[ANY] * 4 + [VMEM] * 8,
        out_specs=(ANY, ANY, VMEM, VMEM, VMEM),
        scratch_shapes=[
            pltpu.VMEM((2, plan.all, half), BF16),
            pltpu.VMEM((2, plan.all, half), BF16),
            pltpu.VMEM((2, half, half), BF16),
            pltpu.VMEM((plan.conv, half), F32),
            pltpu.VMEM((plan.all, half), F32),
            pltpu.VMEM((plan.all, half), F32),
            pltpu.VMEM((rows, half), BF16),
            pltpu.VMEM((land_rows(n, rows), half), BF16),
            pltpu.VMEM((deep, half), F32),
            pltpu.VMEM((deep, group), F32),
            pltpu.VMEM((deep, group), F32),
            pltpu.VMEM((deep, half), F32),
            pltpu.VMEM((2 * deep, group + half), BF16),
            pltpu.VMEM((n, 2 * deep, group + half), BF16),
            pltpu.VMEM((1, 2 * half), F32),
            pltpu.VMEM((n, 1, 2 * half), F32),
            pltpu.SemaphoreType.DMA((6,)),
            pltpu.SemaphoreType.DMA((1,)),
            pltpu.SemaphoreType.DMA((1,)),
            pltpu.SemaphoreType.DMA((2, n)),
            pltpu.SemaphoreType.DMA((2, n)),
            pltpu.SemaphoreType.DMA((bits,)),
            pltpu.SemaphoreType.DMA((bits,)),
        ],
        compiler_params=pltpu.CompilerParams(
            collective_id=2, has_side_effects=True, vmem_limit_bytes=VMEM_BYTES
        ),
    )(
        grad_pre_three, act_three, k_out_all, pre_two, stats, vec, mask, pooled, excite,
        squeeze_pre, w_squeeze, w_excite
    )


def first_kernel(
    plan,
    shard_out_hbm,
    grad_norm_hbm,
    pre_two_hbm,
    pre_one_hbm,
    act_one_hbm,
    x_hbm,
    w_mid_hbm,
    w_in_hbm,
    stats,
    vec,
    sums_two,
    mask,
    gathered_out,
    gathered_mid,
    gathered_in,
    grad_inputs_out,
    sums_out,
    flat,
    conv_rows,
    shifted,
    act_one,
    w_mid,
    grad_pre_one,
    grad_other,
    w_in,
    shard_out,
    work_mid,
    land_mid,
    work_in,
    land_in,
    pay,
    slots,
    local_sem,
    pair_send,
    pair_recv,
    spread_send,
    spread_recv,
    reduce_send,
    reduce_recv,
    gather_send,
    gather_recv,
):
    n, half, group = plan.dp, plan.half, plan.group
    me, core = lax.axis_index("dp"), lax.axis_index("rows")
    entry_barrier(n, me, core)

    def local(source, target, index):
        copy = pltpu.make_async_copy(source, target, local_sem.at[index])
        copy.start()
        return copy

    load_norm = local(grad_norm_hbm, flat, 0)
    load_two = local(pre_two_hbm, conv_rows, 1)
    load_shard = local(shard_out_hbm, shard_out, 2)
    load_act = local(act_one_hbm, act_one, 3)
    load_mid = local(w_mid_hbm, w_mid, 4)
    load_in = local(w_in_hbm, w_in, 5)
    steps = Steps(n, me, core)
    rows_out = gathered_out.shape[0]
    load_shard.wait()
    chains = [
        Gathering(
            steps,
            rows_out,
            shard_place(steps, rows_out),
            shard_out,
            gathered_out,
            gather_send.at[0],
            gather_recv.at[0],
            local_sem.at[6],
        )
    ]
    chains[0].advance()
    for side in range(2):
        shifted[side, : plan.glob_base, :] = jnp.zeros((plan.glob_base, 3 * group), BF16)
        shifted[side, plan.glob_base + plan.glob_all : plan.small_base, :] = jnp.zeros(
            (plan.glob_width, 3 * group), BF16
        )
        for slot in range(plan.slots):
            low = plan.small_base + slot * plan.slot_conv + plan.slot_all
            shifted[side, low : low + plan.small_width, :] = jnp.zeros(
                (plan.small_width, 3 * group), BF16
            )
    mean = stats[MEAN_TWO : MEAN_TWO + 1, :]
    inverse = stats[INVERSE_TWO : INVERSE_TWO + 1, :]
    count = stats[TOTAL : TOTAL + 1, :]
    scale = vec[GAIN_TWO : GAIN_TWO + 1, :] * inverse
    shift_mean = sums_two[SHIFT_TWO_SUM : SHIFT_TWO_SUM + 1, :] / count
    gain_mean = sums_two[GAIN_TWO_SUM : GAIN_TWO_SUM + 1, :] / count * inverse
    load_norm.wait()
    load_two.wait()

    def into_two(start, place, crop, carry):
        rows = pl.ds(start, TILE)
        centered = conv_rows[pl.ds(place, TILE), :] - mean
        grad = scale * (flat[rows, :] - shift_mean - centered * gain_mean)
        grad = grad * widen(mask[rows, :], half)
        after = pltpu.roll(grad, TILE - 1, 0)
        before = pltpu.roll(grad, 1, 0)
        for tap, value in enumerate((after, grad, before)):
            for side in range(2):
                shifted[side, pl.ds(place, TILE), tap * group : (tap + 1) * group] = value[
                    :, side * group : (side + 1) * group
                ].astype(BF16)
        return carry

    plan.sweep(into_two, 0)
    load_one = local(pre_one_hbm, flat, 0)
    load_act.wait()
    chains[0].advance()

    def advance_all():
        for index, chain in enumerate(chains):
            if isinstance(chain, Reduction) and chain.reduced():
                place = pl.ds(pl.multiple_of(chain.at, 16), chain.shard)
                chains[index] = Gathering(
                    steps,
                    chain.rows,
                    chain.at,
                    chain.work.at[place, :],
                    chain.gathered,
                    gather_send.at[index],
                    gather_recv.at[index],
                    local_sem.at[6 + index],
                )
            chains[index].advance()

    for tap in range(3):
        for side in range(2):
            lanes = slice(side * group, (side + 1) * group)
            total = None
            for low, length, width in plan.segments():
                first = low - (tap - 1) * width
                term = dot_tn(
                    act_one[low : low + length, lanes], shifted[side, first : first + length, :]
                )
                total = term if total is None else total + term
            work_mid[tap, lanes, :] = total.astype(BF16)
        chains.append(
            Reduction(
                steps,
                half,
                work_mid.at[tap],
                land_mid.at[tap],
                gathered_mid.at[tap],
                reduce_send.at[tap],
                reduce_recv.at[tap],
                None,
            )
        )
        advance_all()
    load_mid.wait()

    for low, length, width in plan.segments():
        block = length // 2
        for side in range(2):
            lanes = slice(side * group, (side + 1) * group)
            for part in range(2):
                at = low + part * block
                total = None
                for tap in range(3):
                    first = at - (tap - 1) * width
                    for column in range(3):
                        taps = slice(column * group, (column + 1) * group)
                        term = dot_nt(
                            shifted[side, first : first + block, taps], w_mid[tap, taps, lanes]
                        )
                        total = term if total is None else total + term
                conv_rows[at : at + block, lanes] = total
        advance_all()
    load_x = local(x_hbm, shifted.at[:, pl.ds(0, plan.all), pl.ds(0, half)], 1)
    load_one.wait()

    mean = stats[MEAN_ONE : MEAN_ONE + 1, :]
    inverse = stats[INVERSE_ONE : INVERSE_ONE + 1, :]
    gain = vec[GAIN_ONE : GAIN_ONE + 1, :]
    shift = vec[SHIFT_ONE : SHIFT_ONE + 1, :]

    def gradient(start, place, crop, carry):
        rows = pl.ds(start, TILE)
        normed = (flat[rows, :] - mean) * inverse
        norm = normed * gain + shift
        sigma = sigmoid(norm)
        grad = conv_rows[pl.ds(place, TILE), :] * silu_slope(norm, sigma)
        grad = grad * widen(mask[rows, :], half)
        conv_rows[pl.ds(place, TILE), :] = grad
        return carry[0] + rows_down(grad), carry[1] + rows_down(grad * normed)

    zero = jnp.zeros((8, half), F32)
    shift_sum, gain_sum = plan.sweep(gradient, (zero, zero))
    pay[:, :half] = jnp.sum(shift_sum, 0, keepdims=True)
    pay[:, half:] = jnp.sum(gain_sum, 0, keepdims=True)
    spread = Spread(n, me, core, pay, slots, spread_send, spread_recv)
    spread.start()
    advance_all()
    spread.wait()
    totals = gather_sum(slots, n, 2 * half)
    sums_out[...] = jnp.zeros_like(sums_out)
    sums_out[SHIFT_ONE_SUM : SHIFT_ONE_SUM + 1, :] = totals[:, :half]
    sums_out[GAIN_ONE_SUM : GAIN_ONE_SUM + 1, :] = totals[:, half:]
    scale = gain * inverse
    shift_mean = totals[:, :half] / count
    gain_mean = totals[:, half:] / count * inverse

    def into_one(start, place, crop, carry):
        rows = pl.ds(start, TILE)
        centered = flat[rows, :] - mean
        grad = scale * (conv_rows[pl.ds(place, TILE), :] - shift_mean - centered * gain_mean)
        grad_pre_one[rows, :] = (grad * widen(mask[rows, :], half)).astype(BF16)
        return carry

    plan.sweep(into_one, 0)
    swaps = []
    for index, (place, start, length) in enumerate(plan.own_pieces(1 - core)):
        swap = to_partner(
            me,
            core,
            grad_pre_one.at[pl.ds(place, length), :],
            grad_other.at[pl.ds(start, length), :],
            pair_send.at[index],
            pair_recv.at[index],
        )
        swap.start()
        swaps.append(swap)
    load_x.wait()
    for side in range(2):
        for part in range(2):
            lanes = slice(part * group, (part + 1) * group)
            low = side * half + part * group
            work_in[low : low + group, :] = dot_tn(
                shifted[side, : plan.all, lanes], grad_pre_one[...]
            ).astype(BF16)
    chains.append(
        Reduction(
            steps, 2 * half, work_in, land_in, gathered_in, reduce_send.at[3], reduce_recv.at[3], None
        )
    )
    advance_all()
    load_in.wait()
    for swap in swaps:
        swap.wait()
    pieces = plan.own_pieces(core)
    own = [
        grad_pre_one[pl.ds(pieces[0][0], plan.glob_own), :],
        jnp.concatenate([grad_pre_one[pl.ds(spot, size), :] for spot, _, size in pieces[1:]], 0),
    ]
    marks = (0, plan.glob_own, plan.own)
    for part in range(2):
        rows = slice(marks[part], marks[part + 1])
        for side in range(2):
            grad_inputs_out[side, rows, :] = (
                dot_nt(own[part], w_in[core, side])
                + dot_nt(grad_other[rows, :], w_in[1 - core, side])
            ).astype(BF16)
        advance_all()
    while not all(isinstance(chain, Gathering) and chain.done() for chain in chains):
        advance_all()


def first(
    plan, shard_out, grad_norm, pre_two, pre_one, act_one, x_all, w_mid, w_in_all, stats, vec,
    sums_two, mask
):
    n, half, group = plan.dp, plan.half, plan.group
    shape = jax.ShapeDtypeStruct
    bits = n.bit_length() - 1
    pieces = 1 + plan.slots
    return pl.pallas_call(
        functools.partial(first_kernel, plan),
        out_shape=(
            shape((2 * half, half), BF16),
            shape((3, half, 3 * group), BF16),
            shape((2 * half, half), BF16),
            shape((2, plan.own, half), BF16),
            shape((8, half), F32),
        ),
        in_specs=[ANY] * 8 + [VMEM] * 4,
        out_specs=(ANY, ANY, ANY, VMEM, VMEM),
        scratch_shapes=[
            pltpu.VMEM((plan.all, half), F32),
            pltpu.VMEM((plan.conv, half), F32),
            pltpu.VMEM((2, plan.conv, 3 * group), BF16),
            pltpu.VMEM((plan.conv, half), BF16),
            pltpu.VMEM(w_mid.shape, BF16),
            pltpu.VMEM((plan.all, half), BF16),
            pltpu.VMEM((plan.own, half), BF16),
            pltpu.VMEM(w_in_all.shape, BF16),
            pltpu.VMEM(shard_out.shape, BF16),
            pltpu.VMEM((3, half, 3 * group), BF16),
            pltpu.VMEM((3, land_rows(n, half), 3 * group), BF16),
            pltpu.VMEM((2 * half, half), BF16),
            pltpu.VMEM((land_rows(n, 2 * half), half), BF16),
            pltpu.VMEM((1, 2 * half), F32),
            pltpu.VMEM((n, 1, 2 * half), F32),
            pltpu.SemaphoreType.DMA((11,)),
            pltpu.SemaphoreType.DMA((pieces,)),
            pltpu.SemaphoreType.DMA((pieces,)),
            pltpu.SemaphoreType.DMA((n,)),
            pltpu.SemaphoreType.DMA((n,)),
            pltpu.SemaphoreType.DMA((4, bits)),
            pltpu.SemaphoreType.DMA((4, bits)),
            pltpu.SemaphoreType.DMA((5, 4)),
            pltpu.SemaphoreType.DMA((5, 4)),
        ],
        compiler_params=pltpu.CompilerParams(
            collective_id=3, has_side_effects=True, vmem_limit_bytes=VMEM_BYTES
        ),
    )(
        shard_out, grad_norm, pre_two, pre_one, act_one, x_all, w_mid, w_in_all, stats, vec,
        sums_two, mask
    )


def pixels(rows, plan):
    glob = rows[:, : plan.glob_own].reshape(2, plan.glob_height, plan.glob_width, plan.half)
    small = rows[:, plan.glob_own :].reshape(
        2, plan.slots, plan.small_height, plan.small_width, plan.half
    )
    real = plan.half_real

    def join(maps):
        return jnp.concatenate([maps[0, ..., :real], maps[1, ..., :real]], -1)

    return join(glob[:, :, : plan.glob_side])[None], join(small[:, :, :, : plan.small_side])


def ungroup_lanes(array, plan):
    return jnp.concatenate(
        [array[..., : plan.width], array[..., plan.group : plan.group + plan.width]], -1
    )


def per_device(*arguments):
    dp = lax.axis_size("dp")
    core = lax.axis_index("rows")
    (
        plan, x_own, cot_own, w_in, w_mid, k_out, w_squeeze, w_excite, mask_all, mask_own, vec,
        vec_three
    ) = prepare(dp, *arguments)
    half, group, width, real = plan.half, plan.group, plan.width, plan.half_real
    (
        x_all, pre_one, act_one, pre_two, act_three, k_out_all, w_in_all, vec_three_all, stats,
        pooled, excite, squeeze_pre
    ) = forward(plan, x_own, w_in, w_mid, k_out, vec, vec_three, mask_all, w_squeeze, w_excite)
    result, grad_summed, grad_pre_three, sums_three = third(
        plan, act_three, k_out_all, x_own, cot_own, mask_own, vec, vec_three_all
    )
    shard_out, grad_norm, grad_excite, grad_squeeze, sums_two = second(
        plan, grad_pre_three, act_three, k_out_all, pre_two, stats, vec, mask_all, pooled, excite,
        squeeze_pre, w_squeeze, w_excite
    )
    gathered_out, gathered_mid, gathered_in, grad_inputs, sums_one = first(
        plan, shard_out, grad_norm, pre_two, pre_one, act_one, x_all, w_mid, w_in_all, stats, vec,
        sums_two, mask_all
    )
    glob_out, small_out = pixels(result.astype(F32), plan)
    glob_grad, small_grad = pixels(grad_inputs.astype(F32) + grad_summed.astype(F32), plan)
    grad_kernel_out = (
        gathered_out.reshape(4, group, half)[:, :width, :real].reshape(-1, real).astype(F32)
    )
    grad_kernel_in = ungroup_lanes(
        gathered_in.reshape(2, half, half)[:, :real].reshape(-1, half), plan
    ).astype(F32)
    mid = gathered_mid.reshape(3, 2, group, 3, group)[:, :, :width, :, :width]
    grad_kernel_mid = mid.transpose(0, 3, 2, 1, 4).reshape(3, 3, width, real).astype(F32)
    sums = lax.dynamic_index_in_dim(sums_three, core, 0, False)

    def grouped(row):
        return ungroup_lanes(row, plan)

    return (
        glob_out,
        small_out,
        glob_grad,
        small_grad,
        grad_kernel_in,
        grad_kernel_mid,
        grad_kernel_out,
        jnp.concatenate(
            [grad_squeeze[:width, :width], grad_squeeze[group : group + width, :width]], 0
        ),
        sums_two[SQUEEZE_SUM, :width],
        grouped(grad_excite[:width]),
        grouped(sums_two[EXCITE_SUM]),
        grouped(sums_one[GAIN_ONE_SUM]),
        grouped(sums_one[SHIFT_ONE_SUM]),
        grouped(sums_two[GAIN_TWO_SUM]),
        grouped(sums_two[SHIFT_TWO_SUM]),
        sums[1, :real],
        sums[0, :real],
    )


def solution(mesh):
    maps = P("dp", "rows", None, None)
    vector = P("rows")
    columns = P(None, "rows")
    taps = P(None, None, None, "rows")
    return jax.shard_map(
        per_device,
        mesh=mesh,
        in_specs=(
            maps, maps, P("dp"), columns, taps, columns, P("rows", None), P(), columns,
        )
        + (vector,) * 7
        + (maps, maps),
        out_specs=(maps,) * 4
        + (columns, taps, columns, P("rows", None), P(), columns)
        + (vector,) * 7,
        check_vma=False,
    )
```

```python
import functools

import jax
import jax.numpy as jnp
from jax import lax
from jax.experimental import pallas as pl
from jax.experimental.pallas import tpu as pltpu
from jax.sharding import PartitionSpec as P

EPSILON = 1e-05
MESH = pl.DeviceIdType.MESH
F32 = jnp.float32
BF16 = jnp.bfloat16
ANY = pl.BlockSpec(memory_space=pl.ANY)
VMEM = pl.BlockSpec(memory_space=pltpu.VMEM)
LANE = 128
TILE = 64
VMEM_BYTES = 62 * 1024 * 1024


def round_up(value, step):
    return -(-value // step) * step


class Plan:
    def __init__(self, glob_shape, small_shape, group_width, dp):
        self.glob_height, self.glob_side = glob_shape[1], glob_shape[2]
        self.slots, self.small_height, self.small_side = small_shape[:3]
        self.channels = glob_shape[3]
        self.glob_width = round_up(self.glob_side + 1, 32)
        self.small_width = round_up(self.small_side + 1, 16)
        self.glob_own = self.glob_height * self.glob_width
        self.slot_own = self.small_height * self.small_width
        self.own = self.glob_own + self.slots * self.slot_own
        self.glob_all = 2 * self.glob_own
        self.slot_all = 2 * self.slot_own
        self.all = 2 * self.own
        self.glob_base = self.glob_width
        self.small_base = self.glob_all + 2 * self.glob_width
        self.slot_conv = self.slot_all + self.small_width
        self.small_conv = self.slots * self.slot_conv
        self.conv = self.small_base + self.small_conv
        self.width = group_width
        self.group = round_up(group_width, LANE)
        self.half = 2 * self.group
        self.half_real = self.channels // 2
        self.dp = dp
        self.glob_tiles = self.glob_all // TILE
        self.slot_tiles = self.slot_all // TILE
        self.slot_rows = round_up(1 + self.slots, 8)
        self.glob_area = float(2 * self.glob_height * self.glob_side)
        self.slot_area = float(2 * self.small_height * self.small_side)

    def own_pieces(self, core):
        pieces = [(pl.multiple_of(core * self.glob_own, 16), 0, self.glob_own)]
        for slot in range(self.slots):
            place = self.glob_all + slot * self.slot_all + core * self.slot_own
            pieces.append(
                (pl.multiple_of(place, 16), self.glob_own + slot * self.slot_own, self.slot_own)
            )
        return pieces

    def sweep(self, body, carry):
        def glob_step(tile, state):
            start = pl.multiple_of(tile * TILE, TILE)
            return body(start, pl.multiple_of(self.glob_base + start, 16), 0, state)

        def slot_step(tile, state):
            slot = tile // self.slot_tiles
            start = pl.multiple_of(self.glob_all + tile * TILE, TILE)
            place = self.small_base + tile * TILE + slot * self.small_width
            return body(start, pl.multiple_of(place, 16), 1 + slot, state)

        carry = lax.fori_loop(0, self.glob_tiles, glob_step, carry)
        return lax.fori_loop(0, self.slots * self.slot_tiles, slot_step, carry)

    def segments(self):
        return (
            (self.glob_base, self.glob_all, self.glob_width),
            (self.small_base, self.small_conv - self.small_width, self.small_width),
        )


def sigmoid(value):
    return 0.5 * jnp.tanh(0.5 * value) + 0.5


def rows_down(tile):
    return jnp.sum(tile.reshape(tile.shape[0] // 8, 8, tile.shape[1]), 0)


def widen(mask, lanes):
    return jnp.concatenate([mask] * (lanes // mask.shape[1]), 1)


def dot(left, right):
    return jnp.dot(left, right, preferred_element_type=F32)


def dot_nt(left, right):
    return lax.dot_general(left, right, (((1,), (1,)), ((), ())), preferred_element_type=F32)


def dot_tn(left, right):
    return lax.dot_general(left, right, (((0,), (0,)), ((), ())), preferred_element_type=F32)


def split_dot(left, right, nt=False):
    high = left.astype(BF16)
    low = (left - high.astype(F32)).astype(BF16)
    call = dot_nt if nt else dot
    return call(high, right) + call(low, right)


def entry_barrier(n, me, core):
    barrier = pltpu.get_barrier_semaphore()

    def greet(step, carry):
        pl.semaphore_signal(
            barrier, inc=1, device_id=(lax.rem(me + step, n), core), device_id_type=MESH
        )
        return carry

    lax.fori_loop(1, n, greet, 0)
    pl.semaphore_signal(barrier, inc=1, device_id=(me, 1 - core), device_id_type=MESH)
    pl.semaphore_wait(barrier, n)


class Spread:
    def __init__(self, n, me, core, source, slots, send, recv):
        self.n, self.me, self.core = n, me, core
        self.source, self.slots, self.send, self.recv = source, slots, send, recv

    def copy(self, step):
        return pltpu.make_async_remote_copy(
            src_ref=self.source,
            dst_ref=self.slots.at[self.me],
            send_sem=self.send.at[step],
            recv_sem=self.recv.at[step],
            device_id=(lax.rem(self.me + step, self.n), self.core),
            device_id_type=MESH,
        )

    def start(self):
        def begin(step, carry):
            self.copy(step).start()
            return carry

        lax.fori_loop(1, self.n, begin, 0)
        self.slots[pl.ds(self.me, 1)] = self.source[...][None]

    def wait(self):
        def end(step, carry):
            self.copy(step).wait()
            return carry

        lax.fori_loop(1, self.n, end, 0)


def to_partner(me, core, source, target, send, recv):
    return pltpu.make_async_remote_copy(
        src_ref=source,
        dst_ref=target,
        send_sem=send,
        recv_sem=recv,
        device_id=(me, 1 - core),
        device_id_type=MESH,
    )


def merge_moments(slots, n, lanes):
    def add(step, carry):
        total, count = carry
        return (total + slots[step, :, :lanes], count + slots[step, :, 2 * lanes : 2 * lanes + LANE])

    total, count = lax.fori_loop(
        0, n, add, (jnp.zeros((1, lanes), F32), jnp.zeros((1, LANE), F32))
    )
    wide_count = widen(count, lanes)
    mean = total / wide_count

    def spread(step, carry):
        own_count = widen(slots[step, :, 2 * lanes : 2 * lanes + LANE], lanes)
        gap = slots[step, :, :lanes] / own_count - mean
        return carry + slots[step, :, lanes : 2 * lanes] + own_count * gap * gap

    squares = lax.fori_loop(0, n, spread, jnp.zeros((1, lanes), F32))
    return mean, squares / wide_count, wide_count


def local_moments(plan, values, mask, which, count):
    lanes = plan.half

    def add(start, place, crop, carry):
        row = start if which == "all" else place
        tile = values[pl.ds(row, TILE), :] * widen(mask[pl.ds(start, TILE), :], lanes)
        return carry + rows_down(tile)

    total = jnp.sum(plan.sweep(add, jnp.zeros((8, lanes), F32)), 0, keepdims=True)
    mean = total / count

    def spread(start, place, crop, carry):
        row = start if which == "all" else place
        gap = (values[pl.ds(row, TILE), :] - mean) * widen(mask[pl.ds(start, TILE), :], lanes)
        return carry + rows_down(gap * gap)

    squares = jnp.sum(plan.sweep(spread, jnp.zeros((8, lanes), F32)), 0, keepdims=True)
    return total, squares


GAIN_ONE, SHIFT_ONE, GAIN_TWO, SHIFT_TWO, EXCITE_BIAS, SQUEEZE_BIAS, COUNT = range(7)
MEAN_ONE, INVERSE_ONE, MEAN_TWO, INVERSE_TWO, TOTAL = range(5)


def forward_kernel(
    plan,
    x_own,
    w_in,
    w_mid_hbm,
    k_out_hbm,
    vec,
    vec_three,
    mask,
    w_squeeze,
    w_excite,
    x_out,
    pre_one_out,
    act_one_out,
    pre_two_out,
    act_three_out,
    k_out_other_hbm,
    w_in_other_hbm,
    vec_three_other,
    stats,
    pooled_out,
    excite_out,
    squeeze_pre_out,
    x_all,
    pre_one,
    shifted,
    w_mid,
    pre_two,
    act_two,
    act_three,
    pay_one,
    slots_one,
    pay_two,
    slots_two,
    squeeze_send,
    squeeze_recv,
    k_out,
    k_out_other,
    w_in_other,
    local_sem,
    send_sem,
    recv_sem,
    spread_send,
    spread_recv,
):
    n, half, group = plan.dp, plan.half, plan.group
    me, core = lax.axis_index("dp"), lax.axis_index("rows")
    pieces = plan.own_pieces(core)
    entry_barrier(n, me, core)

    def local(source, target, index):
        copy = pltpu.make_async_copy(source, target, local_sem.at[index])
        copy.start()
        return copy

    def partner(source, target, index):
        copy = to_partner(me, core, source, target, send_sem.at[index], recv_sem.at[index])
        copy.start()
        return copy

    x_local, x_remote = [], []
    for index, (place, start, length) in enumerate(pieces):
        source = x_own.at[:, pl.ds(start, length), :]
        target = x_all.at[:, pl.ds(place, length), :]
        x_remote.append(partner(source, target, index))
        x_local.append(local(source, target, index))
    base = len(pieces)
    mid_copy = local(w_mid_hbm, w_mid, base)
    k_out_copy = local(k_out_hbm, k_out, base + 1)
    for side in range(2):
        shifted[side, : plan.glob_base, :] = jnp.zeros((plan.glob_base, 3 * group), BF16)
        shifted[side, plan.glob_base + plan.glob_all : plan.small_base, :] = jnp.zeros(
            (plan.glob_width, 3 * group), BF16
        )
        for slot in range(plan.slots):
            low = plan.small_base + slot * plan.slot_conv + plan.slot_all
            shifted[side, low : low + plan.small_width, :] = jnp.zeros(
                (plan.small_width, 3 * group), BF16
            )

    def product(owner):
        place = pl.multiple_of(owner * plan.glob_own, 16)
        rows = pl.ds(place, plan.glob_own)
        pre_one[rows, :] = dot(x_all[0, rows, :], w_in[0]) + dot(x_all[1, rows, :], w_in[1])
        places = [spot for spot, _, _ in plan.own_pieces(owner)[1:]]
        sides = [
            jnp.concatenate([x_all[side, pl.ds(spot, plan.slot_own), :] for spot in places], 0)
            for side in range(2)
        ]
        result = dot(sides[0], w_in[0]) + dot(sides[1], w_in[1])
        for slot, spot in enumerate(places):
            pre_one[pl.ds(spot, plan.slot_own), :] = result[
                slot * plan.slot_own : (slot + 1) * plan.slot_own
            ]

    for copy in x_local:
        copy.wait()
    product(core)
    for copy in x_remote:
        copy.wait()
    k_out_copy.wait()
    others = [
        partner(k_out, k_out_other, base),
        partner(w_in, w_in_other, base + 1),
        partner(vec_three, vec_three_other, base + 2),
    ]
    product(1 - core)
    saves = [
        local(x_all, x_out, base + 4),
        local(pre_one, pre_one_out, base + 5),
    ]

    chip_count = vec[COUNT : COUNT + 1, :]

    def statistics(values, which, pay, slots, index):
        total, squares = local_moments(plan, values, mask, which, chip_count)
        pay[:, :half] = total
        pay[:, half : 2 * half] = squares
        pay[:, 2 * half :] = chip_count[:, :LANE]
        spread = Spread(n, me, core, pay, slots, spread_send.at[index], spread_recv.at[index])
        spread.start()
        spread.wait()
        mean, variance, count = merge_moments(slots, n, half)
        return mean, lax.rsqrt(variance + EPSILON), count

    mean, inverse, count = statistics(pre_one, "all", pay_one, slots_one, 0)
    stats[...] = jnp.zeros_like(stats)
    stats[MEAN_ONE : MEAN_ONE + 1, :] = mean
    stats[INVERSE_ONE : INVERSE_ONE + 1, :] = inverse
    stats[TOTAL : TOTAL + 1, :] = count
    scale = inverse * vec[GAIN_ONE : GAIN_ONE + 1, :]
    shift = vec[SHIFT_ONE : SHIFT_ONE + 1, :]

    def activate_one(start, place, crop, carry):
        norm = (pre_one[pl.ds(start, TILE), :] - mean) * scale + shift
        act = norm * sigmoid(norm) * widen(mask[pl.ds(start, TILE), :], half)
        before = pltpu.roll(act, 1, 0)
        after = pltpu.roll(act, TILE - 1, 0)
        for tap, value in enumerate((before, act, after)):
            for side in range(2):
                shifted[side, pl.ds(place, TILE), tap * group : (tap + 1) * group] = value[
                    :, side * group : (side + 1) * group
                ].astype(BF16)
        return carry

    plan.sweep(activate_one, 0)
    for side in range(2):
        saves.append(
            local(
                shifted.at[side, :, group : 2 * group],
                act_one_out.at[:, side * group : (side + 1) * group],
                base + 6 + side,
            )
        )
    mid_copy.wait()

    for low, length, width in plan.segments():
        for side in range(2):
            lanes = slice(side * group, (side + 1) * group)
            block = length // 2
            for part in range(2):
                at = low + part * block
                total = None
                for tap in range(3):
                    first = at + (tap - 1) * width
                    term = dot(shifted[side, first : first + block, :], w_mid[tap, :, lanes])
                    total = term if total is None else total + term
                pre_two[at : at + block, lanes] = total
    saves.append(local(pre_two, pre_two_out, base + 8))

    mean_two, inverse_two, _ = statistics(pre_two, "conv", pay_two, slots_two, 1)
    stats[MEAN_TWO : MEAN_TWO + 1, :] = mean_two
    stats[INVERSE_TWO : INVERSE_TWO + 1, :] = inverse_two
    scale_two = inverse_two * vec[GAIN_TWO : GAIN_TWO + 1, :]
    shift_two = vec[SHIFT_TWO : SHIFT_TWO + 1, :]
    pooled_out[...] = jnp.zeros_like(pooled_out)

    def activate_two(start, place, crop, carry):
        norm = (pre_two[pl.ds(place, TILE), :] - mean_two) * scale_two + shift_two
        act = norm * sigmoid(norm) * widen(mask[pl.ds(start, TILE), :], half)
        act_two[pl.ds(start, TILE), :] = act
        pooled_out[pl.ds(crop, 1), :] += jnp.sum(act, 0, keepdims=True)
        return carry

    plan.sweep(activate_two, 0)
    pooled_out[:1, :] = pooled_out[:1, :] * (1.0 / plan.glob_area)
    pooled_out[1:, :] = pooled_out[1:, :] * (1.0 / plan.slot_area)
    part = split_dot(pooled_out[...], w_squeeze[...])
    squeeze_send[...] = part
    swap = partner(squeeze_send, squeeze_recv, base + 3)
    swap.wait()
    squeeze_pre = part + squeeze_recv[...] + vec[SQUEEZE_BIAS : SQUEEZE_BIAS + 1, :group]
    squeeze_pre_out[...] = squeeze_pre
    squeezed = squeeze_pre * sigmoid(squeeze_pre)
    excite_out[...] = sigmoid(
        split_dot(squeezed, w_excite[...]) + vec[EXCITE_BIAS : EXCITE_BIAS + 1, :]
    )

    def activate_three(start, place, crop, carry):
        act_three[core, pl.ds(start, TILE), :] = (
            act_two[pl.ds(start, TILE), :] * excite_out[pl.ds(crop, 1), :]
        ).astype(BF16)
        return carry

    plan.sweep(activate_three, 0)
    exchange = partner(act_three.at[core], act_three.at[core], base + 4)
    for copy in others:
        copy.wait()
    saves.append(local(k_out_other, k_out_other_hbm, base + 2))
    saves.append(local(w_in_other, w_in_other_hbm, base + 3))
    exchange.wait()
    saves.append(local(act_three, act_three_out, base + 9))
    for copy in saves:
        copy.wait()


def forward(plan, x_own, w_in, w_mid, k_out, vec, vec_three, mask, w_squeeze, w_excite):
    n, half, group = plan.dp, plan.half, plan.group
    shape = jax.ShapeDtypeStruct
    copies = 1 + plan.slots
    pay = 2 * half + LANE
    return pl.pallas_call(
        functools.partial(forward_kernel, plan),
        out_shape=(
            shape((2, plan.all, half), BF16),
            shape((plan.all, half), F32),
            shape((plan.conv, half), BF16),
            shape((plan.conv, half), F32),
            shape((2, plan.all, half), BF16),
            shape(k_out.shape, BF16),
            shape(w_in.shape, BF16),
            shape(vec_three.shape, F32),
            shape((8, half), F32),
            shape((plan.slot_rows, half), F32),
            shape((plan.slot_rows, half), F32),
            shape((plan.slot_rows, group), F32),
        ),
        in_specs=[ANY, VMEM, ANY, ANY, VMEM, VMEM, VMEM, VMEM, VMEM],
        out_specs=(ANY,) * 7 + (VMEM,) * 5,
        scratch_shapes=[
            pltpu.VMEM((2, plan.all, half), BF16),
            pltpu.VMEM((plan.all, half), F32),
            pltpu.VMEM((2, plan.conv, 3 * group), BF16),
            pltpu.VMEM(w_mid.shape, BF16),
            pltpu.VMEM((plan.conv, half), F32),
            pltpu.VMEM((plan.all, half), F32),
            pltpu.VMEM((2, plan.all, half), BF16),
            pltpu.VMEM((1, pay), F32),
            pltpu.VMEM((n, 1, pay), F32),
            pltpu.VMEM((1, pay), F32),
            pltpu.VMEM((n, 1, pay), F32),
            pltpu.VMEM((plan.slot_rows, group), F32),
            pltpu.VMEM((plan.slot_rows, group), F32),
            pltpu.VMEM(k_out.shape, BF16),
            pltpu.VMEM(k_out.shape, BF16),
            pltpu.VMEM(w_in.shape, BF16),
            pltpu.SemaphoreType.DMA((copies + 10,)),
            pltpu.SemaphoreType.DMA((copies + 5,)),
            pltpu.SemaphoreType.DMA((copies + 5,)),
            pltpu.SemaphoreType.DMA((2, n)),
            pltpu.SemaphoreType.DMA((2, n)),
        ],
        compiler_params=pltpu.CompilerParams(
            collective_id=0, has_side_effects=True, vmem_limit_bytes=VMEM_BYTES
        ),
    )(x_own, w_in, w_mid, k_out, vec, vec_three, mask, w_squeeze, w_excite)


def halves(rows, plan):
    real = plan.half_real
    pad = ((0, 0), (0, plan.half - real))
    return jnp.stack([jnp.pad(rows[:, :real], pad), jnp.pad(rows[:, real:], pad)], 0)


def own_rows(glob, small, plan):
    glob = jnp.pad(glob[0], ((0, 0), (0, plan.glob_width - plan.glob_side), (0, 0)))
    small = jnp.pad(small, ((0, 0), (0, 0), (0, plan.small_width - plan.small_side), (0, 0)))
    return halves(
        jnp.concatenate(
            [glob.reshape(-1, plan.channels), small.reshape(-1, plan.channels)], 0
        ),
        plan,
    )


def group_lanes(array, plan):
    pad = ((0, 0),) * (array.ndim - 1) + ((0, plan.group - plan.width),)
    return jnp.concatenate(
        [jnp.pad(array[..., : plan.width], pad), jnp.pad(array[..., plan.width :], pad)], -1
    )


def group_rows(array, plan):
    pieces = array.reshape(-1, plan.width, array.shape[1])
    pieces = jnp.pad(pieces, ((0, 0), (0, plan.group - plan.width), (0, 0)))
    return pieces.reshape(-1, array.shape[1])


def pad_to(array, *sizes):
    return jnp.pad(array, [(0, size - have) for size, have in zip(sizes, array.shape)])


def row_masks(plan, small_count):
    glob = (lax.iota(jnp.int32, plan.glob_width) < plan.glob_side).astype(F32)
    small = (lax.iota(jnp.int32, plan.small_width) < plan.small_side).astype(F32)
    live = (lax.iota(jnp.int32, plan.slots) < small_count[0]).astype(F32)

    def build(times):
        first = jnp.tile(glob, times * plan.glob_height)
        rest = (live[:, None] * jnp.tile(small, times * plan.small_height)[None]).reshape(-1)
        return jnp.broadcast_to(jnp.concatenate([first, rest])[:, None], (first.size + rest.size, LANE))

    count = plan.glob_area + plan.slot_area * small_count[0].astype(F32)
    return build(2), build(1), count
def prepare(
    dp,
    glob_in,
    small_in,
    small_count,
    kernel_in,
    kernel_mid,
    kernel_out,
    squeeze_weight,
    squeeze_bias,
    excite_weight,
    excite_bias,
    gain_first,
    shift_first,
    gain_second,
    shift_second,
    gain_third,
    shift_third,
    glob_cotangent,
    small_cotangent,
):
    plan = Plan(glob_in.shape, small_in.shape, kernel_mid.shape[2], dp)
    half, group, real = plan.half, plan.group, plan.half_real
    x_own = own_rows(glob_in, small_in, plan)
    cot_own = own_rows(glob_cotangent, small_cotangent, plan)
    w_in = group_lanes(kernel_in, plan)
    w_in = jnp.stack([pad_to(w_in[:real], half, half), pad_to(w_in[real:], half, half)], 0)
    w_mid = pad_to(group_lanes(kernel_mid, plan), 3, 3, group, half).reshape(3, 3 * group, half)
    k_out = group_rows(pad_to(kernel_out, plan.channels, half), plan).reshape(2, half, half)
    w_squeeze = group_rows(pad_to(squeeze_weight, real, group), plan)
    w_excite = pad_to(group_lanes(excite_weight, plan), group, half)
    mask_all, mask_own, count = row_masks(plan, small_count)

    def grouped(vector):
        return group_lanes(vector.astype(F32)[None], plan)

    vec = jnp.concatenate(
        [
            grouped(gain_first),
            grouped(shift_first),
            grouped(gain_second),
            grouped(shift_second),
            grouped(excite_bias),
            pad_to(squeeze_bias.astype(F32)[None], 1, half),
            jnp.full((1, half), count, F32),
            jnp.zeros((1, half), F32),
        ],
        0,
    )
    vec_three = pad_to(jnp.stack([gain_third, shift_third], 0).astype(F32), 8, half)
    return plan, x_own, cot_own, w_in, w_mid, k_out, w_squeeze, w_excite, mask_all, mask_own, vec, vec_three
def own_steps(plan, body, carry):
    step = 32

    def run(tile, state):
        return body(pl.multiple_of(tile * step, step), step, state)

    return lax.fori_loop(0, plan.own // step, run, carry)


def merge_two(first, second, lanes):
    sums = [part[:, :lanes] for part in (first, second)]
    squares = [part[:, lanes : 2 * lanes] for part in (first, second)]
    counts = [widen(part[:, 2 * lanes :], lanes) for part in (first, second)]
    total = sums[0] + sums[1]
    count = counts[0] + counts[1]
    mean = total / count
    spread = squares[0] + squares[1]
    for index in range(2):
        gap = sums[index] / counts[index] - mean
        spread = spread + counts[index] * gap * gap
    return total, spread, count


def third_kernel(
    plan,
    act_three_hbm,
    k_out_hbm,
    k_out_other_hbm,
    x_own,
    cot_own,
    mask,
    vec,
    vec_three_own,
    vec_three_other,
    result_out,
    grad_summed_out,
    grad_pre_three_out,
    sums_out,
    act_three,
    k_out,
    pre_three,
    grad_summed,
    grad_pre_three,
    pay,
    pair,
    chip,
    slots,
    finals,
    pay_back,
    pair_back,
    chip_back,
    slots_back,
    finals_back,
    vec_three,
    local_sem,
    send_sem,
    recv_sem,
    spread_send,
    spread_recv,
):
    n, half = plan.dp, plan.half
    me, core = lax.axis_index("dp"), lax.axis_index("rows")
    pieces = plan.own_pieces(core)
    entry_barrier(n, me, core)

    def local(source, target, index):
        copy = pltpu.make_async_copy(source, target, local_sem.at[index])
        copy.start()
        return copy

    def partner(source, target, index):
        copy = to_partner(me, core, source, target, send_sem.at[index], recv_sem.at[index])
        copy.start()
        return copy

    loads = [
        local(
            act_three_hbm.at[:, pl.ds(place, length), :],
            act_three.at[:, pl.ds(start, length), :],
            index,
        )
        for index, (place, start, length) in enumerate(pieces)
    ]
    base = len(pieces)
    loads.append(local(k_out_hbm, k_out.at[core], base))
    loads.append(local(k_out_other_hbm, k_out.at[1 - core], 3 * base + 1))
    vec_three[core] = vec_three_own[...]
    vec_three[1 - core] = vec_three_other[...]
    for copy in loads:
        copy.wait()
    own_count = 0.5 * vec[COUNT : COUNT + 1, :]

    block = plan.own // 2
    for side in range(2):

        def product(part, carry, side=side):
            rows = pl.ds(pl.multiple_of(part * block, 16), block)
            pre_three[side, rows, :] = dot(act_three[0, rows, :], k_out[side, 0]) + dot(
                act_three[1, rows, :], k_out[side, 1]
            )
            return carry

        lax.fori_loop(0, 2, product, 0)

    for side in range(2):

        def add(row, step, carry, side=side):
            rows = pl.ds(row, step)
            return carry + rows_down(pre_three[side, rows, :] * widen(mask[rows, :], half))

        total = jnp.sum(own_steps(plan, add, jnp.zeros((8, half), F32)), 0, keepdims=True)
        mean = total / own_count

        def spread(row, step, carry, side=side, mean=mean):
            rows = pl.ds(row, step)
            gap = (pre_three[side, rows, :] - mean) * widen(mask[rows, :], half)
            return carry + rows_down(gap * gap)

        squares = jnp.sum(own_steps(plan, spread, jnp.zeros((8, half), F32)), 0, keepdims=True)
        pay[side, :, :half] = total
        pay[side, :, half : 2 * half] = squares
        pay[side, :, 2 * half :] = own_count[:, :LANE]
    partner(pay.at[1 - core], pair, 0).wait()
    total, squares, count = merge_two(pay[core], pair[...], half)
    chip[:, :half] = total
    chip[:, half : 2 * half] = squares
    chip[:, 2 * half :] = count[:, :LANE]
    exchange = Spread(n, me, core, chip, slots, spread_send.at[0], spread_recv.at[0])
    exchange.start()
    exchange.wait()
    mean, variance, full_count = merge_moments(slots, n, half)
    finals[core, :, :half] = mean
    finals[core, :, half:] = lax.rsqrt(variance + EPSILON)
    partner(finals.at[core], finals.at[core], 1).wait()

    for side in range(2):
        mean = finals[side, :, :half]
        inverse = finals[side, :, half:]
        gain = vec_three[side, :1, :]
        shift = vec_three[side, 1:2, :]

        def outer(row, step, carry, side=side, mean=mean, inverse=inverse, gain=gain, shift=shift):
            rows = pl.ds(row, step)
            seen = widen(mask[rows, :], half)
            normed = (pre_three[side, rows, :] - mean) * inverse
            summed = normed * gain + shift + x_own[side, rows, :].astype(F32)
            sigma = sigmoid(summed)
            result_out[side, rows, :] = (seen * summed * sigma).astype(BF16)
            slope = sigma * (1.0 + summed * (1.0 - sigma))
            grad = cot_own[side, rows, :].astype(F32) * seen * slope
            grad_summed[side, rows, :] = grad
            grad_summed_out[side, rows, :] = grad.astype(BF16)
            return carry[0] + rows_down(grad), carry[1] + rows_down(grad * normed)

        zero = jnp.zeros((8, half), F32)
        shift_sum, gain_sum = own_steps(plan, outer, (zero, zero))
        pay_back[side, :, :half] = jnp.sum(shift_sum, 0, keepdims=True)
        pay_back[side, :, half:] = jnp.sum(gain_sum, 0, keepdims=True)
    partner(pay_back.at[1 - core], pair_back, 2).wait()
    chip_back[...] = pay_back[core] + pair_back[...]
    exchange = Spread(n, me, core, chip_back, slots_back, spread_send.at[1], spread_recv.at[1])
    exchange.start()
    exchange.wait()

    finals_back[core] = gather_sum(slots_back, n, 2 * half)
    partner(finals_back.at[core], finals_back.at[core], 3).wait()
    copies = []
    for side in range(2):
        mean = finals[side, :, :half]
        inverse = finals[side, :, half:]
        shift_sum = finals_back[side, :, :half]
        gain_sum = finals_back[side, :, half:]
        sums_out[side] = jnp.concatenate([shift_sum, gain_sum, jnp.zeros((6, half), F32)], 0)
        scale = vec_three[side, :1, :] * inverse
        shift_mean = shift_sum / full_count
        gain_mean = gain_sum / full_count

        def inner(
            row, step, carry, side=side, mean=mean, inverse=inverse, scale=scale,
            shift_mean=shift_mean, gain_mean=gain_mean
        ):
            rows = pl.ds(row, step)
            normed = (pre_three[side, rows, :] - mean) * inverse
            grad = scale * (grad_summed[side, rows, :] - shift_mean - normed * gain_mean)
            grad_pre_three[side, rows, :] = (grad * widen(mask[rows, :], half)).astype(BF16)
            return carry

        own_steps(plan, inner, 0)
        for index, (place, start, length) in enumerate(pieces):
            source = grad_pre_three.at[side, pl.ds(start, length), :]
            target = grad_pre_three_out.at[side, pl.ds(place, length), :]
            copies.append(partner(source, target, 4 + side * base + index))
            copies.append(local(source, target, base + 1 + side * base + index))
    for copy in copies:
        copy.wait()


def gather_sum(slots, n, lanes):
    def add(step, carry):
        return carry + slots[step]

    return lax.fori_loop(0, n, add, jnp.zeros((1, lanes), F32))


def third(
    plan, act_three, k_out, k_out_other, x_own, cot_own, mask, vec, vec_three, vec_three_other
):
    n, half = plan.dp, plan.half
    shape = jax.ShapeDtypeStruct
    pieces = 1 + plan.slots
    pay = 2 * half + LANE
    own = (2, plan.own, half)
    return pl.pallas_call(
        functools.partial(third_kernel, plan),
        out_shape=(
            shape(own, BF16),
            shape(own, BF16),
            shape((2, plan.all, half), BF16),
            shape((2, 8, half), F32),
        ),
        in_specs=[ANY, ANY, ANY, VMEM, VMEM, VMEM, VMEM, VMEM, VMEM],
        out_specs=(VMEM, VMEM, ANY, VMEM),
        scratch_shapes=[
            pltpu.VMEM(own, BF16),
            pltpu.VMEM((2,) + k_out.shape, BF16),
            pltpu.VMEM(own, F32),
            pltpu.VMEM(own, F32),
            pltpu.VMEM(own, BF16),
            pltpu.VMEM((2, 1, pay), F32),
            pltpu.VMEM((1, pay), F32),
            pltpu.VMEM((1, pay), F32),
            pltpu.VMEM((n, 1, pay), F32),
            pltpu.VMEM((2, 1, 2 * half), F32),
            pltpu.VMEM((2, 1, 2 * half), F32),
            pltpu.VMEM((1, 2 * half), F32),
            pltpu.VMEM((1, 2 * half), F32),
            pltpu.VMEM((n, 1, 2 * half), F32),
            pltpu.VMEM((2, 1, 2 * half), F32),
            pltpu.VMEM((2,) + vec_three.shape, F32),
            pltpu.SemaphoreType.DMA((3 * pieces + 2,)),
            pltpu.SemaphoreType.DMA((2 * pieces + 4,)),
            pltpu.SemaphoreType.DMA((2 * pieces + 4,)),
            pltpu.SemaphoreType.DMA((2, n)),
            pltpu.SemaphoreType.DMA((2, n)),
        ],
        compiler_params=pltpu.CompilerParams(
            collective_id=1, has_side_effects=True, vmem_limit_bytes=VMEM_BYTES
        ),
    )(act_three, k_out, k_out_other, x_own, cot_own, mask, vec, vec_three, vec_three_other)


ORDERS = {
    "A": ((0, 1, 2, 3), (1, 0, 2, 3)),
    "B": ((0, 2, 1, 3), (1, 2, 0, 3)),
    "P": ((0, 1, 2, 3), (2, 1, 0, 3)),
    "Q": ((2, 0, 1, 3), (1, 0, 2, 3)),
}
HANDED = 2


class Steps:
    def __init__(self, n, me, core, order):
        bits = n.bit_length() - 1
        self.halvings = min(bits, 4)
        self.shards = 2**self.halvings
        self.doublings = bits - self.halvings
        self.bit, self.partner = [], []
        chosen = [[bit for bit in one if bit < bits] for one in ORDERS[order]]
        chosen = [one + list(range(self.halvings, bits)) for one in chosen]
        for step in range(bits):
            first, second = 2 ** chosen[0][step], 2 ** chosen[1][step]
            distance = first + (second - first) * core
            bit = lax.rem(me // distance, 2)
            self.bit.append(bit)
            self.partner.append((me + distance * (1 - 2 * bit), core))


class Chain:
    def __init__(self, steps, work, land, send, recv, free, begun=0, until=None):
        self.steps, self.work, self.land, self.free = steps, work, land, free
        self.send, self.recv = send, recv
        self.rows = work.shape[0]
        self.shard = self.rows // steps.shards
        self.halvings = steps.halvings
        self.reduce_steps = steps.halvings + steps.doublings
        self.begun, self.until = begun, until
        self.pending = None
        self.step, self.at, self.length = begun, 0, self.rows >> begun
        for step in range(begun):
            self.at = self.at + steps.bit[step] * (self.rows >> (step + 1))
        self.land_base = self.rows - self.length
        self.back = None

    def rows_at(self, row, length):
        return pl.ds(row if isinstance(row, int) else pl.multiple_of(row, 16), length)

    def here(self):
        return self.work.at[self.rows_at(self.at, self.length), :]

    def remote(self, source, target, step, slot):
        self.pending = pltpu.make_async_remote_copy(
            src_ref=source,
            dst_ref=target,
            send_sem=self.send.at[slot],
            recv_sem=self.recv.at[slot],
            device_id=self.steps.partner[step],
            device_id_type=MESH,
        )
        self.pending.start()

    def begin_reduce(self):
        step = self.step
        if step < self.halvings:
            length = self.rows >> (step + 1)
            bit = self.steps.bit[step]
            self.keep = self.at + bit * length
            gone = self.at + (1 - bit) * length
            low = self.rows - 2 * length
        else:
            length = self.shard
            self.keep = gone = self.at
            low = self.rows - self.shard + (step - self.halvings) * self.shard
        self.length = length
        self.landed = self.land.at[pl.ds(low - self.land_base, length), :]
        self.remote(self.work.at[self.rows_at(gone, length), :], self.landed, step, step)

    def end_reduce(self):
        self.pending.wait()
        if self.free is not None and self.step < self.halvings:
            pl.semaphore_signal(
                self.free.at[self.step],
                inc=1,
                device_id=self.steps.partner[self.step],
                device_id_type=MESH,
            )
        size = 48 if self.shard % 48 == 0 else 16

        def add(tile, carry):
            there = self.rows_at(self.keep + tile * size, size)
            here = pl.ds(pl.multiple_of(tile * size, 16), size)
            total = self.work[there, :].astype(F32) + self.landed[here, :].astype(F32)
            self.work[there, :] = total.astype(BF16)
            return carry

        lax.fori_loop(0, self.length // size, add, 0)
        self.at = self.keep
        self.step += 1

    def begin_gather(self):
        if self.back >= self.begun:
            pl.semaphore_wait(self.free.at[self.back], 1)
        part = self.here()
        self.remote(part, part, self.back, self.reduce_steps + self.back)

    def end_gather(self):
        self.pending.wait()
        self.at = self.at - self.steps.bit[self.back] * self.length
        self.length *= 2
        self.back -= 1

    def advance(self):
        if self.pending is not None:
            if self.back is None:
                self.end_reduce()
            else:
                self.end_gather()
            self.pending = None
        if self.step == self.until:
            return
        if self.step < self.reduce_steps:
            self.begin_reduce()
            return
        if self.back is None:
            self.back = self.halvings - 1
        if self.back >= 0:
            self.begin_gather()

    def done(self):
        return self.pending is None and (self.step == self.until or self.back == -1)


def land_rows(n, rows, begun=0, until=None):
    bits = n.bit_length() - 1
    halvings = min(bits, 4)
    last = halvings if until is None else min(until, halvings)
    extra = bits - halvings if until is None else 0
    return (rows >> begun) - (rows >> last) + extra * (rows >> halvings)


def chain_slots(n):
    bits = n.bit_length() - 1
    return bits + min(bits, 4)


def silu_slope(value, sigma):
    return sigma * (1.0 + value * (1.0 - sigma))
SHIFT_TWO_SUM, GAIN_TWO_SUM, EXCITE_SUM, SQUEEZE_SUM = range(4)
SHIFT_ONE_SUM, GAIN_ONE_SUM = range(2)


def second_kernel(
    plan,
    grad_pre_three_hbm,
    act_three_hbm,
    k_out_hbm,
    k_out_other_hbm,
    pre_two_hbm,
    stats,
    vec,
    mask,
    pooled,
    excite,
    squeeze_pre,
    w_squeeze,
    w_excite,
    shard_out,
    grad_norm_out,
    grad_excite_out,
    grad_squeeze_out,
    sums_out,
    grad_pre_three,
    act_three,
    k_out,
    pre_two,
    grad_act,
    slopes,
    work,
    land,
    grad_excite,
    squeeze_send,
    squeeze_recv,
    grad_pooled,
    factors,
    factor_slots,
    pay,
    slots,
    local_sem,
    pair_send,
    pair_recv,
    spread_send,
    spread_recv,
    reduce_send,
    reduce_recv,
):
    n, half, group = plan.dp, plan.half, plan.group
    me, core = lax.axis_index("dp"), lax.axis_index("rows")
    entry_barrier(n, me, core)

    def local(source, target, index):
        copy = pltpu.make_async_copy(source, target, local_sem.at[index])
        copy.start()
        return copy

    loads = [
        local(grad_pre_three_hbm, grad_pre_three, 0),
        local(act_three_hbm, act_three, 1),
        local(k_out_hbm.at[core], k_out.at[core], 2),
        local(pre_two_hbm, pre_two, 3),
        local(k_out_other_hbm.at[core], k_out.at[1 - core], 6),
    ]
    loads[0].wait()
    loads[1].wait()
    for side in range(2):
        for part in range(2):
            lanes = slice(part * group, (part + 1) * group)
            low = side * half + part * group
            work[low : low + group, :] = dot_tn(
                act_three[side, :, lanes], grad_pre_three[core]
            ).astype(BF16)
    reduction = Chain(
        Steps(n, me, core, ORDER_OUT), work, land, reduce_send, reduce_recv, None, until=HANDED
    )
    reduction.advance()
    loads[2].wait()
    loads[4].wait()

    block = plan.all // 4

    def product(part, carry):
        rows = pl.ds(pl.multiple_of(part * block, 16), block)
        grad_act[rows, :] = dot_nt(grad_pre_three[0, rows, :], k_out[0]) + dot_nt(
            grad_pre_three[1, rows, :], k_out[1]
        )
        return carry

    lax.fori_loop(0, 4, product, 0)
    loads[3].wait()
    reduction.advance()

    mean = stats[MEAN_TWO : MEAN_TWO + 1, :]
    inverse = stats[INVERSE_TWO : INVERSE_TWO + 1, :]
    count = stats[TOTAL : TOTAL + 1, :]
    gain = vec[GAIN_TWO : GAIN_TWO + 1, :]
    shift = vec[SHIFT_TWO : SHIFT_TWO + 1, :]
    grad_excite[...] = jnp.zeros_like(grad_excite)

    def excitation(start, place, crop, carry):
        rows = pl.ds(start, TILE)
        norm = (pre_two[pl.ds(place, TILE), :] - mean) * (inverse * gain) + shift
        sigma = sigmoid(norm)
        seen = widen(mask[rows, :], half)
        slopes[rows, :] = silu_slope(norm, sigma) * seen
        term = grad_act[rows, :] * (norm * sigma * seen)
        grad_excite[pl.ds(crop, 1), :] += jnp.sum(term, 0, keepdims=True)
        return carry

    plan.sweep(excitation, 0)
    level = excite[...]
    grad_excite_pre = grad_excite[...] * level * (1.0 - level)
    part = split_dot(grad_excite_pre, w_excite[...], nt=True)
    squeeze_send[...] = part
    swap = to_partner(me, core, squeeze_send, squeeze_recv, pair_send.at[0], pair_recv.at[0])
    swap.start()
    reduction.advance()
    swap.wait()
    before = squeeze_pre[...]
    sigma = sigmoid(before)
    squeezed = before * sigma
    grad_squeeze_pre = (part + squeeze_recv[...]) * silu_slope(before, sigma)
    back = split_dot(grad_squeeze_pre, w_squeeze[...], nt=True)
    crop_row = lax.broadcasted_iota(jnp.int32, back.shape, 0)
    area = jnp.where(crop_row == 0, 1.0 / plan.glob_area, 1.0 / plan.slot_area)
    grad_pooled[...] = back * area
    deep = plan.slot_rows
    factors[:deep, :group] = squeezed.astype(BF16)
    factors[:deep, group:] = grad_excite_pre.astype(BF16)
    factors[deep:, :group] = grad_squeeze_pre.astype(BF16)
    factors[deep:, group:] = pooled[...].astype(BF16)
    factor_spread = Spread(n, me, core, factors, factor_slots, spread_send.at[0], spread_recv.at[0])
    factor_spread.start()

    def gradient(start, place, crop, carry):
        rows = pl.ds(start, TILE)
        incoming = grad_act[rows, :] * excite[pl.ds(crop, 1), :] + grad_pooled[pl.ds(crop, 1), :]
        grad = incoming * slopes[rows, :]
        grad_act[rows, :] = grad
        normed = (pre_two[pl.ds(place, TILE), :] - mean) * inverse
        return carry[0] + rows_down(grad), carry[1] + rows_down(grad * normed)

    zero = jnp.zeros((8, half), F32)
    shift_sum, gain_sum = plan.sweep(gradient, (zero, zero))
    save = local(grad_act, grad_norm_out, 4)
    pay[:, :half] = jnp.sum(shift_sum, 0, keepdims=True)
    pay[:, half:] = jnp.sum(gain_sum, 0, keepdims=True)
    spread = Spread(n, me, core, pay, slots, spread_send.at[1], spread_recv.at[1])
    spread.start()
    while not reduction.done():
        reduction.advance()
    store = local(reduction.here(), shard_out, 5)
    factor_spread.wait()
    left = factor_slots[:, :, :group].reshape(n * 2 * deep, group)
    right = factor_slots[:, :, group:].reshape(n * 2 * deep, half)
    upper = lax.broadcasted_iota(jnp.int32, left.shape, 0) % (2 * deep) < deep
    zeros = jnp.zeros_like(left)
    excite_left = jnp.where(upper, left, zeros)
    squeeze_left = jnp.where(upper, zeros, left)
    grad_excite_out[...] = dot_tn(excite_left, right)
    grad_squeeze_out[...] = dot_tn(right, squeeze_left)
    wide_upper = lax.broadcasted_iota(jnp.int32, right.shape, 0) % (2 * deep) < deep
    excite_bias = jnp.sum(jnp.where(wide_upper, right.astype(F32), 0.0), 0, keepdims=True)
    squeeze_bias = jnp.sum(squeeze_left.astype(F32), 0, keepdims=True)
    spread.wait()
    totals = gather_sum(slots, n, 2 * half)
    sums_out[...] = jnp.zeros_like(sums_out)
    sums_out[SHIFT_TWO_SUM : SHIFT_TWO_SUM + 1, :] = totals[:, :half]
    sums_out[GAIN_TWO_SUM : GAIN_TWO_SUM + 1, :] = totals[:, half:]
    sums_out[EXCITE_SUM : EXCITE_SUM + 1, :] = excite_bias
    sums_out[SQUEEZE_SUM : SQUEEZE_SUM + 1, :group] = squeeze_bias
    save.wait()
    store.wait()


def second(
    plan, grad_pre_three, act_three, k_out, k_out_other, pre_two, stats, vec, mask, pooled,
    excite, squeeze_pre, w_squeeze, w_excite
):
    n, half, group = plan.dp, plan.half, plan.group
    shape = jax.ShapeDtypeStruct
    rows = 2 * half
    shard = rows >> HANDED
    deep = plan.slot_rows
    bits = n.bit_length() - 1
    return pl.pallas_call(
        functools.partial(second_kernel, plan),
        out_shape=(
            shape((shard, half), BF16),
            shape((plan.all, half), F32),
            shape((group, half), F32),
            shape((half, group), F32),
            shape((8, half), F32),
        ),
        in_specs=[ANY] * 5 + [VMEM] * 8,
        out_specs=(ANY, ANY, VMEM, VMEM, VMEM),
        scratch_shapes=[
            pltpu.VMEM((2, plan.all, half), BF16),
            pltpu.VMEM((2, plan.all, half), BF16),
            pltpu.VMEM((2, half, half), BF16),
            pltpu.VMEM((plan.conv, half), F32),
            pltpu.VMEM((plan.all, half), F32),
            pltpu.VMEM((plan.all, half), F32),
            pltpu.VMEM((rows, half), BF16),
            pltpu.VMEM((land_rows(n, rows, until=HANDED), half), BF16),
            pltpu.VMEM((deep, half), F32),
            pltpu.VMEM((deep, group), F32),
            pltpu.VMEM((deep, group), F32),
            pltpu.VMEM((deep, half), F32),
            pltpu.VMEM((2 * deep, group + half), BF16),
            pltpu.VMEM((n, 2 * deep, group + half), BF16),
            pltpu.VMEM((1, 2 * half), F32),
            pltpu.VMEM((n, 1, 2 * half), F32),
            pltpu.SemaphoreType.DMA((7,)),
            pltpu.SemaphoreType.DMA((1,)),
            pltpu.SemaphoreType.DMA((1,)),
            pltpu.SemaphoreType.DMA((2, n)),
            pltpu.SemaphoreType.DMA((2, n)),
            pltpu.SemaphoreType.DMA((bits,)),
            pltpu.SemaphoreType.DMA((bits,)),
        ],
        compiler_params=pltpu.CompilerParams(
            collective_id=2, has_side_effects=True, vmem_limit_bytes=VMEM_BYTES
        ),
    )(
        grad_pre_three, act_three, k_out, k_out_other, pre_two, stats, vec, mask, pooled, excite,
        squeeze_pre, w_squeeze, w_excite
    )


CHAINS = ("out", "mid0", "mid1", "mid2", "in0", "in1")
ORDER_OUT = "A"
CHAIN_ORDERS = (ORDER_OUT, "B", "P", "Q", "P", "Q")
SCHEDULE = (
    "two", "M0", "M1", "C0", "out", "C1", "C2", "C3", "C4", "C5", "mid0", "out", "mid1", "C6",
    "C7", "sums", "out", "M2", "mid1", "out", "one", "K0", "mid2", "mid0", "mid1", "K1",
    "mid1", "mid2", "in0", "mid0", "mid1", "mid0", "X0", "X1", "in1", "in0", "mid2", "mid0",
    "out", "mid1", "mid2", "in1", "mid2", "X2", "mid0", "in0", "in0", "mid2", "mid1", "in1",
    "in0", "in1", "mid2", "in1", "in1", "in0", "mid0", "mid1", "X3", "in1", "in0", "mid2",
    "out", "mid0", "in0", "in1",
)


def first_kernel(
    plan,
    shard_out_hbm,
    grad_norm_hbm,
    pre_two_hbm,
    pre_one_hbm,
    act_one_hbm,
    x_hbm,
    w_mid_hbm,
    w_in_hbm,
    w_in_other_hbm,
    stats,
    vec,
    sums_two,
    mask,
    gathered_out,
    gathered_mid,
    gathered_in,
    grad_inputs_out,
    sums_out,
    flat,
    conv_rows,
    shifted,
    act_one,
    w_mid,
    grad_pre_one,
    grad_other,
    w_in,
    work_out,
    land_out,
    work_mid,
    land_mid,
    work_in,
    land_in,
    pay,
    slots,
    local_sem,
    pair_send,
    pair_recv,
    spread_send,
    spread_recv,
    chain_send,
    chain_recv,
    free,
):
    n, half, group = plan.dp, plan.half, plan.group
    me, core = lax.axis_index("dp"), lax.axis_index("rows")
    entry_barrier(n, me, core)

    def local(source, target, index):
        copy = pltpu.make_async_copy(source, target, local_sem.at[index])
        copy.start()
        return copy

    chains, targets, saves, waits, state = {}, {}, {}, {}, {}

    def begin(name, work, land, target, begun=0):
        index = CHAINS.index(name)
        steps = Steps(n, me, core, CHAIN_ORDERS[index])
        chains[name] = Chain(
            steps, work, land, chain_send.at[index], chain_recv.at[index], free.at[index], begun
        )
        targets[name] = target
        return chains[name]

    def advance(name):
        chain = chains[name]
        if name in saves:
            return
        chain.advance()
        if chain.done():
            index = CHAINS.index(name)
            saves[name] = local(chain.work, targets[name], 8 + index)

    out = begin("out", work_out, land_out, gathered_out, HANDED)
    load_shard = local(shard_out_hbm, out.here(), 2)
    waits["norm"] = local(grad_norm_hbm, flat, 0)
    waits["two"] = local(pre_two_hbm, conv_rows, 1)
    waits["act"] = local(act_one_hbm, act_one, 3)
    waits["mid"] = local(w_mid_hbm, w_mid, 4)
    waits["in"] = local(w_in_hbm, w_in.at[core], 5)
    waits["other"] = local(w_in_other_hbm, w_in.at[1 - core], 6)
    load_shard.wait()
    advance("out")
    count = stats[TOTAL : TOTAL + 1, :]

    def norm_two():
        for side in range(2):
            shifted[side, : plan.glob_base, :] = jnp.zeros((plan.glob_base, 3 * group), BF16)
            shifted[side, plan.glob_base + plan.glob_all : plan.small_base, :] = jnp.zeros(
                (plan.glob_width, 3 * group), BF16
            )
            for slot in range(plan.slots):
                low = plan.small_base + slot * plan.slot_conv + plan.slot_all
                shifted[side, low : low + plan.small_width, :] = jnp.zeros(
                    (plan.small_width, 3 * group), BF16
                )
        mean = stats[MEAN_TWO : MEAN_TWO + 1, :]
        inverse = stats[INVERSE_TWO : INVERSE_TWO + 1, :]
        scale = vec[GAIN_TWO : GAIN_TWO + 1, :] * inverse
        shift_mean = sums_two[SHIFT_TWO_SUM : SHIFT_TWO_SUM + 1, :] / count
        gain_mean = sums_two[GAIN_TWO_SUM : GAIN_TWO_SUM + 1, :] / count * inverse
        waits["norm"].wait()
        waits["two"].wait()

        def into_two(start, place, crop, carry):
            rows = pl.ds(start, TILE)
            centered = conv_rows[pl.ds(place, TILE), :] - mean
            grad = scale * (flat[rows, :] - shift_mean - centered * gain_mean)
            grad = grad * widen(mask[rows, :], half)
            after = pltpu.roll(grad, TILE - 1, 0)
            before = pltpu.roll(grad, 1, 0)
            for tap, value in enumerate((after, grad, before)):
                for side in range(2):
                    shifted[side, pl.ds(place, TILE), tap * group : (tap + 1) * group] = value[
                        :, side * group : (side + 1) * group
                    ].astype(BF16)
            return carry

        plan.sweep(into_two, 0)
        waits["one"] = local(pre_one_hbm, flat, 0)
        waits["act"].wait()

    def mid(tap):
        for side in range(2):
            lanes = slice(side * group, (side + 1) * group)
            total = None
            for low, length, width in plan.segments():
                first = low - (tap - 1) * width
                term = dot_tn(
                    act_one[low : low + length, lanes], shifted[side, first : first + length, :]
                )
                total = term if total is None else total + term
            work_mid[tap, lanes, :] = total.astype(BF16)
        name = CHAINS[1 + tap]
        begin(name, work_mid.at[tap], land_mid.at[tap], gathered_mid.at[tap])
        advance(name)
        read_shifted()

    def read_shifted():
        state["reads"] = state.get("reads", 0) + 1
        if state["reads"] == 3 + 8:
            waits["x"] = local(x_hbm, shifted.at[:, pl.ds(0, plan.all), pl.ds(0, half)], 7)

    def conv(index):
        if index == 0:
            waits["mid"].wait()
        low, length, width = plan.segments()[index // 4]
        block = length // 2
        side = index // 2 % 2
        at = low + index % 2 * block
        lanes = slice(side * group, (side + 1) * group)
        total = None
        for tap in range(3):
            first = at - (tap - 1) * width
            for column in range(3):
                taps = slice(column * group, (column + 1) * group)
                term = dot_nt(shifted[side, first : first + block, taps], w_mid[tap, taps, lanes])
                total = term if total is None else total + term
        conv_rows[at : at + block, lanes] = total
        read_shifted()

    mean = stats[MEAN_ONE : MEAN_ONE + 1, :]
    inverse = stats[INVERSE_ONE : INVERSE_ONE + 1, :]
    gain = vec[GAIN_ONE : GAIN_ONE + 1, :]
    shift = vec[SHIFT_ONE : SHIFT_ONE + 1, :]
    spread = Spread(n, me, core, pay, slots, spread_send, spread_recv)

    def sums_one():
        waits["one"].wait()

        def gradient(start, place, crop, carry):
            rows = pl.ds(start, TILE)
            normed = (flat[rows, :] - mean) * inverse
            norm = normed * gain + shift
            sigma = sigmoid(norm)
            grad = conv_rows[pl.ds(place, TILE), :] * silu_slope(norm, sigma)
            grad = grad * widen(mask[rows, :], half)
            conv_rows[pl.ds(place, TILE), :] = grad
            return carry[0] + rows_down(grad), carry[1] + rows_down(grad * normed)

        zero = jnp.zeros((8, half), F32)
        shift_sum, gain_sum = plan.sweep(gradient, (zero, zero))
        pay[:, :half] = jnp.sum(shift_sum, 0, keepdims=True)
        pay[:, half:] = jnp.sum(gain_sum, 0, keepdims=True)
        spread.start()

    def norm_one():
        spread.wait()
        totals = gather_sum(slots, n, 2 * half)
        sums_out[...] = jnp.zeros_like(sums_out)
        sums_out[SHIFT_ONE_SUM : SHIFT_ONE_SUM + 1, :] = totals[:, :half]
        sums_out[GAIN_ONE_SUM : GAIN_ONE_SUM + 1, :] = totals[:, half:]
        scale = gain * inverse
        shift_mean = totals[:, :half] / count
        gain_mean = totals[:, half:] / count * inverse

        def into_one(start, place, crop, carry):
            rows = pl.ds(start, TILE)
            centered = flat[rows, :] - mean
            grad = scale * (conv_rows[pl.ds(place, TILE), :] - shift_mean - centered * gain_mean)
            grad_pre_one[rows, :] = (grad * widen(mask[rows, :], half)).astype(BF16)
            return carry

        plan.sweep(into_one, 0)
        state["swaps"] = []
        for index, (place, start, length) in enumerate(plan.own_pieces(1 - core)):
            swap = to_partner(
                me,
                core,
                grad_pre_one.at[pl.ds(place, length), :],
                grad_other.at[pl.ds(start, length), :],
                pair_send.at[index],
                pair_recv.at[index],
            )
            swap.start()
            state["swaps"].append(swap)

    def kernel_in(side):
        if side == 0:
            waits["x"].wait()
        for part in range(2):
            lanes = slice(part * group, (part + 1) * group)
            work_in[side, lanes, :] = dot_tn(
                shifted[side, : plan.all, lanes], grad_pre_one[...]
            ).astype(BF16)
        name = CHAINS[4 + side]
        begin(name, work_in.at[side], land_in.at[side], gathered_in.at[side])
        advance(name)

    def inputs(index):
        if index == 0:
            waits["in"].wait()
            waits["other"].wait()
            for swap in state["swaps"]:
                swap.wait()
        part, side = index // 2, index % 2
        marks = (0, plan.glob_own, plan.own)
        rows = slice(marks[part], marks[part + 1])
        pieces = plan.own_pieces(core)
        pieces = pieces[:1] if part == 0 else pieces[1:]
        own = jnp.concatenate([grad_pre_one[pl.ds(spot, size), :] for spot, _, size in pieces], 0)
        grad_inputs_out[side, rows, :] = (
            dot_nt(own, w_in[core, side]) + dot_nt(grad_other[rows, :], w_in[1 - core, side])
        ).astype(BF16)

    blocks = {
        "two": norm_two,
        "sums": sums_one,
        "one": norm_one,
    }
    for tap in range(3):
        blocks["M%d" % tap] = functools.partial(mid, tap)
    for index in range(8):
        blocks["C%d" % index] = functools.partial(conv, index)
    for side in range(2):
        blocks["K%d" % side] = functools.partial(kernel_in, side)
    for index in range(4):
        blocks["X%d" % index] = functools.partial(inputs, index)
    for item in SCHEDULE:
        if item in blocks:
            blocks[item]()
        else:
            advance(item)
    while len(saves) < len(CHAINS):
        for name in CHAINS:
            advance(name)
    for name in CHAINS:
        saves[name].wait()


def first(
    plan, shard_out, grad_norm, pre_two, pre_one, act_one, x_all, w_mid, w_in, w_in_other, stats,
    vec, sums_two, mask
):
    n, half, group = plan.dp, plan.half, plan.group
    shape = jax.ShapeDtypeStruct
    pieces = 1 + plan.slots
    return pl.pallas_call(
        functools.partial(first_kernel, plan),
        out_shape=(
            shape((2 * half, half), BF16),
            shape((3, half, 3 * group), BF16),
            shape((2, half, half), BF16),
            shape((2, plan.own, half), BF16),
            shape((8, half), F32),
        ),
        in_specs=[ANY] * 9 + [VMEM] * 4,
        out_specs=(ANY, ANY, ANY, VMEM, VMEM),
        scratch_shapes=[
            pltpu.VMEM((plan.all, half), F32),
            pltpu.VMEM((plan.conv, half), F32),
            pltpu.VMEM((2, plan.conv, 3 * group), BF16),
            pltpu.VMEM((plan.conv, half), BF16),
            pltpu.VMEM(w_mid.shape, BF16),
            pltpu.VMEM((plan.all, half), BF16),
            pltpu.VMEM((plan.own, half), BF16),
            pltpu.VMEM((2,) + w_in.shape, BF16),
            pltpu.VMEM((2 * half, half), BF16),
            pltpu.VMEM((land_rows(n, 2 * half, begun=HANDED), half), BF16),
            pltpu.VMEM((3, half, 3 * group), BF16),
            pltpu.VMEM((3, land_rows(n, half), 3 * group), BF16),
            pltpu.VMEM((2, half, half), BF16),
            pltpu.VMEM((2, land_rows(n, half), half), BF16),
            pltpu.VMEM((1, 2 * half), F32),
            pltpu.VMEM((n, 1, 2 * half), F32),
            pltpu.SemaphoreType.DMA((14,)),
            pltpu.SemaphoreType.DMA((pieces,)),
            pltpu.SemaphoreType.DMA((pieces,)),
            pltpu.SemaphoreType.DMA((n,)),
            pltpu.SemaphoreType.DMA((n,)),
            pltpu.SemaphoreType.DMA((len(CHAINS), chain_slots(n))),
            pltpu.SemaphoreType.DMA((len(CHAINS), chain_slots(n))),
            pltpu.SemaphoreType.REGULAR((len(CHAINS), 4)),
        ],
        compiler_params=pltpu.CompilerParams(
            collective_id=3, has_side_effects=True, vmem_limit_bytes=VMEM_BYTES
        ),
    )(
        shard_out, grad_norm, pre_two, pre_one, act_one, x_all, w_mid, w_in, w_in_other, stats,
        vec, sums_two, mask
    )


def join_lanes(low, high, real):
    zeros = jnp.zeros_like(low)
    wide = jnp.concatenate([low, zeros], 1)
    moved = pltpu.roll(jnp.concatenate([high, zeros], 1), real, 1)
    lane = lax.broadcasted_iota(jnp.int32, wide.shape, 1)
    return jnp.where(lane < real, wide, moved)


def finish_kernel(
    plan,
    result_hbm,
    grad_summed_hbm,
    grad_inputs_hbm,
    out_hbm,
    in_hbm,
    mid_hbm,
    excite,
    squeeze,
    glob_out_hbm,
    small_out_hbm,
    glob_grad_hbm,
    small_grad_hbm,
    kernel_in_hbm,
    kernel_mid_hbm,
    kernel_out_hbm,
    squeeze_out,
    excite_out,
    result,
    grad_summed,
    grad_inputs,
    packed_out,
    packed_in,
    packed_mid,
    glob_out,
    small_out,
    glob_grad,
    small_grad,
    kernel_in,
    kernel_mid,
    kernel_out,
    load_sem,
    store_sem,
):
    half, group, width, real = plan.half, plan.group, plan.width, plan.half_real
    loads, stores = {}, []
    sources = (
        (mid_hbm, packed_mid),
        (out_hbm, packed_out),
        (in_hbm, packed_in),
        (result_hbm, result),
        (grad_summed_hbm, grad_summed),
        (grad_inputs_hbm, grad_inputs),
    )
    for index, (source, target) in enumerate(sources):
        loads[index] = pltpu.make_async_copy(source, target, load_sem.at[index])
        loads[index].start()

    def store(source, target):
        copy = pltpu.make_async_copy(source, target, store_sem.at[len(stores)])
        copy.start()
        stores.append(copy)

    loads[0].wait()
    for row_tap in range(3):
        for tap in range(3):
            lanes = slice(tap * group, (tap + 1) * group)
            low = packed_mid[row_tap, :group, lanes].astype(F32)
            high = packed_mid[row_tap, group:, lanes].astype(F32)
            kernel_mid[row_tap, tap] = join_lanes(low, high, width)[:width, :real]
        store(kernel_mid.at[row_tap], kernel_mid_hbm.at[row_tap])
    loads[1].wait()
    for piece in range(4):
        kernel_out[piece * width : (piece + 1) * width, :] = packed_out[
            piece * group : piece * group + width, :real
        ].astype(F32)
    store(kernel_out, kernel_out_hbm)
    loads[2].wait()
    for side in range(2):
        low = packed_in[side, :real, :group].astype(F32)
        high = packed_in[side, :real, group:].astype(F32)
        kernel_in[side * real : (side + 1) * real, :] = join_lanes(low, high, width)[:, :real]
    store(kernel_in, kernel_in_hbm)

    def maps(value, glob, small):
        def glob_row(row, carry):
            rows = pl.ds(pl.multiple_of(row * plan.glob_width, 16), plan.glob_width)
            glob[row, :, 0, :] = join_lanes(value(0, rows), value(1, rows), real)[
                : plan.glob_side, : plan.channels
            ]
            return carry

        def small_row(row, carry):
            place = plan.glob_own + row * plan.small_width
            rows = pl.ds(pl.multiple_of(place, 16), plan.small_width)
            small[row] = join_lanes(value(0, rows), value(1, rows), real)[
                : plan.small_side, : plan.channels
            ]
            return carry

        lax.fori_loop(0, plan.glob_height, glob_row, 0)
        lax.fori_loop(0, plan.slots * plan.small_height, small_row, 0)

    loads[3].wait()
    maps(lambda side, rows: result[side, rows, :].astype(F32), glob_out, small_out)
    store(glob_out, glob_out_hbm)
    store(small_out, small_out_hbm)
    loads[4].wait()
    loads[5].wait()
    maps(
        lambda side, rows: grad_summed[side, rows, :].astype(F32)
        + grad_inputs[side, rows, :].astype(F32),
        glob_grad,
        small_grad,
    )
    store(glob_grad, glob_grad_hbm)
    store(small_grad, small_grad_hbm)
    squeeze_out[:width, :] = squeeze[:width, :width]
    squeeze_out[width:, :] = squeeze[group : group + width, :width]
    excite_out[...] = join_lanes(excite[:, :group], excite[:, group:], width)[:width, :real]
    for copy in stores:
        copy.wait()


def finish(plan, result, grad_summed, grad_inputs, gathered_out, gathered_in, gathered_mid, excite, squeeze):
    shape = jax.ShapeDtypeStruct
    width, real, channels = plan.width, plan.half_real, plan.channels
    glob = (plan.glob_height, plan.glob_side, 1, channels)
    small = (plan.slots * plan.small_height, plan.small_side, channels)
    outs = (glob, small, glob, small, (channels, real), (3, 3, width, real), (channels, real))
    ins = (gathered_mid, gathered_out, gathered_in, result, grad_summed, grad_inputs)
    loaded = (result, grad_summed, grad_inputs, gathered_out, gathered_in, gathered_mid)
    return pl.pallas_call(
        functools.partial(finish_kernel, plan),
        out_shape=tuple(shape(out, F32) for out in outs)
        + (shape((real, width), F32), shape((width, real), F32)),
        in_specs=[ANY] * 6 + [VMEM] * 2,
        out_specs=(ANY,) * 7 + (VMEM,) * 2,
        scratch_shapes=[pltpu.VMEM(array.shape, BF16) for array in loaded]
        + [pltpu.VMEM(out, F32) for out in outs]
        + [pltpu.SemaphoreType.DMA((6,)), pltpu.SemaphoreType.DMA((9,))],
        compiler_params=pltpu.CompilerParams(vmem_limit_bytes=VMEM_BYTES),
    )(result, grad_summed, grad_inputs, gathered_out, gathered_in, gathered_mid, excite, squeeze)


def ungroup_lanes(array, plan):
    return jnp.concatenate(
        [array[..., : plan.width], array[..., plan.group : plan.group + plan.width]], -1
    )


def per_device(*arguments):
    dp = lax.axis_size("dp")
    core = lax.axis_index("rows")
    (
        plan, x_own, cot_own, w_in, w_mid, k_out, w_squeeze, w_excite, mask_all, mask_own, vec,
        vec_three
    ) = prepare(dp, *arguments)
    width, real = plan.width, plan.half_real
    (
        x_all, pre_one, act_one, pre_two, act_three, k_out_other, w_in_other, vec_three_other,
        stats, pooled, excite, squeeze_pre
    ) = forward(plan, x_own, w_in, w_mid, k_out, vec, vec_three, mask_all, w_squeeze, w_excite)
    result, grad_summed, grad_pre_three, sums_three = third(
        plan, act_three, k_out, k_out_other, x_own, cot_own, mask_own, vec, vec_three,
        vec_three_other
    )
    shard_out, grad_norm, grad_excite, grad_squeeze, sums_two = second(
        plan, grad_pre_three, act_three, k_out, k_out_other, pre_two, stats, vec, mask_all, pooled,
        excite, squeeze_pre, w_squeeze, w_excite
    )
    gathered_out, gathered_mid, gathered_in, grad_inputs, sums_one = first(
        plan, shard_out, grad_norm, pre_two, pre_one, act_one, x_all, w_mid, w_in, w_in_other, stats,
        vec, sums_two, mask_all
    )
    (
        glob_out, small_out, glob_grad, small_grad, grad_kernel_in, grad_kernel_mid,
        grad_kernel_out, grad_squeeze, grad_excite
    ) = finish(
        plan, result, grad_summed, grad_inputs, gathered_out, gathered_in, gathered_mid,
        grad_excite, grad_squeeze
    )
    glob_shape, small_shape = arguments[0].shape, arguments[1].shape
    sums = lax.dynamic_index_in_dim(sums_three, core, 0, False)

    def grouped(row):
        return ungroup_lanes(row, plan)

    return (
        glob_out.reshape(glob_shape),
        small_out.reshape(small_shape),
        glob_grad.reshape(glob_shape),
        small_grad.reshape(small_shape),
        grad_kernel_in,
        grad_kernel_mid,
        grad_kernel_out,
        grad_squeeze,
        sums_two[SQUEEZE_SUM, :width],
        grad_excite,
        grouped(sums_two[EXCITE_SUM]),
        grouped(sums_one[GAIN_ONE_SUM]),
        grouped(sums_one[SHIFT_ONE_SUM]),
        grouped(sums_two[GAIN_TWO_SUM]),
        grouped(sums_two[SHIFT_TWO_SUM]),
        sums[1, :real],
        sums[0, :real],
    )


def solution(mesh):
    maps = P("dp", "rows", None, None)
    vector = P("rows")
    columns = P(None, "rows")
    taps = P(None, None, None, "rows")
    return jax.shard_map(
        per_device,
        mesh=mesh,
        in_specs=(
            maps, maps, P("dp"), columns, taps, columns, P("rows", None), P(), columns,
        )
        + (vector,) * 7
        + (maps, maps),
        out_specs=(maps,) * 4
        + (columns, taps, columns, P("rows", None), P(), columns)
        + (vector,) * 7,
        check_vma=False,
    )
```

```python
import functools

import jax
import jax.numpy as jnp
from jax import lax
from jax.experimental import pallas as pl
from jax.experimental.pallas import tpu as pltpu
from jax.sharding import PartitionSpec as P

EPSILON = 1e-05
MESH = pl.DeviceIdType.MESH
F32 = jnp.float32
BF16 = jnp.bfloat16
ANY = pl.BlockSpec(memory_space=pl.ANY)
VMEM = pl.BlockSpec(memory_space=pltpu.VMEM)
LANE = 128
TILE = 64
VMEM_BYTES = 62 * 1024 * 1024


def round_up(value, step):
    return -(-value // step) * step


class Plan:
    def __init__(self, glob_shape, small_shape, group_width, dp):
        self.glob_height, self.glob_side = glob_shape[1], glob_shape[2]
        self.slots, self.small_height, self.small_side = small_shape[:3]
        self.channels = glob_shape[3]
        self.glob_width = round_up(self.glob_side + 1, 32)
        self.small_width = round_up(self.small_side + 1, 16)
        self.glob_own = self.glob_height * self.glob_width
        self.slot_own = self.small_height * self.small_width
        self.own = self.glob_own + self.slots * self.slot_own
        self.glob_all = 2 * self.glob_own
        self.slot_all = 2 * self.slot_own
        self.all = 2 * self.own
        self.glob_base = self.glob_width
        self.small_base = self.glob_all + 2 * self.glob_width
        self.slot_conv = self.slot_all + self.small_width
        self.small_conv = self.slots * self.slot_conv
        self.conv = self.small_base + self.small_conv
        self.width = group_width
        self.group = round_up(group_width, LANE)
        self.half = 2 * self.group
        self.half_real = self.channels // 2
        self.dp = dp
        self.glob_tiles = self.glob_all // TILE
        self.slot_tiles = self.slot_all // TILE
        self.slot_rows = round_up(1 + self.slots, 8)
        self.glob_area = float(2 * self.glob_height * self.glob_side)
        self.slot_area = float(2 * self.small_height * self.small_side)

    def own_pieces(self, core):
        pieces = [(pl.multiple_of(core * self.glob_own, 16), 0, self.glob_own)]
        for slot in range(self.slots):
            place = self.glob_all + slot * self.slot_all + core * self.slot_own
            pieces.append(
                (pl.multiple_of(place, 16), self.glob_own + slot * self.slot_own, self.slot_own)
            )
        return pieces

    def sweep(self, body, carry):
        def glob_step(tile, state):
            start = pl.multiple_of(tile * TILE, TILE)
            return body(start, pl.multiple_of(self.glob_base + start, 16), 0, state)

        def slot_step(tile, state):
            slot = tile // self.slot_tiles
            start = pl.multiple_of(self.glob_all + tile * TILE, TILE)
            place = self.small_base + tile * TILE + slot * self.small_width
            return body(start, pl.multiple_of(place, 16), 1 + slot, state)

        carry = lax.fori_loop(0, self.glob_tiles, glob_step, carry)
        return lax.fori_loop(0, self.slots * self.slot_tiles, slot_step, carry)

    def segments(self):
        return (
            (self.glob_base, self.glob_all, self.glob_width),
            (self.small_base, self.small_conv - self.small_width, self.small_width),
        )


def sigmoid(value):
    return 0.5 * jnp.tanh(0.5 * value) + 0.5


def rows_down(tile):
    return jnp.sum(tile.reshape(tile.shape[0] // 8, 8, tile.shape[1]), 0)


def widen(mask, lanes):
    return jnp.concatenate([mask] * (lanes // mask.shape[1]), 1)


def dot(left, right):
    return jnp.dot(left, right, preferred_element_type=F32)


def dot_nt(left, right):
    return lax.dot_general(left, right, (((1,), (1,)), ((), ())), preferred_element_type=F32)


def dot_tn(left, right):
    return lax.dot_general(left, right, (((0,), (0,)), ((), ())), preferred_element_type=F32)


def split_dot(left, right, nt=False):
    high = left.astype(BF16)
    low = (left - high.astype(F32)).astype(BF16)
    call = dot_nt if nt else dot
    return call(high, right) + call(low, right)


def entry_barrier(n, me, core):
    barrier = pltpu.get_barrier_semaphore()

    def greet(step, carry):
        pl.semaphore_signal(
            barrier, inc=1, device_id=(lax.rem(me + step, n), core), device_id_type=MESH
        )
        return carry

    lax.fori_loop(1, n, greet, 0)
    pl.semaphore_signal(barrier, inc=1, device_id=(me, 1 - core), device_id_type=MESH)
    pl.semaphore_wait(barrier, n)


class Spread:
    def __init__(self, n, me, core, source, slots, send, recv):
        self.n, self.me, self.core = n, me, core
        self.source, self.slots, self.send, self.recv = source, slots, send, recv

    def copy(self, step):
        return pltpu.make_async_remote_copy(
            src_ref=self.source,
            dst_ref=self.slots.at[self.me],
            send_sem=self.send.at[step],
            recv_sem=self.recv.at[step],
            device_id=(lax.rem(self.me + step, self.n), self.core),
            device_id_type=MESH,
        )

    def start(self):
        def begin(step, carry):
            self.copy(step).start()
            return carry

        lax.fori_loop(1, self.n, begin, 0)
        self.slots[pl.ds(self.me, 1)] = self.source[...][None]

    def wait(self):
        def end(step, carry):
            self.copy(step).wait()
            return carry

        lax.fori_loop(1, self.n, end, 0)


def to_partner(me, core, source, target, send, recv):
    return pltpu.make_async_remote_copy(
        src_ref=source,
        dst_ref=target,
        send_sem=send,
        recv_sem=recv,
        device_id=(me, 1 - core),
        device_id_type=MESH,
    )


def merge_moments(slots, n, lanes):
    def add(step, carry):
        total, count = carry
        return (total + slots[step, :, :lanes], count + slots[step, :, 2 * lanes : 2 * lanes + LANE])

    total, count = lax.fori_loop(
        0, n, add, (jnp.zeros((1, lanes), F32), jnp.zeros((1, LANE), F32))
    )
    wide_count = widen(count, lanes)
    mean = total / wide_count

    def spread(step, carry):
        own_count = widen(slots[step, :, 2 * lanes : 2 * lanes + LANE], lanes)
        gap = slots[step, :, :lanes] / own_count - mean
        return carry + slots[step, :, lanes : 2 * lanes] + own_count * gap * gap

    squares = lax.fori_loop(0, n, spread, jnp.zeros((1, lanes), F32))
    return mean, squares / wide_count, wide_count


def local_moments(plan, values, mask, which, count):
    lanes = plan.half

    def add(start, place, crop, carry):
        row = start if which == "all" else place
        tile = values[pl.ds(row, TILE), :] * widen(mask[pl.ds(start, TILE), :], lanes)
        return carry + rows_down(tile)

    total = jnp.sum(plan.sweep(add, jnp.zeros((8, lanes), F32)), 0, keepdims=True)
    mean = total / count

    def spread(start, place, crop, carry):
        row = start if which == "all" else place
        gap = (values[pl.ds(row, TILE), :] - mean) * widen(mask[pl.ds(start, TILE), :], lanes)
        return carry + rows_down(gap * gap)

    squares = jnp.sum(plan.sweep(spread, jnp.zeros((8, lanes), F32)), 0, keepdims=True)
    return total, squares


GAIN_ONE, SHIFT_ONE, GAIN_TWO, SHIFT_TWO, EXCITE_BIAS, SQUEEZE_BIAS, COUNT = range(7)
MEAN_ONE, INVERSE_ONE, MEAN_TWO, INVERSE_TWO, TOTAL = range(5)


def lane_of(shape):
    return lax.broadcasted_iota(jnp.int32, shape, len(shape) - 1)


def row_of(shape):
    return lax.broadcasted_iota(jnp.int32, shape, len(shape) - 2)


def group_lanes(value, plan):
    lane = lane_of(value.shape)
    moved = pltpu.roll(value, plan.group - plan.width, 1)
    return jnp.where(lane < plan.width, value, jnp.where(lane < plan.group, 0.0, moved))


def fill_mask(plan, mask, crops, slot_rows, live_count):
    step = 32
    row = row_of((step, LANE))
    glob = (lax.rem(row, plan.glob_width) < plan.glob_side).astype(F32)
    small = (lax.rem(row, plan.small_width) < plan.small_side).astype(F32)

    def glob_step(tile, carry):
        mask[pl.ds(pl.multiple_of(tile * step, step), step), :] = glob
        return carry

    lax.fori_loop(0, crops // step, glob_step, 0)
    for slot in range(plan.slots):
        live = jnp.clip(live_count - float(slot), 0.0, 1.0)

        def slot_step(tile, carry, slot=slot, live=live):
            start = crops + slot * slot_rows + tile * step
            mask[pl.ds(pl.multiple_of(start, step), step), :] = small * live
            return carry

        lax.fori_loop(0, slot_rows // step, slot_step, 0)


def zero_borders(plan, shifted):
    lanes = shifted.shape[2]
    for side in range(2):
        shifted[side, : plan.glob_base, :] = jnp.zeros((plan.glob_base, lanes), BF16)
        shifted[side, plan.glob_base + plan.glob_all : plan.small_base, :] = jnp.zeros(
            (plan.glob_width, lanes), BF16
        )
        for slot in range(plan.slots):
            low = plan.small_base + slot * plan.slot_conv + plan.slot_all
            shifted[side, low : low + plan.small_width, :] = jnp.zeros(
                (plan.small_width, lanes), BF16
            )


def forward_kernel(
    plan,
    live,
    glob_hbm,
    small_hbm,
    kernel_in_hbm,
    kernel_mid_hbm,
    kernel_out_hbm,
    squeeze_hbm,
    excite_hbm,
    vec_raw,
    x_out,
    pre_one_out,
    act_one_out,
    pre_two_out,
    act_three_out,
    w_mid_out,
    k_out_both,
    w_in_both,
    vec_three_other,
    vec,
    mask,
    w_squeeze,
    w_excite,
    stats,
    pooled_out,
    excite_out,
    squeeze_pre_out,
    glob,
    small,
    kernel_in,
    taps,
    kernel_out,
    squeeze,
    excite,
    wide,
    table,
    x_all,
    pre_one,
    shifted,
    w_in,
    w_mid,
    pre_two,
    act_three,
    k_out,
    pay_one,
    slots_one,
    pay_two,
    slots_two,
    squeeze_send,
    squeeze_recv,
    local_sem,
    send_sem,
    recv_sem,
    spread_send,
    spread_recv,
):
    n, half, group, width = plan.dp, plan.half, plan.group, plan.width
    channels, real = plan.channels, plan.half_real
    me, core = lax.axis_index("dp"), lax.axis_index("rows")
    pieces = plan.own_pieces(core)

    def local(source, target, index):
        copy = pltpu.make_async_copy(source, target, local_sem.at[index])
        copy.start()
        return copy

    load_glob = local(glob_hbm, glob, 0)
    load_small = local(small_hbm, small, 1)
    load_in = local(kernel_in_hbm, kernel_in, 2)
    load_taps = [local(kernel_mid_hbm.at[tap], taps.at[tap], 3 + tap) for tap in range(3)]
    load_out = local(kernel_out_hbm, kernel_out, 6)
    load_squeeze = local(squeeze_hbm, squeeze, 7)
    load_excite = local(excite_hbm, excite, 8)
    entry_barrier(n, me, core)

    def partner(source, target, index):
        copy = to_partner(me, core, source, target, send_sem.at[index], recv_sem.at[index])
        copy.start()
        return copy

    load_glob.wait()

    def glob_row(row, carry):
        start = pieces[0][0] + row * plan.glob_width
        rows = pl.ds(pl.multiple_of(start, 16), plan.glob_width)
        wide[: plan.glob_side, :channels] = glob[row].astype(F32)
        for side in range(2):
            x_all[side, rows, :] = wide[: plan.glob_width, side * half : (side + 1) * half].astype(BF16)
        return carry

    def small_row(row, carry):
        slot = row // plan.small_height
        start = plan.glob_all + slot * plan.slot_all + core * plan.slot_own
        start = start + lax.rem(row, plan.small_height) * plan.small_width
        rows = pl.ds(pl.multiple_of(start, 16), plan.small_width)
        wide[: plan.small_side, :channels] = small[row].astype(F32)
        for side in range(2):
            x_all[side, rows, :] = wide[: plan.small_width, side * half : (side + 1) * half].astype(
                BF16
            )
        return carry

    def send_piece(index):
        part = x_all.at[:, pl.ds(pieces[index][0], pieces[index][2]), :]
        return partner(part, part, index)

    wide[...] = jnp.zeros_like(wide)
    lax.fori_loop(0, plan.glob_height, glob_row, 0)
    x_remote = [send_piece(0)]
    load_small.wait()
    wide[...] = jnp.zeros_like(wide)
    lax.fori_loop(0, plan.slots * plan.small_height, small_row, 0)
    x_remote += [send_piece(1 + slot) for slot in range(plan.slots)]

    table[...] = jnp.zeros_like(table)
    load_in.wait()
    for start in range(0, channels, group):
        length = min(group, channels - start)
        table[:length, :real] = kernel_in[start : start + length, :].astype(F32)
        block = group_lanes(table[:group, :], plan)
        if length < group:
            block = jnp.where(row_of(block.shape) < length, block, 0.0)
        low = start % half
        w_in[start // half, low : low + group, :] = block.astype(BF16)
    base = len(pieces)
    send_in = partner(w_in, w_in_both.at[core], base)

    live_count = live[0].astype(F32)
    raw = vec_raw[:8, :]
    grouped = group_lanes(raw, plan)
    chip_count = jnp.zeros((1, half), F32) + (plan.glob_area + plan.slot_area * live_count)
    row = row_of(raw.shape)
    vec[...] = jnp.where(row == SQUEEZE_BIAS, raw, jnp.where(row == COUNT, chip_count, grouped))
    send_vec = partner(vec_raw.at[pl.ds(8, 8), :], vec_three_other, base + 1)
    fill_mask(plan, mask, plan.glob_all, plan.slot_all, live_count)

    def product(owner):
        place = pl.multiple_of(owner * plan.glob_own, 16)
        rows = pl.ds(place, plan.glob_own)
        pre_one[rows, :] = dot(x_all[0, rows, :], w_in[0]) + dot(x_all[1, rows, :], w_in[1])
        places = [spot for spot, _, _ in plan.own_pieces(owner)[1:]]
        sides = [
            jnp.concatenate([x_all[side, pl.ds(spot, plan.slot_own), :] for spot in places], 0)
            for side in range(2)
        ]
        result = dot(sides[0], w_in[0]) + dot(sides[1], w_in[1])
        for slot, spot in enumerate(places):
            pre_one[pl.ds(spot, plan.slot_own), :] = result[
                slot * plan.slot_own : (slot + 1) * plan.slot_own
            ]

    def prepare_tap(tap):
        load_taps[tap].wait()
        table[:width, :real] = taps[tap % 3].astype(F32)
        block = group_lanes(table[:group, :], plan)
        block = jnp.where(row_of(block.shape) < width, block, 0.0)
        w_mid[tap // 3, tap % 3 * group : (tap % 3 + 1) * group, :] = block.astype(BF16)
        if tap + 3 < 9:
            load_taps.append(local(kernel_mid_hbm.at[tap + 3], taps.at[tap % 3], 3 + tap % 3))

    product(core)
    zero_borders(plan, shifted)
    for copy in x_remote:
        copy.wait()
    product(1 - core)
    saves = [local(x_all, x_out, 9), local(pre_one, pre_one_out, 10)]

    def local_part(values, which, pay):
        total, squares = local_moments(plan, values, mask, which, vec[COUNT : COUNT + 1, :])
        pay[:, :half] = total
        pay[:, half : 2 * half] = squares
        pay[:, 2 * half :] = vec[COUNT : COUNT + 1, :LANE]

    def spread_of(pay, slots, index):
        spread = Spread(n, me, core, pay, slots, spread_send.at[index], spread_recv.at[index])
        spread.start()
        return spread

    local_part(pre_one, "all", pay_one)
    spread = spread_of(pay_one, slots_one, 0)
    for tap in range(9):
        prepare_tap(tap)
    saves.append(local(w_mid, w_mid_out, 11))
    spread.wait()
    mean, variance, count = merge_moments(slots_one, n, half)
    inverse = lax.rsqrt(variance + EPSILON)
    stats[...] = jnp.zeros_like(stats)
    stats[MEAN_ONE : MEAN_ONE + 1, :] = mean
    stats[INVERSE_ONE : INVERSE_ONE + 1, :] = inverse
    stats[TOTAL : TOTAL + 1, :] = count
    scale = inverse * vec[GAIN_ONE : GAIN_ONE + 1, :]
    shift = vec[SHIFT_ONE : SHIFT_ONE + 1, :]

    def activate_one(start, place, crop, carry):
        norm = (pre_one[pl.ds(start, TILE), :] - mean) * scale + shift
        act = norm * sigmoid(norm) * widen(mask[pl.ds(start, TILE), :], half)
        before = pltpu.roll(act, 1, 0)
        after = pltpu.roll(act, TILE - 1, 0)
        for tap, value in enumerate((before, act, after)):
            for side in range(2):
                shifted[side, pl.ds(place, TILE), tap * group : (tap + 1) * group] = value[
                    :, side * group : (side + 1) * group
                ].astype(BF16)
        return carry

    plan.sweep(activate_one, 0)
    for side in range(2):
        saves.append(
            local(
                shifted.at[side, :, group : 2 * group],
                act_one_out.at[:, side * group : (side + 1) * group],
                12 + side,
            )
        )

    for low, length, wide_row in plan.segments():
        for side in range(2):
            lanes = slice(side * group, (side + 1) * group)
            block = length // 2
            for part in range(2):
                at = low + part * block
                total = None
                for tap in range(3):
                    first = at + (tap - 1) * wide_row
                    term = dot(shifted[side, first : first + block, :], w_mid[tap, :, lanes])
                    total = term if total is None else total + term
                pre_two[at : at + block, lanes] = total
    saves.append(local(pre_two, pre_two_out, 14))

    local_part(pre_two, "conv", pay_two)
    spread = spread_of(pay_two, slots_two, 1)
    load_out.wait()
    for piece in range(4):
        low = piece * width // 16 * 16
        length = min(table.shape[0], channels - low)
        table[:length, :real] = kernel_out[low : low + length, :].astype(F32)
        off = piece * width - low
        block = table[off : off + group, :]
        block = jnp.where(row_of(block.shape) < width, block, 0.0)
        place = piece % 2 * group
        k_out[piece // 2, place : place + group, :] = block.astype(BF16)
    send_out = partner(k_out, k_out_both.at[core], base + 2)
    load_squeeze.wait()
    for piece in range(2):
        low = piece * width // 16 * 16
        length = min(table.shape[0], 2 * width - low)
        table[:length, :width] = squeeze[low : low + length, :].astype(F32)
        off = piece * width - low
        block = table[off : off + group, :group]
        keep = (row_of(block.shape) < width) & (lane_of(block.shape) < width)
        w_squeeze[piece * group : (piece + 1) * group, :] = jnp.where(keep, block, 0.0).astype(BF16)
    load_excite.wait()
    table[:width, :real] = excite[...].astype(F32)
    block = group_lanes(table[:group, :], plan)
    w_excite[...] = jnp.where(row_of(block.shape) < width, block, 0.0).astype(BF16)
    spread.wait()
    mean_two, variance, _ = merge_moments(slots_two, n, half)
    inverse_two = lax.rsqrt(variance + EPSILON)
    stats[MEAN_TWO : MEAN_TWO + 1, :] = mean_two
    stats[INVERSE_TWO : INVERSE_TWO + 1, :] = inverse_two
    scale_two = inverse_two * vec[GAIN_TWO : GAIN_TWO + 1, :]
    shift_two = vec[SHIFT_TWO : SHIFT_TWO + 1, :]
    pooled_out[...] = jnp.zeros_like(pooled_out)
    saves[1].wait()
    act_two = pre_one

    def activate_two(start, place, crop, carry):
        norm = (pre_two[pl.ds(place, TILE), :] - mean_two) * scale_two + shift_two
        act = norm * sigmoid(norm) * widen(mask[pl.ds(start, TILE), :], half)
        act_two[pl.ds(start, TILE), :] = act
        pooled_out[pl.ds(crop, 1), :] += jnp.sum(act, 0, keepdims=True)
        return carry

    plan.sweep(activate_two, 0)
    pooled_out[:1, :] = pooled_out[:1, :] * (1.0 / plan.glob_area)
    pooled_out[1:, :] = pooled_out[1:, :] * (1.0 / plan.slot_area)
    part = split_dot(pooled_out[...], w_squeeze[...])
    squeeze_send[...] = part
    swap = partner(squeeze_send, squeeze_recv, base + 3)
    swap.wait()
    squeeze_pre = part + squeeze_recv[...] + vec[SQUEEZE_BIAS : SQUEEZE_BIAS + 1, :group]
    squeeze_pre_out[...] = squeeze_pre
    squeezed = squeeze_pre * sigmoid(squeeze_pre)
    excite_out[...] = sigmoid(
        split_dot(squeezed, w_excite[...]) + vec[EXCITE_BIAS : EXCITE_BIAS + 1, :]
    )
    saves.append(local(w_in, w_in_both.at[core], 15))
    saves.append(local(k_out, k_out_both.at[core], 16))

    def activate_three(start, place, crop, carry):
        act_three[core, pl.ds(start, TILE), :] = (
            act_two[pl.ds(start, TILE), :] * excite_out[pl.ds(crop, 1), :]
        ).astype(BF16)
        return carry

    plan.sweep(activate_three, 0)
    exchange = partner(act_three.at[core], act_three.at[core], base + 4)
    saves.append(local(act_three.at[core], act_three_out.at[core], 17))
    for copy in (send_in, send_vec, send_out, exchange):
        copy.wait()
    saves.append(local(act_three.at[1 - core], act_three_out.at[1 - core], 18))
    for index, copy in enumerate(saves):
        if index != 1:
            copy.wait()


def forward(
    plan, live, glob, small, kernel_in, kernel_mid, kernel_out, squeeze, excite, vec_raw
):
    n, half, group = plan.dp, plan.half, plan.group
    shape = jax.ShapeDtypeStruct
    copies = 1 + plan.slots
    pay = 2 * half + LANE
    smem = pl.BlockSpec(memory_space=pltpu.SMEM)
    return pl.pallas_call(
        functools.partial(forward_kernel, plan),
        out_shape=(
            shape((2, plan.all, half), BF16),
            shape((plan.all, half), F32),
            shape((plan.conv, half), BF16),
            shape((plan.conv, half), F32),
            shape((2, plan.all, half), BF16),
            shape((3, 3 * group, half), BF16),
            shape((2, 2, half, half), BF16),
            shape((2, 2, half, half), BF16),
            shape((8, half), F32),
            shape((8, half), F32),
            shape((plan.all, LANE), F32),
            shape((half, group), BF16),
            shape((group, half), BF16),
            shape((8, half), F32),
            shape((plan.slot_rows, half), F32),
            shape((plan.slot_rows, half), F32),
            shape((plan.slot_rows, group), F32),
        ),
        in_specs=[smem] + [ANY] * 7 + [VMEM],
        out_specs=(ANY,) * 8 + (VMEM,) * 9,
        scratch_shapes=[
            pltpu.VMEM(glob.shape, BF16),
            pltpu.VMEM(small.shape, BF16),
            pltpu.VMEM(kernel_in.shape, BF16),
            pltpu.VMEM((3,) + kernel_mid.shape[1:], BF16),
            pltpu.VMEM(kernel_out.shape, BF16),
            pltpu.VMEM(squeeze.shape, BF16),
            pltpu.VMEM(excite.shape, BF16),
            pltpu.VMEM((32, 2 * half), F32),
            pltpu.VMEM((group + 16, half), F32),
            pltpu.VMEM((2, plan.all, half), BF16),
            pltpu.VMEM((plan.all, half), F32),
            pltpu.VMEM((2, plan.conv, 3 * group), BF16),
            pltpu.VMEM((2, half, half), BF16),
            pltpu.VMEM((3, 3 * group, half), BF16),
            pltpu.VMEM((plan.conv, half), F32),
            pltpu.VMEM((2, plan.all, half), BF16),
            pltpu.VMEM((2, half, half), BF16),
            pltpu.VMEM((1, pay), F32),
            pltpu.VMEM((n, 1, pay), F32),
            pltpu.VMEM((1, pay), F32),
            pltpu.VMEM((n, 1, pay), F32),
            pltpu.VMEM((plan.slot_rows, group), F32),
            pltpu.VMEM((plan.slot_rows, group), F32),
            pltpu.SemaphoreType.DMA((19,)),
            pltpu.SemaphoreType.DMA((copies + 5,)),
            pltpu.SemaphoreType.DMA((copies + 5,)),
            pltpu.SemaphoreType.DMA((2, n)),
            pltpu.SemaphoreType.DMA((2, n)),
        ],
        compiler_params=pltpu.CompilerParams(
            collective_id=0, has_side_effects=True, vmem_limit_bytes=VMEM_BYTES
        ),
    )(live, glob, small, kernel_in, kernel_mid, kernel_out, squeeze, excite, vec_raw)


def vector_table(vectors, plan):
    pieces = []
    for vector in vectors:
        size = 0
        if vector is not None:
            size = vector.shape[0]
            pieces.append(vector.astype(F32))
        if plan.half > size:
            pieces.append(jnp.zeros((plan.half - size,), F32))
    return jnp.concatenate(pieces).reshape(len(vectors), plan.half)


def own_steps(plan, body, carry):
    step = 32

    def run(tile, state):
        return body(pl.multiple_of(tile * step, step), step, state)

    return lax.fori_loop(0, plan.own // step, run, carry)


def merge_two(first, second, lanes):
    sums = [part[:, :lanes] for part in (first, second)]
    squares = [part[:, lanes : 2 * lanes] for part in (first, second)]
    counts = [widen(part[:, 2 * lanes :], lanes) for part in (first, second)]
    total = sums[0] + sums[1]
    count = counts[0] + counts[1]
    mean = total / count
    spread = squares[0] + squares[1]
    for index in range(2):
        gap = sums[index] / counts[index] - mean
        spread = spread + counts[index] * gap * gap
    return total, spread, count


def split_maps(plan, glob, small, target, wide):
    half, real = plan.half, plan.half_real
    low = real // LANE * LANE

    def place(source, row, start, size, real_size):
        wide[:real_size, : plan.channels] = source[row].astype(F32)
        rows = pl.ds(pl.multiple_of(start, 16), size)
        first = wide[:size, :half]
        target[0, rows, :] = jnp.where(lane_of(first.shape) < real, first, 0.0).astype(BF16)
        second = wide[:size, low:]
        moved = pltpu.roll(second, second.shape[1] - (real - low), 1)
        target[1, rows, :] = moved[:, :half].astype(BF16)

    def glob_row(row, carry):
        place(glob, row, row * plan.glob_width, plan.glob_width, plan.glob_side)
        return carry

    def small_row(row, carry):
        start = plan.glob_own + row * plan.small_width
        place(small, row, start, plan.small_width, plan.small_side)
        return carry

    wide[...] = jnp.zeros_like(wide)
    lax.fori_loop(0, plan.glob_height, glob_row, 0)
    wide[...] = jnp.zeros_like(wide)
    lax.fori_loop(0, plan.slots * plan.small_height, small_row, 0)


def third_kernel(
    plan,
    live,
    act_three_hbm,
    k_out_hbm,
    glob_hbm,
    small_hbm,
    glob_cot_hbm,
    small_cot_hbm,
    vec,
    vec_raw,
    vec_three_other,
    result_out,
    grad_summed_out,
    grad_pre_three_out,
    sums_out,
    act_three,
    k_out,
    pre_three,
    grad_summed,
    grad_pre_three,
    pay,
    pair,
    chip,
    slots,
    finals,
    pay_back,
    pair_back,
    chip_back,
    slots_back,
    finals_back,
    vec_three,
    glob,
    small,
    glob_cot,
    small_cot,
    x_own,
    cot_own,
    mask,
    wide,
    local_sem,
    send_sem,
    recv_sem,
    spread_send,
    spread_recv,
):
    n, half = plan.dp, plan.half
    me, core = lax.axis_index("dp"), lax.axis_index("rows")
    pieces = plan.own_pieces(core)

    def local(source, target, index):
        copy = pltpu.make_async_copy(source, target, local_sem.at[index])
        copy.start()
        return copy

    def partner(source, target, index):
        copy = to_partner(me, core, source, target, send_sem.at[index], recv_sem.at[index])
        copy.start()
        return copy

    loads = [
        local(
            act_three_hbm.at[:, pl.ds(place, length), :],
            act_three.at[:, pl.ds(start, length), :],
            index,
        )
        for index, (place, start, length) in enumerate(pieces)
    ]
    base = len(pieces)
    loads.append(local(k_out_hbm, k_out, base))
    raws = [
        local(source, target, 3 * base + 1 + index)
        for index, (source, target) in enumerate(
            (
                (glob_hbm, glob),
                (small_hbm, small),
                (glob_cot_hbm, glob_cot),
                (small_cot_hbm, small_cot),
            )
        )
    ]
    entry_barrier(n, me, core)
    vec_three[core] = vec_raw[8:, :]
    vec_three[1 - core] = vec_three_other[...]
    fill_mask(plan, mask, plan.glob_own, plan.slot_own, live[0].astype(F32))
    for copy in loads:
        copy.wait()
    own_count = 0.5 * vec[COUNT : COUNT + 1, :]

    block = plan.own // 2
    for side in range(2):

        def product(part, carry, side=side):
            rows = pl.ds(pl.multiple_of(part * block, 16), block)
            pre_three[side, rows, :] = dot(act_three[0, rows, :], k_out[side, 0]) + dot(
                act_three[1, rows, :], k_out[side, 1]
            )
            return carry

        lax.fori_loop(0, 2, product, 0)

    for side in range(2):

        def add(row, step, carry, side=side):
            rows = pl.ds(row, step)
            return carry + rows_down(pre_three[side, rows, :] * widen(mask[rows, :], half))

        total = jnp.sum(own_steps(plan, add, jnp.zeros((8, half), F32)), 0, keepdims=True)
        mean = total / own_count

        def spread(row, step, carry, side=side, mean=mean):
            rows = pl.ds(row, step)
            gap = (pre_three[side, rows, :] - mean) * widen(mask[rows, :], half)
            return carry + rows_down(gap * gap)

        squares = jnp.sum(own_steps(plan, spread, jnp.zeros((8, half), F32)), 0, keepdims=True)
        pay[side, :, :half] = total
        pay[side, :, half : 2 * half] = squares
        pay[side, :, 2 * half :] = own_count[:, :LANE]
    partner(pay.at[1 - core], pair, 0).wait()
    total, squares, count = merge_two(pay[core], pair[...], half)
    chip[:, :half] = total
    chip[:, half : 2 * half] = squares
    chip[:, 2 * half :] = count[:, :LANE]
    exchange = Spread(n, me, core, chip, slots, spread_send.at[0], spread_recv.at[0])
    exchange.start()
    for copy in raws:
        copy.wait()
    split_maps(plan, glob, small, x_own, wide)
    split_maps(plan, glob_cot, small_cot, cot_own, wide)
    exchange.wait()
    mean, variance, full_count = merge_moments(slots, n, half)
    finals[core, :, :half] = mean
    finals[core, :, half:] = lax.rsqrt(variance + EPSILON)
    partner(finals.at[core], finals.at[core], 1).wait()

    for side in range(2):
        mean = finals[side, :, :half]
        inverse = finals[side, :, half:]
        gain = vec_three[side, :1, :]
        shift = vec_three[side, 1:2, :]

        def outer(row, step, carry, side=side, mean=mean, inverse=inverse, gain=gain, shift=shift):
            rows = pl.ds(row, step)
            seen = widen(mask[rows, :], half)
            normed = (pre_three[side, rows, :] - mean) * inverse
            summed = normed * gain + shift + x_own[side, rows, :].astype(F32)
            sigma = sigmoid(summed)
            result_out[side, rows, :] = (seen * summed * sigma).astype(BF16)
            slope = sigma * (1.0 + summed * (1.0 - sigma))
            grad = cot_own[side, rows, :].astype(F32) * seen * slope
            grad_summed[side, rows, :] = grad
            grad_summed_out[side, rows, :] = grad.astype(BF16)
            return carry[0] + rows_down(grad), carry[1] + rows_down(grad * normed)

        zero = jnp.zeros((8, half), F32)
        shift_sum, gain_sum = own_steps(plan, outer, (zero, zero))
        pay_back[side, :, :half] = jnp.sum(shift_sum, 0, keepdims=True)
        pay_back[side, :, half:] = jnp.sum(gain_sum, 0, keepdims=True)
    partner(pay_back.at[1 - core], pair_back, 2).wait()
    chip_back[...] = pay_back[core] + pair_back[...]
    exchange = Spread(n, me, core, chip_back, slots_back, spread_send.at[1], spread_recv.at[1])
    exchange.start()
    exchange.wait()

    finals_back[core] = gather_sum(slots_back, n, 2 * half)
    partner(finals_back.at[core], finals_back.at[core], 3).wait()
    copies = []
    for side in range(2):
        mean = finals[side, :, :half]
        inverse = finals[side, :, half:]
        shift_sum = finals_back[side, :, :half]
        gain_sum = finals_back[side, :, half:]
        sums_out[side] = jnp.concatenate([shift_sum, gain_sum, jnp.zeros((6, half), F32)], 0)
        scale = vec_three[side, :1, :] * inverse
        shift_mean = shift_sum / full_count
        gain_mean = gain_sum / full_count

        def inner(
            row, step, carry, side=side, mean=mean, inverse=inverse, scale=scale,
            shift_mean=shift_mean, gain_mean=gain_mean
        ):
            rows = pl.ds(row, step)
            normed = (pre_three[side, rows, :] - mean) * inverse
            grad = scale * (grad_summed[side, rows, :] - shift_mean - normed * gain_mean)
            grad_pre_three[side, rows, :] = (grad * widen(mask[rows, :], half)).astype(BF16)
            return carry

        own_steps(plan, inner, 0)
        for index, (place, start, length) in enumerate(pieces):
            source = grad_pre_three.at[side, pl.ds(start, length), :]
            target = grad_pre_three_out.at[side, pl.ds(place, length), :]
            copies.append(partner(source, target, 4 + side * base + index))
            copies.append(local(source, target, base + 1 + side * base + index))
    for copy in copies:
        copy.wait()


def gather_sum(slots, n, lanes):
    def add(step, carry):
        return carry + slots[step]

    return lax.fori_loop(0, n, add, jnp.zeros((1, lanes), F32))


def third(
    plan, live, act_three, k_out, glob, small, glob_cot, small_cot, vec, vec_raw, vec_three_other
):
    n, half = plan.dp, plan.half
    shape = jax.ShapeDtypeStruct
    pieces = 1 + plan.slots
    pay = 2 * half + LANE
    own = (2, plan.own, half)
    return pl.pallas_call(
        functools.partial(third_kernel, plan),
        out_shape=(
            shape(own, BF16),
            shape(own, BF16),
            shape((2, plan.all, half), BF16),
            shape((2, 8, half), F32),
        ),
        in_specs=[pl.BlockSpec(memory_space=pltpu.SMEM)] + [ANY] * 6 + [VMEM] * 3,
        out_specs=(VMEM, VMEM, ANY, VMEM),
        scratch_shapes=[
            pltpu.VMEM(own, BF16),
            pltpu.VMEM(k_out.shape, BF16),
            pltpu.VMEM(own, F32),
            pltpu.VMEM(own, F32),
            pltpu.VMEM(own, BF16),
            pltpu.VMEM((2, 1, pay), F32),
            pltpu.VMEM((1, pay), F32),
            pltpu.VMEM((1, pay), F32),
            pltpu.VMEM((n, 1, pay), F32),
            pltpu.VMEM((2, 1, 2 * half), F32),
            pltpu.VMEM((2, 1, 2 * half), F32),
            pltpu.VMEM((1, 2 * half), F32),
            pltpu.VMEM((1, 2 * half), F32),
            pltpu.VMEM((n, 1, 2 * half), F32),
            pltpu.VMEM((2, 1, 2 * half), F32),
            pltpu.VMEM((2,) + vec_three_other.shape, F32),
            pltpu.VMEM(glob.shape, BF16),
            pltpu.VMEM(small.shape, BF16),
            pltpu.VMEM(glob.shape, BF16),
            pltpu.VMEM(small.shape, BF16),
            pltpu.VMEM(own, BF16),
            pltpu.VMEM(own, BF16),
            pltpu.VMEM((plan.own, LANE), F32),
            pltpu.VMEM((32, 2 * half), F32),
            pltpu.SemaphoreType.DMA((3 * pieces + 5,)),
            pltpu.SemaphoreType.DMA((2 * pieces + 4,)),
            pltpu.SemaphoreType.DMA((2 * pieces + 4,)),
            pltpu.SemaphoreType.DMA((2, n)),
            pltpu.SemaphoreType.DMA((2, n)),
        ],
        compiler_params=pltpu.CompilerParams(
            collective_id=1, has_side_effects=True, vmem_limit_bytes=VMEM_BYTES
        ),
    )(live, act_three, k_out, glob, small, glob_cot, small_cot, vec, vec_raw, vec_three_other)


ORDERS = {
    "A": ((0, 1, 2, 3), (1, 0, 2, 3)),
    "B": ((0, 2, 1, 3), (1, 2, 0, 3)),
    "P": ((0, 1, 2, 3), (2, 1, 0, 3)),
    "Q": ((2, 0, 1, 3), (1, 0, 2, 3)),
}
HANDED = 2


class Steps:
    def __init__(self, n, me, core, order):
        bits = n.bit_length() - 1
        self.halvings = min(bits, 4)
        self.shards = 2**self.halvings
        self.doublings = bits - self.halvings
        self.bit, self.partner = [], []
        chosen = [[bit for bit in one if bit < bits] for one in ORDERS[order]]
        chosen = [one + list(range(self.halvings, bits)) for one in chosen]
        for step in range(bits):
            first, second = 2 ** chosen[0][step], 2 ** chosen[1][step]
            distance = first + (second - first) * core
            bit = lax.rem(me // distance, 2)
            self.bit.append(bit)
            self.partner.append((me + distance * (1 - 2 * bit), core))


class Chain:
    def __init__(self, steps, work, land, send, recv, free, begun=0, until=None):
        self.steps, self.work, self.land, self.free = steps, work, land, free
        self.send, self.recv = send, recv
        self.rows = work.shape[0]
        self.shard = self.rows // steps.shards
        self.halvings = steps.halvings
        self.reduce_steps = steps.halvings + steps.doublings
        self.begun, self.until = begun, until
        self.pending = None
        self.step, self.at, self.length = begun, 0, self.rows >> begun
        for step in range(begun):
            self.at = self.at + steps.bit[step] * (self.rows >> (step + 1))
        self.land_base = self.rows - self.length
        self.back = None

    def rows_at(self, row, length):
        return pl.ds(row if isinstance(row, int) else pl.multiple_of(row, 16), length)

    def here(self):
        return self.work.at[self.rows_at(self.at, self.length), :]

    def remote(self, source, target, step, slot):
        self.pending = pltpu.make_async_remote_copy(
            src_ref=source,
            dst_ref=target,
            send_sem=self.send.at[slot],
            recv_sem=self.recv.at[slot],
            device_id=self.steps.partner[step],
            device_id_type=MESH,
        )
        self.pending.start()

    def begin_reduce(self):
        step = self.step
        if step < self.halvings:
            length = self.rows >> (step + 1)
            bit = self.steps.bit[step]
            self.keep = self.at + bit * length
            gone = self.at + (1 - bit) * length
            low = self.rows - 2 * length
        else:
            length = self.shard
            self.keep = gone = self.at
            low = self.rows - self.shard + (step - self.halvings) * self.shard
        self.length = length
        self.landed = self.land.at[pl.ds(low - self.land_base, length), :]
        self.remote(self.work.at[self.rows_at(gone, length), :], self.landed, step, step)

    def end_reduce(self):
        self.pending.wait()
        if self.free is not None and self.step < self.halvings:
            pl.semaphore_signal(
                self.free.at[self.step],
                inc=1,
                device_id=self.steps.partner[self.step],
                device_id_type=MESH,
            )
        size = 48 if self.shard % 48 == 0 else 16

        def add(tile, carry):
            there = self.rows_at(self.keep + tile * size, size)
            here = pl.ds(pl.multiple_of(tile * size, 16), size)
            total = self.work[there, :].astype(F32) + self.landed[here, :].astype(F32)
            self.work[there, :] = total.astype(BF16)
            return carry

        lax.fori_loop(0, self.length // size, add, 0)
        self.at = self.keep
        self.step += 1

    def begin_gather(self):
        if self.back >= self.begun:
            pl.semaphore_wait(self.free.at[self.back], 1)
        part = self.here()
        self.remote(part, part, self.back, self.reduce_steps + self.back)

    def end_gather(self):
        self.pending.wait()
        self.at = self.at - self.steps.bit[self.back] * self.length
        self.length *= 2
        self.back -= 1

    def advance(self):
        if self.pending is not None:
            if self.back is None:
                self.end_reduce()
            else:
                self.end_gather()
            self.pending = None
        if self.step == self.until:
            return
        if self.step < self.reduce_steps:
            self.begin_reduce()
            return
        if self.back is None:
            self.back = self.halvings - 1
        if self.back >= 0:
            self.begin_gather()

    def done(self):
        return self.pending is None and (self.step == self.until or self.back == -1)


def land_rows(n, rows, begun=0, until=None):
    bits = n.bit_length() - 1
    halvings = min(bits, 4)
    last = halvings if until is None else min(until, halvings)
    extra = bits - halvings if until is None else 0
    return (rows >> begun) - (rows >> last) + extra * (rows >> halvings)


def chain_slots(n):
    bits = n.bit_length() - 1
    return bits + min(bits, 4)


def silu_slope(value, sigma):
    return sigma * (1.0 + value * (1.0 - sigma))
SHIFT_TWO_SUM, GAIN_TWO_SUM, EXCITE_SUM, SQUEEZE_SUM = range(4)
SHIFT_ONE_SUM, GAIN_ONE_SUM = range(2)


def second_kernel(
    plan,
    grad_pre_three_hbm,
    act_three_hbm,
    k_out_hbm,
    pre_two_hbm,
    stats,
    vec,
    mask,
    pooled,
    excite,
    squeeze_pre,
    w_squeeze,
    w_excite,
    shard_out,
    grad_norm_out,
    grad_excite_out,
    grad_squeeze_out,
    sums_out,
    grad_pre_three,
    act_three,
    k_out,
    pre_two,
    grad_act,
    slopes,
    work,
    land,
    grad_excite,
    squeeze_send,
    squeeze_recv,
    grad_pooled,
    factors,
    factor_slots,
    pay,
    slots,
    local_sem,
    pair_send,
    pair_recv,
    spread_send,
    spread_recv,
    reduce_send,
    reduce_recv,
):
    n, half, group = plan.dp, plan.half, plan.group
    me, core = lax.axis_index("dp"), lax.axis_index("rows")
    entry_barrier(n, me, core)

    def local(source, target, index):
        copy = pltpu.make_async_copy(source, target, local_sem.at[index])
        copy.start()
        return copy

    loads = [
        local(grad_pre_three_hbm, grad_pre_three, 0),
        local(act_three_hbm, act_three, 1),
        local(k_out_hbm.at[:, core], k_out, 2),
        local(pre_two_hbm, pre_two, 3),
    ]
    loads[0].wait()
    loads[1].wait()
    for side in range(2):
        for part in range(2):
            lanes = slice(part * group, (part + 1) * group)
            low = side * half + part * group
            work[low : low + group, :] = dot_tn(
                act_three[side, :, lanes], grad_pre_three[core]
            ).astype(BF16)
    reduction = Chain(
        Steps(n, me, core, ORDER_OUT), work, land, reduce_send, reduce_recv, None, until=HANDED
    )
    reduction.advance()
    loads[2].wait()

    block = plan.all // 4

    def product(part, carry):
        rows = pl.ds(pl.multiple_of(part * block, 16), block)
        grad_act[rows, :] = dot_nt(grad_pre_three[0, rows, :], k_out[0]) + dot_nt(
            grad_pre_three[1, rows, :], k_out[1]
        )
        return carry

    lax.fori_loop(0, 4, product, 0)
    loads[3].wait()

    mean = stats[MEAN_TWO : MEAN_TWO + 1, :]
    inverse = stats[INVERSE_TWO : INVERSE_TWO + 1, :]
    count = stats[TOTAL : TOTAL + 1, :]
    gain = vec[GAIN_TWO : GAIN_TWO + 1, :]
    shift = vec[SHIFT_TWO : SHIFT_TWO + 1, :]
    grad_excite[...] = jnp.zeros_like(grad_excite)

    def excitation(start, place, crop, carry):
        rows = pl.ds(start, TILE)
        norm = (pre_two[pl.ds(place, TILE), :] - mean) * (inverse * gain) + shift
        sigma = sigmoid(norm)
        seen = widen(mask[rows, :], half)
        slopes[rows, :] = silu_slope(norm, sigma) * seen
        term = grad_act[rows, :] * (norm * sigma * seen)
        grad_excite[pl.ds(crop, 1), :] += jnp.sum(term, 0, keepdims=True)
        return carry

    plan.sweep(excitation, 0)
    level = excite[...]
    grad_excite_pre = grad_excite[...] * level * (1.0 - level)
    part = split_dot(grad_excite_pre, w_excite[...], nt=True)
    squeeze_send[...] = part
    swap = to_partner(me, core, squeeze_send, squeeze_recv, pair_send.at[0], pair_recv.at[0])
    swap.start()
    reduction.advance()
    swap.wait()
    before = squeeze_pre[...]
    sigma = sigmoid(before)
    squeezed = before * sigma
    grad_squeeze_pre = (part + squeeze_recv[...]) * silu_slope(before, sigma)
    back = split_dot(grad_squeeze_pre, w_squeeze[...], nt=True)
    crop_row = lax.broadcasted_iota(jnp.int32, back.shape, 0)
    area = jnp.where(crop_row == 0, 1.0 / plan.glob_area, 1.0 / plan.slot_area)
    grad_pooled[...] = back * area
    deep = plan.slot_rows
    factors[:deep, :group] = squeezed.astype(BF16)
    factors[:deep, group:] = grad_excite_pre.astype(BF16)
    factors[deep:, :group] = grad_squeeze_pre.astype(BF16)
    factors[deep:, group:] = pooled[...].astype(BF16)
    factor_spread = Spread(n, me, core, factors, factor_slots, spread_send.at[0], spread_recv.at[0])
    factor_spread.start()

    def gradient(start, place, crop, carry):
        rows = pl.ds(start, TILE)
        incoming = grad_act[rows, :] * excite[pl.ds(crop, 1), :] + grad_pooled[pl.ds(crop, 1), :]
        grad = incoming * slopes[rows, :]
        grad_act[rows, :] = grad
        normed = (pre_two[pl.ds(place, TILE), :] - mean) * inverse
        return carry[0] + rows_down(grad), carry[1] + rows_down(grad * normed)

    zero = jnp.zeros((8, half), F32)
    shift_sum, gain_sum = plan.sweep(gradient, (zero, zero))
    save = local(grad_act, grad_norm_out, 4)
    pay[:, :half] = jnp.sum(shift_sum, 0, keepdims=True)
    pay[:, half:] = jnp.sum(gain_sum, 0, keepdims=True)
    spread = Spread(n, me, core, pay, slots, spread_send.at[1], spread_recv.at[1])
    spread.start()
    while not reduction.done():
        reduction.advance()
    store = local(reduction.here(), shard_out, 5)
    factor_spread.wait()
    left = factor_slots[:, :, :group].reshape(n * 2 * deep, group)
    right = factor_slots[:, :, group:].reshape(n * 2 * deep, half)
    upper = lax.broadcasted_iota(jnp.int32, left.shape, 0) % (2 * deep) < deep
    zeros = jnp.zeros_like(left)
    excite_left = jnp.where(upper, left, zeros)
    squeeze_left = jnp.where(upper, zeros, left)
    grad_excite_out[...] = dot_tn(excite_left, right)
    grad_squeeze_out[...] = dot_tn(right, squeeze_left)
    wide_upper = lax.broadcasted_iota(jnp.int32, right.shape, 0) % (2 * deep) < deep
    excite_bias = jnp.sum(jnp.where(wide_upper, right.astype(F32), 0.0), 0, keepdims=True)
    squeeze_bias = jnp.sum(squeeze_left.astype(F32), 0, keepdims=True)
    spread.wait()
    totals = gather_sum(slots, n, 2 * half)
    sums_out[...] = jnp.zeros_like(sums_out)
    sums_out[SHIFT_TWO_SUM : SHIFT_TWO_SUM + 1, :] = totals[:, :half]
    sums_out[GAIN_TWO_SUM : GAIN_TWO_SUM + 1, :] = totals[:, half:]
    sums_out[EXCITE_SUM : EXCITE_SUM + 1, :] = excite_bias
    sums_out[SQUEEZE_SUM : SQUEEZE_SUM + 1, :group] = squeeze_bias
    save.wait()
    store.wait()


def second(
    plan, grad_pre_three, act_three, k_out, pre_two, stats, vec, mask, pooled, excite,
    squeeze_pre, w_squeeze, w_excite
):
    n, half, group = plan.dp, plan.half, plan.group
    shape = jax.ShapeDtypeStruct
    rows = 2 * half
    shard = rows >> HANDED
    deep = plan.slot_rows
    bits = n.bit_length() - 1
    return pl.pallas_call(
        functools.partial(second_kernel, plan),
        out_shape=(
            shape((shard, half), BF16),
            shape((plan.all, half), F32),
            shape((group, half), F32),
            shape((half, group), F32),
            shape((8, half), F32),
        ),
        in_specs=[ANY] * 4 + [VMEM] * 8,
        out_specs=(ANY, ANY, VMEM, VMEM, VMEM),
        scratch_shapes=[
            pltpu.VMEM((2, plan.all, half), BF16),
            pltpu.VMEM((2, plan.all, half), BF16),
            pltpu.VMEM((2, half, half), BF16),
            pltpu.VMEM((plan.conv, half), F32),
            pltpu.VMEM((plan.all, half), F32),
            pltpu.VMEM((plan.all, half), F32),
            pltpu.VMEM((rows, half), BF16),
            pltpu.VMEM((land_rows(n, rows, until=HANDED), half), BF16),
            pltpu.VMEM((deep, half), F32),
            pltpu.VMEM((deep, group), F32),
            pltpu.VMEM((deep, group), F32),
            pltpu.VMEM((deep, half), F32),
            pltpu.VMEM((2 * deep, group + half), BF16),
            pltpu.VMEM((n, 2 * deep, group + half), BF16),
            pltpu.VMEM((1, 2 * half), F32),
            pltpu.VMEM((n, 1, 2 * half), F32),
            pltpu.SemaphoreType.DMA((6,)),
            pltpu.SemaphoreType.DMA((1,)),
            pltpu.SemaphoreType.DMA((1,)),
            pltpu.SemaphoreType.DMA((2, n)),
            pltpu.SemaphoreType.DMA((2, n)),
            pltpu.SemaphoreType.DMA((bits,)),
            pltpu.SemaphoreType.DMA((bits,)),
        ],
        compiler_params=pltpu.CompilerParams(
            collective_id=2, has_side_effects=True, vmem_limit_bytes=VMEM_BYTES
        ),
    )(
        grad_pre_three, act_three, k_out, pre_two, stats, vec, mask, pooled, excite, squeeze_pre,
        w_squeeze, w_excite
    )


CHAINS = ("out", "mid0", "mid1", "mid2", "in0", "in1")
ORDER_OUT = "A"
CHAIN_ORDERS = (ORDER_OUT, "B", "P", "Q", "P", "Q")
SCHEDULE = (
    "two", "M0", "M1", "C0", "out", "C1", "C2", "C3", "C4", "C5", "mid0", "out", "mid1", "C6",
    "C7", "sums", "out", "M2", "mid1", "out", "one", "K0", "mid2", "mid0", "mid1", "K1",
    "mid1", "mid2", "in0", "mid0", "mid1", "mid0", "X0", "X1", "in1", "in0", "mid2", "mid0",
    "out", "mid1", "mid2", "in1", "mid2", "X2", "mid0", "in0", "in0", "mid2", "mid1", "in1",
    "in0", "in1", "mid2", "in1", "in1", "in0", "mid0", "mid1", "X3", "in1", "in0", "mid2",
    "out", "mid0", "in0", "in1",
)


def first_kernel(
    plan,
    shard_out_hbm,
    grad_norm_hbm,
    pre_two_hbm,
    pre_one_hbm,
    act_one_hbm,
    x_hbm,
    w_mid_hbm,
    w_in_hbm,
    stats,
    vec,
    sums_two,
    mask,
    gathered_out,
    gathered_mid,
    gathered_in,
    grad_inputs_out,
    sums_out,
    flat,
    conv_rows,
    shifted,
    act_one,
    w_mid,
    grad_pre_one,
    grad_other,
    w_in,
    work_out,
    land_out,
    work_mid,
    land_mid,
    work_in,
    land_in,
    pay,
    slots,
    local_sem,
    pair_send,
    pair_recv,
    spread_send,
    spread_recv,
    chain_send,
    chain_recv,
    free,
):
    n, half, group = plan.dp, plan.half, plan.group
    me, core = lax.axis_index("dp"), lax.axis_index("rows")
    entry_barrier(n, me, core)

    def local(source, target, index):
        copy = pltpu.make_async_copy(source, target, local_sem.at[index])
        copy.start()
        return copy

    chains, targets, saves, waits, state = {}, {}, {}, {}, {}

    def begin(name, work, land, target, begun=0):
        index = CHAINS.index(name)
        steps = Steps(n, me, core, CHAIN_ORDERS[index])
        chains[name] = Chain(
            steps, work, land, chain_send.at[index], chain_recv.at[index], free.at[index], begun
        )
        targets[name] = target
        return chains[name]

    def advance(name):
        chain = chains[name]
        if name in saves:
            return
        chain.advance()
        if chain.done():
            index = CHAINS.index(name)
            saves[name] = local(chain.work, targets[name], 8 + index)

    out = begin("out", work_out, land_out, gathered_out, HANDED)
    load_shard = local(shard_out_hbm, out.here(), 2)
    waits["norm"] = local(grad_norm_hbm, flat, 0)
    waits["two"] = local(pre_two_hbm, conv_rows, 1)
    waits["act"] = local(act_one_hbm, act_one, 3)
    waits["mid"] = local(w_mid_hbm, w_mid, 4)
    waits["in"] = local(w_in_hbm, w_in, 5)
    load_shard.wait()
    advance("out")
    count = stats[TOTAL : TOTAL + 1, :]

    def norm_two():
        zero_borders(plan, shifted)
        mean = stats[MEAN_TWO : MEAN_TWO + 1, :]
        inverse = stats[INVERSE_TWO : INVERSE_TWO + 1, :]
        scale = vec[GAIN_TWO : GAIN_TWO + 1, :] * inverse
        shift_mean = sums_two[SHIFT_TWO_SUM : SHIFT_TWO_SUM + 1, :] / count
        gain_mean = sums_two[GAIN_TWO_SUM : GAIN_TWO_SUM + 1, :] / count * inverse
        waits["norm"].wait()
        waits["two"].wait()

        def into_two(start, place, crop, carry):
            rows = pl.ds(start, TILE)
            centered = conv_rows[pl.ds(place, TILE), :] - mean
            grad = scale * (flat[rows, :] - shift_mean - centered * gain_mean)
            grad = grad * widen(mask[rows, :], half)
            after = pltpu.roll(grad, TILE - 1, 0)
            before = pltpu.roll(grad, 1, 0)
            for tap, value in enumerate((after, grad, before)):
                for side in range(2):
                    shifted[side, pl.ds(place, TILE), tap * group : (tap + 1) * group] = value[
                        :, side * group : (side + 1) * group
                    ].astype(BF16)
            return carry

        plan.sweep(into_two, 0)
        waits["one"] = local(pre_one_hbm, flat, 0)
        waits["act"].wait()

    def mid(tap):
        for side in range(2):
            lanes = slice(side * group, (side + 1) * group)
            total = None
            for low, length, width in plan.segments():
                first = low - (tap - 1) * width
                term = dot_tn(
                    act_one[low : low + length, lanes], shifted[side, first : first + length, :]
                )
                total = term if total is None else total + term
            work_mid[tap, lanes, :] = total.astype(BF16)
        name = CHAINS[1 + tap]
        begin(name, work_mid.at[tap], land_mid.at[tap], gathered_mid.at[tap])
        advance(name)
        read_shifted()

    def read_shifted():
        state["reads"] = state.get("reads", 0) + 1
        if state["reads"] == 3 + 8:
            waits["x"] = local(x_hbm, shifted.at[:, pl.ds(0, plan.all), pl.ds(0, half)], 7)

    def conv(index):
        if index == 0:
            waits["mid"].wait()
        low, length, width = plan.segments()[index // 4]
        block = length // 2
        side = index // 2 % 2
        at = low + index % 2 * block
        lanes = slice(side * group, (side + 1) * group)
        total = None
        for tap in range(3):
            first = at - (tap - 1) * width
            for column in range(3):
                taps = slice(column * group, (column + 1) * group)
                term = dot_nt(shifted[side, first : first + block, taps], w_mid[tap, taps, lanes])
                total = term if total is None else total + term
        conv_rows[at : at + block, lanes] = total
        read_shifted()

    mean = stats[MEAN_ONE : MEAN_ONE + 1, :]
    inverse = stats[INVERSE_ONE : INVERSE_ONE + 1, :]
    gain = vec[GAIN_ONE : GAIN_ONE + 1, :]
    shift = vec[SHIFT_ONE : SHIFT_ONE + 1, :]
    spread = Spread(n, me, core, pay, slots, spread_send, spread_recv)

    def sums_one():
        waits["one"].wait()

        def gradient(start, place, crop, carry):
            rows = pl.ds(start, TILE)
            normed = (flat[rows, :] - mean) * inverse
            norm = normed * gain + shift
            sigma = sigmoid(norm)
            grad = conv_rows[pl.ds(place, TILE), :] * silu_slope(norm, sigma)
            grad = grad * widen(mask[rows, :], half)
            conv_rows[pl.ds(place, TILE), :] = grad
            return carry[0] + rows_down(grad), carry[1] + rows_down(grad * normed)

        zero = jnp.zeros((8, half), F32)
        shift_sum, gain_sum = plan.sweep(gradient, (zero, zero))
        pay[:, :half] = jnp.sum(shift_sum, 0, keepdims=True)
        pay[:, half:] = jnp.sum(gain_sum, 0, keepdims=True)
        spread.start()

    def norm_one():
        spread.wait()
        totals = gather_sum(slots, n, 2 * half)
        sums_out[...] = jnp.zeros_like(sums_out)
        sums_out[SHIFT_ONE_SUM : SHIFT_ONE_SUM + 1, :] = totals[:, :half]
        sums_out[GAIN_ONE_SUM : GAIN_ONE_SUM + 1, :] = totals[:, half:]
        scale = gain * inverse
        shift_mean = totals[:, :half] / count
        gain_mean = totals[:, half:] / count * inverse

        def into_one(start, place, crop, carry):
            rows = pl.ds(start, TILE)
            centered = flat[rows, :] - mean
            grad = scale * (conv_rows[pl.ds(place, TILE), :] - shift_mean - centered * gain_mean)
            grad_pre_one[rows, :] = (grad * widen(mask[rows, :], half)).astype(BF16)
            return carry

        plan.sweep(into_one, 0)
        state["swaps"] = []
        for index, (place, start, length) in enumerate(plan.own_pieces(1 - core)):
            swap = to_partner(
                me,
                core,
                grad_pre_one.at[pl.ds(place, length), :],
                grad_other.at[pl.ds(start, length), :],
                pair_send.at[index],
                pair_recv.at[index],
            )
            swap.start()
            state["swaps"].append(swap)

    def kernel_in(side):
        if side == 0:
            waits["x"].wait()
        for part in range(2):
            lanes = slice(part * group, (part + 1) * group)
            work_in[side, lanes, :] = dot_tn(
                shifted[side, : plan.all, lanes], grad_pre_one[...]
            ).astype(BF16)
        name = CHAINS[4 + side]
        begin(name, work_in.at[side], land_in.at[side], gathered_in.at[side])
        advance(name)

    def inputs(index):
        if index == 0:
            waits["in"].wait()
            for swap in state["swaps"]:
                swap.wait()
        part, side = index // 2, index % 2
        marks = (0, plan.glob_own, plan.own)
        rows = slice(marks[part], marks[part + 1])
        pieces = plan.own_pieces(core)
        pieces = pieces[:1] if part == 0 else pieces[1:]
        own = jnp.concatenate([grad_pre_one[pl.ds(spot, size), :] for spot, _, size in pieces], 0)
        grad_inputs_out[side, rows, :] = (
            dot_nt(own, w_in[core, side]) + dot_nt(grad_other[rows, :], w_in[1 - core, side])
        ).astype(BF16)

    blocks = {
        "two": norm_two,
        "sums": sums_one,
        "one": norm_one,
    }
    for tap in range(3):
        blocks["M%d" % tap] = functools.partial(mid, tap)
    for index in range(8):
        blocks["C%d" % index] = functools.partial(conv, index)
    for side in range(2):
        blocks["K%d" % side] = functools.partial(kernel_in, side)
    for index in range(4):
        blocks["X%d" % index] = functools.partial(inputs, index)
    for item in SCHEDULE:
        if item in blocks:
            blocks[item]()
        else:
            advance(item)
    while len(saves) < len(CHAINS):
        for name in CHAINS:
            advance(name)
    for name in CHAINS:
        saves[name].wait()


def first(
    plan, shard_out, grad_norm, pre_two, pre_one, act_one, x_all, w_mid, w_in, stats, vec,
    sums_two, mask
):
    n, half, group = plan.dp, plan.half, plan.group
    shape = jax.ShapeDtypeStruct
    pieces = 1 + plan.slots
    return pl.pallas_call(
        functools.partial(first_kernel, plan),
        out_shape=(
            shape((2 * half, half), BF16),
            shape((3, half, 3 * group), BF16),
            shape((2, half, half), BF16),
            shape((2, plan.own, half), BF16),
            shape((8, half), F32),
        ),
        in_specs=[ANY] * 8 + [VMEM] * 4,
        out_specs=(ANY, ANY, ANY, VMEM, VMEM),
        scratch_shapes=[
            pltpu.VMEM((plan.all, half), F32),
            pltpu.VMEM((plan.conv, half), F32),
            pltpu.VMEM((2, plan.conv, 3 * group), BF16),
            pltpu.VMEM((plan.conv, half), BF16),
            pltpu.VMEM(w_mid.shape, BF16),
            pltpu.VMEM((plan.all, half), BF16),
            pltpu.VMEM((plan.own, half), BF16),
            pltpu.VMEM(w_in.shape, BF16),
            pltpu.VMEM((2 * half, half), BF16),
            pltpu.VMEM((land_rows(n, 2 * half, begun=HANDED), half), BF16),
            pltpu.VMEM((3, half, 3 * group), BF16),
            pltpu.VMEM((3, land_rows(n, half), 3 * group), BF16),
            pltpu.VMEM((2, half, half), BF16),
            pltpu.VMEM((2, land_rows(n, half), half), BF16),
            pltpu.VMEM((1, 2 * half), F32),
            pltpu.VMEM((n, 1, 2 * half), F32),
            pltpu.SemaphoreType.DMA((14,)),
            pltpu.SemaphoreType.DMA((pieces,)),
            pltpu.SemaphoreType.DMA((pieces,)),
            pltpu.SemaphoreType.DMA((n,)),
            pltpu.SemaphoreType.DMA((n,)),
            pltpu.SemaphoreType.DMA((len(CHAINS), chain_slots(n))),
            pltpu.SemaphoreType.DMA((len(CHAINS), chain_slots(n))),
            pltpu.SemaphoreType.REGULAR((len(CHAINS), 4)),
        ],
        compiler_params=pltpu.CompilerParams(
            collective_id=3, has_side_effects=True, vmem_limit_bytes=VMEM_BYTES
        ),
    )(
        shard_out, grad_norm, pre_two, pre_one, act_one, x_all, w_mid, w_in, stats, vec, sums_two,
        mask
    )


def join_lanes(low, high, real):
    zeros = jnp.zeros_like(low)
    wide = jnp.concatenate([low, zeros], 1)
    moved = pltpu.roll(jnp.concatenate([high, zeros], 1), real, 1)
    lane = lax.broadcasted_iota(jnp.int32, wide.shape, 1)
    return jnp.where(lane < real, wide, moved)


def finish_kernel(
    plan,
    result_hbm,
    grad_summed_hbm,
    grad_inputs_hbm,
    out_hbm,
    in_hbm,
    mid_hbm,
    excite,
    squeeze,
    glob_out_hbm,
    small_out_hbm,
    glob_grad_hbm,
    small_grad_hbm,
    kernel_in_hbm,
    kernel_mid_hbm,
    kernel_out_hbm,
    squeeze_out,
    excite_out,
    result,
    grad_summed,
    grad_inputs,
    packed_out,
    packed_in,
    packed_mid,
    glob_out,
    small_out,
    glob_grad,
    small_grad,
    kernel_in,
    kernel_mid,
    kernel_out,
    load_sem,
    store_sem,
):
    half, group, width, real = plan.half, plan.group, plan.width, plan.half_real
    loads, stores = {}, []
    sources = (
        (mid_hbm, packed_mid),
        (out_hbm, packed_out),
        (in_hbm, packed_in),
        (result_hbm, result),
        (grad_summed_hbm, grad_summed),
        (grad_inputs_hbm, grad_inputs),
    )
    for index, (source, target) in enumerate(sources):
        loads[index] = pltpu.make_async_copy(source, target, load_sem.at[index])
        loads[index].start()

    def store(source, target):
        copy = pltpu.make_async_copy(source, target, store_sem.at[len(stores)])
        copy.start()
        stores.append(copy)

    loads[0].wait()
    for row_tap in range(3):
        for tap in range(3):
            lanes = slice(tap * group, (tap + 1) * group)
            low = packed_mid[row_tap, :group, lanes].astype(F32)
            high = packed_mid[row_tap, group:, lanes].astype(F32)
            kernel_mid[row_tap, tap] = join_lanes(low, high, width)[:width, :real]
        store(kernel_mid.at[row_tap], kernel_mid_hbm.at[row_tap])
    loads[1].wait()
    for piece in range(4):
        kernel_out[piece * width : (piece + 1) * width, :] = packed_out[
            piece * group : piece * group + width, :real
        ].astype(F32)
    store(kernel_out, kernel_out_hbm)
    loads[2].wait()
    for side in range(2):
        rows = min(half, plan.channels - side * half)
        low = packed_in[side, :rows, :group].astype(F32)
        high = packed_in[side, :rows, group:].astype(F32)
        kernel_in[side * half : side * half + rows, :] = join_lanes(low, high, width)[:, :real]
    store(kernel_in, kernel_in_hbm)

    def maps(value, glob, small):
        def glob_row(row, carry):
            rows = pl.ds(pl.multiple_of(row * plan.glob_width, 16), plan.glob_width)
            glob[row, :, 0, :] = value(rows)[: plan.glob_side, : plan.channels]
            return carry

        def small_row(row, carry):
            place = plan.glob_own + row * plan.small_width
            rows = pl.ds(pl.multiple_of(place, 16), plan.small_width)
            small[row] = value(rows)[: plan.small_side, : plan.channels]
            return carry

        lax.fori_loop(0, plan.glob_height, glob_row, 0)
        lax.fori_loop(0, plan.slots * plan.small_height, small_row, 0)

    loads[3].wait()
    def joined(array, rows):
        return join_lanes(array[0, rows, :].astype(F32), array[1, rows, :].astype(F32), real)

    maps(lambda rows: joined(result, rows), glob_out, small_out)
    store(glob_out, glob_out_hbm)
    store(small_out, small_out_hbm)
    loads[4].wait()
    loads[5].wait()
    maps(
        lambda rows: joined(grad_summed, rows)
        + jnp.concatenate([grad_inputs[0, rows, :], grad_inputs[1, rows, :]], 1).astype(F32),
        glob_grad,
        small_grad,
    )
    store(glob_grad, glob_grad_hbm)
    store(small_grad, small_grad_hbm)
    squeeze_out[:width, :] = squeeze[:width, :width]
    squeeze_out[width:, :] = squeeze[group : group + width, :width]
    excite_out[...] = join_lanes(excite[:, :group], excite[:, group:], width)[:width, :real]
    for copy in stores:
        copy.wait()


def finish(plan, result, grad_summed, grad_inputs, gathered_out, gathered_in, gathered_mid, excite, squeeze):
    shape = jax.ShapeDtypeStruct
    width, real, channels = plan.width, plan.half_real, plan.channels
    glob = (plan.glob_height, plan.glob_side, 1, channels)
    small = (plan.slots * plan.small_height, plan.small_side, channels)
    outs = (glob, small, glob, small, (channels, real), (3, 3, width, real), (channels, real))
    ins = (gathered_mid, gathered_out, gathered_in, result, grad_summed, grad_inputs)
    loaded = (result, grad_summed, grad_inputs, gathered_out, gathered_in, gathered_mid)
    return pl.pallas_call(
        functools.partial(finish_kernel, plan),
        out_shape=tuple(shape(out, F32) for out in outs)
        + (shape((real, width), F32), shape((width, real), F32)),
        in_specs=[ANY] * 6 + [VMEM] * 2,
        out_specs=(ANY,) * 7 + (VMEM,) * 2,
        scratch_shapes=[pltpu.VMEM(array.shape, BF16) for array in loaded]
        + [pltpu.VMEM(out, F32) for out in outs]
        + [pltpu.SemaphoreType.DMA((6,)), pltpu.SemaphoreType.DMA((9,))],
        compiler_params=pltpu.CompilerParams(vmem_limit_bytes=VMEM_BYTES),
    )(result, grad_summed, grad_inputs, gathered_out, gathered_in, gathered_mid, excite, squeeze)


def ungroup_lanes(array, plan):
    return jnp.concatenate(
        [array[..., : plan.width], array[..., plan.group : plan.group + plan.width]], -1
    )


def per_device(
    glob_in,
    small_in,
    small_count,
    kernel_in,
    kernel_mid,
    kernel_out,
    squeeze_weight,
    squeeze_bias,
    excite_weight,
    excite_bias,
    gain_first,
    shift_first,
    gain_second,
    shift_second,
    gain_third,
    shift_third,
    glob_cotangent,
    small_cotangent,
):
    plan = Plan(glob_in.shape, small_in.shape, kernel_mid.shape[2], lax.axis_size("dp"))
    core = lax.axis_index("rows")
    width, real = plan.width, plan.half_real

    def images(maps):
        return maps.reshape((-1,) + maps.shape[2:])

    glob, small = images(glob_in), images(small_in)
    vec_raw = vector_table(
        [gain_first, shift_first, gain_second, shift_second, excite_bias, squeeze_bias, None, None]
        + [gain_third, shift_third]
        + [None] * 6,
        plan,
    )
    (
        x_all, pre_one, act_one, pre_two, act_three, w_mid, k_out, w_in, vec_three_other, vec, mask,
        w_squeeze, w_excite, stats, pooled, excite, squeeze_pre
    ) = forward(
        plan, small_count, glob, small, kernel_in, images(kernel_mid), kernel_out, squeeze_weight,
        excite_weight, vec_raw
    )
    result, grad_summed, grad_pre_three, sums_three = third(
        plan, small_count, act_three, k_out, glob, small, images(glob_cotangent),
        images(small_cotangent), vec, vec_raw, vec_three_other
    )
    shard_out, grad_norm, grad_excite, grad_squeeze, sums_two = second(
        plan, grad_pre_three, act_three, k_out, pre_two, stats, vec, mask, pooled, excite,
        squeeze_pre, w_squeeze, w_excite
    )
    gathered_out, gathered_mid, gathered_in, grad_inputs, sums_one = first(
        plan, shard_out, grad_norm, pre_two, pre_one, act_one, x_all, w_mid, w_in, stats, vec,
        sums_two, mask
    )
    (
        glob_out, small_out, glob_grad, small_grad, grad_kernel_in, grad_kernel_mid,
        grad_kernel_out, grad_squeeze, grad_excite
    ) = finish(
        plan, result, grad_summed, grad_inputs, gathered_out, gathered_in, gathered_mid,
        grad_excite, grad_squeeze
    )
    sums = lax.dynamic_index_in_dim(sums_three, core, 0, False)

    def grouped(row):
        return ungroup_lanes(row, plan)

    return (
        glob_out.reshape(glob_in.shape),
        small_out.reshape(small_in.shape),
        glob_grad.reshape(glob_in.shape),
        small_grad.reshape(small_in.shape),
        grad_kernel_in,
        grad_kernel_mid,
        grad_kernel_out,
        grad_squeeze,
        sums_two[SQUEEZE_SUM, :width],
        grad_excite,
        grouped(sums_two[EXCITE_SUM]),
        grouped(sums_one[GAIN_ONE_SUM]),
        grouped(sums_one[SHIFT_ONE_SUM]),
        grouped(sums_two[GAIN_TWO_SUM]),
        grouped(sums_two[SHIFT_TWO_SUM]),
        sums[1, :real],
        sums[0, :real],
    )


def solution(mesh):
    maps = P("dp", "rows", None, None)
    vector = P("rows")
    columns = P(None, "rows")
    taps = P(None, None, None, "rows")
    return jax.shard_map(
        per_device,
        mesh=mesh,
        in_specs=(
            maps, maps, P("dp"), columns, taps, columns, P("rows", None), P(), columns,
        )
        + (vector,) * 7
        + (maps, maps),
        out_specs=(maps,) * 4
        + (columns, taps, columns, P("rows", None), P(), columns)
        + (vector,) * 7,
        check_vma=False,
    )
```

```python
import functools

import jax
import jax.numpy as jnp
from jax import lax
from jax.experimental import pallas as pl
from jax.experimental.pallas import tpu as pltpu
from jax.sharding import PartitionSpec as P

EPSILON = 1e-05
MESH = pl.DeviceIdType.MESH
F32 = jnp.float32
BF16 = jnp.bfloat16
ANY = pl.BlockSpec(memory_space=pl.ANY)
VMEM = pl.BlockSpec(memory_space=pltpu.VMEM)
LANE = 128
TILE = 64
VMEM_BYTES = 62 * 1024 * 1024


def round_up(value, step):
    return -(-value // step) * step


class Plan:
    def __init__(self, glob_shape, small_shape, group_width, dp):
        self.glob_height, self.glob_side = glob_shape[1], glob_shape[2]
        self.slots, self.small_height, self.small_side = small_shape[:3]
        self.channels = glob_shape[3]
        self.glob_width = round_up(self.glob_side + 1, 32)
        self.small_width = round_up(self.small_side + 1, 16)
        self.glob_own = self.glob_height * self.glob_width
        self.slot_own = self.small_height * self.small_width
        self.own = self.glob_own + self.slots * self.slot_own
        self.glob_all = 2 * self.glob_own
        self.slot_all = 2 * self.slot_own
        self.all = 2 * self.own
        self.glob_base = self.glob_width
        self.small_base = self.glob_all + 2 * self.glob_width
        self.slot_conv = self.slot_all + self.small_width
        self.small_conv = self.slots * self.slot_conv
        self.conv = self.small_base + self.small_conv
        self.width = group_width
        self.group = round_up(group_width, LANE)
        self.half = 2 * self.group
        self.half_real = self.channels // 2
        self.dp = dp
        self.glob_tiles = self.glob_all // TILE
        self.slot_tiles = self.slot_all // TILE
        self.slot_rows = round_up(1 + self.slots, 8)
        self.glob_area = float(2 * self.glob_height * self.glob_side)
        self.slot_area = float(2 * self.small_height * self.small_side)

    def own_pieces(self, core):
        pieces = [(pl.multiple_of(core * self.glob_own, 16), 0, self.glob_own)]
        for slot in range(self.slots):
            place = self.glob_all + slot * self.slot_all + core * self.slot_own
            pieces.append(
                (pl.multiple_of(place, 16), self.glob_own + slot * self.slot_own, self.slot_own)
            )
        return pieces

    def sweep(self, body, carry):
        def glob_step(tile, state):
            start = pl.multiple_of(tile * TILE, TILE)
            return body(start, pl.multiple_of(self.glob_base + start, 16), 0, state)

        def slot_step(tile, state):
            slot = tile // self.slot_tiles
            start = pl.multiple_of(self.glob_all + tile * TILE, TILE)
            place = self.small_base + tile * TILE + slot * self.small_width
            return body(start, pl.multiple_of(place, 16), 1 + slot, state)

        carry = lax.fori_loop(0, self.glob_tiles, glob_step, carry)
        return lax.fori_loop(0, self.slots * self.slot_tiles, slot_step, carry)

    def segments(self):
        return (
            (self.glob_base, self.glob_all, self.glob_width),
            (self.small_base, self.small_conv - self.small_width, self.small_width),
        )


def sigmoid(value):
    return 0.5 * jnp.tanh(0.5 * value) + 0.5


def rows_down(tile):
    return jnp.sum(tile.reshape(tile.shape[0] // 8, 8, tile.shape[1]), 0)


def widen(mask, lanes):
    return jnp.concatenate([mask] * (lanes // mask.shape[1]), 1)


def dot(left, right):
    return jnp.dot(left, right, preferred_element_type=F32)


def dot_nt(left, right):
    return lax.dot_general(left, right, (((1,), (1,)), ((), ())), preferred_element_type=F32)


def dot_tn(left, right):
    return lax.dot_general(left, right, (((0,), (0,)), ((), ())), preferred_element_type=F32)


def split_dot(left, right, nt=False):
    high = left.astype(BF16)
    low = (left - high.astype(F32)).astype(BF16)
    call = dot_nt if nt else dot
    return call(high, right) + call(low, right)


def entry_barrier(n, me, core):
    barrier = pltpu.get_barrier_semaphore()

    def greet(step, carry):
        pl.semaphore_signal(
            barrier, inc=1, device_id=(lax.rem(me + step, n), core), device_id_type=MESH
        )
        return carry

    lax.fori_loop(1, n, greet, 0)
    pl.semaphore_signal(barrier, inc=1, device_id=(me, 1 - core), device_id_type=MESH)
    pl.semaphore_wait(barrier, n)


class Spread:
    def __init__(self, n, me, core, source, slots, send, recv):
        self.n, self.me, self.core = n, me, core
        self.source, self.slots, self.send, self.recv = source, slots, send, recv

    def copy(self, step):
        return pltpu.make_async_remote_copy(
            src_ref=self.source,
            dst_ref=self.slots.at[self.me],
            send_sem=self.send.at[step],
            recv_sem=self.recv.at[step],
            device_id=(lax.rem(self.me + step, self.n), self.core),
            device_id_type=MESH,
        )

    def start(self):
        def begin(step, carry):
            self.copy(step).start()
            return carry

        lax.fori_loop(1, self.n, begin, 0)
        self.slots[pl.ds(self.me, 1)] = self.source[...][None]

    def wait(self):
        def end(step, carry):
            self.copy(step).wait()
            return carry

        lax.fori_loop(1, self.n, end, 0)


def to_partner(me, core, source, target, send, recv):
    return pltpu.make_async_remote_copy(
        src_ref=source,
        dst_ref=target,
        send_sem=send,
        recv_sem=recv,
        device_id=(me, 1 - core),
        device_id_type=MESH,
    )


def merge_moments(slots, n, lanes):
    def add(step, carry):
        total, count = carry
        return (total + slots[step, :, :lanes], count + slots[step, :, 2 * lanes : 2 * lanes + LANE])

    total, count = lax.fori_loop(
        0, n, add, (jnp.zeros((1, lanes), F32), jnp.zeros((1, LANE), F32))
    )
    wide_count = widen(count, lanes)
    mean = total / wide_count

    def spread(step, carry):
        own_count = widen(slots[step, :, 2 * lanes : 2 * lanes + LANE], lanes)
        gap = slots[step, :, :lanes] / own_count - mean
        return carry + slots[step, :, lanes : 2 * lanes] + own_count * gap * gap

    squares = lax.fori_loop(0, n, spread, jnp.zeros((1, lanes), F32))
    return mean, squares / wide_count, wide_count


def local_moments(plan, values, mask, which, count):
    lanes = plan.half

    def add(start, place, crop, carry):
        row = start if which == "all" else place
        tile = values[pl.ds(row, TILE), :] * widen(mask[pl.ds(start, TILE), :], lanes)
        return carry + rows_down(tile)

    total = jnp.sum(plan.sweep(add, jnp.zeros((8, lanes), F32)), 0, keepdims=True)
    mean = total / count

    def spread(start, place, crop, carry):
        row = start if which == "all" else place
        gap = (values[pl.ds(row, TILE), :] - mean) * widen(mask[pl.ds(start, TILE), :], lanes)
        return carry + rows_down(gap * gap)

    squares = jnp.sum(plan.sweep(spread, jnp.zeros((8, lanes), F32)), 0, keepdims=True)
    return total, squares


GAIN_ONE, SHIFT_ONE, GAIN_TWO, SHIFT_TWO, EXCITE_BIAS, SQUEEZE_BIAS, COUNT = range(7)
MEAN_ONE, INVERSE_ONE, MEAN_TWO, INVERSE_TWO, TOTAL = range(5)


def lane_of(shape):
    return lax.broadcasted_iota(jnp.int32, shape, len(shape) - 1)


def row_of(shape):
    return lax.broadcasted_iota(jnp.int32, shape, len(shape) - 2)


def group_lanes(value, plan):
    lane = lane_of(value.shape)
    moved = pltpu.roll(value, plan.group - plan.width, 1)
    return jnp.where(lane < plan.width, value, jnp.where(lane < plan.group, 0.0, moved))


def fill_mask(plan, mask, crops, slot_rows, live_count):
    step = 32
    row = row_of((step, LANE))
    glob = (lax.rem(row, plan.glob_width) < plan.glob_side).astype(F32)
    small = (lax.rem(row, plan.small_width) < plan.small_side).astype(F32)

    def glob_step(tile, carry):
        mask[pl.ds(pl.multiple_of(tile * step, step), step), :] = glob
        return carry

    lax.fori_loop(0, crops // step, glob_step, 0)
    for slot in range(plan.slots):
        live = jnp.clip(live_count - float(slot), 0.0, 1.0)

        def slot_step(tile, carry, slot=slot, live=live):
            start = crops + slot * slot_rows + tile * step
            mask[pl.ds(pl.multiple_of(start, step), step), :] = small * live
            return carry

        lax.fori_loop(0, slot_rows // step, slot_step, 0)


def zero_borders(plan, shifted):
    lanes = shifted.shape[2]
    for side in range(2):
        shifted[side, : plan.glob_base, :] = jnp.zeros((plan.glob_base, lanes), BF16)
        shifted[side, plan.glob_base + plan.glob_all : plan.small_base, :] = jnp.zeros(
            (plan.glob_width, lanes), BF16
        )
        for slot in range(plan.slots):
            low = plan.small_base + slot * plan.slot_conv + plan.slot_all
            shifted[side, low : low + plan.small_width, :] = jnp.zeros(
                (plan.small_width, lanes), BF16
            )


def forward_kernel(
    plan,
    live,
    glob_hbm,
    small_hbm,
    kernel_in_hbm,
    kernel_mid_hbm,
    kernel_out_hbm,
    squeeze_hbm,
    excite_hbm,
    gain_one,
    shift_one,
    gain_two,
    shift_two,
    excite_bias,
    squeeze_bias,
    gain_three,
    shift_three,
    x_out,
    pre_one_out,
    act_one_out,
    pre_two_out,
    act_three_out,
    w_mid_out,
    k_out_both,
    w_in_both,
    vec_three,
    vec_three_other,
    vec,
    mask,
    w_squeeze,
    w_excite,
    stats,
    pooled_out,
    excite_out,
    squeeze_pre_out,
    glob,
    small,
    kernel_in,
    taps,
    kernel_out,
    squeeze,
    excite,
    wide,
    table,
    x_all,
    pre_one,
    shifted,
    w_in,
    w_mid,
    pre_two,
    act_three,
    k_out,
    pay_one,
    slots_one,
    pay_two,
    slots_two,
    squeeze_send,
    squeeze_recv,
    local_sem,
    send_sem,
    recv_sem,
    spread_send,
    spread_recv,
):
    n, half, group, width = plan.dp, plan.half, plan.group, plan.width
    channels, real = plan.channels, plan.half_real
    me, core = lax.axis_index("dp"), lax.axis_index("rows")
    pieces = plan.own_pieces(core)

    def local(source, target, index):
        copy = pltpu.make_async_copy(source, target, local_sem.at[index])
        copy.start()
        return copy

    load_glob = local(glob_hbm, glob, 0)
    load_small = local(small_hbm, small, 1)
    load_in = local(kernel_in_hbm, kernel_in, 2)
    load_taps = [local(kernel_mid_hbm.at[tap], taps.at[tap], 3 + tap) for tap in range(3)]
    load_out = local(kernel_out_hbm, kernel_out, 6)
    load_squeeze = local(squeeze_hbm, squeeze, 7)
    load_excite = local(excite_hbm, excite, 8)
    entry_barrier(n, me, core)

    def partner(source, target, index):
        copy = to_partner(me, core, source, target, send_sem.at[index], recv_sem.at[index])
        copy.start()
        return copy

    load_glob.wait()

    def glob_row(row, carry):
        start = pieces[0][0] + row * plan.glob_width
        rows = pl.ds(pl.multiple_of(start, 16), plan.glob_width)
        wide[: plan.glob_side, :channels] = glob[row].astype(F32)
        for side in range(2):
            x_all[side, rows, :] = wide[: plan.glob_width, side * half : (side + 1) * half].astype(BF16)
        return carry

    def small_row(row, carry):
        slot = row // plan.small_height
        start = plan.glob_all + slot * plan.slot_all + core * plan.slot_own
        start = start + lax.rem(row, plan.small_height) * plan.small_width
        rows = pl.ds(pl.multiple_of(start, 16), plan.small_width)
        wide[: plan.small_side, :channels] = small[row].astype(F32)
        for side in range(2):
            x_all[side, rows, :] = wide[: plan.small_width, side * half : (side + 1) * half].astype(
                BF16
            )
        return carry

    def send_piece(index):
        part = x_all.at[:, pl.ds(pieces[index][0], pieces[index][2]), :]
        return partner(part, part, index)

    wide[...] = jnp.zeros_like(wide)
    lax.fori_loop(0, plan.glob_height, glob_row, 0)
    x_remote = [send_piece(0)]
    load_small.wait()
    wide[...] = jnp.zeros_like(wide)
    lax.fori_loop(0, plan.slots * plan.small_height, small_row, 0)
    x_remote += [send_piece(1 + slot) for slot in range(plan.slots)]

    table[...] = jnp.zeros_like(table)
    load_in.wait()
    for start in range(0, channels, group):
        length = min(group, channels - start)
        table[:length, :real] = kernel_in[start : start + length, :].astype(F32)
        block = group_lanes(table[:group, :], plan)
        if length < group:
            block = jnp.where(row_of(block.shape) < length, block, 0.0)
        low = start % half
        w_in[start // half, low : low + group, :] = block.astype(BF16)
    base = len(pieces)
    send_in = partner(w_in, w_in_both.at[core], base)

    live_count = live[0].astype(F32)
    vec[...] = jnp.zeros_like(vec)
    for index, vector in enumerate(
        (gain_one, shift_one, gain_two, shift_two, excite_bias, squeeze_bias)
    ):
        vec[index : index + 1, : vector.shape[0]] = vector[...].astype(F32).reshape(1, -1)
    vec_three[...] = jnp.zeros_like(vec_three)
    for index, vector in enumerate((gain_three, shift_three)):
        vec_three[index : index + 1, : vector.shape[0]] = vector[...].astype(F32).reshape(1, -1)
    raw = vec[...]
    grouped = group_lanes(raw, plan)
    chip_count = jnp.zeros((1, half), F32) + (plan.glob_area + plan.slot_area * live_count)
    row = row_of(raw.shape)
    vec[...] = jnp.where(row == SQUEEZE_BIAS, raw, jnp.where(row == COUNT, chip_count, grouped))
    send_vec = partner(vec_three, vec_three_other, base + 1)
    fill_mask(plan, mask, plan.glob_all, plan.slot_all, live_count)

    def product(owner):
        place = pl.multiple_of(owner * plan.glob_own, 16)
        rows = pl.ds(place, plan.glob_own)
        pre_one[rows, :] = dot(x_all[0, rows, :], w_in[0]) + dot(x_all[1, rows, :], w_in[1])
        places = [spot for spot, _, _ in plan.own_pieces(owner)[1:]]
        sides = [
            jnp.concatenate([x_all[side, pl.ds(spot, plan.slot_own), :] for spot in places], 0)
            for side in range(2)
        ]
        result = dot(sides[0], w_in[0]) + dot(sides[1], w_in[1])
        for slot, spot in enumerate(places):
            pre_one[pl.ds(spot, plan.slot_own), :] = result[
                slot * plan.slot_own : (slot + 1) * plan.slot_own
            ]

    def prepare_tap(tap):
        load_taps[tap].wait()
        table[:width, :real] = taps[tap % 3].astype(F32)
        block = group_lanes(table[:group, :], plan)
        block = jnp.where(row_of(block.shape) < width, block, 0.0)
        w_mid[tap // 3, tap % 3 * group : (tap % 3 + 1) * group, :] = block.astype(BF16)
        if tap + 3 < 9:
            load_taps.append(local(kernel_mid_hbm.at[tap + 3], taps.at[tap % 3], 3 + tap % 3))

    product(core)
    zero_borders(plan, shifted)
    for copy in x_remote:
        copy.wait()
    product(1 - core)
    saves = [local(x_all, x_out, 9), local(pre_one, pre_one_out, 10)]

    def local_part(values, which, pay):
        total, squares = local_moments(plan, values, mask, which, vec[COUNT : COUNT + 1, :])
        pay[:, :half] = total
        pay[:, half : 2 * half] = squares
        pay[:, 2 * half :] = vec[COUNT : COUNT + 1, :LANE]

    def spread_of(pay, slots, index):
        spread = Spread(n, me, core, pay, slots, spread_send.at[index], spread_recv.at[index])
        spread.start()
        return spread

    local_part(pre_one, "all", pay_one)
    spread = spread_of(pay_one, slots_one, 0)
    for tap in range(9):
        prepare_tap(tap)
    saves.append(local(w_mid, w_mid_out, 11))
    spread.wait()
    mean, variance, count = merge_moments(slots_one, n, half)
    inverse = lax.rsqrt(variance + EPSILON)
    stats[...] = jnp.zeros_like(stats)
    stats[MEAN_ONE : MEAN_ONE + 1, :] = mean
    stats[INVERSE_ONE : INVERSE_ONE + 1, :] = inverse
    stats[TOTAL : TOTAL + 1, :] = count
    scale = inverse * vec[GAIN_ONE : GAIN_ONE + 1, :]
    shift = vec[SHIFT_ONE : SHIFT_ONE + 1, :]

    def activate_one(start, place, crop, carry):
        norm = (pre_one[pl.ds(start, TILE), :] - mean) * scale + shift
        act = norm * sigmoid(norm) * widen(mask[pl.ds(start, TILE), :], half)
        before = pltpu.roll(act, 1, 0)
        after = pltpu.roll(act, TILE - 1, 0)
        for tap, value in enumerate((before, act, after)):
            for side in range(2):
                shifted[side, pl.ds(place, TILE), tap * group : (tap + 1) * group] = value[
                    :, side * group : (side + 1) * group
                ].astype(BF16)
        return carry

    plan.sweep(activate_one, 0)
    for side in range(2):
        saves.append(
            local(
                shifted.at[side, :, group : 2 * group],
                act_one_out.at[:, side * group : (side + 1) * group],
                12 + side,
            )
        )

    for low, length, wide_row in plan.segments():
        for side in range(2):
            lanes = slice(side * group, (side + 1) * group)
            block = length // 2
            for part in range(2):
                at = low + part * block
                total = None
                for tap in range(3):
                    first = at + (tap - 1) * wide_row
                    term = dot(shifted[side, first : first + block, :], w_mid[tap, :, lanes])
                    total = term if total is None else total + term
                pre_two[at : at + block, lanes] = total
    saves.append(local(pre_two, pre_two_out, 14))

    local_part(pre_two, "conv", pay_two)
    spread = spread_of(pay_two, slots_two, 1)
    load_out.wait()
    for piece in range(4):
        low = piece * width // 16 * 16
        length = min(table.shape[0], channels - low)
        table[:length, :real] = kernel_out[low : low + length, :].astype(F32)
        off = piece * width - low
        block = table[off : off + group, :]
        block = jnp.where(row_of(block.shape) < width, block, 0.0)
        place = piece % 2 * group
        k_out[piece // 2, place : place + group, :] = block.astype(BF16)
    send_out = partner(k_out, k_out_both.at[core], base + 2)
    load_squeeze.wait()
    for piece in range(2):
        low = piece * width // 16 * 16
        length = min(table.shape[0], 2 * width - low)
        table[:length, :width] = squeeze[low : low + length, :].astype(F32)
        off = piece * width - low
        block = table[off : off + group, :group]
        keep = (row_of(block.shape) < width) & (lane_of(block.shape) < width)
        w_squeeze[piece * group : (piece + 1) * group, :] = jnp.where(keep, block, 0.0).astype(BF16)
    load_excite.wait()
    table[:width, :real] = excite[...].astype(F32)
    block = group_lanes(table[:group, :], plan)
    w_excite[...] = jnp.where(row_of(block.shape) < width, block, 0.0).astype(BF16)
    spread.wait()
    mean_two, variance, _ = merge_moments(slots_two, n, half)
    inverse_two = lax.rsqrt(variance + EPSILON)
    stats[MEAN_TWO : MEAN_TWO + 1, :] = mean_two
    stats[INVERSE_TWO : INVERSE_TWO + 1, :] = inverse_two
    scale_two = inverse_two * vec[GAIN_TWO : GAIN_TWO + 1, :]
    shift_two = vec[SHIFT_TWO : SHIFT_TWO + 1, :]
    pooled_out[...] = jnp.zeros_like(pooled_out)
    saves[1].wait()
    act_two = pre_one

    def activate_two(start, place, crop, carry):
        norm = (pre_two[pl.ds(place, TILE), :] - mean_two) * scale_two + shift_two
        act = norm * sigmoid(norm) * widen(mask[pl.ds(start, TILE), :], half)
        act_two[pl.ds(start, TILE), :] = act
        pooled_out[pl.ds(crop, 1), :] += jnp.sum(act, 0, keepdims=True)
        return carry

    plan.sweep(activate_two, 0)
    pooled_out[:1, :] = pooled_out[:1, :] * (1.0 / plan.glob_area)
    pooled_out[1:, :] = pooled_out[1:, :] * (1.0 / plan.slot_area)
    part = split_dot(pooled_out[...], w_squeeze[...])
    squeeze_send[...] = part
    swap = partner(squeeze_send, squeeze_recv, base + 3)
    swap.wait()
    squeeze_pre = part + squeeze_recv[...] + vec[SQUEEZE_BIAS : SQUEEZE_BIAS + 1, :group]
    squeeze_pre_out[...] = squeeze_pre
    squeezed = squeeze_pre * sigmoid(squeeze_pre)
    excite_out[...] = sigmoid(
        split_dot(squeezed, w_excite[...]) + vec[EXCITE_BIAS : EXCITE_BIAS + 1, :]
    )
    saves.append(local(w_in, w_in_both.at[core], 15))
    saves.append(local(k_out, k_out_both.at[core], 16))

    def activate_three(start, place, crop, carry):
        act_three[core, pl.ds(start, TILE), :] = (
            act_two[pl.ds(start, TILE), :] * excite_out[pl.ds(crop, 1), :]
        ).astype(BF16)
        return carry

    plan.sweep(activate_three, 0)
    exchange = partner(act_three.at[core], act_three.at[core], base + 4)
    saves.append(local(act_three.at[core], act_three_out.at[core], 17))
    for copy in (send_in, send_vec, send_out, exchange):
        copy.wait()
    saves.append(local(act_three.at[1 - core], act_three_out.at[1 - core], 18))
    for index, copy in enumerate(saves):
        if index != 1:
            copy.wait()


def forward(
    plan, live, glob, small, kernel_in, kernel_mid, kernel_out, squeeze, excite, vectors
):
    n, half, group = plan.dp, plan.half, plan.group
    shape = jax.ShapeDtypeStruct
    copies = 1 + plan.slots
    pay = 2 * half + LANE
    smem = pl.BlockSpec(memory_space=pltpu.SMEM)
    return pl.pallas_call(
        functools.partial(forward_kernel, plan),
        out_shape=(
            shape((2, plan.all, half), BF16),
            shape((plan.all, half), F32),
            shape((plan.conv, half), BF16),
            shape((plan.conv, half), F32),
            shape((2, plan.all, half), BF16),
            shape((3, 3 * group, half), BF16),
            shape((2, 2, half, half), BF16),
            shape((2, 2, half, half), BF16),
            shape((8, half), F32),
            shape((8, half), F32),
            shape((8, half), F32),
            shape((plan.all, LANE), F32),
            shape((half, group), BF16),
            shape((group, half), BF16),
            shape((8, half), F32),
            shape((plan.slot_rows, half), F32),
            shape((plan.slot_rows, half), F32),
            shape((plan.slot_rows, group), F32),
        ),
        in_specs=[smem] + [ANY] * 7 + [VMEM] * 8,
        out_specs=(ANY,) * 8 + (VMEM,) * 10,
        scratch_shapes=[
            pltpu.VMEM(glob.shape, BF16),
            pltpu.VMEM(small.shape, BF16),
            pltpu.VMEM(kernel_in.shape, BF16),
            pltpu.VMEM((3,) + kernel_mid.shape[1:], BF16),
            pltpu.VMEM(kernel_out.shape, BF16),
            pltpu.VMEM(squeeze.shape, BF16),
            pltpu.VMEM(excite.shape, BF16),
            pltpu.VMEM((32, 2 * half), F32),
            pltpu.VMEM((group + 16, half), F32),
            pltpu.VMEM((2, plan.all, half), BF16),
            pltpu.VMEM((plan.all, half), F32),
            pltpu.VMEM((2, plan.conv, 3 * group), BF16),
            pltpu.VMEM((2, half, half), BF16),
            pltpu.VMEM((3, 3 * group, half), BF16),
            pltpu.VMEM((plan.conv, half), F32),
            pltpu.VMEM((2, plan.all, half), BF16),
            pltpu.VMEM((2, half, half), BF16),
            pltpu.VMEM((1, pay), F32),
            pltpu.VMEM((n, 1, pay), F32),
            pltpu.VMEM((1, pay), F32),
            pltpu.VMEM((n, 1, pay), F32),
            pltpu.VMEM((plan.slot_rows, group), F32),
            pltpu.VMEM((plan.slot_rows, group), F32),
            pltpu.SemaphoreType.DMA((19,)),
            pltpu.SemaphoreType.DMA((copies + 5,)),
            pltpu.SemaphoreType.DMA((copies + 5,)),
            pltpu.SemaphoreType.DMA((2, n)),
            pltpu.SemaphoreType.DMA((2, n)),
        ],
        compiler_params=pltpu.CompilerParams(
            collective_id=0, has_side_effects=True, vmem_limit_bytes=VMEM_BYTES
        ),
    )(live, glob, small, kernel_in, kernel_mid, kernel_out, squeeze, excite, *vectors)


def own_steps(plan, body, carry):
    step = 32

    def run(tile, state):
        return body(pl.multiple_of(tile * step, step), step, state)

    return lax.fori_loop(0, plan.own // step, run, carry)


def merge_two(first, second, lanes):
    sums = [part[:, :lanes] for part in (first, second)]
    squares = [part[:, lanes : 2 * lanes] for part in (first, second)]
    counts = [widen(part[:, 2 * lanes :], lanes) for part in (first, second)]
    total = sums[0] + sums[1]
    count = counts[0] + counts[1]
    mean = total / count
    spread = squares[0] + squares[1]
    for index in range(2):
        gap = sums[index] / counts[index] - mean
        spread = spread + counts[index] * gap * gap
    return total, spread, count


def split_maps(plan, glob, small, target, base, wide):
    half, real = plan.half, plan.half_real
    low = real // LANE * LANE

    def place(source, row, start, size, real_size):
        wide[:real_size, : plan.channels] = source[row].astype(F32)
        rows = pl.ds(pl.multiple_of(base + start, 16), size)
        first = wide[:size, :half]
        target[0, rows, :] = jnp.where(lane_of(first.shape) < real, first, 0.0).astype(BF16)
        second = wide[:size, low:]
        moved = pltpu.roll(second, second.shape[1] - (real - low), 1)
        target[1, rows, :] = moved[:, :half].astype(BF16)

    def glob_row(row, carry):
        place(glob, row, row * plan.glob_width, plan.glob_width, plan.glob_side)
        return carry

    def small_row(row, carry):
        start = plan.glob_own + row * plan.small_width
        place(small, row, start, plan.small_width, plan.small_side)
        return carry

    wide[...] = jnp.zeros_like(wide)
    lax.fori_loop(0, plan.glob_height, glob_row, 0)
    wide[...] = jnp.zeros_like(wide)
    lax.fori_loop(0, plan.slots * plan.small_height, small_row, 0)


def gather_sum(slots, n, lanes):
    def add(step, carry):
        return carry + slots[step]

    return lax.fori_loop(0, n, add, jnp.zeros((1, lanes), F32))


ORDERS = {
    "A": ((0, 1, 2, 3), (1, 0, 2, 3)),
    "B": ((0, 2, 1, 3), (1, 2, 0, 3)),
    "P": ((0, 1, 2, 3), (2, 1, 0, 3)),
    "Q": ((2, 0, 1, 3), (1, 0, 2, 3)),
}
HALVINGS = 3
HANDED = 2


class Steps:
    def __init__(self, n, me, core, order):
        bits = n.bit_length() - 1
        self.halvings = min(bits, HALVINGS)
        self.shards = 2**self.halvings
        self.doublings = bits - self.halvings
        self.bit, self.partner = [], []
        chosen = [[bit for bit in one if bit < bits] for one in ORDERS[order]]
        chosen = [one + list(range(len(one), bits)) for one in chosen]
        for step in range(bits):
            first, second = 2 ** chosen[0][step], 2 ** chosen[1][step]
            distance = first + (second - first) * core
            bit = lax.rem(me // distance, 2)
            self.bit.append(bit)
            self.partner.append((me + distance * (1 - 2 * bit), core))


class Chain:
    def __init__(self, steps, work, land, send, recv, free, begun=0, until=None):
        self.steps, self.work, self.land, self.free = steps, work, land, free
        self.send, self.recv = send, recv
        self.rows = work.shape[0]
        self.shard = self.rows // steps.shards
        self.halvings = steps.halvings
        self.reduce_steps = steps.halvings + steps.doublings
        self.begun, self.until = begun, until
        self.pending = None
        self.step, self.at, self.length = begun, 0, self.rows >> begun
        for step in range(begun):
            self.at = self.at + steps.bit[step] * (self.rows >> (step + 1))
        self.land_base = self.rows - self.length
        self.back = None

    def rows_at(self, row, length):
        return pl.ds(row if isinstance(row, int) else pl.multiple_of(row, 16), length)

    def here(self):
        return self.work.at[self.rows_at(self.at, self.length), :]

    def remote(self, source, target, step, slot):
        self.pending = pltpu.make_async_remote_copy(
            src_ref=source,
            dst_ref=target,
            send_sem=self.send.at[slot],
            recv_sem=self.recv.at[slot],
            device_id=self.steps.partner[step],
            device_id_type=MESH,
        )
        self.pending.start()

    def begin_reduce(self):
        step = self.step
        if step < self.halvings:
            length = self.rows >> (step + 1)
            bit = self.steps.bit[step]
            self.keep = self.at + bit * length
            gone = self.at + (1 - bit) * length
            low = self.rows - 2 * length
        else:
            length = self.shard
            self.keep = gone = self.at
            low = self.rows - self.shard + (step - self.halvings) * self.shard
        self.length = length
        self.landed = self.land.at[pl.ds(low - self.land_base, length), :]
        self.remote(self.work.at[self.rows_at(gone, length), :], self.landed, step, step)

    def end_reduce(self):
        self.pending.wait()
        if self.free is not None and self.step < self.halvings:
            pl.semaphore_signal(
                self.free.at[self.step],
                inc=1,
                device_id=self.steps.partner[self.step],
                device_id_type=MESH,
            )
        size = 48 if self.shard % 48 == 0 else 16

        def add(tile, carry):
            there = self.rows_at(self.keep + tile * size, size)
            here = pl.ds(pl.multiple_of(tile * size, 16), size)
            total = self.work[there, :].astype(F32) + self.landed[here, :].astype(F32)
            self.work[there, :] = total.astype(BF16)
            return carry

        lax.fori_loop(0, self.length // size, add, 0)
        self.at = self.keep
        self.step += 1

    def begin_gather(self):
        if self.back >= self.begun:
            pl.semaphore_wait(self.free.at[self.back], 1)
        part = self.here()
        self.remote(part, part, self.back, self.reduce_steps + self.back)

    def end_gather(self):
        self.pending.wait()
        self.at = self.at - self.steps.bit[self.back] * self.length
        self.length *= 2
        self.back -= 1

    def advance(self):
        if self.pending is not None:
            if self.back is None:
                self.end_reduce()
            else:
                self.end_gather()
            self.pending = None
        if self.step == self.until:
            return
        if self.step < self.reduce_steps:
            self.begin_reduce()
            return
        if self.back is None:
            self.back = self.halvings - 1
        if self.back >= 0:
            self.begin_gather()

    def done(self):
        return self.pending is None and (self.step == self.until or self.back == -1)


def land_rows(n, rows, begun=0, until=None):
    bits = n.bit_length() - 1
    halvings = min(bits, HALVINGS)
    last = halvings if until is None else min(until, halvings)
    extra = bits - halvings if until is None else 0
    return (rows >> begun) - (rows >> last) + extra * (rows >> halvings)


def chain_slots(n):
    bits = n.bit_length() - 1
    return bits + min(bits, HALVINGS)


def silu_slope(value, sigma):
    return sigma * (1.0 + value * (1.0 - sigma))
OUTS = 2
MIDS = 6
INS = 4
CHAINS = (
    tuple("out%d" % i for i in range(OUTS))
    + tuple("mid%d" % i for i in range(MIDS))
    + tuple("in%d" % i for i in range(INS))
)
CHAIN_ORDERS = tuple("AAPQAPQAPQPQ")

SHIFT_TWO_SUM, GAIN_TWO_SUM = range(2)
SHIFT_ONE_SUM, GAIN_ONE_SUM = range(2)


def middle_kernel(
    plan,
    live,
    act_three_hbm,
    k_out_hbm,
    glob_hbm,
    small_hbm,
    glob_cot_hbm,
    small_cot_hbm,
    pre_two_hbm,
    stats,
    vec,
    vec_three_own,
    vec_three_other,
    mask,
    pooled,
    excite,
    squeeze_pre,
    w_squeeze,
    w_excite,
    result_out,
    grad_summed_out,
    shard_out,
    grad_norm_out,
    slots_ahead,
    slots_behind,
    sums_three_out,
    sums_out,
    act_three,
    k_out,
    flat,
    flat_two,
    maps,
    pay,
    pair,
    chip,
    slots,
    finals,
    pay_back,
    pair_back,
    chip_back,
    slots_back,
    finals_back,
    vec_three,
    glob,
    small,
    glob_cot,
    small_cot,
    mask_own,
    wide,
    pre_two,
    work,
    land,
    grad_excite,
    squeeze_send,
    squeeze_recv,
    grad_pooled,
    ahead,
    behind,
    pay_two,
    slots_two,
    local_sem,
    send_sem,
    recv_sem,
    spread_send,
    spread_recv,
    reduce_send,
    reduce_recv,
):
    n, half, group = plan.dp, plan.half, plan.group
    me, core = lax.axis_index("dp"), lax.axis_index("rows")
    pieces = plan.own_pieces(core)
    base = len(pieces)

    def local(source, target, index):
        copy = pltpu.make_async_copy(source, target, local_sem.at[index])
        copy.start()
        return copy

    def partner(source, target, index):
        copy = to_partner(me, core, source, target, send_sem.at[index], recv_sem.at[index])
        copy.start()
        return copy

    load_act = local(act_three_hbm, act_three, 0)
    load_k = local(k_out_hbm, k_out, 1)
    raws = [
        local(source, target, 2 + index)
        for index, (source, target) in enumerate(
            (
                (glob_hbm, glob),
                (small_hbm, small),
                (glob_cot_hbm, glob_cot),
                (small_cot_hbm, small_cot),
            )
        )
    ]
    load_two = local(pre_two_hbm, pre_two, 6)
    entry_barrier(n, me, core)
    vec_three[core] = vec_three_own[...]
    vec_three[1 - core] = vec_three_other[...]
    fill_mask(plan, mask_own, plan.glob_own, plan.slot_own, live[0].astype(F32))
    own_count = 0.5 * vec[COUNT : COUNT + 1, :]
    own = plan.own

    def spread_of(source, target, index):
        spread = Spread(n, me, core, source, target, spread_send.at[index], spread_recv.at[index])
        spread.start()
        return spread

    deep = plan.slot_rows
    before = squeeze_pre[...]
    sigma = sigmoid(before)
    squeezed = before * sigma
    ahead[...] = jnp.zeros_like(ahead)
    ahead[:deep, :] = pooled[...].astype(BF16)
    ahead[deep:, :group] = squeezed.astype(BF16)
    ahead_spread = spread_of(ahead, slots_ahead, 3)

    def own_part(array, side, part):
        if part == 0:
            return array[side, pl.ds(pieces[0][0], plan.glob_own), :]
        return jnp.concatenate(
            [array[side, pl.ds(spot, size), :] for spot, _, size in pieces[1:]], 0
        )

    marks = (0, plan.glob_own, own)
    load_act.wait()
    load_k.wait()
    for part in range(2):
        lefts = [own_part(act_three, index, part) for index in range(2)]
        for side in range(2):
            flat[side * own + marks[part] : side * own + marks[part + 1], :] = dot(
                lefts[0], k_out[side, 0]
            ) + dot(lefts[1], k_out[side, 1])

    for side in range(2):

        def add(row, step, carry, side=side):
            seen = widen(mask_own[pl.ds(row, step), :], half)
            return carry + rows_down(flat[pl.ds(side * own + row, step), :] * seen)

        total = jnp.sum(own_steps(plan, add, jnp.zeros((8, half), F32)), 0, keepdims=True)
        mean = total / own_count

        def spread_out(row, step, carry, side=side, mean=mean):
            seen = widen(mask_own[pl.ds(row, step), :], half)
            gap = (flat[pl.ds(side * own + row, step), :] - mean) * seen
            return carry + rows_down(gap * gap)

        squares = jnp.sum(own_steps(plan, spread_out, jnp.zeros((8, half), F32)), 0, keepdims=True)
        pay[side, :, :half] = total
        pay[side, :, half : 2 * half] = squares
        pay[side, :, 2 * half :] = own_count[:, :LANE]
    partner(pay.at[1 - core], pair, 0).wait()
    total, squares, count = merge_two(pay[core], pair[...], half)
    chip[:, :half] = total
    chip[:, half : 2 * half] = squares
    chip[:, 2 * half :] = count[:, :LANE]
    exchange = spread_of(chip, slots, 0)
    for copy in raws:
        copy.wait()
    split_maps(plan, glob, small, maps, 0, wide)
    split_maps(plan, glob_cot, small_cot, maps, own, wide)
    exchange.wait()
    mean, variance, full_count = merge_moments(slots, n, half)
    finals[core, :, :half] = mean
    finals[core, :, half:] = lax.rsqrt(variance + EPSILON)
    partner(finals.at[core], finals.at[core], 1).wait()

    for side in range(2):
        mean = finals[side, :, :half]
        inverse = finals[side, :, half:]
        gain = vec_three[side, :1, :]
        shift = vec_three[side, 1:2, :]

        def outer(row, step, carry, side=side, mean=mean, inverse=inverse, gain=gain, shift=shift):
            rows = pl.ds(row, step)
            low = pl.ds(side * own + row, step)
            seen = widen(mask_own[rows, :], half)
            normed = (flat[low, :] - mean) * inverse
            summed = normed * gain + shift + maps[side, rows, :].astype(F32)
            sigma = sigmoid(summed)
            result_out[side, rows, :] = (seen * summed * sigma).astype(BF16)
            slope = sigma * (1.0 + summed * (1.0 - sigma))
            cot = maps[side, pl.ds(pl.multiple_of(own + row, 16), step), :]
            grad = cot.astype(F32) * seen * slope
            flat_two[low, :] = grad
            grad_summed_out[side, rows, :] = grad.astype(BF16)
            return carry[0] + rows_down(grad), carry[1] + rows_down(grad * normed)

        zero = jnp.zeros((8, half), F32)
        shift_sum, gain_sum = own_steps(plan, outer, (zero, zero))
        pay_back[side, :, :half] = jnp.sum(shift_sum, 0, keepdims=True)
        pay_back[side, :, half:] = jnp.sum(gain_sum, 0, keepdims=True)
    partner(pay_back.at[1 - core], pair_back, 2).wait()
    chip_back[...] = pay_back[core] + pair_back[...]
    spread_of(chip_back, slots_back, 1).wait()
    finals_back[core] = gather_sum(slots_back, n, 2 * half)
    partner(finals_back.at[core], finals_back.at[core], 3).wait()

    grad_pre_three = maps
    swaps = []
    for side in range(2):
        mean = finals[side, :, :half]
        inverse = finals[side, :, half:]
        shift_sum = finals_back[side, :, :half]
        gain_sum = finals_back[side, :, half:]
        sums_three_out[side] = jnp.concatenate([shift_sum, gain_sum, jnp.zeros((6, half), F32)], 0)
        scale = vec_three[side, :1, :] * inverse
        shift_mean = shift_sum / full_count
        gain_mean = gain_sum / full_count * inverse

        def inner(
            place, row, side=side, mean=mean, scale=scale, shift_mean=shift_mean,
            gain_mean=gain_mean
        ):
            step = 32
            low = pl.ds(side * own + row, step)
            seen = widen(mask_own[pl.ds(row, step), :], half)
            centered = flat[low, :] - mean
            grad = scale * (flat_two[low, :] - shift_mean - centered * gain_mean)
            grad_pre_three[side, pl.ds(pl.multiple_of(place, 16), step), :] = (grad * seen).astype(
                BF16
            )

        def glob_step(tile, carry):
            row = pl.multiple_of(tile * 32, 32)
            inner(pieces[0][0] + row, row)
            return carry

        def slot_step(tile, carry):
            row = pl.multiple_of(plan.glob_own + tile * 32, 32)
            slot = tile // (plan.slot_own // 32)
            inner(pieces[1][0] + tile * 32 + slot * plan.slot_own, row)
            return carry

        lax.fori_loop(0, plan.glob_own // 32, glob_step, 0)
        lax.fori_loop(0, plan.slots * plan.slot_own // 32, slot_step, 0)
        for index, (place, _, length) in enumerate(pieces):
            part = grad_pre_three.at[side, pl.ds(place, length), :]
            swaps.append(partner(part, part, 5 + side * base + index))

    grad_act = flat

    def product(owner):
        spots = plan.own_pieces(owner)
        rows = pl.ds(spots[0][0], plan.glob_own)
        grad_act[rows, :] = dot_nt(grad_pre_three[0, rows, :], k_out[0, core]) + dot_nt(
            grad_pre_three[1, rows, :], k_out[1, core]
        )
        sides = [
            jnp.concatenate(
                [grad_pre_three[side, pl.ds(spot, size), :] for spot, _, size in spots[1:]], 0
            )
            for side in range(2)
        ]
        result = dot_nt(sides[0], k_out[0, core]) + dot_nt(sides[1], k_out[1, core])
        for spot, start, size in spots[1:]:
            low = start - plan.glob_own
            grad_act[pl.ds(spot, size), :] = result[low : low + size]

    product(core)
    for swap in swaps:
        swap.wait()
    chains, size = [], 2 * half // OUTS
    for side in range(2):
        for part in range(2):
            lanes = slice(part * group, (part + 1) * group)
            low = side * half + part * group
            work[low : low + group, :] = dot_tn(
                act_three[side, :, lanes], grad_pre_three[core]
            ).astype(BF16)
            if (low + group) % size == 0:
                index = low // size
                chain = Chain(
                    Steps(n, me, core, CHAIN_ORDERS[index]), work.at[pl.ds(index * size, size), :],
                    land.at[index], reduce_send.at[index], reduce_recv.at[index], None, until=HANDED
                )
                chain.advance()
                chains.append(chain)
    product(1 - core)
    load_two.wait()

    mean = stats[MEAN_TWO : MEAN_TWO + 1, :]
    inverse = stats[INVERSE_TWO : INVERSE_TWO + 1, :]
    count = stats[TOTAL : TOTAL + 1, :]
    gain = vec[GAIN_TWO : GAIN_TWO + 1, :]
    shift = vec[SHIFT_TWO : SHIFT_TWO + 1, :]
    slopes = flat_two
    grad_excite[...] = jnp.zeros_like(grad_excite)

    def excitation(start, place, crop, carry):
        rows = pl.ds(start, TILE)
        norm = (pre_two[pl.ds(place, TILE), :] - mean) * (inverse * gain) + shift
        sigma = sigmoid(norm)
        seen = widen(mask[rows, :], half)
        slopes[rows, :] = silu_slope(norm, sigma) * seen
        term = grad_act[rows, :] * (norm * sigma * seen)
        grad_excite[pl.ds(crop, 1), :] += jnp.sum(term, 0, keepdims=True)
        return carry

    plan.sweep(excitation, 0)
    level = excite[...]
    grad_excite_pre = grad_excite[...] * level * (1.0 - level)
    part = split_dot(grad_excite_pre, w_excite[...], nt=True)
    squeeze_send[...] = part
    swap = partner(squeeze_send, squeeze_recv, 4)
    swap.wait()
    grad_squeeze_pre = (part + squeeze_recv[...]) * silu_slope(before, sigma)
    back = split_dot(grad_squeeze_pre, w_squeeze[...], nt=True)
    crop_row = lax.broadcasted_iota(jnp.int32, back.shape, 0)
    area = jnp.where(crop_row == 0, 1.0 / plan.glob_area, 1.0 / plan.slot_area)
    grad_pooled[...] = back * area
    behind[...] = jnp.zeros_like(behind)
    behind[:deep, :] = grad_excite_pre.astype(BF16)
    behind[deep:, :group] = grad_squeeze_pre.astype(BF16)

    def gradient(start, place, crop, carry):
        rows = pl.ds(start, TILE)
        incoming = grad_act[rows, :] * excite[pl.ds(crop, 1), :] + grad_pooled[pl.ds(crop, 1), :]
        grad = incoming * slopes[rows, :]
        grad_act[rows, :] = grad
        normed = (pre_two[pl.ds(place, TILE), :] - mean) * inverse
        return carry[0] + rows_down(grad), carry[1] + rows_down(grad * normed)

    zero = jnp.zeros((8, half), F32)
    shift_sum, gain_sum = plan.sweep(gradient, (zero, zero))
    save = local(grad_act, grad_norm_out, 7)
    pay_two[:, :half] = jnp.sum(shift_sum, 0, keepdims=True)
    pay_two[:, half:] = jnp.sum(gain_sum, 0, keepdims=True)
    spread = spread_of(pay_two, slots_two, 2)
    behind_spread = spread_of(behind, slots_behind, 4)
    for chain in chains:
        chain.advance()
    ahead_spread.wait()
    spread.wait()
    totals = gather_sum(slots_two, n, 2 * half)
    stores = []
    for index, chain in enumerate(chains):
        while not chain.done():
            chain.advance()
        stores.append(local(chain.here(), shard_out.at[index], 8 + index))
    sums_out[...] = jnp.zeros_like(sums_out)
    sums_out[SHIFT_TWO_SUM : SHIFT_TWO_SUM + 1, :] = totals[:, :half]
    sums_out[GAIN_TWO_SUM : GAIN_TWO_SUM + 1, :] = totals[:, half:]
    behind_spread.wait()
    for copy in [save] + stores:
        copy.wait()


def middle(
    plan, live, act_three, k_out, glob, small, glob_cot, small_cot, pre_two, stats, vec, vec_three,
    vec_three_other, mask, pooled, excite, squeeze_pre, w_squeeze, w_excite
):
    n, half, group = plan.dp, plan.half, plan.group
    shape = jax.ShapeDtypeStruct
    pieces = 1 + plan.slots
    pay = 2 * half + LANE
    own = (2, plan.own, half)
    rows = 2 * half
    deep = plan.slot_rows
    return pl.pallas_call(
        functools.partial(middle_kernel, plan),
        out_shape=(
            shape(own, BF16),
            shape(own, BF16),
            shape((OUTS, rows // OUTS >> HANDED, half), BF16),
            shape((plan.all, half), F32),
            shape((n, 2 * deep, half), BF16),
            shape((n, 2 * deep, half), BF16),
            shape((2, 8, half), F32),
            shape((8, half), F32),
        ),
        in_specs=[pl.BlockSpec(memory_space=pltpu.SMEM)] + [ANY] * 7 + [VMEM] * 10,
        out_specs=(VMEM, VMEM, ANY, ANY, VMEM, VMEM, VMEM, VMEM),
        scratch_shapes=[
            pltpu.VMEM((2, plan.all, half), BF16),
            pltpu.VMEM(k_out.shape, BF16),
            pltpu.VMEM((plan.all, half), F32),
            pltpu.VMEM((plan.all, half), F32),
            pltpu.VMEM((2, plan.all, half), BF16),
            pltpu.VMEM((2, 1, pay), F32),
            pltpu.VMEM((1, pay), F32),
            pltpu.VMEM((1, pay), F32),
            pltpu.VMEM((n, 1, pay), F32),
            pltpu.VMEM((2, 1, 2 * half), F32),
            pltpu.VMEM((2, 1, 2 * half), F32),
            pltpu.VMEM((1, 2 * half), F32),
            pltpu.VMEM((1, 2 * half), F32),
            pltpu.VMEM((n, 1, 2 * half), F32),
            pltpu.VMEM((2, 1, 2 * half), F32),
            pltpu.VMEM((2,) + vec_three.shape, F32),
            pltpu.VMEM(glob.shape, BF16),
            pltpu.VMEM(small.shape, BF16),
            pltpu.VMEM(glob.shape, BF16),
            pltpu.VMEM(small.shape, BF16),
            pltpu.VMEM((plan.own, LANE), F32),
            pltpu.VMEM((32, 2 * half), F32),
            pltpu.VMEM((plan.conv, half), F32),
            pltpu.VMEM((rows, half), BF16),
            pltpu.VMEM((OUTS, land_rows(n, rows // OUTS, until=HANDED), half), BF16),
            pltpu.VMEM((deep, half), F32),
            pltpu.VMEM((deep, group), F32),
            pltpu.VMEM((deep, group), F32),
            pltpu.VMEM((deep, half), F32),
            pltpu.VMEM((2 * deep, half), BF16),
            pltpu.VMEM((2 * deep, half), BF16),
            pltpu.VMEM((1, 2 * half), F32),
            pltpu.VMEM((n, 1, 2 * half), F32),
            pltpu.SemaphoreType.DMA((8 + OUTS,)),
            pltpu.SemaphoreType.DMA((2 * pieces + 5,)),
            pltpu.SemaphoreType.DMA((2 * pieces + 5,)),
            pltpu.SemaphoreType.DMA((5, n)),
            pltpu.SemaphoreType.DMA((5, n)),
            pltpu.SemaphoreType.DMA((OUTS, HANDED)),
            pltpu.SemaphoreType.DMA((OUTS, HANDED)),
        ],
        compiler_params=pltpu.CompilerParams(
            collective_id=1, has_side_effects=True, vmem_limit_bytes=VMEM_BYTES
        ),
    )(
        live, act_three, k_out, glob, small, glob_cot, small_cot, pre_two, stats, vec, vec_three,
        vec_three_other, mask, pooled, excite, squeeze_pre, w_squeeze, w_excite
    )


SCHEDULE = (
    "two", "M0", "M1", "C0", "out1", "M2", "M3", "M4", "mid0", "M5", "mid2", "out0", "C1",
    "C2", "mid3", "C3", "out1", "mid1", "mid4", "mid2", "C4", "out0", "C5", "out1", "mid0",
    "mid2", "C6", "out0", "C7", "mid1", "mid2", "mid5", "mid0", "sums", "mid4", "out1",
    "mid3", "mid5", "mid2", "mid0", "mid1", "mid4", "one", "K0", "K1", "K2", "mid2", "K3",
    "mid3", "in0", "X0", "in1", "X1", "mid5", "mid4", "in2", "mid1", "in3", "in1", "mid3",
    "mid0", "in0", "mid4", "mid5", "in3", "in2", "X2", "in0", "out0", "mid1", "in1", "mid0",
    "mid5", "in3", "mid3", "X3", "in2", "mid2", "in1", "mid4", "in3", "in0", "in2", "mid1",
    "in1", "in3", "in2", "mid0", "mid3", "mid4", "out1", "in0", "in3", "mid5", "in0", "in2",
    "in1", "mid3", "mid1", "mid5", "in0", "in3", "out0", "in1", "in2",
)


def first_kernel(
    plan,
    shard_out_hbm,
    grad_norm_hbm,
    pre_two_hbm,
    pre_one_hbm,
    act_one_hbm,
    x_hbm,
    w_mid_hbm,
    w_in_hbm,
    stats,
    vec,
    sums_two,
    mask,
    gathered_out,
    gathered_mid,
    gathered_in,
    grad_inputs_out,
    sums_out,
    flat,
    conv_rows,
    shifted,
    act_one,
    w_mid,
    grad_pre_one,
    grad_other,
    w_in,
    work_out,
    land_out,
    work_mid,
    land_mid,
    work_in,
    land_in,
    pay,
    slots,
    local_sem,
    pair_send,
    pair_recv,
    spread_send,
    spread_recv,
    chain_send,
    chain_recv,
    free,
):
    n, half, group = plan.dp, plan.half, plan.group
    me, core = lax.axis_index("dp"), lax.axis_index("rows")
    entry_barrier(n, me, core)

    def local(source, target, index):
        copy = pltpu.make_async_copy(source, target, local_sem.at[index])
        copy.start()
        return copy

    chains, targets, saves, waits, state = {}, {}, {}, {}, {}

    def begin(name, work, land, target, begun=0):
        index = CHAINS.index(name)
        steps = Steps(n, me, core, CHAIN_ORDERS[index])
        chains[name] = Chain(
            steps, work, land, chain_send.at[index], chain_recv.at[index], free.at[index], begun
        )
        targets[name] = target
        return chains[name]

    def advance(name):
        chain = chains[name]
        if name in saves:
            return
        chain.advance()
        if chain.done():
            index = CHAINS.index(name)
            saves[name] = local(chain.work, targets[name], 8 + index)

    outs = CHAINS[:OUTS]
    loads = []
    for index, name in enumerate(outs):
        rows = pl.ds(index * (2 * half // OUTS), 2 * half // OUTS)
        out = begin(
            name, work_out.at[rows, :], land_out.at[index], gathered_out.at[rows, :], HANDED
        )
        loads.append(local(shard_out_hbm.at[index], out.here(), 8 + index))
    waits["norm"] = local(grad_norm_hbm, flat, 0)
    waits["two"] = local(pre_two_hbm, conv_rows, 1)
    waits["act"] = local(act_one_hbm, act_one, 3)
    waits["mid"] = local(w_mid_hbm, w_mid, 4)
    waits["in"] = local(w_in_hbm, w_in, 5)
    for name, load in zip(outs, loads):
        load.wait()
        advance(name)
    count = stats[TOTAL : TOTAL + 1, :]

    def norm_two():
        zero_borders(plan, shifted)
        mean = stats[MEAN_TWO : MEAN_TWO + 1, :]
        inverse = stats[INVERSE_TWO : INVERSE_TWO + 1, :]
        scale = vec[GAIN_TWO : GAIN_TWO + 1, :] * inverse
        shift_mean = sums_two[SHIFT_TWO_SUM : SHIFT_TWO_SUM + 1, :] / count
        gain_mean = sums_two[GAIN_TWO_SUM : GAIN_TWO_SUM + 1, :] / count * inverse
        waits["norm"].wait()
        waits["two"].wait()

        def into_two(start, place, crop, carry):
            rows = pl.ds(start, TILE)
            centered = conv_rows[pl.ds(place, TILE), :] - mean
            grad = scale * (flat[rows, :] - shift_mean - centered * gain_mean)
            grad = grad * widen(mask[rows, :], half)
            after = pltpu.roll(grad, TILE - 1, 0)
            before = pltpu.roll(grad, 1, 0)
            for tap, value in enumerate((after, grad, before)):
                for side in range(2):
                    shifted[side, pl.ds(place, TILE), tap * group : (tap + 1) * group] = value[
                        :, side * group : (side + 1) * group
                    ].astype(BF16)
            return carry

        plan.sweep(into_two, 0)
        waits["one"] = local(pre_one_hbm, flat, 0)
        waits["act"].wait()

    def mid(index):
        tap = index * 3 // MIDS
        sides = range(2) if MIDS == 3 else (index % 2,)
        for side in sides:
            lanes = slice(side * group, (side + 1) * group)
            total = None
            for low, length, width in plan.segments():
                first = low - (tap - 1) * width
                term = dot_tn(
                    act_one[low : low + length, lanes], shifted[side, first : first + length, :]
                )
                total = term if total is None else total + term
            work_mid[tap, lanes, :] = total.astype(BF16)
        name = CHAINS[OUTS + index]
        rows = pl.ds(sides[0] * group, len(sides) * group)
        begin(name, work_mid.at[tap, rows, :], land_mid.at[index], gathered_mid.at[tap, rows, :])
        advance(name)
        read_shifted()

    def read_shifted():
        state["reads"] = state.get("reads", 0) + 1
        if state["reads"] == MIDS + 8:
            waits["x"] = local(x_hbm, shifted.at[:, pl.ds(0, plan.all), pl.ds(0, half)], 7)

    def conv(index):
        if index == 0:
            waits["mid"].wait()
        low, length, width = plan.segments()[index // 4]
        block = length // 2
        side = index // 2 % 2
        at = low + index % 2 * block
        lanes = slice(side * group, (side + 1) * group)
        total = None
        for tap in range(3):
            first = at - (tap - 1) * width
            for column in range(3):
                taps = slice(column * group, (column + 1) * group)
                term = dot_nt(shifted[side, first : first + block, taps], w_mid[tap, taps, lanes])
                total = term if total is None else total + term
        conv_rows[at : at + block, lanes] = total
        read_shifted()

    mean = stats[MEAN_ONE : MEAN_ONE + 1, :]
    inverse = stats[INVERSE_ONE : INVERSE_ONE + 1, :]
    gain = vec[GAIN_ONE : GAIN_ONE + 1, :]
    shift = vec[SHIFT_ONE : SHIFT_ONE + 1, :]
    spread = Spread(n, me, core, pay, slots, spread_send, spread_recv)

    def sums_one():
        waits["one"].wait()

        def gradient(start, place, crop, carry):
            rows = pl.ds(start, TILE)
            normed = (flat[rows, :] - mean) * inverse
            norm = normed * gain + shift
            sigma = sigmoid(norm)
            grad = conv_rows[pl.ds(place, TILE), :] * silu_slope(norm, sigma)
            grad = grad * widen(mask[rows, :], half)
            conv_rows[pl.ds(place, TILE), :] = grad
            return carry[0] + rows_down(grad), carry[1] + rows_down(grad * normed)

        zero = jnp.zeros((8, half), F32)
        shift_sum, gain_sum = plan.sweep(gradient, (zero, zero))
        pay[:, :half] = jnp.sum(shift_sum, 0, keepdims=True)
        pay[:, half:] = jnp.sum(gain_sum, 0, keepdims=True)
        spread.start()

    def norm_one():
        spread.wait()
        totals = gather_sum(slots, n, 2 * half)
        sums_out[...] = jnp.zeros_like(sums_out)
        sums_out[SHIFT_ONE_SUM : SHIFT_ONE_SUM + 1, :] = totals[:, :half]
        sums_out[GAIN_ONE_SUM : GAIN_ONE_SUM + 1, :] = totals[:, half:]
        scale = gain * inverse
        shift_mean = totals[:, :half] / count
        gain_mean = totals[:, half:] / count * inverse

        def into_one(start, place, crop, carry):
            rows = pl.ds(start, TILE)
            centered = flat[rows, :] - mean
            grad = scale * (conv_rows[pl.ds(place, TILE), :] - shift_mean - centered * gain_mean)
            grad_pre_one[rows, :] = (grad * widen(mask[rows, :], half)).astype(BF16)
            return carry

        plan.sweep(into_one, 0)
        state["swaps"] = []
        for index, (place, start, length) in enumerate(plan.own_pieces(1 - core)):
            swap = to_partner(
                me,
                core,
                grad_pre_one.at[pl.ds(place, length), :],
                grad_other.at[pl.ds(start, length), :],
                pair_send.at[index],
                pair_recv.at[index],
            )
            swap.start()
            state["swaps"].append(swap)

    def kernel_in(index):
        if index == 0:
            waits["x"].wait()
        size = 2 * half // INS
        side, start = index * size // half, index * size % half
        for low in range(start, start + size, group):
            work_in[side, low : low + group, :] = dot_tn(
                shifted[side, : plan.all, low : low + group], grad_pre_one[...]
            ).astype(BF16)
        name = CHAINS[OUTS + MIDS + index]
        rows = pl.ds(start, size)
        begin(name, work_in.at[side, rows, :], land_in.at[index], gathered_in.at[side, rows, :])
        advance(name)

    def inputs(index):
        if index == 0:
            waits["in"].wait()
            for swap in state["swaps"]:
                swap.wait()
        part, side = index // 2, index % 2
        marks = (0, plan.glob_own, plan.own)
        rows = slice(marks[part], marks[part + 1])
        pieces = plan.own_pieces(core)
        pieces = pieces[:1] if part == 0 else pieces[1:]
        own = jnp.concatenate([grad_pre_one[pl.ds(spot, size), :] for spot, _, size in pieces], 0)
        low = side * plan.own + marks[part]
        act_one[low : low + own.shape[0], :] = (
            dot_nt(own, w_in[core, side]) + dot_nt(grad_other[rows, :], w_in[1 - core, side])
        ).astype(BF16)
        if part == 1:
            waits["result%d" % side] = local(
                act_one.at[pl.ds(side * plan.own, plan.own), :],
                grad_inputs_out.at[side],
                8 + len(CHAINS) + side,
            )

    blocks = {
        "two": norm_two,
        "sums": sums_one,
        "one": norm_one,
    }
    for index in range(MIDS):
        blocks["M%d" % index] = functools.partial(mid, index)
    for index in range(8):
        blocks["C%d" % index] = functools.partial(conv, index)
    for index in range(INS):
        blocks["K%d" % index] = functools.partial(kernel_in, index)
    for index in range(4):
        blocks["X%d" % index] = functools.partial(inputs, index)
    for item in SCHEDULE:
        if item in blocks:
            blocks[item]()
        else:
            advance(item)
    while len(saves) < len(CHAINS):
        for name in CHAINS:
            advance(name)
    for name in CHAINS:
        saves[name].wait()
    for side in range(2):
        waits["result%d" % side].wait()


def first(
    plan, shard_out, grad_norm, pre_two, pre_one, act_one, x_all, w_mid, w_in, stats, vec,
    sums_two, mask
):
    n, half, group = plan.dp, plan.half, plan.group
    shape = jax.ShapeDtypeStruct
    pieces = 1 + plan.slots
    return pl.pallas_call(
        functools.partial(first_kernel, plan),
        out_shape=(
            shape((2 * half, half), BF16),
            shape((3, half, 3 * group), BF16),
            shape((2, half, half), BF16),
            shape((2, plan.own, half), BF16),
            shape((8, half), F32),
        ),
        in_specs=[ANY] * 8 + [VMEM] * 4,
        out_specs=(ANY, ANY, ANY, ANY, VMEM),
        scratch_shapes=[
            pltpu.VMEM((plan.all, half), F32),
            pltpu.VMEM((plan.conv, half), F32),
            pltpu.VMEM((2, plan.conv, 3 * group), BF16),
            pltpu.VMEM((plan.conv, half), BF16),
            pltpu.VMEM(w_mid.shape, BF16),
            pltpu.VMEM((plan.all, half), BF16),
            pltpu.VMEM((plan.own, half), BF16),
            pltpu.VMEM(w_in.shape, BF16),
            pltpu.VMEM((2 * half, half), BF16),
            pltpu.VMEM((OUTS, land_rows(n, 2 * half // OUTS, begun=HANDED), half), BF16),
            pltpu.VMEM((3, half, 3 * group), BF16),
            pltpu.VMEM((MIDS, land_rows(n, 3 * half // MIDS), 3 * group), BF16),
            pltpu.VMEM((2, half, half), BF16),
            pltpu.VMEM((INS, land_rows(n, 2 * half // INS), half), BF16),
            pltpu.VMEM((1, 2 * half), F32),
            pltpu.VMEM((n, 1, 2 * half), F32),
            pltpu.SemaphoreType.DMA((10 + len(CHAINS),)),
            pltpu.SemaphoreType.DMA((pieces,)),
            pltpu.SemaphoreType.DMA((pieces,)),
            pltpu.SemaphoreType.DMA((n,)),
            pltpu.SemaphoreType.DMA((n,)),
            pltpu.SemaphoreType.DMA((len(CHAINS), chain_slots(n))),
            pltpu.SemaphoreType.DMA((len(CHAINS), chain_slots(n))),
            pltpu.SemaphoreType.REGULAR((len(CHAINS), HALVINGS)),
        ],
        compiler_params=pltpu.CompilerParams(
            collective_id=2, has_side_effects=True, vmem_limit_bytes=VMEM_BYTES
        ),
    )(
        shard_out, grad_norm, pre_two, pre_one, act_one, x_all, w_mid, w_in, stats, vec, sums_two,
        mask
    )


def join_lanes(low, high, real):
    zeros = jnp.zeros_like(low)
    wide = jnp.concatenate([low, zeros], 1)
    moved = pltpu.roll(jnp.concatenate([high, zeros], 1), real, 1)
    lane = lax.broadcasted_iota(jnp.int32, wide.shape, 1)
    return jnp.where(lane < real, wide, moved)


def finish_kernel(
    plan,
    result_hbm,
    grad_summed_hbm,
    grad_inputs_hbm,
    out_hbm,
    in_hbm,
    mid_hbm,
    slots_ahead,
    slots_behind,
    sums_one,
    sums_two,
    sums_three,
    glob_out_hbm,
    small_out_hbm,
    glob_grad_hbm,
    small_grad_hbm,
    kernel_in_hbm,
    kernel_mid_hbm,
    kernel_out_hbm,
    squeeze_out,
    squeeze_bias,
    excite_out,
    excite_bias,
    gain_one,
    shift_one,
    gain_two,
    shift_two,
    gain_three,
    shift_three,
    result,
    grad_summed,
    grad_inputs,
    packed_out,
    packed_in,
    packed_mid,
    glob_out,
    small_out,
    glob_grad,
    small_grad,
    kernel_in,
    kernel_mid,
    kernel_out,
    load_sem,
    store_sem,
):
    half, group, width, real = plan.half, plan.group, plan.width, plan.half_real
    loads, stores = {}, []
    sources = (
        (mid_hbm, packed_mid),
        (out_hbm, packed_out),
        (in_hbm, packed_in),
        (result_hbm, result),
        (grad_summed_hbm, grad_summed),
        (grad_inputs_hbm, grad_inputs),
    )
    for index, (source, target) in enumerate(sources):
        loads[index] = pltpu.make_async_copy(source, target, load_sem.at[index])
        loads[index].start()

    def store(source, target):
        copy = pltpu.make_async_copy(source, target, store_sem.at[len(stores)])
        copy.start()
        stores.append(copy)

    loads[0].wait()
    for row_tap in range(3):
        for tap in range(3):
            lanes = slice(tap * group, (tap + 1) * group)
            low = packed_mid[row_tap, :group, lanes].astype(F32)
            high = packed_mid[row_tap, group:, lanes].astype(F32)
            kernel_mid[row_tap, tap] = join_lanes(low, high, width)[:width, :real]
        store(kernel_mid.at[row_tap], kernel_mid_hbm.at[row_tap])
    loads[1].wait()
    for piece in range(4):
        kernel_out[piece * width : (piece + 1) * width, :] = packed_out[
            piece * group : piece * group + width, :real
        ].astype(F32)
    store(kernel_out, kernel_out_hbm)
    loads[2].wait()
    for side in range(2):
        rows = min(half, plan.channels - side * half)
        low = packed_in[side, :rows, :group].astype(F32)
        high = packed_in[side, :rows, group:].astype(F32)
        kernel_in[side * half : side * half + rows, :] = join_lanes(low, high, width)[:, :real]
    store(kernel_in, kernel_in_hbm)

    def maps(value, glob, small):
        def glob_row(row, carry):
            rows = pl.ds(pl.multiple_of(row * plan.glob_width, 16), plan.glob_width)
            glob[row, :, 0, :] = value(rows)[: plan.glob_side, : plan.channels]
            return carry

        def small_row(row, carry):
            place = plan.glob_own + row * plan.small_width
            rows = pl.ds(pl.multiple_of(place, 16), plan.small_width)
            small[row] = value(rows)[: plan.small_side, : plan.channels]
            return carry

        lax.fori_loop(0, plan.glob_height, glob_row, 0)
        lax.fori_loop(0, plan.slots * plan.small_height, small_row, 0)

    loads[3].wait()
    def joined(array, rows):
        return join_lanes(array[0, rows, :].astype(F32), array[1, rows, :].astype(F32), real)

    maps(lambda rows: joined(result, rows), glob_out, small_out)
    store(glob_out, glob_out_hbm)
    store(small_out, small_out_hbm)
    loads[4].wait()
    loads[5].wait()
    maps(
        lambda rows: joined(grad_summed, rows)
        + jnp.concatenate([grad_inputs[0, rows, :], grad_inputs[1, rows, :]], 1).astype(F32),
        glob_grad,
        small_grad,
    )
    store(glob_grad, glob_grad_hbm)
    store(small_grad, small_grad_hbm)
    n, deep = plan.dp, plan.slot_rows

    def crops(slots, low, lanes):
        rows = slots[...].astype(F32)[:, low : low + deep, :lanes]
        return rows.reshape(n * deep, lanes)

    wide_pooled, squeezed = crops(slots_ahead, 0, half), crops(slots_ahead, deep, group)
    grad_excite, grad_squeeze = crops(slots_behind, 0, half), crops(slots_behind, deep, group)
    excite = dot_tn(squeezed.astype(BF16), grad_excite.astype(BF16))
    squeeze = dot_tn(wide_pooled.astype(BF16), grad_squeeze.astype(BF16))
    squeeze_out[:width, :] = squeeze[:width, :width]
    squeeze_out[width:, :] = squeeze[group : group + width, :width]
    excite_out[...] = join_lanes(excite[:, :group], excite[:, group:], width)[:width, :real]
    bias = jnp.sum(grad_excite, 0, keepdims=True)
    bias = join_lanes(bias[:, :group], bias[:, group:], width)
    two = join_lanes(sums_two[:, :group], sums_two[:, group:], width)
    one = join_lanes(sums_one[:, :group], sums_one[:, group:], width)
    three = sums_three[lax.axis_index("rows")]
    squeeze_bias[...] = jnp.sum(grad_squeeze, 0)[:width]
    excite_bias[...] = bias[0, :real]
    gain_one[...] = one[GAIN_ONE_SUM, :real]
    shift_one[...] = one[SHIFT_ONE_SUM, :real]
    gain_two[...] = two[GAIN_TWO_SUM, :real]
    shift_two[...] = two[SHIFT_TWO_SUM, :real]
    gain_three[...] = three[1, :real]
    shift_three[...] = three[0, :real]
    for copy in stores:
        copy.wait()


def finish(
    plan, result, grad_summed, grad_inputs, gathered_out, gathered_in, gathered_mid, slots_ahead,
    slots_behind, sums_one, sums_two, sums_three
):
    shape = jax.ShapeDtypeStruct
    width, real, channels = plan.width, plan.half_real, plan.channels
    glob = (plan.glob_height, plan.glob_side, 1, channels)
    small = (plan.slots * plan.small_height, plan.small_side, channels)
    outs = (glob, small, glob, small, (channels, real), (3, 3, width, real), (channels, real))
    ins = (gathered_mid, gathered_out, gathered_in, result, grad_summed, grad_inputs)
    loaded = (result, grad_summed, grad_inputs, gathered_out, gathered_in, gathered_mid)
    return pl.pallas_call(
        functools.partial(finish_kernel, plan),
        out_shape=tuple(shape(out, F32) for out in outs)
        + (shape((real, width), F32), shape((width,), F32), shape((width, real), F32))
        + (shape((real,), F32),) * 7,
        in_specs=[ANY] * 6 + [VMEM] * 5,
        out_specs=(ANY,) * 7 + (VMEM,) * 10,
        scratch_shapes=[pltpu.VMEM(array.shape, BF16) for array in loaded]
        + [pltpu.VMEM(out, F32) for out in outs]
        + [pltpu.SemaphoreType.DMA((6,)), pltpu.SemaphoreType.DMA((9,))],
        compiler_params=pltpu.CompilerParams(vmem_limit_bytes=VMEM_BYTES),
    )(
        result, grad_summed, grad_inputs, gathered_out, gathered_in, gathered_mid, slots_ahead,
        slots_behind, sums_one, sums_two, sums_three
    )


def per_device(
    glob_in,
    small_in,
    small_count,
    kernel_in,
    kernel_mid,
    kernel_out,
    squeeze_weight,
    squeeze_bias,
    excite_weight,
    excite_bias,
    gain_first,
    shift_first,
    gain_second,
    shift_second,
    gain_third,
    shift_third,
    glob_cotangent,
    small_cotangent,
):
    plan = Plan(glob_in.shape, small_in.shape, kernel_mid.shape[2], lax.axis_size("dp"))

    def images(maps):
        return maps.reshape((-1,) + maps.shape[2:])

    glob, small = images(glob_in), images(small_in)
    vectors = (
        gain_first, shift_first, gain_second, shift_second, excite_bias, squeeze_bias, gain_third,
        shift_third
    )
    (
        x_all, pre_one, act_one, pre_two, act_three, w_mid, k_out, w_in, vec_three,
        vec_three_other, vec, mask, w_squeeze, w_excite, stats, pooled, excite, squeeze_pre
    ) = forward(
        plan, small_count, glob, small, kernel_in, images(kernel_mid), kernel_out, squeeze_weight,
        excite_weight, vectors
    )
    (
        result, grad_summed, shard_out, grad_norm, slots_ahead, slots_behind, sums_three, sums_two
    ) = middle(
        plan, small_count, act_three, k_out, glob, small, images(glob_cotangent),
        images(small_cotangent), pre_two, stats, vec, vec_three, vec_three_other, mask, pooled,
        excite, squeeze_pre, w_squeeze, w_excite
    )
    gathered_out, gathered_mid, gathered_in, grad_inputs, sums_one = first(
        plan, shard_out, grad_norm, pre_two, pre_one, act_one, x_all, w_mid, w_in, stats, vec,
        sums_two, mask
    )
    outputs = finish(
        plan, result, grad_summed, grad_inputs, gathered_out, gathered_in, gathered_mid,
        slots_ahead, slots_behind, sums_one, sums_two, sums_three
    )
    shapes = (glob_in.shape, small_in.shape) * 2
    return tuple(out.reshape(shape) for out, shape in zip(outputs, shapes)) + outputs[4:]


def solution(mesh):
    maps = P("dp", "rows", None, None)
    vector = P("rows")
    columns = P(None, "rows")
    taps = P(None, None, None, "rows")
    return jax.shard_map(
        per_device,
        mesh=mesh,
        in_specs=(
            maps, maps, P("dp"), columns, taps, columns, P("rows", None), P(), columns,
        )
        + (vector,) * 7
        + (maps, maps),
        out_specs=(maps,) * 4
        + (columns, taps, columns, P("rows", None), P(), columns)
        + (vector,) * 7,
        check_vma=False,
    )
```

```python
import functools

import jax
import jax.numpy as jnp
from jax import lax
from jax.experimental import pallas as pl
from jax.experimental.pallas import tpu as pltpu
from jax.sharding import PartitionSpec as P

EPSILON = 1e-05
MESH = pl.DeviceIdType.MESH
F32 = jnp.float32
BF16 = jnp.bfloat16
ANY = pl.BlockSpec(memory_space=pl.ANY)
VMEM = pl.BlockSpec(memory_space=pltpu.VMEM)
LANE = 128
TILE = 64
VMEM_BYTES = 62 * 1024 * 1024


def round_up(value, step):
    return -(-value // step) * step


class Plan:
    def __init__(self, glob_shape, small_shape, group_width, dp):
        self.glob_height, self.glob_side = glob_shape[1], glob_shape[2]
        self.slots, self.small_height, self.small_side = small_shape[:3]
        self.channels = glob_shape[3]
        self.glob_width = round_up(self.glob_side + 1, 32)
        self.small_width = round_up(self.small_side + 1, 16)
        self.glob_own = self.glob_height * self.glob_width
        self.slot_own = self.small_height * self.small_width
        self.own = self.glob_own + self.slots * self.slot_own
        self.glob_all = 2 * self.glob_own
        self.slot_all = 2 * self.slot_own
        self.all = 2 * self.own
        self.glob_base = self.glob_width
        self.small_base = self.glob_all + 2 * self.glob_width
        self.slot_conv = self.slot_all + self.small_width
        self.small_conv = self.slots * self.slot_conv
        self.conv = self.small_base + self.small_conv
        self.width = group_width
        self.group = round_up(group_width, LANE)
        self.half = 2 * self.group
        self.half_real = self.channels // 2
        self.dp = dp
        self.slot_rows = round_up(1 + self.slots, 8)
        self.glob_area = float(2 * self.glob_height * self.glob_side)
        self.slot_area = float(2 * self.small_height * self.small_side)

    def rows_of(self, core, start=0, size=None):
        return pl.ds(pl.multiple_of(core * self.own + start, 16), size or self.own)

    def sweep(self, body, carry):
        tiles = self.glob_own // TILE

        def glob_step(tile, state):
            start = tile // tiles * self.own + lax.rem(tile, tiles) * TILE
            place = self.glob_base + tile * TILE
            return body(pl.multiple_of(start, 16), TILE, pl.multiple_of(place, 16), 0, state)

        def slot_step(tile, state):
            core, slot = tile // self.slots, lax.rem(tile, self.slots)
            start = core * self.own + self.glob_own + slot * self.slot_own
            place = self.small_base + slot * self.slot_conv + core * self.slot_own
            return body(
                pl.multiple_of(start, 16), self.slot_own, pl.multiple_of(place, 16), 1 + slot, state
            )

        carry = lax.fori_loop(0, 2 * tiles, glob_step, carry)
        return lax.fori_loop(0, 2 * self.slots, slot_step, carry)

    def segments(self):
        return (
            (self.glob_base, self.glob_all, self.glob_width),
            (self.small_base, self.small_conv - self.small_width, self.small_width),
        )


def sigmoid(value):
    return 0.5 * jnp.tanh(0.5 * value) + 0.5


def rows_down(tile):
    return jnp.sum(tile.reshape(tile.shape[0] // 8, 8, tile.shape[1]), 0)


def widen(mask, lanes):
    return jnp.concatenate([mask] * (lanes // mask.shape[1]), 1)


def dot(left, right):
    return jnp.dot(left, right, preferred_element_type=F32)


def dot_nt(left, right):
    return lax.dot_general(left, right, (((1,), (1,)), ((), ())), preferred_element_type=F32)


def dot_tn(left, right):
    return lax.dot_general(left, right, (((0,), (0,)), ((), ())), preferred_element_type=F32)


def split_dot(left, right, nt=False):
    high = left.astype(BF16)
    low = (left - high.astype(F32)).astype(BF16)
    call = dot_nt if nt else dot
    return call(high, right) + call(low, right)


def entry_barrier(n, me, core):
    barrier = pltpu.get_barrier_semaphore()

    def greet(step, carry):
        pl.semaphore_signal(
            barrier, inc=1, device_id=(lax.rem(me + step, n), core), device_id_type=MESH
        )
        return carry

    lax.fori_loop(1, n, greet, 0)
    pl.semaphore_signal(barrier, inc=1, device_id=(me, 1 - core), device_id_type=MESH)
    pl.semaphore_wait(barrier, n)


class Spread:
    def __init__(self, n, me, core, source, slots, send, recv):
        self.n, self.me, self.core = n, me, core
        self.source, self.slots, self.send, self.recv = source, slots, send, recv

    def copy(self, step):
        return pltpu.make_async_remote_copy(
            src_ref=self.source,
            dst_ref=self.slots.at[self.me],
            send_sem=self.send.at[step],
            recv_sem=self.recv.at[step],
            device_id=(lax.rem(self.me + step, self.n), self.core),
            device_id_type=MESH,
        )

    def start(self):
        def begin(step, carry):
            self.copy(step).start()
            return carry

        lax.fori_loop(1, self.n, begin, 0)
        self.slots[pl.ds(self.me, 1)] = self.source[...][None]

    def wait(self):
        def end(step, carry):
            self.copy(step).wait()
            return carry

        lax.fori_loop(1, self.n, end, 0)


def to_partner(me, core, source, target, send, recv):
    return pltpu.make_async_remote_copy(
        src_ref=source,
        dst_ref=target,
        send_sem=send,
        recv_sem=recv,
        device_id=(me, 1 - core),
        device_id_type=MESH,
    )


def merge_moments(slots, n, lanes):
    def add(step, carry):
        total, count = carry
        return (total + slots[step, :, :lanes], count + slots[step, :, 2 * lanes : 2 * lanes + LANE])

    total, count = lax.fori_loop(
        0, n, add, (jnp.zeros((1, lanes), F32), jnp.zeros((1, LANE), F32))
    )
    wide_count = widen(count, lanes)
    mean = total / wide_count

    def spread(step, carry):
        own_count = widen(slots[step, :, 2 * lanes : 2 * lanes + LANE], lanes)
        gap = slots[step, :, :lanes] / own_count - mean
        return carry + slots[step, :, lanes : 2 * lanes] + own_count * gap * gap

    squares = lax.fori_loop(0, n, spread, jnp.zeros((1, lanes), F32))
    return mean, squares / wide_count, wide_count


def local_moments(plan, values, mask, which, count):
    lanes = plan.half

    def add(start, size, place, crop, carry):
        row = start if which == "all" else place
        tile = values[pl.ds(row, size), :] * widen(mask[pl.ds(start, size), :], lanes)
        return carry + rows_down(tile)

    total = jnp.sum(plan.sweep(add, jnp.zeros((8, lanes), F32)), 0, keepdims=True)
    mean = total / count

    def spread(start, size, place, crop, carry):
        row = start if which == "all" else place
        gap = (values[pl.ds(row, size), :] - mean) * widen(mask[pl.ds(start, size), :], lanes)
        return carry + rows_down(gap * gap)

    squares = jnp.sum(plan.sweep(spread, jnp.zeros((8, lanes), F32)), 0, keepdims=True)
    return total, squares


GAIN_ONE, SHIFT_ONE, GAIN_TWO, SHIFT_TWO, EXCITE_BIAS, SQUEEZE_BIAS, COUNT = range(7)
MEAN_ONE, INVERSE_ONE, MEAN_TWO, INVERSE_TWO, TOTAL = range(5)


def lane_of(shape):
    return lax.broadcasted_iota(jnp.int32, shape, len(shape) - 1)


def row_of(shape):
    return lax.broadcasted_iota(jnp.int32, shape, len(shape) - 2)


def group_lanes(value, plan):
    lane = lane_of(value.shape)
    moved = pltpu.roll(value, plan.group - plan.width, 1)
    return jnp.where(lane < plan.width, value, jnp.where(lane < plan.group, 0.0, moved))


def fill_mask(plan, mask, base, live_count):
    step = 32
    row = row_of((step, LANE))
    glob = (lax.rem(row, plan.glob_width) < plan.glob_side).astype(F32)
    small = (lax.rem(row, plan.small_width) < plan.small_side).astype(F32)

    def glob_step(tile, carry):
        mask[pl.ds(pl.multiple_of(base + tile * step, step), step), :] = glob
        return carry

    lax.fori_loop(0, plan.glob_own // step, glob_step, 0)
    for slot in range(plan.slots):
        live = jnp.clip(live_count - float(slot), 0.0, 1.0)

        def slot_step(tile, carry, slot=slot, live=live):
            start = base + plan.glob_own + slot * plan.slot_own + tile * step
            mask[pl.ds(pl.multiple_of(start, step), step), :] = small * live
            return carry

        lax.fori_loop(0, plan.slot_own // step, slot_step, 0)


def zero_borders(plan, shifted):
    lanes = shifted.shape[2]
    for side in range(2):
        shifted[side, : plan.glob_base, :] = jnp.zeros((plan.glob_base, lanes), BF16)
        shifted[side, plan.glob_base + plan.glob_all : plan.small_base, :] = jnp.zeros(
            (plan.glob_width, lanes), BF16
        )
        for slot in range(plan.slots):
            low = plan.small_base + slot * plan.slot_conv + plan.slot_all
            shifted[side, low : low + plan.small_width, :] = jnp.zeros(
                (plan.small_width, lanes), BF16
            )


def forward_kernel(
    plan,
    live,
    glob_hbm,
    small_hbm,
    kernel_in_hbm,
    kernel_mid_hbm,
    kernel_out_hbm,
    squeeze_hbm,
    excite_hbm,
    gain_one,
    shift_one,
    gain_two,
    shift_two,
    excite_bias,
    squeeze_bias,
    gain_three,
    shift_three,
    x_out,
    pre_one_out,
    act_one_out,
    pre_two_out,
    act_three_out,
    w_mid_out,
    k_out_both,
    w_in_both,
    vec_three,
    vec_three_other,
    vec,
    mask,
    w_squeeze,
    w_excite,
    stats,
    pooled_out,
    excite_out,
    squeeze_pre_out,
    glob,
    small,
    kernel_in,
    taps,
    kernel_out,
    squeeze,
    excite,
    wide,
    table,
    x_all,
    pre_one,
    shifted,
    w_in,
    w_mid,
    w_turned,
    pre_two,
    act_three,
    k_out,
    pay_one,
    slots_one,
    pay_two,
    slots_two,
    squeeze_send,
    squeeze_recv,
    local_sem,
    send_sem,
    recv_sem,
    spread_send,
    spread_recv,
):
    n, half, group, width = plan.dp, plan.half, plan.group, plan.width
    channels, real = plan.channels, plan.half_real
    me, core = lax.axis_index("dp"), lax.axis_index("rows")

    def local(source, target, index):
        copy = pltpu.make_async_copy(source, target, local_sem.at[index])
        copy.start()
        return copy

    load_glob = local(glob_hbm, glob, 0)
    load_small = local(small_hbm, small, 1)
    load_in = local(kernel_in_hbm, kernel_in, 2)
    entry_barrier(n, me, core)

    def partner(source, target, index):
        copy = to_partner(me, core, source, target, send_sem.at[index], recv_sem.at[index])
        copy.start()
        return copy

    load_glob.wait()

    def glob_row(row, carry):
        rows = plan.rows_of(core, row * plan.glob_width, plan.glob_width)
        wide[: plan.glob_side, :channels] = glob[row].astype(F32)
        for side in range(2):
            x_all[side, rows, :] = wide[: plan.glob_width, side * half : (side + 1) * half].astype(BF16)
        return carry

    def small_row(row, carry):
        rows = plan.rows_of(core, plan.glob_own + row * plan.small_width, plan.small_width)
        wide[: plan.small_side, :channels] = small[row].astype(F32)
        for side in range(2):
            x_all[side, rows, :] = wide[: plan.small_width, side * half : (side + 1) * half].astype(
                BF16
            )
        return carry

    def send_piece(index):
        start = (0, plan.glob_own)[index]
        rows = plan.rows_of(core, start, (plan.glob_own, plan.own - plan.glob_own)[index])
        part = x_all.at[:, rows, :]
        return partner(part, part, index)

    wide[...] = jnp.zeros_like(wide)
    lax.fori_loop(0, plan.glob_height, glob_row, 0)
    x_remote = [send_piece(0)]
    load_small.wait()
    wide[...] = jnp.zeros_like(wide)
    lax.fori_loop(0, plan.slots * plan.small_height, small_row, 0)
    x_remote.append(send_piece(1))

    table[...] = jnp.zeros_like(table)
    load_in.wait()
    load_taps = [local(kernel_mid_hbm.at[tap], taps.at[tap], 3 + tap) for tap in range(3)]
    load_out = local(kernel_out_hbm, kernel_out, 6)
    load_squeeze = local(squeeze_hbm, squeeze, 7)
    load_excite = local(excite_hbm, excite, 8)
    for start in range(0, channels, group):
        length = min(group, channels - start)
        table[:length, :real] = kernel_in[start : start + length, :].astype(F32)
        block = group_lanes(table[:group, :], plan)
        if length < group:
            block = jnp.where(row_of(block.shape) < length, block, 0.0)
        low = start % half
        w_in[start // half, low : low + group, :] = block.astype(BF16)
    base = 2
    send_in = partner(w_in, w_in_both.at[core], base)

    live_count = live[0].astype(F32)
    vec[...] = jnp.zeros_like(vec)
    for index, vector in enumerate(
        (gain_one, shift_one, gain_two, shift_two, excite_bias, squeeze_bias)
    ):
        vec[index : index + 1, : vector.shape[0]] = vector[...].astype(F32).reshape(1, -1)
    vec_three[...] = jnp.zeros_like(vec_three)
    for index, vector in enumerate((gain_three, shift_three)):
        vec_three[index : index + 1, : vector.shape[0]] = vector[...].astype(F32).reshape(1, -1)
    raw = vec[...]
    grouped = group_lanes(raw, plan)
    chip_count = jnp.zeros((1, half), F32) + (plan.glob_area + plan.slot_area * live_count)
    row = row_of(raw.shape)
    vec[...] = jnp.where(row == SQUEEZE_BIAS, raw, jnp.where(row == COUNT, chip_count, grouped))
    send_vec = partner(vec_three, vec_three_other, base + 1)
    for owner in range(2):
        fill_mask(plan, mask, owner * plan.own, live_count)

    def product(owner):
        size = plan.own // 2
        for part in range(2):
            rows = plan.rows_of(owner, part * size, size)
            pre_one[rows, :] = dot(x_all[0, rows, :], w_in[0]) + dot(x_all[1, rows, :], w_in[1])

    def prepare_tap(tap):
        load_taps[tap].wait()
        table[:width, :real] = taps[tap % 3].astype(F32)
        block = group_lanes(table[:group, :], plan)
        block = jnp.where(row_of(block.shape) < width, block, 0.0)
        w_mid[tap // 3, tap % 3 * group : (tap % 3 + 1) * group, :] = block.astype(BF16)
        for side in range(2):
            turned = block[:, side * group : (side + 1) * group].T
            w_turned[side, :, tap * group : (tap + 1) * group] = turned.astype(BF16)
        if tap + 3 < 9:
            load_taps.append(local(kernel_mid_hbm.at[tap + 3], taps.at[tap % 3], 3 + tap % 3))

    product(core)
    zero_borders(plan, shifted)
    for copy in x_remote:
        copy.wait()
    product(1 - core)
    saves = [local(x_all, x_out, 9), local(pre_one, pre_one_out, 10)]

    def local_part(values, which, pay):
        total, squares = local_moments(plan, values, mask, which, vec[COUNT : COUNT + 1, :])
        pay[:, :half] = total
        pay[:, half : 2 * half] = squares
        pay[:, 2 * half :] = vec[COUNT : COUNT + 1, :LANE]

    def spread_of(pay, slots, index):
        spread = Spread(n, me, core, pay, slots, spread_send.at[index], spread_recv.at[index])
        spread.start()
        return spread

    local_part(pre_one, "all", pay_one)
    spread = spread_of(pay_one, slots_one, 0)
    for tap in range(9):
        prepare_tap(tap)
    saves.append(local(w_mid, w_mid_out, 11))
    spread.wait()
    mean, variance, count = merge_moments(slots_one, n, half)
    inverse = lax.rsqrt(variance + EPSILON)
    stats[...] = jnp.zeros_like(stats)
    stats[MEAN_ONE : MEAN_ONE + 1, :] = mean
    stats[INVERSE_ONE : INVERSE_ONE + 1, :] = inverse
    stats[TOTAL : TOTAL + 1, :] = count
    scale = inverse * vec[GAIN_ONE : GAIN_ONE + 1, :]
    shift = vec[SHIFT_ONE : SHIFT_ONE + 1, :]

    def activate_one(start, size, place, crop, carry):
        norm = (pre_one[pl.ds(start, size), :] - mean) * scale + shift
        act = norm * sigmoid(norm) * widen(mask[pl.ds(start, size), :], half)
        before = pltpu.roll(act, 1, 0)
        after = pltpu.roll(act, size - 1, 0)
        for tap, value in enumerate((before, act, after)):
            for side in range(2):
                shifted[side, pl.ds(place, size), tap * group : (tap + 1) * group] = value[
                    :, side * group : (side + 1) * group
                ].astype(BF16)
        return carry

    plan.sweep(activate_one, 0)
    for side in range(2):
        saves.append(
            local(
                shifted.at[side, :, group : 2 * group],
                act_one_out.at[:, side * group : (side + 1) * group],
                12 + side,
            )
        )

    for low, length, wide_row in plan.segments():
        for side in range(2):
            lanes = slice(side * group, (side + 1) * group)
            block = length // 2
            for part in range(2):
                at = low + part * block
                windows = [
                    shifted[side, at + shift_row : at + shift_row + block, :]
                    for shift_row in (-wide_row, 0, wide_row)
                ]
                turned = dot_nt(w_turned[side], jnp.concatenate(windows, 1))
                pre_two[at : at + block, lanes] = turned.T
    saves.append(local(pre_two, pre_two_out, 14))

    local_part(pre_two, "conv", pay_two)
    spread = spread_of(pay_two, slots_two, 1)
    load_out.wait()
    for piece in range(4):
        low = piece * width // 16 * 16
        length = min(table.shape[0], channels - low)
        table[:length, :real] = kernel_out[low : low + length, :].astype(F32)
        off = piece * width - low
        block = table[off : off + group, :]
        block = jnp.where(row_of(block.shape) < width, block, 0.0)
        place = piece % 2 * group
        k_out[piece // 2, place : place + group, :] = block.astype(BF16)
    send_out = partner(k_out, k_out_both.at[core], base + 2)
    load_squeeze.wait()
    for piece in range(2):
        low = piece * width // 16 * 16
        length = min(table.shape[0], 2 * width - low)
        table[:length, :width] = squeeze[low : low + length, :].astype(F32)
        off = piece * width - low
        block = table[off : off + group, :group]
        keep = (row_of(block.shape) < width) & (lane_of(block.shape) < width)
        w_squeeze[piece * group : (piece + 1) * group, :] = jnp.where(keep, block, 0.0).astype(BF16)
    load_excite.wait()
    table[:width, :real] = excite[...].astype(F32)
    block = group_lanes(table[:group, :], plan)
    w_excite[...] = jnp.where(row_of(block.shape) < width, block, 0.0).astype(BF16)
    spread.wait()
    mean_two, variance, _ = merge_moments(slots_two, n, half)
    inverse_two = lax.rsqrt(variance + EPSILON)
    stats[MEAN_TWO : MEAN_TWO + 1, :] = mean_two
    stats[INVERSE_TWO : INVERSE_TWO + 1, :] = inverse_two
    scale_two = inverse_two * vec[GAIN_TWO : GAIN_TWO + 1, :]
    shift_two = vec[SHIFT_TWO : SHIFT_TWO + 1, :]
    pooled_out[...] = jnp.zeros_like(pooled_out)
    saves[1].wait()
    act_two = pre_one

    def activate_two(start, size, place, crop, carry):
        norm = (pre_two[pl.ds(place, size), :] - mean_two) * scale_two + shift_two
        act = norm * sigmoid(norm) * widen(mask[pl.ds(start, size), :], half)
        act_two[pl.ds(start, size), :] = act
        pooled_out[pl.ds(crop, 1), :] += jnp.sum(act, 0, keepdims=True)
        return carry

    plan.sweep(activate_two, 0)
    pooled_out[:1, :] = pooled_out[:1, :] * (1.0 / plan.glob_area)
    pooled_out[1:, :] = pooled_out[1:, :] * (1.0 / plan.slot_area)
    part = split_dot(pooled_out[...], w_squeeze[...])
    squeeze_send[...] = part
    swap = partner(squeeze_send, squeeze_recv, base + 3)
    swap.wait()
    squeeze_pre = part + squeeze_recv[...] + vec[SQUEEZE_BIAS : SQUEEZE_BIAS + 1, :group]
    squeeze_pre_out[...] = squeeze_pre
    squeezed = squeeze_pre * sigmoid(squeeze_pre)
    excite_out[...] = sigmoid(
        split_dot(squeezed, w_excite[...]) + vec[EXCITE_BIAS : EXCITE_BIAS + 1, :]
    )
    saves.append(local(w_in, w_in_both.at[core], 15))
    saves.append(local(k_out, k_out_both.at[core], 16))

    def activate_three(start, size, place, crop, carry):
        act_three[core, pl.ds(start, size), :] = (
            act_two[pl.ds(start, size), :] * excite_out[pl.ds(crop, 1), :]
        ).astype(BF16)
        return carry

    plan.sweep(activate_three, 0)
    part = act_three.at[core, plan.rows_of(1 - core), :]
    exchange = partner(part, part, base + 4)
    saves.append(local(act_three.at[core], act_three_out.at[core], 17))
    for copy in (send_in, send_vec, send_out, exchange):
        copy.wait()
    part = act_three.at[1 - core, plan.rows_of(core), :]
    saves.append(local(part, act_three_out.at[1 - core, plan.rows_of(core), :], 18))
    for index, copy in enumerate(saves):
        if index != 1:
            copy.wait()


def forward(
    plan, live, glob, small, kernel_in, kernel_mid, kernel_out, squeeze, excite, vectors
):
    n, half, group = plan.dp, plan.half, plan.group
    shape = jax.ShapeDtypeStruct
    pay = 2 * half + LANE
    smem = pl.BlockSpec(memory_space=pltpu.SMEM)
    return pl.pallas_call(
        functools.partial(forward_kernel, plan),
        out_shape=(
            shape((2, plan.all, half), BF16),
            shape((plan.all, half), F32),
            shape((plan.conv, half), BF16),
            shape((plan.conv, half), F32),
            shape((2, plan.all, half), BF16),
            shape((3, 3 * group, half), BF16),
            shape((2, 2, half, half), BF16),
            shape((2, 2, half, half), BF16),
            shape((8, half), F32),
            shape((8, half), F32),
            shape((8, half), F32),
            shape((plan.all, LANE), F32),
            shape((half, group), BF16),
            shape((group, half), BF16),
            shape((8, half), F32),
            shape((plan.slot_rows, half), F32),
            shape((plan.slot_rows, half), F32),
            shape((plan.slot_rows, group), F32),
        ),
        in_specs=[smem] + [ANY] * 7 + [VMEM] * 8,
        out_specs=(ANY,) * 8 + (VMEM,) * 10,
        scratch_shapes=[
            pltpu.VMEM(glob.shape, BF16),
            pltpu.VMEM(small.shape, BF16),
            pltpu.VMEM(kernel_in.shape, BF16),
            pltpu.VMEM((3,) + kernel_mid.shape[1:], BF16),
            pltpu.VMEM(kernel_out.shape, BF16),
            pltpu.VMEM(squeeze.shape, BF16),
            pltpu.VMEM(excite.shape, BF16),
            pltpu.VMEM((32, 2 * half), F32),
            pltpu.VMEM((group + 16, half), F32),
            pltpu.VMEM((2, plan.all, half), BF16),
            pltpu.VMEM((plan.all, half), F32),
            pltpu.VMEM((2, plan.conv, 3 * group), BF16),
            pltpu.VMEM((2, half, half), BF16),
            pltpu.VMEM((3, 3 * group, half), BF16),
            pltpu.VMEM((2, group, 9 * group), BF16),
            pltpu.VMEM((plan.conv, half), F32),
            pltpu.VMEM((2, plan.all, half), BF16),
            pltpu.VMEM((2, half, half), BF16),
            pltpu.VMEM((1, pay), F32),
            pltpu.VMEM((n, 1, pay), F32),
            pltpu.VMEM((1, pay), F32),
            pltpu.VMEM((n, 1, pay), F32),
            pltpu.VMEM((plan.slot_rows, group), F32),
            pltpu.VMEM((plan.slot_rows, group), F32),
            pltpu.SemaphoreType.DMA((19,)),
            pltpu.SemaphoreType.DMA((7,)),
            pltpu.SemaphoreType.DMA((7,)),
            pltpu.SemaphoreType.DMA((2, n)),
            pltpu.SemaphoreType.DMA((2, n)),
        ],
        compiler_params=pltpu.CompilerParams(
            collective_id=0, has_side_effects=True, vmem_limit_bytes=VMEM_BYTES
        ),
    )(live, glob, small, kernel_in, kernel_mid, kernel_out, squeeze, excite, *vectors)


def own_steps(plan, body, carry):
    step = 32

    def run(tile, state):
        return body(pl.multiple_of(tile * step, step), step, state)

    return lax.fori_loop(0, plan.own // step, run, carry)


def merge_two(first, second, lanes):
    sums = [part[:, :lanes] for part in (first, second)]
    squares = [part[:, lanes : 2 * lanes] for part in (first, second)]
    counts = [widen(part[:, 2 * lanes :], lanes) for part in (first, second)]
    total = sums[0] + sums[1]
    count = counts[0] + counts[1]
    mean = total / count
    spread = squares[0] + squares[1]
    for index in range(2):
        gap = sums[index] / counts[index] - mean
        spread = spread + counts[index] * gap * gap
    return total, spread, count


def split_maps(plan, glob, small, target, base, wide):
    half, real = plan.half, plan.half_real
    low = real // LANE * LANE

    def place(source, row, start, size, real_size):
        wide[:real_size, : plan.channels] = source[row].astype(F32)
        rows = pl.ds(pl.multiple_of(base + start, 16), size)
        first = wide[:size, :half]
        target[0, rows, :] = jnp.where(lane_of(first.shape) < real, first, 0.0).astype(BF16)
        second = wide[:size, low:]
        moved = pltpu.roll(second, second.shape[1] - (real - low), 1)
        target[1, rows, :] = moved[:, :half].astype(BF16)

    def glob_row(row, carry):
        place(glob, row, row * plan.glob_width, plan.glob_width, plan.glob_side)
        return carry

    def small_row(row, carry):
        start = plan.glob_own + row * plan.small_width
        place(small, row, start, plan.small_width, plan.small_side)
        return carry

    if glob is not None:
        wide[...] = jnp.zeros_like(wide)
        lax.fori_loop(0, plan.glob_height, glob_row, 0)
    if small is not None:
        wide[...] = jnp.zeros_like(wide)
        lax.fori_loop(0, plan.slots * plan.small_height, small_row, 0)


def gather_sum(slots, n, lanes):
    def add(step, carry):
        return carry + slots[step]

    return lax.fori_loop(0, n, add, jnp.zeros((1, lanes), F32))


ORDERS = {
    "A": ((0, 1, 2, 3), (1, 0, 2, 3)),
    "B": ((0, 2, 1, 3), (1, 2, 0, 3)),
    "P": ((0, 1, 2, 3), (2, 1, 0, 3)),
    "Q": ((2, 0, 1, 3), (1, 0, 2, 3)),
}
HALVINGS = 3
HANDED = 2


class Steps:
    def __init__(self, n, me, core, order):
        bits = n.bit_length() - 1
        self.halvings = min(bits, HALVINGS)
        self.shards = 2**self.halvings
        self.doublings = bits - self.halvings
        self.bit, self.partner = [], []
        chosen = [[bit for bit in one if bit < bits] for one in ORDERS[order]]
        chosen = [one + list(range(len(one), bits)) for one in chosen]
        for step in range(bits):
            first, second = 2 ** chosen[0][step], 2 ** chosen[1][step]
            distance = first + (second - first) * core
            bit = lax.rem(me // distance, 2)
            self.bit.append(bit)
            self.partner.append((me + distance * (1 - 2 * bit), core))


class Chain:
    def __init__(self, steps, work, land, send, recv, free, begun=0, until=None):
        self.steps, self.work, self.land, self.free = steps, work, land, free
        self.send, self.recv = send, recv
        self.rows = work.shape[0]
        self.shard = self.rows // steps.shards
        self.halvings = steps.halvings
        self.reduce_steps = steps.halvings + steps.doublings
        self.begun, self.until = begun, until
        self.pending = None
        self.step, self.at, self.length = begun, 0, self.rows >> begun
        for step in range(begun):
            self.at = self.at + steps.bit[step] * (self.rows >> (step + 1))
        self.land_base = self.rows - self.length
        self.back = None

    def rows_at(self, row, length):
        return pl.ds(row if isinstance(row, int) else pl.multiple_of(row, 16), length)

    def here(self):
        return self.work.at[self.rows_at(self.at, self.length), :]

    def remote(self, source, target, step, slot):
        self.pending = pltpu.make_async_remote_copy(
            src_ref=source,
            dst_ref=target,
            send_sem=self.send.at[slot],
            recv_sem=self.recv.at[slot],
            device_id=self.steps.partner[step],
            device_id_type=MESH,
        )
        self.pending.start()

    def begin_reduce(self):
        step = self.step
        if step < self.halvings:
            length = self.rows >> (step + 1)
            bit = self.steps.bit[step]
            self.keep = self.at + bit * length
            gone = self.at + (1 - bit) * length
            low = self.rows - 2 * length
        else:
            length = self.shard
            self.keep = gone = self.at
            low = self.rows - self.shard + (step - self.halvings) * self.shard
        self.length = length
        self.landed = self.land.at[pl.ds(low - self.land_base, length), :]
        self.remote(self.work.at[self.rows_at(gone, length), :], self.landed, step, step)

    def end_reduce(self):
        self.pending.wait()
        if self.free is not None and self.step < self.halvings:
            pl.semaphore_signal(
                self.free.at[self.step],
                inc=1,
                device_id=self.steps.partner[self.step],
                device_id_type=MESH,
            )
        size = 48 if self.shard % 48 == 0 else 16

        def add(tile, carry):
            there = self.rows_at(self.keep + tile * size, size)
            here = pl.ds(pl.multiple_of(tile * size, 16), size)
            total = self.work[there, :].astype(F32) + self.landed[here, :].astype(F32)
            self.work[there, :] = total.astype(BF16)
            return carry

        lax.fori_loop(0, self.length // size, add, 0)
        self.at = self.keep
        self.step += 1

    def begin_gather(self):
        if self.back >= self.begun:
            pl.semaphore_wait(self.free.at[self.back], 1)
        part = self.here()
        self.remote(part, part, self.back, self.reduce_steps + self.back)

    def end_gather(self):
        self.pending.wait()
        self.at = self.at - self.steps.bit[self.back] * self.length
        self.length *= 2
        self.back -= 1

    def advance(self):
        if self.pending is not None:
            if self.back is None:
                self.end_reduce()
            else:
                self.end_gather()
            self.pending = None
        if self.step == self.until:
            return
        if self.step < self.reduce_steps:
            self.begin_reduce()
            return
        if self.back is None:
            self.back = self.halvings - 1
        if self.back >= 0:
            self.begin_gather()

    def done(self):
        return self.pending is None and (self.step == self.until or self.back == -1)


def land_rows(n, rows, begun=0, until=None):
    bits = n.bit_length() - 1
    halvings = min(bits, HALVINGS)
    last = halvings if until is None else min(until, halvings)
    extra = bits - halvings if until is None else 0
    return (rows >> begun) - (rows >> last) + extra * (rows >> halvings)


def chain_slots(n):
    bits = n.bit_length() - 1
    return bits + min(bits, HALVINGS)


def silu_slope(value, sigma):
    return sigma * (1.0 + value * (1.0 - sigma))
OUTS = 2
MIDS = 6
INS = 4
CHAINS = (
    tuple("out%d" % i for i in range(OUTS))
    + tuple("mid%d" % i for i in range(MIDS))
    + tuple("in%d" % i for i in range(INS))
)
CHAIN_ORDERS = tuple("AAABPQABPQPQ")

SHIFT_TWO_SUM, GAIN_TWO_SUM = range(2)
SHIFT_ONE_SUM, GAIN_ONE_SUM = range(2)


def middle_kernel(
    plan,
    live,
    act_three_hbm,
    k_out_hbm,
    glob_hbm,
    small_hbm,
    glob_cot_hbm,
    small_cot_hbm,
    pre_two_hbm,
    stats,
    vec,
    vec_three_own,
    vec_three_other,
    mask,
    pooled,
    excite,
    squeeze_pre,
    w_squeeze,
    w_excite,
    result_hbm,
    grad_summed_hbm,
    shard_out,
    grad_norm_out,
    slots_ahead,
    slots_behind,
    sums_three_out,
    sums_out,
    result_out,
    grad_summed_out,
    act_three,
    k_out,
    flat,
    flat_two,
    maps,
    pay,
    pair,
    chip,
    slots,
    finals,
    pay_back,
    pair_back,
    chip_back,
    slots_back,
    finals_back,
    vec_three,
    glob,
    small,
    glob_cot,
    small_cot,
    mask_own,
    wide,
    pre_two,
    work,
    land,
    grad_excite,
    squeeze_send,
    squeeze_recv,
    grad_pooled,
    ahead,
    behind,
    pay_two,
    slots_two,
    local_sem,
    send_sem,
    recv_sem,
    spread_send,
    spread_recv,
    reduce_send,
    reduce_recv,
):
    n, half, group = plan.dp, plan.half, plan.group
    me, core = lax.axis_index("dp"), lax.axis_index("rows")
    own = plan.own
    size = own // 2

    def local(source, target, index):
        copy = pltpu.make_async_copy(source, target, local_sem.at[index])
        copy.start()
        return copy

    def partner(source, target, index):
        copy = to_partner(me, core, source, target, send_sem.at[index], recv_sem.at[index])
        copy.start()
        return copy

    load_act = [local(act_three_hbm.at[core], act_three.at[core], 0)]
    mine = act_three.at[1 - core, plan.rows_of(core), :]
    load_act.append(local(act_three_hbm.at[1 - core, plan.rows_of(core), :], mine, 7 + 1 + OUTS))
    load_k = local(k_out_hbm, k_out, 1)
    entry_barrier(n, me, core)
    vec_three[core] = vec_three_own[...]
    vec_three[1 - core] = vec_three_other[...]
    fill_mask(plan, mask_own, 0, live[0].astype(F32))
    own_count = 0.5 * vec[COUNT : COUNT + 1, :]

    def spread_of(source, target, index):
        spread = Spread(n, me, core, source, target, spread_send.at[index], spread_recv.at[index])
        spread.start()
        return spread

    deep = plan.slot_rows
    before = squeeze_pre[...]
    sigma = sigmoid(before)
    squeezed = before * sigma
    ahead[...] = jnp.zeros_like(ahead)
    ahead[:deep, :] = pooled[...].astype(BF16)
    ahead[deep:, :group] = squeezed.astype(BF16)
    ahead_spread = spread_of(ahead, slots_ahead, 3)

    for copy in load_act:
        copy.wait()
    mine = act_three.at[core, plan.rows_of(core), :]
    act_swap = partner(mine, mine, 5)
    load_k.wait()
    raws = [
        local(source, target, 2 + index)
        for index, (source, target) in enumerate(
            (
                (glob_hbm, glob),
                (small_hbm, small),
                (glob_cot_hbm, glob_cot),
                (small_cot_hbm, small_cot),
            )
        )
    ]
    load_two = local(pre_two_hbm, pre_two, 6)
    for part in range(2):
        rows = plan.rows_of(core, part * size, size)
        for side in range(2):
            low = side * own + part * size
            flat[low : low + size, :] = dot(act_three[0, rows, :], k_out[side, 0]) + dot(
                act_three[1, rows, :], k_out[side, 1]
            )

    for side in range(2):

        def add(row, step, carry, side=side):
            seen = widen(mask_own[pl.ds(row, step), :], half)
            return carry + rows_down(flat[pl.ds(side * own + row, step), :] * seen)

        total = jnp.sum(own_steps(plan, add, jnp.zeros((8, half), F32)), 0, keepdims=True)
        mean = total / own_count

        def spread_out(row, step, carry, side=side, mean=mean):
            seen = widen(mask_own[pl.ds(row, step), :], half)
            gap = (flat[pl.ds(side * own + row, step), :] - mean) * seen
            return carry + rows_down(gap * gap)

        squares = jnp.sum(own_steps(plan, spread_out, jnp.zeros((8, half), F32)), 0, keepdims=True)
        pay[side, :, :half] = total
        pay[side, :, half : 2 * half] = squares
        pay[side, :, 2 * half :] = own_count[:, :LANE]
    partner(pay.at[1 - core], pair, 0).wait()
    total, squares, count = merge_two(pay[core], pair[...], half)
    chip[:, :half] = total
    chip[:, half : 2 * half] = squares
    chip[:, 2 * half :] = count[:, :LANE]
    exchange = spread_of(chip, slots, 0)
    for copy in raws:
        copy.wait()
    split_maps(plan, glob, small, maps, 0, wide)
    split_maps(plan, glob_cot, None, maps, own, wide)
    exchange.wait()
    mean, variance, full_count = merge_moments(slots, n, half)
    finals[core, :, :half] = mean
    finals[core, :, half:] = lax.rsqrt(variance + EPSILON)
    swap = partner(finals.at[core], finals.at[core], 1)
    split_maps(plan, None, small_cot, maps, own, wide)
    swap.wait()

    for side in range(2):
        mean = finals[side, :, :half]
        inverse = finals[side, :, half:]
        gain = vec_three[side, :1, :]
        shift = vec_three[side, 1:2, :]

        def outer(row, step, carry, side=side, mean=mean, inverse=inverse, gain=gain, shift=shift):
            rows = pl.ds(row, step)
            low = pl.ds(side * own + row, step)
            seen = widen(mask_own[rows, :], half)
            normed = (flat[low, :] - mean) * inverse
            summed = normed * gain + shift + maps[side, rows, :].astype(F32)
            sigma = sigmoid(summed)
            result_out[side, rows, :] = (seen * summed * sigma).astype(BF16)
            slope = sigma * (1.0 + summed * (1.0 - sigma))
            cot = maps[side, pl.ds(pl.multiple_of(own + row, 16), step), :]
            grad = cot.astype(F32) * seen * slope
            flat_two[low, :] = grad
            grad_summed_out[side, rows, :] = grad.astype(BF16)
            return carry[0] + rows_down(grad), carry[1] + rows_down(grad * normed)

        zero = jnp.zeros((8, half), F32)
        shift_sum, gain_sum = own_steps(plan, outer, (zero, zero))
        pay_back[side, :, :half] = jnp.sum(shift_sum, 0, keepdims=True)
        pay_back[side, :, half:] = jnp.sum(gain_sum, 0, keepdims=True)
    saves = [
        local(result_out, result_hbm, 9 + OUTS),
        local(grad_summed_out, grad_summed_hbm, 10 + OUTS),
    ]
    partner(pay_back.at[1 - core], pair_back, 2).wait()
    chip_back[...] = pay_back[core] + pair_back[...]
    spread_of(chip_back, slots_back, 1).wait()
    finals_back[core] = gather_sum(slots_back, n, 2 * half)
    partner(finals_back.at[core], finals_back.at[core], 3).wait()

    grad_pre_three = maps
    swaps = []
    for side in range(2):
        mean = finals[side, :, :half]
        inverse = finals[side, :, half:]
        shift_sum = finals_back[side, :, :half]
        gain_sum = finals_back[side, :, half:]
        sums_three_out[side] = jnp.concatenate([shift_sum, gain_sum, jnp.zeros((6, half), F32)], 0)
        scale = vec_three[side, :1, :] * inverse
        shift_mean = shift_sum / full_count
        gain_mean = gain_sum / full_count * inverse

        def inner(
            row, step, carry, side=side, mean=mean, scale=scale, shift_mean=shift_mean,
            gain_mean=gain_mean
        ):
            low = pl.ds(side * own + row, step)
            seen = widen(mask_own[pl.ds(row, step), :], half)
            centered = flat[low, :] - mean
            grad = scale * (flat_two[low, :] - shift_mean - centered * gain_mean)
            grad_pre_three[side, plan.rows_of(core, row, step), :] = (grad * seen).astype(BF16)
            return carry

        own_steps(plan, inner, 0)
        part = grad_pre_three.at[side, plan.rows_of(core), :]
        swaps.append(partner(part, part, 6 + side))

    grad_act = flat

    def product(owner):
        for part in range(2):
            rows = plan.rows_of(owner, part * size, size)
            grad_act[rows, :] = dot_nt(grad_pre_three[0, rows, :], k_out[0, core]) + dot_nt(
                grad_pre_three[1, rows, :], k_out[1, core]
            )

    product(core)
    for swap in swaps + [act_swap]:
        swap.wait()
    chains, span = [], 2 * half // OUTS
    for side in range(2):
        for part in range(2):
            lanes = slice(part * group, (part + 1) * group)
            low = side * half + part * group
            work[low : low + group, :] = dot_tn(
                act_three[side, :, lanes], grad_pre_three[core]
            ).astype(BF16)
            if (low + group) % span == 0:
                index = low // span
                chain = Chain(
                    Steps(n, me, core, CHAIN_ORDERS[index]), work.at[pl.ds(index * span, span), :],
                    land.at[index], reduce_send.at[index], reduce_recv.at[index], None, until=HANDED
                )
                chain.advance()
                chains.append(chain)
    product(1 - core)
    load_two.wait()

    mean = stats[MEAN_TWO : MEAN_TWO + 1, :]
    inverse = stats[INVERSE_TWO : INVERSE_TWO + 1, :]
    count = stats[TOTAL : TOTAL + 1, :]
    gain = vec[GAIN_TWO : GAIN_TWO + 1, :]
    shift = vec[SHIFT_TWO : SHIFT_TWO + 1, :]
    slopes = flat_two
    grad_excite[...] = jnp.zeros_like(grad_excite)

    def excitation(start, size, place, crop, carry):
        rows = pl.ds(start, size)
        norm = (pre_two[pl.ds(place, size), :] - mean) * (inverse * gain) + shift
        sigma = sigmoid(norm)
        seen = widen(mask[rows, :], half)
        slopes[rows, :] = silu_slope(norm, sigma) * seen
        term = grad_act[rows, :] * (norm * sigma * seen)
        grad_excite[pl.ds(crop, 1), :] += jnp.sum(term, 0, keepdims=True)
        return carry

    plan.sweep(excitation, 0)
    level = excite[...]
    grad_excite_pre = grad_excite[...] * level * (1.0 - level)
    part = split_dot(grad_excite_pre, w_excite[...], nt=True)
    squeeze_send[...] = part
    swap = partner(squeeze_send, squeeze_recv, 4)
    swap.wait()
    grad_squeeze_pre = (part + squeeze_recv[...]) * silu_slope(before, sigma)
    back = split_dot(grad_squeeze_pre, w_squeeze[...], nt=True)
    crop_row = lax.broadcasted_iota(jnp.int32, back.shape, 0)
    area = jnp.where(crop_row == 0, 1.0 / plan.glob_area, 1.0 / plan.slot_area)
    grad_pooled[...] = back * area
    behind[...] = jnp.zeros_like(behind)
    behind[:deep, :] = grad_excite_pre.astype(BF16)
    behind[deep:, :group] = grad_squeeze_pre.astype(BF16)

    def gradient(start, size, place, crop, carry):
        rows = pl.ds(start, size)
        incoming = grad_act[rows, :] * excite[pl.ds(crop, 1), :] + grad_pooled[pl.ds(crop, 1), :]
        grad = incoming * slopes[rows, :]
        grad_act[rows, :] = grad
        normed = (pre_two[pl.ds(place, size), :] - mean) * inverse
        return carry[0] + rows_down(grad), carry[1] + rows_down(grad * normed)

    zero = jnp.zeros((8, half), F32)
    shift_sum, gain_sum = plan.sweep(gradient, (zero, zero))
    saves.append(local(grad_act, grad_norm_out, 7))
    pay_two[:, :half] = jnp.sum(shift_sum, 0, keepdims=True)
    pay_two[:, half:] = jnp.sum(gain_sum, 0, keepdims=True)
    spread = spread_of(pay_two, slots_two, 2)
    behind_spread = spread_of(behind, slots_behind, 4)
    for chain in chains:
        chain.advance()
    ahead_spread.wait()
    spread.wait()
    totals = gather_sum(slots_two, n, 2 * half)
    stores = []
    for index, chain in enumerate(chains):
        while not chain.done():
            chain.advance()
        stores.append(local(chain.here(), shard_out.at[index], 8 + index))
    sums_out[...] = jnp.zeros_like(sums_out)
    sums_out[SHIFT_TWO_SUM : SHIFT_TWO_SUM + 1, :] = totals[:, :half]
    sums_out[GAIN_TWO_SUM : GAIN_TWO_SUM + 1, :] = totals[:, half:]
    behind_spread.wait()
    for copy in saves + stores:
        copy.wait()


def middle(
    plan, live, act_three, k_out, glob, small, glob_cot, small_cot, pre_two, stats, vec, vec_three,
    vec_three_other, mask, pooled, excite, squeeze_pre, w_squeeze, w_excite
):
    n, half, group = plan.dp, plan.half, plan.group
    shape = jax.ShapeDtypeStruct
    pay = 2 * half + LANE
    own = (2, plan.own, half)
    rows = 2 * half
    deep = plan.slot_rows
    return pl.pallas_call(
        functools.partial(middle_kernel, plan),
        out_shape=(
            shape(own, BF16),
            shape(own, BF16),
            shape((OUTS, rows // OUTS >> HANDED, half), BF16),
            shape((plan.all, half), F32),
            shape((n, 2 * deep, half), BF16),
            shape((n, 2 * deep, half), BF16),
            shape((2, 8, half), F32),
            shape((8, half), F32),
        ),
        in_specs=[pl.BlockSpec(memory_space=pltpu.SMEM)] + [ANY] * 7 + [VMEM] * 10,
        out_specs=(ANY, ANY, ANY, ANY, VMEM, VMEM, VMEM, VMEM),
        scratch_shapes=[
            pltpu.VMEM(own, BF16),
            pltpu.VMEM(own, BF16),
            pltpu.VMEM((2, plan.all, half), BF16),
            pltpu.VMEM(k_out.shape, BF16),
            pltpu.VMEM((plan.all, half), F32),
            pltpu.VMEM((plan.all, half), F32),
            pltpu.VMEM((2, plan.all, half), BF16),
            pltpu.VMEM((2, 1, pay), F32),
            pltpu.VMEM((1, pay), F32),
            pltpu.VMEM((1, pay), F32),
            pltpu.VMEM((n, 1, pay), F32),
            pltpu.VMEM((2, 1, 2 * half), F32),
            pltpu.VMEM((2, 1, 2 * half), F32),
            pltpu.VMEM((1, 2 * half), F32),
            pltpu.VMEM((1, 2 * half), F32),
            pltpu.VMEM((n, 1, 2 * half), F32),
            pltpu.VMEM((2, 1, 2 * half), F32),
            pltpu.VMEM((2,) + vec_three.shape, F32),
            pltpu.VMEM(glob.shape, BF16),
            pltpu.VMEM(small.shape, BF16),
            pltpu.VMEM(glob.shape, BF16),
            pltpu.VMEM(small.shape, BF16),
            pltpu.VMEM((plan.own, LANE), F32),
            pltpu.VMEM((32, 2 * half), F32),
            pltpu.VMEM((plan.conv, half), F32),
            pltpu.VMEM((rows, half), BF16),
            pltpu.VMEM((OUTS, land_rows(n, rows // OUTS, until=HANDED), half), BF16),
            pltpu.VMEM((deep, half), F32),
            pltpu.VMEM((deep, group), F32),
            pltpu.VMEM((deep, group), F32),
            pltpu.VMEM((deep, half), F32),
            pltpu.VMEM((2 * deep, half), BF16),
            pltpu.VMEM((2 * deep, half), BF16),
            pltpu.VMEM((1, 2 * half), F32),
            pltpu.VMEM((n, 1, 2 * half), F32),
            pltpu.SemaphoreType.DMA((11 + OUTS,)),
            pltpu.SemaphoreType.DMA((8,)),
            pltpu.SemaphoreType.DMA((8,)),
            pltpu.SemaphoreType.DMA((5, n)),
            pltpu.SemaphoreType.DMA((5, n)),
            pltpu.SemaphoreType.DMA((OUTS, HANDED)),
            pltpu.SemaphoreType.DMA((OUTS, HANDED)),
        ],
        compiler_params=pltpu.CompilerParams(
            collective_id=1, has_side_effects=True, vmem_limit_bytes=VMEM_BYTES
        ),
    )(
        live, act_three, k_out, glob, small, glob_cot, small_cot, pre_two, stats, vec, vec_three,
        vec_three_other, mask, pooled, excite, squeeze_pre, w_squeeze, w_excite
    )


SCHEDULE = (
    "two", "M0", "out1", "M1", "M2", "mid0", "M3", "M4", "C0", "out1", "C1", "mid0", "out0",
    "M5", "mid1", "C2", "C3", "out1", "C4", "out0", "mid0", "mid3", "mid4", "mid2", "mid5",
    "out1", "C5", "C6", "C7", "mid3", "sums", "mid0", "mid4", "out0", "mid2", "mid5", "mid3",
    "mid0", "mid1", "one", "K0", "K1", "mid5", "mid0", "X0", "mid1", "mid2", "in0", "K2",
    "in1", "K3", "mid3", "mid4", "out0", "mid1", "in2", "mid2", "in1", "mid1", "in0", "in3",
    "mid3", "mid2", "in1", "mid4", "mid1", "in2", "mid5", "in0", "in1", "in3", "mid4", "in2",
    "mid2", "in3", "out1", "in1", "in0", "in2", "mid3", "mid4", "mid0", "in3", "in2", "X1",
    "mid5", "mid1", "in0", "out0", "in3", "in1", "in2", "mid5", "mid3", "in0", "in3", "X2",
    "X3", "mid2", "in2", "in1", "mid5", "mid4", "in3", "in0",
)


def first_kernel(
    plan,
    shard_out_hbm,
    grad_norm_hbm,
    pre_two_hbm,
    pre_one_hbm,
    act_one_hbm,
    x_hbm,
    w_mid_hbm,
    w_in_hbm,
    stats,
    vec,
    sums_two,
    mask,
    gathered_out,
    gathered_mid,
    gathered_in,
    grad_inputs_out,
    sums_out,
    flat,
    conv_rows,
    shifted,
    act_one,
    w_mid,
    grad_pre_one,
    grad_other,
    w_in,
    work_out,
    land_out,
    work_mid,
    land_mid,
    work_in,
    land_in,
    pay,
    slots,
    local_sem,
    pair_send,
    pair_recv,
    spread_send,
    spread_recv,
    chain_send,
    chain_recv,
    free,
):
    n, half, group = plan.dp, plan.half, plan.group
    me, core = lax.axis_index("dp"), lax.axis_index("rows")

    def local(source, target, index):
        copy = pltpu.make_async_copy(source, target, local_sem.at[index])
        copy.start()
        return copy

    waits = {"norm": local(grad_norm_hbm, flat, 0), "two": local(pre_two_hbm, conv_rows, 1)}
    chains, targets, saves, state = {}, {}, {}, {}

    def begin(name, work, land, target, begun=0):
        index = CHAINS.index(name)
        steps = Steps(n, me, core, CHAIN_ORDERS[index])
        chains[name] = Chain(
            steps, work, land, chain_send.at[index], chain_recv.at[index], free.at[index], begun
        )
        targets[name] = target
        return chains[name]

    def advance(name):
        chain = chains[name]
        if name in saves:
            return
        chain.advance()
        if chain.done():
            index = CHAINS.index(name)
            saves[name] = local(chain.work, targets[name], 8 + index)

    outs = CHAINS[:OUTS]
    loads = []
    for index, name in enumerate(outs):
        rows = pl.ds(index * (2 * half // OUTS), 2 * half // OUTS)
        out = begin(
            name, work_out.at[rows, :], land_out.at[index], gathered_out.at[rows, :], HANDED
        )
        loads.append(local(shard_out_hbm.at[index], out.here(), 8 + index))
    entry_barrier(n, me, core)
    for name, load in zip(outs, loads):
        load.wait()
        advance(name)
    count = stats[TOTAL : TOTAL + 1, :]

    def norm_two():
        zero_borders(plan, shifted)
        mean = stats[MEAN_TWO : MEAN_TWO + 1, :]
        inverse = stats[INVERSE_TWO : INVERSE_TWO + 1, :]
        scale = vec[GAIN_TWO : GAIN_TWO + 1, :] * inverse
        shift_mean = sums_two[SHIFT_TWO_SUM : SHIFT_TWO_SUM + 1, :] / count
        gain_mean = sums_two[GAIN_TWO_SUM : GAIN_TWO_SUM + 1, :] / count * inverse
        waits["norm"].wait()
        waits["two"].wait()
        waits["act"] = local(act_one_hbm, act_one, 3)
        waits["mid"] = local(w_mid_hbm, w_mid, 4)
        waits["in"] = local(w_in_hbm, w_in, 5)

        def into_two(start, size, place, crop, carry):
            rows = pl.ds(start, size)
            centered = conv_rows[pl.ds(place, size), :] - mean
            grad = scale * (flat[rows, :] - shift_mean - centered * gain_mean)
            grad = grad * widen(mask[rows, :], half)
            after = pltpu.roll(grad, size - 1, 0)
            before = pltpu.roll(grad, 1, 0)
            for tap, value in enumerate((after, grad, before)):
                for side in range(2):
                    shifted[side, pl.ds(place, size), tap * group : (tap + 1) * group] = value[
                        :, side * group : (side + 1) * group
                    ].astype(BF16)
            return carry

        plan.sweep(into_two, 0)
        waits["one"] = local(pre_one_hbm, flat, 0)
        waits["act"].wait()

    def mid(index):
        tap = index * 3 // MIDS
        sides = range(2) if MIDS == 3 else (index % 2,)
        for side in sides:
            lanes = slice(side * group, (side + 1) * group)
            total = None
            for low, length, width in plan.segments():
                first = low - (tap - 1) * width
                term = dot_tn(
                    act_one[low : low + length, lanes], shifted[side, first : first + length, :]
                )
                total = term if total is None else total + term
            work_mid[tap, lanes, :] = total.astype(BF16)
        name = CHAINS[OUTS + index]
        rows = pl.ds(sides[0] * group, len(sides) * group)
        begin(name, work_mid.at[tap, rows, :], land_mid.at[index], gathered_mid.at[tap, rows, :])
        advance(name)
        read_shifted()

    def read_shifted():
        state["reads"] = state.get("reads", 0) + 1
        if state["reads"] == MIDS + 8:
            waits["x"] = local(x_hbm, shifted.at[:, pl.ds(0, plan.all), pl.ds(0, half)], 7)

    def conv(index):
        if index == 0:
            waits["mid"].wait()
        low, length, width = plan.segments()[index // 4]
        block = length // 2
        side = index // 2 % 2
        at = low + index % 2 * block
        lanes = slice(side * group, (side + 1) * group)
        weights = [
            w_mid[tap, column * group : (column + 1) * group, lanes]
            for tap in range(3)
            for column in range(3)
        ]
        windows = [
            shifted[side, at + shift_row : at + shift_row + block, :]
            for shift_row in (width, 0, -width)
        ]
        turned = dot_nt(jnp.concatenate(weights, 1), jnp.concatenate(windows, 1))
        conv_rows[at : at + block, lanes] = turned.T
        read_shifted()

    mean = stats[MEAN_ONE : MEAN_ONE + 1, :]
    inverse = stats[INVERSE_ONE : INVERSE_ONE + 1, :]
    gain = vec[GAIN_ONE : GAIN_ONE + 1, :]
    shift = vec[SHIFT_ONE : SHIFT_ONE + 1, :]
    spread = Spread(n, me, core, pay, slots, spread_send, spread_recv)

    def sums_one():
        waits["one"].wait()

        def gradient(start, size, place, crop, carry):
            rows = pl.ds(start, size)
            normed = (flat[rows, :] - mean) * inverse
            norm = normed * gain + shift
            sigma = sigmoid(norm)
            grad = conv_rows[pl.ds(place, size), :] * silu_slope(norm, sigma)
            grad = grad * widen(mask[rows, :], half)
            conv_rows[pl.ds(place, size), :] = grad
            return carry[0] + rows_down(grad), carry[1] + rows_down(grad * normed)

        zero = jnp.zeros((8, half), F32)
        shift_sum, gain_sum = plan.sweep(gradient, (zero, zero))
        pay[:, :half] = jnp.sum(shift_sum, 0, keepdims=True)
        pay[:, half:] = jnp.sum(gain_sum, 0, keepdims=True)
        spread.start()

    def norm_one():
        spread.wait()
        totals = gather_sum(slots, n, 2 * half)
        sums_out[...] = jnp.zeros_like(sums_out)
        sums_out[SHIFT_ONE_SUM : SHIFT_ONE_SUM + 1, :] = totals[:, :half]
        sums_out[GAIN_ONE_SUM : GAIN_ONE_SUM + 1, :] = totals[:, half:]
        scale = gain * inverse
        shift_mean = totals[:, :half] / count
        gain_mean = totals[:, half:] / count * inverse

        def into_one(start, size, place, crop, carry):
            rows = pl.ds(start, size)
            centered = flat[rows, :] - mean
            grad = scale * (conv_rows[pl.ds(place, size), :] - shift_mean - centered * gain_mean)
            grad_pre_one[rows, :] = (grad * widen(mask[rows, :], half)).astype(BF16)
            return carry

        plan.sweep(into_one, 0)
        state["swap"] = to_partner(
            me, core, grad_pre_one.at[plan.rows_of(1 - core), :], grad_other, pair_send, pair_recv
        )
        state["swap"].start()

    def kernel_in(index):
        if index == 0:
            waits["x"].wait()
        size = 2 * half // INS
        side, start = index * size // half, index * size % half
        for low in range(start, start + size, group):
            work_in[side, low : low + group, :] = dot_tn(
                shifted[side, : plan.all, low : low + group], grad_pre_one[...]
            ).astype(BF16)
        name = CHAINS[OUTS + MIDS + index]
        rows = pl.ds(start, size)
        begin(name, work_in.at[side, rows, :], land_in.at[index], gathered_in.at[side, rows, :])
        advance(name)

    def inputs(index):
        if index == 0:
            waits["in"].wait()
            state["swap"].wait()
        part, side = index // 2, index % 2
        size = plan.own // 2
        rows = slice(part * size, (part + 1) * size)
        own = grad_pre_one[plan.rows_of(core, part * size, size), :]
        low = side * plan.own + part * size
        act_one[low : low + size, :] = (
            dot_nt(own, w_in[core, side]) + dot_nt(grad_other[rows, :], w_in[1 - core, side])
        ).astype(BF16)
        if part == 1:
            waits["result%d" % side] = local(
                act_one.at[pl.ds(side * plan.own, plan.own), :],
                grad_inputs_out.at[side],
                8 + len(CHAINS) + side,
            )

    blocks = {
        "two": norm_two,
        "sums": sums_one,
        "one": norm_one,
    }
    for index in range(MIDS):
        blocks["M%d" % index] = functools.partial(mid, index)
    for index in range(8):
        blocks["C%d" % index] = functools.partial(conv, index)
    for index in range(INS):
        blocks["K%d" % index] = functools.partial(kernel_in, index)
    for index in range(4):
        blocks["X%d" % index] = functools.partial(inputs, index)
    for item in SCHEDULE:
        if item in blocks:
            blocks[item]()
        else:
            advance(item)
    while len(saves) < len(CHAINS):
        for name in CHAINS:
            advance(name)
    for name in CHAINS:
        saves[name].wait()
    for side in range(2):
        waits["result%d" % side].wait()


def first(
    plan, shard_out, grad_norm, pre_two, pre_one, act_one, x_all, w_mid, w_in, stats, vec,
    sums_two, mask
):
    n, half, group = plan.dp, plan.half, plan.group
    shape = jax.ShapeDtypeStruct
    return pl.pallas_call(
        functools.partial(first_kernel, plan),
        out_shape=(
            shape((2 * half, half), BF16),
            shape((3, half, 3 * group), BF16),
            shape((2, half, half), BF16),
            shape((2, plan.own, half), BF16),
            shape((8, half), F32),
        ),
        in_specs=[ANY] * 8 + [VMEM] * 4,
        out_specs=(ANY, ANY, ANY, ANY, VMEM),
        scratch_shapes=[
            pltpu.VMEM((plan.all, half), F32),
            pltpu.VMEM((plan.conv, half), F32),
            pltpu.VMEM((2, plan.conv, 3 * group), BF16),
            pltpu.VMEM((plan.conv, half), BF16),
            pltpu.VMEM(w_mid.shape, BF16),
            pltpu.VMEM((plan.all, half), BF16),
            pltpu.VMEM((plan.own, half), BF16),
            pltpu.VMEM(w_in.shape, BF16),
            pltpu.VMEM((2 * half, half), BF16),
            pltpu.VMEM((OUTS, land_rows(n, 2 * half // OUTS, begun=HANDED), half), BF16),
            pltpu.VMEM((3, half, 3 * group), BF16),
            pltpu.VMEM((MIDS, land_rows(n, 3 * half // MIDS), 3 * group), BF16),
            pltpu.VMEM((2, half, half), BF16),
            pltpu.VMEM((INS, land_rows(n, 2 * half // INS), half), BF16),
            pltpu.VMEM((1, 2 * half), F32),
            pltpu.VMEM((n, 1, 2 * half), F32),
            pltpu.SemaphoreType.DMA((10 + len(CHAINS),)),
            pltpu.SemaphoreType.DMA,
            pltpu.SemaphoreType.DMA,
            pltpu.SemaphoreType.DMA((n,)),
            pltpu.SemaphoreType.DMA((n,)),
            pltpu.SemaphoreType.DMA((len(CHAINS), chain_slots(n))),
            pltpu.SemaphoreType.DMA((len(CHAINS), chain_slots(n))),
            pltpu.SemaphoreType.REGULAR((len(CHAINS), HALVINGS)),
        ],
        compiler_params=pltpu.CompilerParams(
            collective_id=2, has_side_effects=True, vmem_limit_bytes=VMEM_BYTES
        ),
    )(
        shard_out, grad_norm, pre_two, pre_one, act_one, x_all, w_mid, w_in, stats, vec, sums_two,
        mask
    )


def join_lanes(low, high, real):
    zeros = jnp.zeros_like(low)
    wide = jnp.concatenate([low, zeros], 1)
    moved = pltpu.roll(jnp.concatenate([high, zeros], 1), real, 1)
    lane = lax.broadcasted_iota(jnp.int32, wide.shape, 1)
    return jnp.where(lane < real, wide, moved)


def finish_kernel(
    plan,
    result_hbm,
    grad_summed_hbm,
    grad_inputs_hbm,
    out_hbm,
    in_hbm,
    mid_hbm,
    slots_ahead,
    slots_behind,
    sums_one,
    sums_two,
    sums_three,
    glob_out_hbm,
    small_out_hbm,
    glob_grad_hbm,
    small_grad_hbm,
    kernel_in_hbm,
    kernel_mid_hbm,
    kernel_out_hbm,
    squeeze_out,
    squeeze_bias,
    excite_out,
    excite_bias,
    gain_one,
    shift_one,
    gain_two,
    shift_two,
    gain_three,
    shift_three,
    result,
    grad_summed,
    grad_inputs,
    packed_out,
    packed_in,
    packed_mid,
    glob_out,
    small_out,
    glob_grad,
    small_grad,
    kernel_in,
    kernel_mid,
    kernel_out,
    load_sem,
    store_sem,
):
    half, group, width, real = plan.half, plan.group, plan.width, plan.half_real
    sources = [(mid_hbm.at[tap], packed_mid.at[tap]) for tap in range(3)] + [
        (out_hbm, packed_out),
        (in_hbm, packed_in),
        (result_hbm, result),
        (grad_summed_hbm, grad_summed),
        (grad_inputs_hbm, grad_inputs),
    ]
    loads, stores = [], []

    for source, target in sources:
        copy = pltpu.make_async_copy(source, target, load_sem.at[len(loads)])
        copy.start()
        loads.append(copy)

    def loaded(index):
        loads[index].wait()

    def store(source, target):
        copy = pltpu.make_async_copy(source, target, store_sem.at[len(stores)])
        copy.start()
        stores.append(copy)

    for row_tap in range(3):
        loaded(row_tap)
        for tap in range(3):
            lanes = slice(tap * group, (tap + 1) * group)
            low = packed_mid[row_tap, :group, lanes].astype(F32)
            high = packed_mid[row_tap, group:, lanes].astype(F32)
            kernel_mid[row_tap, tap] = join_lanes(low, high, width)[:width, :real]
        store(kernel_mid.at[row_tap], kernel_mid_hbm.at[row_tap])
    loaded(3)
    for piece in range(4):
        kernel_out[piece * width : (piece + 1) * width, :] = packed_out[
            piece * group : piece * group + width, :real
        ].astype(F32)
    store(kernel_out, kernel_out_hbm)
    loaded(4)
    for side in range(2):
        rows = min(half, plan.channels - side * half)
        low = packed_in[side, :rows, :group].astype(F32)
        high = packed_in[side, :rows, group:].astype(F32)
        kernel_in[side * half : side * half + rows, :] = join_lanes(low, high, width)[:, :real]
    store(kernel_in, kernel_in_hbm)

    def maps(value, glob, small):
        def glob_row(row, carry):
            rows = pl.ds(pl.multiple_of(row * plan.glob_width, 16), plan.glob_width)
            glob[row, :, 0, :] = value(rows)[: plan.glob_side, : plan.channels]
            return carry

        def small_row(row, carry):
            place = plan.glob_own + row * plan.small_width
            rows = pl.ds(pl.multiple_of(place, 16), plan.small_width)
            small[row] = value(rows)[: plan.small_side, : plan.channels]
            return carry

        lax.fori_loop(0, plan.glob_height, glob_row, 0)
        lax.fori_loop(0, plan.slots * plan.small_height, small_row, 0)

    loaded(5)
    def joined(array, rows):
        return join_lanes(array[0, rows, :].astype(F32), array[1, rows, :].astype(F32), real)

    maps(lambda rows: joined(result, rows), glob_out, small_out)
    store(glob_out, glob_out_hbm)
    store(small_out, small_out_hbm)
    loaded(6)
    loaded(7)
    maps(
        lambda rows: joined(grad_summed, rows)
        + jnp.concatenate([grad_inputs[0, rows, :], grad_inputs[1, rows, :]], 1).astype(F32),
        glob_grad,
        small_grad,
    )
    store(glob_grad, glob_grad_hbm)
    store(small_grad, small_grad_hbm)
    n, deep = plan.dp, plan.slot_rows

    def crops(slots, low, lanes):
        rows = slots[...].astype(F32)[:, low : low + deep, :lanes]
        return rows.reshape(n * deep, lanes)

    wide_pooled, squeezed = crops(slots_ahead, 0, half), crops(slots_ahead, deep, group)
    grad_excite, grad_squeeze = crops(slots_behind, 0, half), crops(slots_behind, deep, group)
    excite = dot_tn(squeezed.astype(BF16), grad_excite.astype(BF16))
    squeeze = dot_tn(wide_pooled.astype(BF16), grad_squeeze.astype(BF16))
    squeeze_out[:width, :] = squeeze[:width, :width]
    squeeze_out[width:, :] = squeeze[group : group + width, :width]
    excite_out[...] = join_lanes(excite[:, :group], excite[:, group:], width)[:width, :real]
    bias = jnp.sum(grad_excite, 0, keepdims=True)
    bias = join_lanes(bias[:, :group], bias[:, group:], width)
    two = join_lanes(sums_two[:, :group], sums_two[:, group:], width)
    one = join_lanes(sums_one[:, :group], sums_one[:, group:], width)
    three = sums_three[lax.axis_index("rows")]
    squeeze_bias[...] = jnp.sum(grad_squeeze, 0)[:width]
    excite_bias[...] = bias[0, :real]
    gain_one[...] = one[GAIN_ONE_SUM, :real]
    shift_one[...] = one[SHIFT_ONE_SUM, :real]
    gain_two[...] = two[GAIN_TWO_SUM, :real]
    shift_two[...] = two[SHIFT_TWO_SUM, :real]
    gain_three[...] = three[1, :real]
    shift_three[...] = three[0, :real]
    for copy in stores:
        copy.wait()


def finish(
    plan, result, grad_summed, grad_inputs, gathered_out, gathered_in, gathered_mid, slots_ahead,
    slots_behind, sums_one, sums_two, sums_three
):
    shape = jax.ShapeDtypeStruct
    width, real, channels = plan.width, plan.half_real, plan.channels
    glob = (plan.glob_height, plan.glob_side, 1, channels)
    small = (plan.slots * plan.small_height, plan.small_side, channels)
    outs = (glob, small, glob, small, (channels, real), (3, 3, width, real), (channels, real))
    ins = (gathered_mid, gathered_out, gathered_in, result, grad_summed, grad_inputs)
    loaded = (result, grad_summed, grad_inputs, gathered_out, gathered_in, gathered_mid)
    return pl.pallas_call(
        functools.partial(finish_kernel, plan),
        out_shape=tuple(shape(out, F32) for out in outs)
        + (shape((real, width), F32), shape((width,), F32), shape((width, real), F32))
        + (shape((real,), F32),) * 7,
        in_specs=[ANY] * 6 + [VMEM] * 5,
        out_specs=(ANY,) * 7 + (VMEM,) * 10,
        scratch_shapes=[pltpu.VMEM(array.shape, BF16) for array in loaded]
        + [pltpu.VMEM(out, F32) for out in outs]
        + [pltpu.SemaphoreType.DMA((8,)), pltpu.SemaphoreType.DMA((9,))],
        compiler_params=pltpu.CompilerParams(vmem_limit_bytes=VMEM_BYTES),
    )(
        result, grad_summed, grad_inputs, gathered_out, gathered_in, gathered_mid, slots_ahead,
        slots_behind, sums_one, sums_two, sums_three
    )


def per_device(
    glob_in,
    small_in,
    small_count,
    kernel_in,
    kernel_mid,
    kernel_out,
    squeeze_weight,
    squeeze_bias,
    excite_weight,
    excite_bias,
    gain_first,
    shift_first,
    gain_second,
    shift_second,
    gain_third,
    shift_third,
    glob_cotangent,
    small_cotangent,
):
    plan = Plan(glob_in.shape, small_in.shape, kernel_mid.shape[2], lax.axis_size("dp"))

    def images(maps):
        return maps.reshape((-1,) + maps.shape[2:])

    glob, small = images(glob_in), images(small_in)
    vectors = (
        gain_first, shift_first, gain_second, shift_second, excite_bias, squeeze_bias, gain_third,
        shift_third
    )
    (
        x_all, pre_one, act_one, pre_two, act_three, w_mid, k_out, w_in, vec_three,
        vec_three_other, vec, mask, w_squeeze, w_excite, stats, pooled, excite, squeeze_pre
    ) = forward(
        plan, small_count, glob, small, kernel_in, images(kernel_mid), kernel_out, squeeze_weight,
        excite_weight, vectors
    )
    (
        result, grad_summed, shard_out, grad_norm, slots_ahead, slots_behind, sums_three, sums_two
    ) = middle(
        plan, small_count, act_three, k_out, glob, small, images(glob_cotangent),
        images(small_cotangent), pre_two, stats, vec, vec_three, vec_three_other, mask, pooled,
        excite, squeeze_pre, w_squeeze, w_excite
    )
    gathered_out, gathered_mid, gathered_in, grad_inputs, sums_one = first(
        plan, shard_out, grad_norm, pre_two, pre_one, act_one, x_all, w_mid, w_in, stats, vec,
        sums_two, mask
    )
    outputs = finish(
        plan, result, grad_summed, grad_inputs, gathered_out, gathered_in, gathered_mid,
        slots_ahead, slots_behind, sums_one, sums_two, sums_three
    )
    shapes = (glob_in.shape, small_in.shape) * 2
    return tuple(out.reshape(shape) for out, shape in zip(outputs, shapes)) + outputs[4:]


def solution(mesh):
    maps = P("dp", "rows", None, None)
    vector = P("rows")
    columns = P(None, "rows")
    taps = P(None, None, None, "rows")
    return jax.shard_map(
        per_device,
        mesh=mesh,
        in_specs=(
            maps, maps, P("dp"), columns, taps, columns, P("rows", None), P(), columns,
        )
        + (vector,) * 7
        + (maps, maps),
        out_specs=(maps,) * 4
        + (columns, taps, columns, P("rows", None), P(), columns)
        + (vector,) * 7,
        check_vma=False,
    )
```

```python
import functools

import jax
import jax.numpy as jnp
from jax import lax
from jax.experimental import pallas as pl
from jax.experimental.pallas import tpu as pltpu
from jax.sharding import PartitionSpec as P

EPSILON = 1e-05
MESH = pl.DeviceIdType.MESH
F32 = jnp.float32
BF16 = jnp.bfloat16
ANY = pl.BlockSpec(memory_space=pl.ANY)
VMEM = pl.BlockSpec(memory_space=pltpu.VMEM)
LANE = 128
TILE = 64
VMEM_BYTES = 62 * 1024 * 1024


def round_up(value, step):
    return -(-value // step) * step


class Plan:
    def __init__(self, glob_shape, small_shape, group_width, dp):
        self.glob_height, self.glob_side = glob_shape[1], glob_shape[2]
        self.slots, self.small_height, self.small_side = small_shape[:3]
        self.channels = glob_shape[3]
        self.glob_width = round_up(self.glob_side + 1, 32)
        self.small_width = round_up(self.small_side + 1, 16)
        self.glob_own = self.glob_height * self.glob_width
        self.slot_own = self.small_height * self.small_width
        self.own = self.glob_own + self.slots * self.slot_own
        self.glob_all = 2 * self.glob_own
        self.slot_all = 2 * self.slot_own
        self.all = 2 * self.own
        self.glob_base = self.glob_width
        self.small_base = self.glob_all + 2 * self.glob_width
        self.slot_conv = self.slot_all + self.small_width
        self.small_conv = self.slots * self.slot_conv
        self.conv = self.small_base + self.small_conv
        self.width = group_width
        self.group = round_up(group_width, LANE)
        self.half = 2 * self.group
        self.half_real = self.channels // 2
        self.dp = dp
        self.slot_rows = round_up(1 + self.slots, 8)
        self.glob_area = float(2 * self.glob_height * self.glob_side)
        self.slot_area = float(2 * self.small_height * self.small_side)

    def rows_of(self, core, start=0, size=None):
        return pl.ds(pl.multiple_of(core * self.own + start, 16), size or self.own)

    def sweep(self, body, carry):
        tiles = self.glob_own // TILE

        def glob_step(tile, state):
            start = tile // tiles * self.own + lax.rem(tile, tiles) * TILE
            place = self.glob_base + tile * TILE
            return body(pl.multiple_of(start, 16), TILE, pl.multiple_of(place, 16), 0, state)

        def slot_step(tile, state):
            core, slot = tile // self.slots, lax.rem(tile, self.slots)
            start = core * self.own + self.glob_own + slot * self.slot_own
            place = self.small_base + slot * self.slot_conv + core * self.slot_own
            return body(
                pl.multiple_of(start, 16), self.slot_own, pl.multiple_of(place, 16), 1 + slot, state
            )

        carry = lax.fori_loop(0, 2 * tiles, glob_step, carry)
        return lax.fori_loop(0, 2 * self.slots, slot_step, carry)

    def segments(self):
        return (
            (self.glob_base, self.glob_all, self.glob_width),
            (self.small_base, self.small_conv - self.small_width, self.small_width),
        )


def sigmoid(value):
    return 0.5 * jnp.tanh(0.5 * value) + 0.5


def rows_down(tile):
    return jnp.sum(tile.reshape(tile.shape[0] // 8, 8, tile.shape[1]), 0)


def widen(mask, lanes):
    return jnp.concatenate([mask] * (lanes // mask.shape[1]), 1)


def dot(left, right):
    return jnp.dot(left, right, preferred_element_type=F32)


def dot_nt(left, right):
    return lax.dot_general(left, right, (((1,), (1,)), ((), ())), preferred_element_type=F32)


def dot_tn(left, right):
    return lax.dot_general(left, right, (((0,), (0,)), ((), ())), preferred_element_type=F32)


def split_dot(left, right, nt=False):
    high = left.astype(BF16)
    low = (left - high.astype(F32)).astype(BF16)
    call = dot_nt if nt else dot
    return call(high, right) + call(low, right)


def entry_barrier(n, me, core):
    barrier = pltpu.get_barrier_semaphore()

    def greet(step, carry):
        pl.semaphore_signal(
            barrier, inc=1, device_id=(lax.rem(me + step, n), core), device_id_type=MESH
        )
        return carry

    lax.fori_loop(1, n, greet, 0)
    pl.semaphore_signal(barrier, inc=1, device_id=(me, 1 - core), device_id_type=MESH)
    pl.semaphore_wait(barrier, n)


class Spread:
    def __init__(self, n, me, core, source, slots, send, recv):
        self.n, self.me, self.core = n, me, core
        self.source, self.slots, self.send, self.recv = source, slots, send, recv

    def copy(self, step):
        return pltpu.make_async_remote_copy(
            src_ref=self.source,
            dst_ref=self.slots.at[self.me],
            send_sem=self.send.at[step],
            recv_sem=self.recv.at[step],
            device_id=(lax.rem(self.me + step, self.n), self.core),
            device_id_type=MESH,
        )

    def start(self):
        def begin(step, carry):
            self.copy(step).start()
            return carry

        lax.fori_loop(1, self.n, begin, 0)
        self.slots[pl.ds(self.me, 1)] = self.source[...][None]

    def wait(self):
        def end(step, carry):
            self.copy(step).wait()
            return carry

        lax.fori_loop(1, self.n, end, 0)


def to_partner(me, core, source, target, send, recv):
    return pltpu.make_async_remote_copy(
        src_ref=source,
        dst_ref=target,
        send_sem=send,
        recv_sem=recv,
        device_id=(me, 1 - core),
        device_id_type=MESH,
    )


def merge_moments(slots, n, lanes):
    def add(step, carry):
        total, count = carry
        return (total + slots[step, :, :lanes], count + slots[step, :, 2 * lanes : 2 * lanes + LANE])

    total, count = lax.fori_loop(
        0, n, add, (jnp.zeros((1, lanes), F32), jnp.zeros((1, LANE), F32))
    )
    wide_count = widen(count, lanes)
    mean = total / wide_count

    def spread(step, carry):
        own_count = widen(slots[step, :, 2 * lanes : 2 * lanes + LANE], lanes)
        gap = slots[step, :, :lanes] / own_count - mean
        return carry + slots[step, :, lanes : 2 * lanes] + own_count * gap * gap

    squares = lax.fori_loop(0, n, spread, jnp.zeros((1, lanes), F32))
    return mean, squares / wide_count, wide_count


def local_moments(plan, values, mask, which, count):
    lanes = plan.half

    def add(start, size, place, crop, carry):
        row = start if which == "all" else place
        tile = values[pl.ds(row, size), :] * widen(mask[pl.ds(start, size), :], lanes)
        return carry + rows_down(tile)

    total = jnp.sum(plan.sweep(add, jnp.zeros((8, lanes), F32)), 0, keepdims=True)
    mean = total / count

    def spread(start, size, place, crop, carry):
        row = start if which == "all" else place
        gap = (values[pl.ds(row, size), :] - mean) * widen(mask[pl.ds(start, size), :], lanes)
        return carry + rows_down(gap * gap)

    squares = jnp.sum(plan.sweep(spread, jnp.zeros((8, lanes), F32)), 0, keepdims=True)
    return total, squares


GAIN_ONE, SHIFT_ONE, GAIN_TWO, SHIFT_TWO, EXCITE_BIAS, SQUEEZE_BIAS, COUNT = range(7)
MEAN_ONE, INVERSE_ONE, MEAN_TWO, INVERSE_TWO, TOTAL = range(5)


def lane_of(shape):
    return lax.broadcasted_iota(jnp.int32, shape, len(shape) - 1)


def row_of(shape):
    return lax.broadcasted_iota(jnp.int32, shape, len(shape) - 2)


def group_lanes(value, plan):
    lane = lane_of(value.shape)
    moved = pltpu.roll(value, plan.group - plan.width, 1)
    return jnp.where(lane < plan.width, value, jnp.where(lane < plan.group, 0.0, moved))


def fill_mask(plan, mask, base, live_count):
    step = 32
    row = row_of((step, LANE))
    glob = (lax.rem(row, plan.glob_width) < plan.glob_side).astype(F32)
    small = (lax.rem(row, plan.small_width) < plan.small_side).astype(F32)

    def glob_step(tile, carry):
        mask[pl.ds(pl.multiple_of(base + tile * step, step), step), :] = glob
        return carry

    lax.fori_loop(0, plan.glob_own // step, glob_step, 0)
    for slot in range(plan.slots):
        live = jnp.clip(live_count - float(slot), 0.0, 1.0)

        def slot_step(tile, carry, slot=slot, live=live):
            start = base + plan.glob_own + slot * plan.slot_own + tile * step
            mask[pl.ds(pl.multiple_of(start, step), step), :] = small * live
            return carry

        lax.fori_loop(0, plan.slot_own // step, slot_step, 0)


def zero_borders(plan, shifted):
    lanes = shifted.shape[2]
    for side in range(2):
        shifted[side, : plan.glob_base, :] = jnp.zeros((plan.glob_base, lanes), BF16)
        shifted[side, plan.glob_base + plan.glob_all : plan.small_base, :] = jnp.zeros(
            (plan.glob_width, lanes), BF16
        )
        for slot in range(plan.slots):
            low = plan.small_base + slot * plan.slot_conv + plan.slot_all
            shifted[side, low : low + plan.small_width, :] = jnp.zeros(
                (plan.small_width, lanes), BF16
            )


def forward_kernel(
    plan,
    live,
    glob_hbm,
    small_hbm,
    kernel_in_hbm,
    kernel_mid_hbm,
    kernel_out_hbm,
    squeeze_hbm,
    excite_hbm,
    gain_one,
    shift_one,
    gain_two,
    shift_two,
    excite_bias,
    squeeze_bias,
    gain_three,
    shift_three,
    x_out,
    pre_one_out,
    act_one_out,
    pre_two_out,
    act_three_out,
    w_mid_out,
    k_out_both,
    w_in_both,
    vec_three,
    vec_three_other,
    mask_hbm,
    w_squeeze_hbm,
    w_excite_hbm,
    vec,
    stats,
    pooled_out,
    excite_out,
    squeeze_pre_out,
    glob,
    small,
    kernel_in,
    taps,
    kernel_out,
    squeeze,
    excite,
    wide,
    table,
    x_all,
    pre_one,
    shifted,
    w_in,
    w_mid,
    w_turned,
    pre_two,
    act_three,
    k_out,
    pay_one,
    slots_one,
    pay_two,
    slots_two,
    squeeze_send,
    squeeze_recv,
    mask,
    w_squeeze,
    w_excite,
    local_sem,
    send_sem,
    recv_sem,
    spread_send,
    spread_recv,
):
    n, half, group, width = plan.dp, plan.half, plan.group, plan.width
    channels, real = plan.channels, plan.half_real
    me, core = lax.axis_index("dp"), lax.axis_index("rows")

    def local(source, target, index):
        copy = pltpu.make_async_copy(source, target, local_sem.at[index])
        copy.start()
        return copy

    load_glob = local(glob_hbm, glob, 0)
    load_small = local(small_hbm, small, 1)
    load_in = local(kernel_in_hbm, kernel_in, 2)
    entry_barrier(n, me, core)

    def partner(source, target, index):
        copy = to_partner(me, core, source, target, send_sem.at[index], recv_sem.at[index])
        copy.start()
        return copy

    load_glob.wait()

    def glob_row(row, carry):
        rows = plan.rows_of(core, row * plan.glob_width, plan.glob_width)
        wide[: plan.glob_side, :channels] = glob[row].astype(F32)
        for side in range(2):
            x_all[side, rows, :] = wide[: plan.glob_width, side * half : (side + 1) * half].astype(BF16)
        return carry

    def small_row(row, carry):
        rows = plan.rows_of(core, plan.glob_own + row * plan.small_width, plan.small_width)
        wide[: plan.small_side, :channels] = small[row].astype(F32)
        for side in range(2):
            x_all[side, rows, :] = wide[: plan.small_width, side * half : (side + 1) * half].astype(
                BF16
            )
        return carry

    def send_piece(index):
        start = (0, plan.glob_own)[index]
        rows = plan.rows_of(core, start, (plan.glob_own, plan.own - plan.glob_own)[index])
        part = x_all.at[:, rows, :]
        return partner(part, part, index)

    wide[...] = jnp.zeros_like(wide)
    lax.fori_loop(0, plan.glob_height, glob_row, 0)
    x_remote = [send_piece(0)]
    load_small.wait()
    wide[...] = jnp.zeros_like(wide)
    lax.fori_loop(0, plan.slots * plan.small_height, small_row, 0)
    x_remote.append(send_piece(1))

    table[...] = jnp.zeros_like(table)
    load_in.wait()
    load_taps = [local(kernel_mid_hbm.at[tap], taps.at[tap], 3 + tap) for tap in range(3)]
    load_out = local(kernel_out_hbm, kernel_out, 6)
    load_squeeze = local(squeeze_hbm, squeeze, 7)
    load_excite = local(excite_hbm, excite, 8)
    for start in range(0, channels, group):
        length = min(group, channels - start)
        table[:length, :real] = kernel_in[start : start + length, :].astype(F32)
        block = group_lanes(table[:group, :], plan)
        if length < group:
            block = jnp.where(row_of(block.shape) < length, block, 0.0)
        low = start % half
        w_in[start // half, low : low + group, :] = block.astype(BF16)
    base = 2
    send_in = partner(w_in, w_in_both.at[core], base)

    live_count = live[0].astype(F32)
    vec[...] = jnp.zeros_like(vec)
    for index, vector in enumerate(
        (gain_one, shift_one, gain_two, shift_two, excite_bias, squeeze_bias)
    ):
        vec[index : index + 1, : vector.shape[0]] = vector[...].astype(F32).reshape(1, -1)
    vec_three[...] = jnp.zeros_like(vec_three)
    for index, vector in enumerate((gain_three, shift_three)):
        vec_three[index : index + 1, : vector.shape[0]] = vector[...].astype(F32).reshape(1, -1)
    raw = vec[...]
    grouped = group_lanes(raw, plan)
    chip_count = jnp.zeros((1, half), F32) + (plan.glob_area + plan.slot_area * live_count)
    row = row_of(raw.shape)
    vec[...] = jnp.where(row == SQUEEZE_BIAS, raw, jnp.where(row == COUNT, chip_count, grouped))
    send_vec = partner(vec_three, vec_three_other, base + 1)
    for owner in range(2):
        fill_mask(plan, mask, owner * plan.own, live_count)

    def product(owner):
        size = plan.own // 2
        for part in range(2):
            rows = plan.rows_of(owner, part * size, size)
            pre_one[rows, :] = dot(x_all[0, rows, :], w_in[0]) + dot(x_all[1, rows, :], w_in[1])

    def prepare_tap(tap):
        load_taps[tap].wait()
        table[:width, :real] = taps[tap % 3].astype(F32)
        block = group_lanes(table[:group, :], plan)
        block = jnp.where(row_of(block.shape) < width, block, 0.0)
        w_mid[tap // 3, tap % 3 * group : (tap % 3 + 1) * group, :] = block.astype(BF16)
        for side in range(2):
            turned = block[:, side * group : (side + 1) * group].T
            w_turned[side, :, tap * group : (tap + 1) * group] = turned.astype(BF16)
        if tap + 3 < 9:
            load_taps.append(local(kernel_mid_hbm.at[tap + 3], taps.at[tap % 3], 3 + tap % 3))

    product(core)
    zero_borders(plan, shifted)
    for copy in x_remote:
        copy.wait()
    product(1 - core)
    saves = [
        local(x_all, x_out, 9),
        local(pre_one, pre_one_out, 10),
        local(mask, mask_hbm, 19),
    ]

    def local_part(values, which, pay):
        total, squares = local_moments(plan, values, mask, which, vec[COUNT : COUNT + 1, :])
        pay[:, :half] = total
        pay[:, half : 2 * half] = squares
        pay[:, 2 * half :] = vec[COUNT : COUNT + 1, :LANE]

    def spread_of(pay, slots, index):
        spread = Spread(n, me, core, pay, slots, spread_send.at[index], spread_recv.at[index])
        spread.start()
        return spread

    local_part(pre_one, "all", pay_one)
    spread = spread_of(pay_one, slots_one, 0)
    for tap in range(9):
        prepare_tap(tap)
    saves.append(local(w_mid, w_mid_out, 11))
    spread.wait()
    mean, variance, count = merge_moments(slots_one, n, half)
    inverse = lax.rsqrt(variance + EPSILON)
    stats[...] = jnp.zeros_like(stats)
    stats[MEAN_ONE : MEAN_ONE + 1, :] = mean
    stats[INVERSE_ONE : INVERSE_ONE + 1, :] = inverse
    stats[TOTAL : TOTAL + 1, :] = count
    scale = inverse * vec[GAIN_ONE : GAIN_ONE + 1, :]
    shift = vec[SHIFT_ONE : SHIFT_ONE + 1, :]

    def activate_one(start, size, place, crop, carry):
        norm = (pre_one[pl.ds(start, size), :] - mean) * scale + shift
        act = norm * sigmoid(norm) * widen(mask[pl.ds(start, size), :], half)
        before = pltpu.roll(act, 1, 0)
        after = pltpu.roll(act, size - 1, 0)
        for tap, value in enumerate((before, act, after)):
            for side in range(2):
                shifted[side, pl.ds(place, size), tap * group : (tap + 1) * group] = value[
                    :, side * group : (side + 1) * group
                ].astype(BF16)
        return carry

    plan.sweep(activate_one, 0)
    for side in range(2):
        saves.append(
            local(
                shifted.at[side, :, group : 2 * group],
                act_one_out.at[:, side * group : (side + 1) * group],
                12 + side,
            )
        )

    for low, length, wide_row in plan.segments():
        for side in range(2):
            lanes = slice(side * group, (side + 1) * group)
            block = length // 2
            for part in range(2):
                at = low + part * block
                windows = [
                    shifted[side, at + shift_row : at + shift_row + block, :]
                    for shift_row in (-wide_row, 0, wide_row)
                ]
                turned = dot_nt(w_turned[side], jnp.concatenate(windows, 1))
                pre_two[at : at + block, lanes] = turned.T
    saves.append(local(pre_two, pre_two_out, 14))

    local_part(pre_two, "conv", pay_two)
    spread = spread_of(pay_two, slots_two, 1)
    load_out.wait()
    for piece in range(4):
        low = piece * width // 16 * 16
        length = min(table.shape[0], channels - low)
        table[:length, :real] = kernel_out[low : low + length, :].astype(F32)
        off = piece * width - low
        block = table[off : off + group, :]
        block = jnp.where(row_of(block.shape) < width, block, 0.0)
        place = piece % 2 * group
        k_out[piece // 2, place : place + group, :] = block.astype(BF16)
    send_out = partner(k_out, k_out_both.at[core], base + 2)
    load_squeeze.wait()
    for piece in range(2):
        low = piece * width // 16 * 16
        length = min(table.shape[0], 2 * width - low)
        table[:length, :width] = squeeze[low : low + length, :].astype(F32)
        off = piece * width - low
        block = table[off : off + group, :group]
        keep = (row_of(block.shape) < width) & (lane_of(block.shape) < width)
        w_squeeze[piece * group : (piece + 1) * group, :] = jnp.where(keep, block, 0.0).astype(BF16)
    load_excite.wait()
    table[:width, :real] = excite[...].astype(F32)
    block = group_lanes(table[:group, :], plan)
    w_excite[...] = jnp.where(row_of(block.shape) < width, block, 0.0).astype(BF16)
    saves.append(local(w_squeeze, w_squeeze_hbm, 20))
    saves.append(local(w_excite, w_excite_hbm, 21))
    spread.wait()
    mean_two, variance, _ = merge_moments(slots_two, n, half)
    inverse_two = lax.rsqrt(variance + EPSILON)
    stats[MEAN_TWO : MEAN_TWO + 1, :] = mean_two
    stats[INVERSE_TWO : INVERSE_TWO + 1, :] = inverse_two
    scale_two = inverse_two * vec[GAIN_TWO : GAIN_TWO + 1, :]
    shift_two = vec[SHIFT_TWO : SHIFT_TWO + 1, :]
    pooled_out[...] = jnp.zeros_like(pooled_out)
    saves[1].wait()
    act_two = pre_one

    def activate_two(start, size, place, crop, carry):
        norm = (pre_two[pl.ds(place, size), :] - mean_two) * scale_two + shift_two
        act = norm * sigmoid(norm) * widen(mask[pl.ds(start, size), :], half)
        act_two[pl.ds(start, size), :] = act
        pooled_out[pl.ds(crop, 1), :] += jnp.sum(act, 0, keepdims=True)
        return carry

    plan.sweep(activate_two, 0)
    pooled_out[:1, :] = pooled_out[:1, :] * (1.0 / plan.glob_area)
    pooled_out[1:, :] = pooled_out[1:, :] * (1.0 / plan.slot_area)
    part = split_dot(pooled_out[...], w_squeeze[...])
    squeeze_send[...] = part
    swap = partner(squeeze_send, squeeze_recv, base + 3)
    swap.wait()
    squeeze_pre = part + squeeze_recv[...] + vec[SQUEEZE_BIAS : SQUEEZE_BIAS + 1, :group]
    squeeze_pre_out[...] = squeeze_pre
    squeezed = squeeze_pre * sigmoid(squeeze_pre)
    excite_out[...] = sigmoid(
        split_dot(squeezed, w_excite[...]) + vec[EXCITE_BIAS : EXCITE_BIAS + 1, :]
    )
    saves.append(local(w_in, w_in_both.at[core], 15))
    saves.append(local(k_out, k_out_both.at[core], 16))

    def activate_three(start, size, place, crop, carry):
        act_three[core, pl.ds(start, size), :] = (
            act_two[pl.ds(start, size), :] * excite_out[pl.ds(crop, 1), :]
        ).astype(BF16)
        return carry

    plan.sweep(activate_three, 0)
    part = act_three.at[core, plan.rows_of(1 - core), :]
    exchange = partner(part, part, base + 4)
    saves.append(local(act_three.at[core], act_three_out.at[core], 17))
    for copy in (send_in, send_vec, send_out, exchange):
        copy.wait()
    part = act_three.at[1 - core, plan.rows_of(core), :]
    saves.append(local(part, act_three_out.at[1 - core, plan.rows_of(core), :], 18))
    for index, copy in enumerate(saves):
        if index != 1:
            copy.wait()


def forward(
    plan, live, glob, small, kernel_in, kernel_mid, kernel_out, squeeze, excite, vectors
):
    n, half, group = plan.dp, plan.half, plan.group
    shape = jax.ShapeDtypeStruct
    pay = 2 * half + LANE
    smem = pl.BlockSpec(memory_space=pltpu.SMEM)
    return pl.pallas_call(
        functools.partial(forward_kernel, plan),
        out_shape=(
            shape((2, plan.all, half), BF16),
            shape((plan.all, half), F32),
            shape((plan.conv, half), BF16),
            shape((plan.conv, half), F32),
            shape((2, plan.all, half), BF16),
            shape((3, 3 * group, half), BF16),
            shape((2, 2, half, half), BF16),
            shape((2, 2, half, half), BF16),
            shape((8, half), F32),
            shape((8, half), F32),
            shape((plan.all, LANE), F32),
            shape((half, group), BF16),
            shape((group, half), BF16),
            shape((8, half), F32),
            shape((8, half), F32),
            shape((plan.slot_rows, half), F32),
            shape((plan.slot_rows, half), F32),
            shape((plan.slot_rows, group), F32),
        ),
        in_specs=[smem] + [ANY] * 7 + [VMEM] * 8,
        out_specs=(ANY,) * 8 + (VMEM,) * 2 + (ANY,) * 3 + (VMEM,) * 5,
        scratch_shapes=[
            pltpu.VMEM(glob.shape, BF16),
            pltpu.VMEM(small.shape, BF16),
            pltpu.VMEM(kernel_in.shape, BF16),
            pltpu.VMEM((3,) + kernel_mid.shape[1:], BF16),
            pltpu.VMEM(kernel_out.shape, BF16),
            pltpu.VMEM(squeeze.shape, BF16),
            pltpu.VMEM(excite.shape, BF16),
            pltpu.VMEM((32, 2 * half), F32),
            pltpu.VMEM((group + 16, half), F32),
            pltpu.VMEM((2, plan.all, half), BF16),
            pltpu.VMEM((plan.all, half), F32),
            pltpu.VMEM((2, plan.conv, 3 * group), BF16),
            pltpu.VMEM((2, half, half), BF16),
            pltpu.VMEM((3, 3 * group, half), BF16),
            pltpu.VMEM((2, group, 9 * group), BF16),
            pltpu.VMEM((plan.conv, half), F32),
            pltpu.VMEM((2, plan.all, half), BF16),
            pltpu.VMEM((2, half, half), BF16),
            pltpu.VMEM((1, pay), F32),
            pltpu.VMEM((n, 1, pay), F32),
            pltpu.VMEM((1, pay), F32),
            pltpu.VMEM((n, 1, pay), F32),
            pltpu.VMEM((plan.slot_rows, group), F32),
            pltpu.VMEM((plan.slot_rows, group), F32),
            pltpu.VMEM((plan.all, LANE), F32),
            pltpu.VMEM((half, group), BF16),
            pltpu.VMEM((group, half), BF16),
            pltpu.SemaphoreType.DMA((22,)),
            pltpu.SemaphoreType.DMA((7,)),
            pltpu.SemaphoreType.DMA((7,)),
            pltpu.SemaphoreType.DMA((2, n)),
            pltpu.SemaphoreType.DMA((2, n)),
        ],
        compiler_params=pltpu.CompilerParams(
            collective_id=0, has_side_effects=True, vmem_limit_bytes=VMEM_BYTES
        ),
    )(live, glob, small, kernel_in, kernel_mid, kernel_out, squeeze, excite, *vectors)


def own_steps(plan, body, carry):
    step = 32

    def run(tile, state):
        return body(pl.multiple_of(tile * step, step), step, state)

    return lax.fori_loop(0, plan.own // step, run, carry)


def merge_two(first, second, lanes):
    sums = [part[:, :lanes] for part in (first, second)]
    squares = [part[:, lanes : 2 * lanes] for part in (first, second)]
    counts = [widen(part[:, 2 * lanes :], lanes) for part in (first, second)]
    total = sums[0] + sums[1]
    count = counts[0] + counts[1]
    mean = total / count
    spread = squares[0] + squares[1]
    for index in range(2):
        gap = sums[index] / counts[index] - mean
        spread = spread + counts[index] * gap * gap
    return total, spread, count


def split_maps(plan, glob, small, target, base, wide):
    half, real = plan.half, plan.half_real
    low = real // LANE * LANE

    def place(source, row, start, size, real_size):
        wide[:real_size, : plan.channels] = source[row].astype(F32)
        rows = pl.ds(pl.multiple_of(base + start, 16), size)
        first = wide[:size, :half]
        target[0, rows, :] = jnp.where(lane_of(first.shape) < real, first, 0.0).astype(BF16)
        second = wide[:size, low:]
        moved = pltpu.roll(second, second.shape[1] - (real - low), 1)
        target[1, rows, :] = moved[:, :half].astype(BF16)

    def glob_row(row, carry):
        place(glob, row, row * plan.glob_width, plan.glob_width, plan.glob_side)
        return carry

    def small_row(row, carry):
        start = plan.glob_own + row * plan.small_width
        place(small, row, start, plan.small_width, plan.small_side)
        return carry

    if glob is not None:
        wide[...] = jnp.zeros_like(wide)
        lax.fori_loop(0, plan.glob_height, glob_row, 0)
    if small is not None:
        wide[...] = jnp.zeros_like(wide)
        lax.fori_loop(0, plan.slots * plan.small_height, small_row, 0)


def gather_sum(slots, n, lanes):
    def add(step, carry):
        return carry + slots[step]

    return lax.fori_loop(0, n, add, jnp.zeros((1, lanes), F32))


ORDERS = {
    "A": ((0, 1, 2, 3), (1, 0, 2, 3)),
    "B": ((0, 2, 1, 3), (1, 2, 0, 3)),
    "P": ((0, 1, 2, 3), (2, 1, 0, 3)),
    "Q": ((2, 0, 1, 3), (1, 0, 2, 3)),
}
HALVINGS = 3
HANDED = 2


class Steps:
    def __init__(self, n, me, core, order):
        bits = n.bit_length() - 1
        self.halvings = min(bits, HALVINGS)
        self.shards = 2**self.halvings
        self.doublings = bits - self.halvings
        self.bit, self.partner = [], []
        chosen = [[bit for bit in one if bit < bits] for one in ORDERS[order]]
        chosen = [one + list(range(len(one), bits)) for one in chosen]
        for step in range(bits):
            first, second = 2 ** chosen[0][step], 2 ** chosen[1][step]
            distance = first + (second - first) * core
            bit = lax.rem(me // distance, 2)
            self.bit.append(bit)
            self.partner.append((me + distance * (1 - 2 * bit), core))


class Chain:
    def __init__(self, steps, work, land, send, recv, free, begun=0, until=None):
        self.steps, self.work, self.land, self.free = steps, work, land, free
        self.send, self.recv = send, recv
        self.rows = work.shape[0]
        self.shard = self.rows // steps.shards
        self.halvings = steps.halvings
        self.reduce_steps = steps.halvings + steps.doublings
        self.begun, self.until = begun, until
        self.pending = None
        self.step, self.at, self.length = begun, 0, self.rows >> begun
        for step in range(begun):
            self.at = self.at + steps.bit[step] * (self.rows >> (step + 1))
        self.land_base = self.rows - self.length
        self.back = None

    def rows_at(self, row, length):
        return pl.ds(row if isinstance(row, int) else pl.multiple_of(row, 16), length)

    def here(self):
        return self.work.at[self.rows_at(self.at, self.length), :]

    def remote(self, source, target, step, slot):
        self.pending = pltpu.make_async_remote_copy(
            src_ref=source,
            dst_ref=target,
            send_sem=self.send.at[slot],
            recv_sem=self.recv.at[slot],
            device_id=self.steps.partner[step],
            device_id_type=MESH,
        )
        self.pending.start()

    def begin_reduce(self):
        step = self.step
        if step < self.halvings:
            length = self.rows >> (step + 1)
            bit = self.steps.bit[step]
            self.keep = self.at + bit * length
            gone = self.at + (1 - bit) * length
            low = self.rows - 2 * length
        else:
            length = self.shard
            self.keep = gone = self.at
            low = self.rows - self.shard + (step - self.halvings) * self.shard
        self.length = length
        self.landed = self.land.at[pl.ds(low - self.land_base, length), :]
        self.remote(self.work.at[self.rows_at(gone, length), :], self.landed, step, step)

    def end_reduce(self):
        self.pending.wait()
        if self.free is not None and self.step < self.halvings:
            pl.semaphore_signal(
                self.free.at[self.step],
                inc=1,
                device_id=self.steps.partner[self.step],
                device_id_type=MESH,
            )
        size = 48 if self.shard % 48 == 0 else 16

        def add(tile, carry):
            there = self.rows_at(self.keep + tile * size, size)
            here = pl.ds(pl.multiple_of(tile * size, 16), size)
            total = self.work[there, :].astype(F32) + self.landed[here, :].astype(F32)
            self.work[there, :] = total.astype(BF16)
            return carry

        lax.fori_loop(0, self.length // size, add, 0)
        self.at = self.keep
        self.step += 1

    def begin_gather(self):
        if self.back >= self.begun:
            pl.semaphore_wait(self.free.at[self.back], 1)
        part = self.here()
        self.remote(part, part, self.back, self.reduce_steps + self.back)

    def end_gather(self):
        self.pending.wait()
        self.at = self.at - self.steps.bit[self.back] * self.length
        self.length *= 2
        self.back -= 1

    def advance(self):
        if self.pending is not None:
            if self.back is None:
                self.end_reduce()
            else:
                self.end_gather()
            self.pending = None
        if self.step == self.until:
            return
        if self.step < self.reduce_steps:
            self.begin_reduce()
            return
        if self.back is None:
            self.back = self.halvings - 1
        if self.back >= 0:
            self.begin_gather()

    def done(self):
        return self.pending is None and (self.step == self.until or self.back == -1)


def land_rows(n, rows, begun=0, until=None):
    bits = n.bit_length() - 1
    halvings = min(bits, HALVINGS)
    last = halvings if until is None else min(until, halvings)
    extra = bits - halvings if until is None else 0
    return (rows >> begun) - (rows >> last) + extra * (rows >> halvings)


def chain_slots(n):
    bits = n.bit_length() - 1
    return bits + min(bits, HALVINGS)


def silu_slope(value, sigma):
    return sigma * (1.0 + value * (1.0 - sigma))
OUTS = 2
MIDS = 6
INS = 4
CHAINS = (
    tuple("out%d" % i for i in range(OUTS))
    + tuple("mid%d" % i for i in range(MIDS))
    + tuple("in%d" % i for i in range(INS))
)
CHAIN_ORDERS = tuple("AAABPQABPQPQ")

SHIFT_TWO_SUM, GAIN_TWO_SUM = range(2)
SHIFT_ONE_SUM, GAIN_ONE_SUM = range(2)


def middle_kernel(
    plan,
    live,
    act_three_hbm,
    k_out_hbm,
    glob_hbm,
    small_hbm,
    glob_cot_hbm,
    small_cot_hbm,
    pre_two_hbm,
    mask_hbm,
    w_squeeze_hbm,
    w_excite_hbm,
    stats,
    vec,
    vec_three_own,
    vec_three_other,
    pooled,
    excite,
    squeeze_pre,
    result_hbm,
    grad_summed_hbm,
    shard_out,
    grad_norm_out,
    slots_ahead,
    slots_behind,
    sums_three_out,
    sums_out,
    result_out,
    grad_summed_out,
    mask,
    w_squeeze,
    w_excite,
    act_three,
    k_out,
    flat,
    flat_two,
    maps,
    pay,
    pair,
    chip,
    slots,
    finals,
    pay_back,
    pair_back,
    chip_back,
    slots_back,
    finals_back,
    vec_three,
    glob,
    small,
    glob_cot,
    small_cot,
    mask_own,
    wide,
    pre_two,
    work,
    land,
    grad_excite,
    squeeze_send,
    squeeze_recv,
    grad_pooled,
    ahead,
    behind,
    pay_two,
    slots_two,
    local_sem,
    send_sem,
    recv_sem,
    spread_send,
    spread_recv,
    reduce_send,
    reduce_recv,
):
    n, half, group = plan.dp, plan.half, plan.group
    me, core = lax.axis_index("dp"), lax.axis_index("rows")
    own = plan.own
    size = own // 2

    def local(source, target, index):
        copy = pltpu.make_async_copy(source, target, local_sem.at[index])
        copy.start()
        return copy

    def partner(source, target, index):
        copy = to_partner(me, core, source, target, send_sem.at[index], recv_sem.at[index])
        copy.start()
        return copy

    load_act = [local(act_three_hbm.at[core], act_three.at[core], 0)]
    mine = act_three.at[1 - core, plan.rows_of(core), :]
    load_act.append(local(act_three_hbm.at[1 - core, plan.rows_of(core), :], mine, 7 + 1 + OUTS))
    load_k = local(k_out_hbm, k_out, 1)
    entry_barrier(n, me, core)
    vec_three[core] = vec_three_own[...]
    vec_three[1 - core] = vec_three_other[...]
    fill_mask(plan, mask_own, 0, live[0].astype(F32))
    own_count = 0.5 * vec[COUNT : COUNT + 1, :]

    def spread_of(source, target, index):
        spread = Spread(n, me, core, source, target, spread_send.at[index], spread_recv.at[index])
        spread.start()
        return spread

    deep = plan.slot_rows
    before = squeeze_pre[...]
    sigma = sigmoid(before)
    squeezed = before * sigma
    ahead[...] = jnp.zeros_like(ahead)
    ahead[:deep, :] = pooled[...].astype(BF16)
    ahead[deep:, :group] = squeezed.astype(BF16)
    ahead_spread = spread_of(ahead, slots_ahead, 3)

    for copy in load_act:
        copy.wait()
    mine = act_three.at[core, plan.rows_of(core), :]
    act_swap = partner(mine, mine, 5)
    load_k.wait()
    raws = [
        local(source, target, 2 + index)
        for index, (source, target) in enumerate(
            (
                (glob_hbm, glob),
                (small_hbm, small),
                (glob_cot_hbm, glob_cot),
                (small_cot_hbm, small_cot),
            )
        )
    ]
    load_two = [
        local(pre_two_hbm, pre_two, 6),
        local(mask_hbm, mask, 11 + OUTS),
        local(w_squeeze_hbm, w_squeeze, 12 + OUTS),
        local(w_excite_hbm, w_excite, 13 + OUTS),
    ]
    for part in range(2):
        rows = plan.rows_of(core, part * size, size)
        for side in range(2):
            low = side * own + part * size
            flat[low : low + size, :] = dot(act_three[0, rows, :], k_out[side, 0]) + dot(
                act_three[1, rows, :], k_out[side, 1]
            )

    for side in range(2):

        def add(row, step, carry, side=side):
            seen = widen(mask_own[pl.ds(row, step), :], half)
            return carry + rows_down(flat[pl.ds(side * own + row, step), :] * seen)

        total = jnp.sum(own_steps(plan, add, jnp.zeros((8, half), F32)), 0, keepdims=True)
        mean = total / own_count

        def spread_out(row, step, carry, side=side, mean=mean):
            seen = widen(mask_own[pl.ds(row, step), :], half)
            gap = (flat[pl.ds(side * own + row, step), :] - mean) * seen
            return carry + rows_down(gap * gap)

        squares = jnp.sum(own_steps(plan, spread_out, jnp.zeros((8, half), F32)), 0, keepdims=True)
        pay[side, :, :half] = total
        pay[side, :, half : 2 * half] = squares
        pay[side, :, 2 * half :] = own_count[:, :LANE]
    partner(pay.at[1 - core], pair, 0).wait()
    total, squares, count = merge_two(pay[core], pair[...], half)
    chip[:, :half] = total
    chip[:, half : 2 * half] = squares
    chip[:, 2 * half :] = count[:, :LANE]
    exchange = spread_of(chip, slots, 0)
    for copy in raws:
        copy.wait()
    split_maps(plan, glob, small, maps, 0, wide)
    split_maps(plan, glob_cot, None, maps, own, wide)
    exchange.wait()
    mean, variance, full_count = merge_moments(slots, n, half)
    finals[core, :, :half] = mean
    finals[core, :, half:] = lax.rsqrt(variance + EPSILON)
    swap = partner(finals.at[core], finals.at[core], 1)
    split_maps(plan, None, small_cot, maps, own, wide)
    swap.wait()

    for side in range(2):
        mean = finals[side, :, :half]
        inverse = finals[side, :, half:]
        gain = vec_three[side, :1, :]
        shift = vec_three[side, 1:2, :]

        def outer(row, step, carry, side=side, mean=mean, inverse=inverse, gain=gain, shift=shift):
            rows = pl.ds(row, step)
            low = pl.ds(side * own + row, step)
            seen = widen(mask_own[rows, :], half)
            normed = (flat[low, :] - mean) * inverse
            summed = normed * gain + shift + maps[side, rows, :].astype(F32)
            sigma = sigmoid(summed)
            result_out[side, rows, :] = (seen * summed * sigma).astype(BF16)
            slope = sigma * (1.0 + summed * (1.0 - sigma))
            cot = maps[side, pl.ds(pl.multiple_of(own + row, 16), step), :]
            grad = cot.astype(F32) * seen * slope
            flat_two[low, :] = grad
            grad_summed_out[side, rows, :] = grad.astype(BF16)
            return carry[0] + rows_down(grad), carry[1] + rows_down(grad * normed)

        zero = jnp.zeros((8, half), F32)
        shift_sum, gain_sum = own_steps(plan, outer, (zero, zero))
        pay_back[side, :, :half] = jnp.sum(shift_sum, 0, keepdims=True)
        pay_back[side, :, half:] = jnp.sum(gain_sum, 0, keepdims=True)
    saves = [
        local(result_out, result_hbm, 9 + OUTS),
        local(grad_summed_out, grad_summed_hbm, 10 + OUTS),
    ]
    partner(pay_back.at[1 - core], pair_back, 2).wait()
    chip_back[...] = pay_back[core] + pair_back[...]
    spread_of(chip_back, slots_back, 1).wait()
    finals_back[core] = gather_sum(slots_back, n, 2 * half)
    partner(finals_back.at[core], finals_back.at[core], 3).wait()

    grad_pre_three = maps
    swaps = []
    for side in range(2):
        mean = finals[side, :, :half]
        inverse = finals[side, :, half:]
        shift_sum = finals_back[side, :, :half]
        gain_sum = finals_back[side, :, half:]
        sums_three_out[side] = jnp.concatenate([shift_sum, gain_sum, jnp.zeros((6, half), F32)], 0)
        scale = vec_three[side, :1, :] * inverse
        shift_mean = shift_sum / full_count
        gain_mean = gain_sum / full_count * inverse

        def inner(
            row, step, carry, side=side, mean=mean, scale=scale, shift_mean=shift_mean,
            gain_mean=gain_mean
        ):
            low = pl.ds(side * own + row, step)
            seen = widen(mask_own[pl.ds(row, step), :], half)
            centered = flat[low, :] - mean
            grad = scale * (flat_two[low, :] - shift_mean - centered * gain_mean)
            grad_pre_three[side, plan.rows_of(core, row, step), :] = (grad * seen).astype(BF16)
            return carry

        own_steps(plan, inner, 0)
        part = grad_pre_three.at[side, plan.rows_of(core), :]
        swaps.append(partner(part, part, 6 + side))

    grad_act = flat

    def product(owner):
        for part in range(2):
            rows = plan.rows_of(owner, part * size, size)
            grad_act[rows, :] = dot_nt(grad_pre_three[0, rows, :], k_out[0, core]) + dot_nt(
                grad_pre_three[1, rows, :], k_out[1, core]
            )

    product(core)
    for swap in swaps + [act_swap]:
        swap.wait()
    chains, span = [], 2 * half // OUTS
    for side in range(2):
        for part in range(2):
            lanes = slice(part * group, (part + 1) * group)
            low = side * half + part * group
            work[low : low + group, :] = dot_tn(
                act_three[side, :, lanes], grad_pre_three[core]
            ).astype(BF16)
            if (low + group) % span == 0:
                index = low // span
                chain = Chain(
                    Steps(n, me, core, CHAIN_ORDERS[index]), work.at[pl.ds(index * span, span), :],
                    land.at[index], reduce_send.at[index], reduce_recv.at[index], None, until=HANDED
                )
                chain.advance()
                chains.append(chain)
    product(1 - core)
    for copy in load_two:
        copy.wait()

    mean = stats[MEAN_TWO : MEAN_TWO + 1, :]
    inverse = stats[INVERSE_TWO : INVERSE_TWO + 1, :]
    count = stats[TOTAL : TOTAL + 1, :]
    gain = vec[GAIN_TWO : GAIN_TWO + 1, :]
    shift = vec[SHIFT_TWO : SHIFT_TWO + 1, :]
    slopes = flat_two
    grad_excite[...] = jnp.zeros_like(grad_excite)

    def excitation(start, size, place, crop, carry):
        rows = pl.ds(start, size)
        norm = (pre_two[pl.ds(place, size), :] - mean) * (inverse * gain) + shift
        sigma = sigmoid(norm)
        seen = widen(mask[rows, :], half)
        slopes[rows, :] = silu_slope(norm, sigma) * seen
        term = grad_act[rows, :] * (norm * sigma * seen)
        grad_excite[pl.ds(crop, 1), :] += jnp.sum(term, 0, keepdims=True)
        return carry

    plan.sweep(excitation, 0)
    level = excite[...]
    grad_excite_pre = grad_excite[...] * level * (1.0 - level)
    part = split_dot(grad_excite_pre, w_excite[...], nt=True)
    squeeze_send[...] = part
    swap = partner(squeeze_send, squeeze_recv, 4)
    swap.wait()
    grad_squeeze_pre = (part + squeeze_recv[...]) * silu_slope(before, sigma)
    back = split_dot(grad_squeeze_pre, w_squeeze[...], nt=True)
    crop_row = lax.broadcasted_iota(jnp.int32, back.shape, 0)
    area = jnp.where(crop_row == 0, 1.0 / plan.glob_area, 1.0 / plan.slot_area)
    grad_pooled[...] = back * area
    behind[...] = jnp.zeros_like(behind)
    behind[:deep, :] = grad_excite_pre.astype(BF16)
    behind[deep:, :group] = grad_squeeze_pre.astype(BF16)

    def gradient(start, size, place, crop, carry):
        rows = pl.ds(start, size)
        incoming = grad_act[rows, :] * excite[pl.ds(crop, 1), :] + grad_pooled[pl.ds(crop, 1), :]
        grad = incoming * slopes[rows, :]
        grad_act[rows, :] = grad
        normed = (pre_two[pl.ds(place, size), :] - mean) * inverse
        return carry[0] + rows_down(grad), carry[1] + rows_down(grad * normed)

    zero = jnp.zeros((8, half), F32)
    shift_sum, gain_sum = plan.sweep(gradient, (zero, zero))
    saves.append(local(grad_act, grad_norm_out, 7))
    pay_two[:, :half] = jnp.sum(shift_sum, 0, keepdims=True)
    pay_two[:, half:] = jnp.sum(gain_sum, 0, keepdims=True)
    spread = spread_of(pay_two, slots_two, 2)
    behind_spread = spread_of(behind, slots_behind, 4)
    for chain in chains:
        chain.advance()
    ahead_spread.wait()
    spread.wait()
    totals = gather_sum(slots_two, n, 2 * half)
    stores = []
    for index, chain in enumerate(chains):
        while not chain.done():
            chain.advance()
        stores.append(local(chain.here(), shard_out.at[index], 8 + index))
    sums_out[...] = jnp.zeros_like(sums_out)
    sums_out[SHIFT_TWO_SUM : SHIFT_TWO_SUM + 1, :] = totals[:, :half]
    sums_out[GAIN_TWO_SUM : GAIN_TWO_SUM + 1, :] = totals[:, half:]
    behind_spread.wait()
    for copy in saves + stores:
        copy.wait()


def middle(
    plan, live, act_three, k_out, glob, small, glob_cot, small_cot, pre_two, stats, vec, vec_three,
    vec_three_other, mask, pooled, excite, squeeze_pre, w_squeeze, w_excite
):
    n, half, group = plan.dp, plan.half, plan.group
    shape = jax.ShapeDtypeStruct
    pay = 2 * half + LANE
    own = (2, plan.own, half)
    rows = 2 * half
    deep = plan.slot_rows
    return pl.pallas_call(
        functools.partial(middle_kernel, plan),
        out_shape=(
            shape(own, BF16),
            shape(own, BF16),
            shape((OUTS, rows // OUTS >> HANDED, half), BF16),
            shape((plan.all, half), F32),
            shape((n, 2 * deep, half), BF16),
            shape((n, 2 * deep, half), BF16),
            shape((2, 8, half), F32),
            shape((8, half), F32),
        ),
        in_specs=[pl.BlockSpec(memory_space=pltpu.SMEM)] + [ANY] * 10 + [VMEM] * 7,
        out_specs=(ANY, ANY, ANY, ANY, VMEM, VMEM, VMEM, VMEM),
        scratch_shapes=[
            pltpu.VMEM(own, BF16),
            pltpu.VMEM(own, BF16),
            pltpu.VMEM(mask.shape, F32),
            pltpu.VMEM(w_squeeze.shape, BF16),
            pltpu.VMEM(w_excite.shape, BF16),
            pltpu.VMEM((2, plan.all, half), BF16),
            pltpu.VMEM(k_out.shape, BF16),
            pltpu.VMEM((plan.all, half), F32),
            pltpu.VMEM((plan.all, half), F32),
            pltpu.VMEM((2, plan.all, half), BF16),
            pltpu.VMEM((2, 1, pay), F32),
            pltpu.VMEM((1, pay), F32),
            pltpu.VMEM((1, pay), F32),
            pltpu.VMEM((n, 1, pay), F32),
            pltpu.VMEM((2, 1, 2 * half), F32),
            pltpu.VMEM((2, 1, 2 * half), F32),
            pltpu.VMEM((1, 2 * half), F32),
            pltpu.VMEM((1, 2 * half), F32),
            pltpu.VMEM((n, 1, 2 * half), F32),
            pltpu.VMEM((2, 1, 2 * half), F32),
            pltpu.VMEM((2,) + vec_three.shape, F32),
            pltpu.VMEM(glob.shape, BF16),
            pltpu.VMEM(small.shape, BF16),
            pltpu.VMEM(glob.shape, BF16),
            pltpu.VMEM(small.shape, BF16),
            pltpu.VMEM((plan.own, LANE), F32),
            pltpu.VMEM((32, 2 * half), F32),
            pltpu.VMEM((plan.conv, half), F32),
            pltpu.VMEM((rows, half), BF16),
            pltpu.VMEM((OUTS, land_rows(n, rows // OUTS, until=HANDED), half), BF16),
            pltpu.VMEM((deep, half), F32),
            pltpu.VMEM((deep, group), F32),
            pltpu.VMEM((deep, group), F32),
            pltpu.VMEM((deep, half), F32),
            pltpu.VMEM((2 * deep, half), BF16),
            pltpu.VMEM((2 * deep, half), BF16),
            pltpu.VMEM((1, 2 * half), F32),
            pltpu.VMEM((n, 1, 2 * half), F32),
            pltpu.SemaphoreType.DMA((14 + OUTS,)),
            pltpu.SemaphoreType.DMA((8,)),
            pltpu.SemaphoreType.DMA((8,)),
            pltpu.SemaphoreType.DMA((5, n)),
            pltpu.SemaphoreType.DMA((5, n)),
            pltpu.SemaphoreType.DMA((OUTS, HANDED)),
            pltpu.SemaphoreType.DMA((OUTS, HANDED)),
        ],
        compiler_params=pltpu.CompilerParams(
            collective_id=1, has_side_effects=True, vmem_limit_bytes=VMEM_BYTES
        ),
    )(
        live, act_three, k_out, glob, small, glob_cot, small_cot, pre_two, mask, w_squeeze, w_excite,
        stats, vec, vec_three, vec_three_other, pooled, excite, squeeze_pre
    )


SCHEDULE = (
    "two", "M0", "out1", "M1", "M2", "mid0", "M3", "M4", "C0", "out1", "C1", "mid0", "out0",
    "M5", "mid1", "C2", "C3", "out1", "C4", "out0", "mid0", "mid3", "mid4", "mid2", "mid5",
    "out1", "C5", "C6", "C7", "mid3", "sums", "mid0", "mid4", "out0", "mid2", "mid5", "mid3",
    "mid0", "mid1", "one", "K0", "K1", "mid5", "mid0", "X0", "mid1", "mid2", "in0", "K2",
    "in1", "K3", "mid3", "mid4", "out0", "mid1", "in2", "mid2", "in1", "mid1", "in0", "in3",
    "mid3", "mid2", "in1", "mid4", "mid1", "in2", "mid5", "in0", "in1", "in3", "mid4", "in2",
    "mid2", "in3", "out1", "in1", "in0", "in2", "mid3", "mid4", "mid0", "in3", "in2", "X1",
    "mid5", "mid1", "in0", "out0", "in3", "in1", "in2", "mid5", "mid3", "in0", "in3", "X2",
    "X3", "mid2", "in2", "in1", "mid5", "mid4", "in3", "in0",
)


def first_kernel(
    plan,
    shard_out_hbm,
    grad_norm_hbm,
    pre_two_hbm,
    pre_one_hbm,
    act_one_hbm,
    x_hbm,
    w_mid_hbm,
    w_in_hbm,
    mask_hbm,
    stats,
    vec,
    sums_two,
    gathered_out,
    gathered_mid,
    gathered_in,
    grad_inputs_out,
    sums_out,
    mask,
    flat,
    conv_rows,
    shifted,
    act_one,
    w_mid,
    grad_pre_one,
    grad_other,
    w_in,
    work_out,
    land_out,
    work_mid,
    land_mid,
    work_in,
    land_in,
    pay,
    slots,
    local_sem,
    pair_send,
    pair_recv,
    spread_send,
    spread_recv,
    chain_send,
    chain_recv,
    free,
):
    n, half, group = plan.dp, plan.half, plan.group
    me, core = lax.axis_index("dp"), lax.axis_index("rows")

    def local(source, target, index):
        copy = pltpu.make_async_copy(source, target, local_sem.at[index])
        copy.start()
        return copy

    waits = {
        "norm": local(grad_norm_hbm, flat, 0),
        "two": local(pre_two_hbm, conv_rows, 1),
        "mask": local(mask_hbm, mask, 2),
    }
    chains, targets, saves, state = {}, {}, {}, {}

    def begin(name, work, land, target, begun=0):
        index = CHAINS.index(name)
        steps = Steps(n, me, core, CHAIN_ORDERS[index])
        chains[name] = Chain(
            steps, work, land, chain_send.at[index], chain_recv.at[index], free.at[index], begun
        )
        targets[name] = target
        return chains[name]

    def advance(name):
        chain = chains[name]
        if name in saves:
            return
        chain.advance()
        if chain.done():
            index = CHAINS.index(name)
            saves[name] = local(chain.work, targets[name], 8 + index)

    outs = CHAINS[:OUTS]
    loads = []
    for index, name in enumerate(outs):
        rows = pl.ds(index * (2 * half // OUTS), 2 * half // OUTS)
        out = begin(
            name, work_out.at[rows, :], land_out.at[index], gathered_out.at[rows, :], HANDED
        )
        loads.append(local(shard_out_hbm.at[index], out.here(), 8 + index))
    entry_barrier(n, me, core)
    for name, load in zip(outs, loads):
        load.wait()
        advance(name)
    count = stats[TOTAL : TOTAL + 1, :]

    def norm_two():
        zero_borders(plan, shifted)
        mean = stats[MEAN_TWO : MEAN_TWO + 1, :]
        inverse = stats[INVERSE_TWO : INVERSE_TWO + 1, :]
        scale = vec[GAIN_TWO : GAIN_TWO + 1, :] * inverse
        shift_mean = sums_two[SHIFT_TWO_SUM : SHIFT_TWO_SUM + 1, :] / count
        gain_mean = sums_two[GAIN_TWO_SUM : GAIN_TWO_SUM + 1, :] / count * inverse
        for name in ("norm", "two", "mask"):
            waits[name].wait()
        waits["act"] = local(act_one_hbm, act_one, 3)
        waits["mid"] = local(w_mid_hbm, w_mid, 4)
        waits["in"] = local(w_in_hbm, w_in, 5)

        def into_two(start, size, place, crop, carry):
            rows = pl.ds(start, size)
            centered = conv_rows[pl.ds(place, size), :] - mean
            grad = scale * (flat[rows, :] - shift_mean - centered * gain_mean)
            grad = grad * widen(mask[rows, :], half)
            after = pltpu.roll(grad, size - 1, 0)
            before = pltpu.roll(grad, 1, 0)
            for tap, value in enumerate((after, grad, before)):
                for side in range(2):
                    shifted[side, pl.ds(place, size), tap * group : (tap + 1) * group] = value[
                        :, side * group : (side + 1) * group
                    ].astype(BF16)
            return carry

        plan.sweep(into_two, 0)
        waits["one"] = local(pre_one_hbm, flat, 0)
        waits["act"].wait()

    def mid(index):
        tap = index * 3 // MIDS
        sides = range(2) if MIDS == 3 else (index % 2,)
        for side in sides:
            lanes = slice(side * group, (side + 1) * group)
            total = None
            for low, length, width in plan.segments():
                first = low - (tap - 1) * width
                term = dot_tn(
                    act_one[low : low + length, lanes], shifted[side, first : first + length, :]
                )
                total = term if total is None else total + term
            work_mid[tap, lanes, :] = total.astype(BF16)
        name = CHAINS[OUTS + index]
        rows = pl.ds(sides[0] * group, len(sides) * group)
        begin(name, work_mid.at[tap, rows, :], land_mid.at[index], gathered_mid.at[tap, rows, :])
        advance(name)
        read_shifted()

    def read_shifted():
        state["reads"] = state.get("reads", 0) + 1
        if state["reads"] == MIDS + 8:
            waits["x"] = local(x_hbm, shifted.at[:, pl.ds(0, plan.all), pl.ds(0, half)], 7)

    def conv(index):
        if index == 0:
            waits["mid"].wait()
        low, length, width = plan.segments()[index // 4]
        block = length // 2
        side = index // 2 % 2
        at = low + index % 2 * block
        lanes = slice(side * group, (side + 1) * group)
        weights = [
            w_mid[tap, column * group : (column + 1) * group, lanes]
            for tap in range(3)
            for column in range(3)
        ]
        windows = [
            shifted[side, at + shift_row : at + shift_row + block, :]
            for shift_row in (width, 0, -width)
        ]
        turned = dot_nt(jnp.concatenate(weights, 1), jnp.concatenate(windows, 1))
        conv_rows[at : at + block, lanes] = turned.T
        read_shifted()

    mean = stats[MEAN_ONE : MEAN_ONE + 1, :]
    inverse = stats[INVERSE_ONE : INVERSE_ONE + 1, :]
    gain = vec[GAIN_ONE : GAIN_ONE + 1, :]
    shift = vec[SHIFT_ONE : SHIFT_ONE + 1, :]
    spread = Spread(n, me, core, pay, slots, spread_send, spread_recv)

    def sums_one():
        waits["one"].wait()

        def gradient(start, size, place, crop, carry):
            rows = pl.ds(start, size)
            normed = (flat[rows, :] - mean) * inverse
            norm = normed * gain + shift
            sigma = sigmoid(norm)
            grad = conv_rows[pl.ds(place, size), :] * silu_slope(norm, sigma)
            grad = grad * widen(mask[rows, :], half)
            conv_rows[pl.ds(place, size), :] = grad
            return carry[0] + rows_down(grad), carry[1] + rows_down(grad * normed)

        zero = jnp.zeros((8, half), F32)
        shift_sum, gain_sum = plan.sweep(gradient, (zero, zero))
        pay[:, :half] = jnp.sum(shift_sum, 0, keepdims=True)
        pay[:, half:] = jnp.sum(gain_sum, 0, keepdims=True)
        spread.start()

    def norm_one():
        spread.wait()
        totals = gather_sum(slots, n, 2 * half)
        sums_out[...] = jnp.zeros_like(sums_out)
        sums_out[SHIFT_ONE_SUM : SHIFT_ONE_SUM + 1, :] = totals[:, :half]
        sums_out[GAIN_ONE_SUM : GAIN_ONE_SUM + 1, :] = totals[:, half:]
        scale = gain * inverse
        shift_mean = totals[:, :half] / count
        gain_mean = totals[:, half:] / count * inverse

        def into_one(start, size, place, crop, carry):
            rows = pl.ds(start, size)
            centered = flat[rows, :] - mean
            grad = scale * (conv_rows[pl.ds(place, size), :] - shift_mean - centered * gain_mean)
            grad_pre_one[rows, :] = (grad * widen(mask[rows, :], half)).astype(BF16)
            return carry

        plan.sweep(into_one, 0)
        state["swap"] = to_partner(
            me, core, grad_pre_one.at[plan.rows_of(1 - core), :], grad_other, pair_send, pair_recv
        )
        state["swap"].start()

    def kernel_in(index):
        if index == 0:
            waits["x"].wait()
        size = 2 * half // INS
        side, start = index * size // half, index * size % half
        for low in range(start, start + size, group):
            work_in[side, low : low + group, :] = dot_tn(
                shifted[side, : plan.all, low : low + group], grad_pre_one[...]
            ).astype(BF16)
        name = CHAINS[OUTS + MIDS + index]
        rows = pl.ds(start, size)
        begin(name, work_in.at[side, rows, :], land_in.at[index], gathered_in.at[side, rows, :])
        advance(name)

    def inputs(index):
        if index == 0:
            waits["in"].wait()
            state["swap"].wait()
        part, side = index // 2, index % 2
        size = plan.own // 2
        rows = slice(part * size, (part + 1) * size)
        own = grad_pre_one[plan.rows_of(core, part * size, size), :]
        low = side * plan.own + part * size
        act_one[low : low + size, :] = (
            dot_nt(own, w_in[core, side]) + dot_nt(grad_other[rows, :], w_in[1 - core, side])
        ).astype(BF16)
        if part == 1:
            waits["result%d" % side] = local(
                act_one.at[pl.ds(side * plan.own, plan.own), :],
                grad_inputs_out.at[side],
                8 + len(CHAINS) + side,
            )

    blocks = {
        "two": norm_two,
        "sums": sums_one,
        "one": norm_one,
    }
    for index in range(MIDS):
        blocks["M%d" % index] = functools.partial(mid, index)
    for index in range(8):
        blocks["C%d" % index] = functools.partial(conv, index)
    for index in range(INS):
        blocks["K%d" % index] = functools.partial(kernel_in, index)
    for index in range(4):
        blocks["X%d" % index] = functools.partial(inputs, index)
    for item in SCHEDULE:
        if item in blocks:
            blocks[item]()
        else:
            advance(item)
    while len(saves) < len(CHAINS):
        for name in CHAINS:
            advance(name)
    for name in CHAINS:
        saves[name].wait()
    for side in range(2):
        waits["result%d" % side].wait()


def first(
    plan, shard_out, grad_norm, pre_two, pre_one, act_one, x_all, w_mid, w_in, stats, vec,
    sums_two, mask
):
    n, half, group = plan.dp, plan.half, plan.group
    shape = jax.ShapeDtypeStruct
    return pl.pallas_call(
        functools.partial(first_kernel, plan),
        out_shape=(
            shape((2 * half, half), BF16),
            shape((3, half, 3 * group), BF16),
            shape((2, half, half), BF16),
            shape((2, plan.own, half), BF16),
            shape((8, half), F32),
        ),
        in_specs=[ANY] * 9 + [VMEM] * 3,
        out_specs=(ANY, ANY, ANY, ANY, VMEM),
        scratch_shapes=[
            pltpu.VMEM(mask.shape, F32),
            pltpu.VMEM((plan.all, half), F32),
            pltpu.VMEM((plan.conv, half), F32),
            pltpu.VMEM((2, plan.conv, 3 * group), BF16),
            pltpu.VMEM((plan.conv, half), BF16),
            pltpu.VMEM(w_mid.shape, BF16),
            pltpu.VMEM((plan.all, half), BF16),
            pltpu.VMEM((plan.own, half), BF16),
            pltpu.VMEM(w_in.shape, BF16),
            pltpu.VMEM((2 * half, half), BF16),
            pltpu.VMEM((OUTS, land_rows(n, 2 * half // OUTS, begun=HANDED), half), BF16),
            pltpu.VMEM((3, half, 3 * group), BF16),
            pltpu.VMEM((MIDS, land_rows(n, 3 * half // MIDS), 3 * group), BF16),
            pltpu.VMEM((2, half, half), BF16),
            pltpu.VMEM((INS, land_rows(n, 2 * half // INS), half), BF16),
            pltpu.VMEM((1, 2 * half), F32),
            pltpu.VMEM((n, 1, 2 * half), F32),
            pltpu.SemaphoreType.DMA((10 + len(CHAINS),)),
            pltpu.SemaphoreType.DMA,
            pltpu.SemaphoreType.DMA,
            pltpu.SemaphoreType.DMA((n,)),
            pltpu.SemaphoreType.DMA((n,)),
            pltpu.SemaphoreType.DMA((len(CHAINS), chain_slots(n))),
            pltpu.SemaphoreType.DMA((len(CHAINS), chain_slots(n))),
            pltpu.SemaphoreType.REGULAR((len(CHAINS), HALVINGS)),
        ],
        compiler_params=pltpu.CompilerParams(
            collective_id=2, has_side_effects=True, vmem_limit_bytes=VMEM_BYTES
        ),
    )(
        shard_out, grad_norm, pre_two, pre_one, act_one, x_all, w_mid, w_in, mask, stats, vec,
        sums_two
    )


def join_lanes(low, high, real):
    zeros = jnp.zeros_like(low)
    wide = jnp.concatenate([low, zeros], 1)
    moved = pltpu.roll(jnp.concatenate([high, zeros], 1), real, 1)
    lane = lax.broadcasted_iota(jnp.int32, wide.shape, 1)
    return jnp.where(lane < real, wide, moved)


def finish_kernel(
    plan,
    result_hbm,
    grad_summed_hbm,
    grad_inputs_hbm,
    out_hbm,
    in_hbm,
    mid_hbm,
    slots_ahead,
    slots_behind,
    sums_one,
    sums_two,
    sums_three,
    glob_out_hbm,
    small_out_hbm,
    glob_grad_hbm,
    small_grad_hbm,
    kernel_in_hbm,
    kernel_mid_hbm,
    kernel_out_hbm,
    squeeze_hbm,
    squeeze_bias,
    excite_hbm,
    excite_bias,
    gain_one,
    shift_one,
    gain_two,
    shift_two,
    gain_three,
    shift_three,
    result,
    grad_summed,
    grad_inputs,
    packed_out,
    packed_in,
    packed_mid,
    glob_out,
    small_out,
    glob_grad,
    small_grad,
    kernel_in,
    kernel_mid,
    kernel_out,
    squeeze_out,
    excite_out,
    load_sem,
    store_sem,
):
    half, group, width, real = plan.half, plan.group, plan.width, plan.half_real
    sources = [(mid_hbm.at[tap], packed_mid.at[tap]) for tap in range(3)] + [
        (out_hbm, packed_out),
        (in_hbm, packed_in),
        (result_hbm, result),
        (grad_summed_hbm, grad_summed),
        (grad_inputs_hbm, grad_inputs),
    ]
    loads, stores = [], []

    for source, target in sources:
        copy = pltpu.make_async_copy(source, target, load_sem.at[len(loads)])
        copy.start()
        loads.append(copy)

    def loaded(index):
        loads[index].wait()

    def store(source, target):
        copy = pltpu.make_async_copy(source, target, store_sem.at[len(stores)])
        copy.start()
        stores.append(copy)

    for row_tap in range(3):
        loaded(row_tap)
        for tap in range(3):
            lanes = slice(tap * group, (tap + 1) * group)
            low = packed_mid[row_tap, :group, lanes].astype(F32)
            high = packed_mid[row_tap, group:, lanes].astype(F32)
            kernel_mid[row_tap, tap] = join_lanes(low, high, width)[:width, :real]
        store(kernel_mid.at[row_tap], kernel_mid_hbm.at[row_tap])
    loaded(3)
    for piece in range(4):
        kernel_out[piece * width : (piece + 1) * width, :] = packed_out[
            piece * group : piece * group + width, :real
        ].astype(F32)
    store(kernel_out, kernel_out_hbm)
    loaded(4)
    for side in range(2):
        rows = min(half, plan.channels - side * half)
        low = packed_in[side, :rows, :group].astype(F32)
        high = packed_in[side, :rows, group:].astype(F32)
        kernel_in[side * half : side * half + rows, :] = join_lanes(low, high, width)[:, :real]
    store(kernel_in, kernel_in_hbm)

    def maps(value, glob, small):
        def glob_row(row, carry):
            rows = pl.ds(pl.multiple_of(row * plan.glob_width, 16), plan.glob_width)
            glob[row, :, 0, :] = value(rows)[: plan.glob_side, : plan.channels]
            return carry

        def small_row(row, carry):
            place = plan.glob_own + row * plan.small_width
            rows = pl.ds(pl.multiple_of(place, 16), plan.small_width)
            small[row] = value(rows)[: plan.small_side, : plan.channels]
            return carry

        lax.fori_loop(0, plan.glob_height, glob_row, 0)
        lax.fori_loop(0, plan.slots * plan.small_height, small_row, 0)

    loaded(5)
    def joined(array, rows):
        return join_lanes(array[0, rows, :].astype(F32), array[1, rows, :].astype(F32), real)

    maps(lambda rows: joined(result, rows), glob_out, small_out)
    store(glob_out, glob_out_hbm)
    store(small_out, small_out_hbm)
    n, deep = plan.dp, plan.slot_rows

    def crops(slots, low, lanes):
        rows = slots[...].astype(F32)[:, low : low + deep, :lanes]
        return rows.reshape(n * deep, lanes)

    wide_pooled, squeezed = crops(slots_ahead, 0, half), crops(slots_ahead, deep, group)
    grad_excite, grad_squeeze = crops(slots_behind, 0, half), crops(slots_behind, deep, group)
    excite = dot_tn(squeezed.astype(BF16), grad_excite.astype(BF16))
    squeeze = dot_tn(wide_pooled.astype(BF16), grad_squeeze.astype(BF16))
    squeeze_out[:width, :] = squeeze[:width, :width]
    squeeze_out[width:, :] = squeeze[group : group + width, :width]
    excite_out[...] = join_lanes(excite[:, :group], excite[:, group:], width)[:width, :real]
    bias = jnp.sum(grad_excite, 0, keepdims=True)
    bias = join_lanes(bias[:, :group], bias[:, group:], width)
    store(squeeze_out, squeeze_hbm)
    store(excite_out, excite_hbm)
    loaded(6)
    loaded(7)
    maps(
        lambda rows: joined(grad_summed, rows)
        + jnp.concatenate([grad_inputs[0, rows, :], grad_inputs[1, rows, :]], 1).astype(F32),
        glob_grad,
        small_grad,
    )
    store(glob_grad, glob_grad_hbm)
    store(small_grad, small_grad_hbm)
    two = join_lanes(sums_two[:, :group], sums_two[:, group:], width)
    one = join_lanes(sums_one[:, :group], sums_one[:, group:], width)
    three = sums_three[lax.axis_index("rows")]
    squeeze_bias[...] = jnp.sum(grad_squeeze, 0)[:width]
    excite_bias[...] = bias[0, :real]
    gain_one[...] = one[GAIN_ONE_SUM, :real]
    shift_one[...] = one[SHIFT_ONE_SUM, :real]
    gain_two[...] = two[GAIN_TWO_SUM, :real]
    shift_two[...] = two[SHIFT_TWO_SUM, :real]
    gain_three[...] = three[1, :real]
    shift_three[...] = three[0, :real]
    for copy in stores:
        copy.wait()


def finish(
    plan, result, grad_summed, grad_inputs, gathered_out, gathered_in, gathered_mid, slots_ahead,
    slots_behind, sums_one, sums_two, sums_three
):
    shape = jax.ShapeDtypeStruct
    width, real, channels = plan.width, plan.half_real, plan.channels
    glob = (plan.glob_height, plan.glob_side, 1, channels)
    small = (plan.slots * plan.small_height, plan.small_side, channels)
    outs = (glob, small, glob, small, (channels, real), (3, 3, width, real), (channels, real))
    ins = (gathered_mid, gathered_out, gathered_in, result, grad_summed, grad_inputs)
    loaded = (result, grad_summed, grad_inputs, gathered_out, gathered_in, gathered_mid)
    return pl.pallas_call(
        functools.partial(finish_kernel, plan),
        out_shape=tuple(shape(out, F32) for out in outs)
        + (shape((real, width), F32), shape((width,), F32), shape((width, real), F32))
        + (shape((real,), F32),) * 7,
        in_specs=[ANY] * 6 + [VMEM] * 5,
        out_specs=(ANY,) * 8 + (VMEM, ANY) + (VMEM,) * 7,
        scratch_shapes=[pltpu.VMEM(array.shape, BF16) for array in loaded]
        + [pltpu.VMEM(out, F32) for out in outs + ((real, width), (width, real))]
        + [pltpu.SemaphoreType.DMA((8,)), pltpu.SemaphoreType.DMA((11,))],
        compiler_params=pltpu.CompilerParams(vmem_limit_bytes=VMEM_BYTES),
    )(
        result, grad_summed, grad_inputs, gathered_out, gathered_in, gathered_mid, slots_ahead,
        slots_behind, sums_one, sums_two, sums_three
    )


def per_device(
    glob_in,
    small_in,
    small_count,
    kernel_in,
    kernel_mid,
    kernel_out,
    squeeze_weight,
    squeeze_bias,
    excite_weight,
    excite_bias,
    gain_first,
    shift_first,
    gain_second,
    shift_second,
    gain_third,
    shift_third,
    glob_cotangent,
    small_cotangent,
):
    plan = Plan(glob_in.shape, small_in.shape, kernel_mid.shape[2], lax.axis_size("dp"))

    def images(maps):
        return maps.reshape((-1,) + maps.shape[2:])

    glob, small = images(glob_in), images(small_in)
    vectors = (
        gain_first, shift_first, gain_second, shift_second, excite_bias, squeeze_bias, gain_third,
        shift_third
    )
    (
        x_all, pre_one, act_one, pre_two, act_three, w_mid, k_out, w_in, vec_three,
        vec_three_other, mask, w_squeeze, w_excite, vec, stats, pooled, excite, squeeze_pre
    ) = forward(
        plan, small_count, glob, small, kernel_in, images(kernel_mid), kernel_out, squeeze_weight,
        excite_weight, vectors
    )
    (
        result, grad_summed, shard_out, grad_norm, slots_ahead, slots_behind, sums_three, sums_two
    ) = middle(
        plan, small_count, act_three, k_out, glob, small, images(glob_cotangent),
        images(small_cotangent), pre_two, stats, vec, vec_three, vec_three_other, mask, pooled,
        excite, squeeze_pre, w_squeeze, w_excite
    )
    gathered_out, gathered_mid, gathered_in, grad_inputs, sums_one = first(
        plan, shard_out, grad_norm, pre_two, pre_one, act_one, x_all, w_mid, w_in, stats, vec,
        sums_two, mask
    )
    outputs = finish(
        plan, result, grad_summed, grad_inputs, gathered_out, gathered_in, gathered_mid,
        slots_ahead, slots_behind, sums_one, sums_two, sums_three
    )
    shapes = (glob_in.shape, small_in.shape) * 2
    return tuple(out.reshape(shape) for out, shape in zip(outputs, shapes)) + outputs[4:]


def solution(mesh):
    maps = P("dp", "rows", None, None)
    vector = P("rows")
    columns = P(None, "rows")
    taps = P(None, None, None, "rows")
    return jax.shard_map(
        per_device,
        mesh=mesh,
        in_specs=(
            maps, maps, P("dp"), columns, taps, columns, P("rows", None), P(), columns,
        )
        + (vector,) * 7
        + (maps, maps),
        out_specs=(maps,) * 4
        + (columns, taps, columns, P("rows", None), P(), columns)
        + (vector,) * 7,
        check_vma=False,
    )
```

```python
import functools

import jax
import jax.numpy as jnp
from jax import lax
from jax.experimental import pallas as pl
from jax.experimental.pallas import tpu as pltpu
from jax.sharding import PartitionSpec as P

EPSILON = 1e-05
MESH = pl.DeviceIdType.MESH
F32 = jnp.float32
BF16 = jnp.bfloat16
ANY = pl.BlockSpec(memory_space=pl.ANY)
VMEM = pl.BlockSpec(memory_space=pltpu.VMEM)
LANE = 128
TILE = 64
VMEM_BYTES = 62 * 1024 * 1024


def round_up(value, step):
    return -(-value // step) * step


class Plan:
    def __init__(self, glob_shape, small_shape, group_width, dp):
        self.glob_height, self.glob_side = glob_shape[1], glob_shape[2]
        self.slots, self.small_height, self.small_side = small_shape[:3]
        self.channels = glob_shape[3]
        self.glob_width = round_up(self.glob_side + 1, 32)
        self.small_width = round_up(self.small_side + 1, 16)
        self.glob_own = self.glob_height * self.glob_width
        self.slot_own = self.small_height * self.small_width
        self.own = self.glob_own + self.slots * self.slot_own
        self.glob_all = 2 * self.glob_own
        self.slot_all = 2 * self.slot_own
        self.all = 2 * self.own
        self.glob_base = self.glob_width
        self.small_base = self.glob_all + 2 * self.glob_width
        self.slot_conv = self.slot_all + self.small_width
        self.small_conv = self.slots * self.slot_conv
        self.conv = self.small_base + self.small_conv
        self.width = group_width
        self.group = round_up(group_width, LANE)
        self.half = 2 * self.group
        self.half_real = self.channels // 2
        self.packed = round_up(-(-(self.half + self.group) // 2), LANE)
        self.dp = dp
        self.slot_rows = round_up(1 + self.slots, 8)
        self.glob_area = float(2 * self.glob_height * self.glob_side)
        self.slot_area = float(2 * self.small_height * self.small_side)

    def rows_of(self, core, start=0, size=None):
        return pl.ds(pl.multiple_of(core * self.own + start, 16), size or self.own)

    def sweep(self, body, carry):
        tiles = self.glob_own // TILE

        def glob_step(tile, state):
            start = tile // tiles * self.own + lax.rem(tile, tiles) * TILE
            place = self.glob_base + tile * TILE
            return body(pl.multiple_of(start, 16), TILE, pl.multiple_of(place, 16), 0, state)

        def slot_step(tile, state):
            core, slot = tile // self.slots, lax.rem(tile, self.slots)
            start = core * self.own + self.glob_own + slot * self.slot_own
            place = self.small_base + slot * self.slot_conv + core * self.slot_own
            return body(
                pl.multiple_of(start, 16), self.slot_own, pl.multiple_of(place, 16), 1 + slot, state
            )

        carry = lax.fori_loop(0, 2 * tiles, glob_step, carry)
        return lax.fori_loop(0, 2 * self.slots, slot_step, carry)

    def segments(self):
        return (
            (self.glob_base, self.glob_all, self.glob_width),
            (self.small_base, self.small_conv - self.small_width, self.small_width),
        )


def sigmoid(value):
    return 0.5 * jnp.tanh(0.5 * value) + 0.5


def rows_down(tile):
    return jnp.sum(tile.reshape(tile.shape[0] // 8, 8, tile.shape[1]), 0)


def widen(mask, lanes):
    return jnp.concatenate([mask] * (lanes // mask.shape[1]), 1)


def dot(left, right):
    return jnp.dot(left, right, preferred_element_type=F32)


def dot_nt(left, right):
    return lax.dot_general(left, right, (((1,), (1,)), ((), ())), preferred_element_type=F32)


def dot_tn(left, right):
    return lax.dot_general(left, right, (((0,), (0,)), ((), ())), preferred_element_type=F32)


def split_dot(left, right, nt=False):
    high = left.astype(BF16)
    low = (left - high.astype(F32)).astype(BF16)
    call = dot_nt if nt else dot
    return call(high, right) + call(low, right)


def entry_barrier(n, me, core):
    barrier = pltpu.get_barrier_semaphore()

    def greet(step, carry):
        pl.semaphore_signal(
            barrier, inc=1, device_id=(lax.rem(me + step, n), core), device_id_type=MESH
        )
        return carry

    lax.fori_loop(1, n, greet, 0)
    pl.semaphore_signal(barrier, inc=1, device_id=(me, 1 - core), device_id_type=MESH)
    pl.semaphore_wait(barrier, n)


class Spread:
    def __init__(self, n, me, core, source, slots, send, recv):
        self.n, self.me, self.core = n, me, core
        self.source, self.slots, self.send, self.recv = source, slots, send, recv

    def copy(self, step):
        return pltpu.make_async_remote_copy(
            src_ref=self.source,
            dst_ref=self.slots.at[self.me],
            send_sem=self.send.at[step],
            recv_sem=self.recv.at[step],
            device_id=(lax.rem(self.me + step, self.n), self.core),
            device_id_type=MESH,
        )

    def start(self):
        def begin(step, carry):
            self.copy(step).start()
            return carry

        lax.fori_loop(1, self.n, begin, 0)
        self.slots[pl.ds(self.me, 1)] = self.source[...][None]

    def wait(self):
        def end(step, carry):
            self.copy(step).wait()
            return carry

        lax.fori_loop(1, self.n, end, 0)


def to_partner(me, core, source, target, send, recv):
    return pltpu.make_async_remote_copy(
        src_ref=source,
        dst_ref=target,
        send_sem=send,
        recv_sem=recv,
        device_id=(me, 1 - core),
        device_id_type=MESH,
    )


def merge_moments(slots, n, lanes):
    def add(step, carry):
        total, count = carry
        return (total + slots[step, :, :lanes], count + slots[step, :, 2 * lanes : 2 * lanes + LANE])

    total, count = lax.fori_loop(
        0, n, add, (jnp.zeros((1, lanes), F32), jnp.zeros((1, LANE), F32))
    )
    wide_count = widen(count, lanes)
    mean = total / wide_count

    def spread(step, carry):
        own_count = widen(slots[step, :, 2 * lanes : 2 * lanes + LANE], lanes)
        gap = slots[step, :, :lanes] / own_count - mean
        return carry + slots[step, :, lanes : 2 * lanes] + own_count * gap * gap

    squares = lax.fori_loop(0, n, spread, jnp.zeros((1, lanes), F32))
    return mean, squares / wide_count, wide_count


def local_moments(plan, values, mask, which, count):
    lanes = plan.half

    def add(start, size, place, crop, carry):
        row = start if which == "all" else place
        tile = values[pl.ds(row, size), :] * widen(mask[pl.ds(start, size), :], lanes)
        return carry + rows_down(tile)

    total = jnp.sum(plan.sweep(add, jnp.zeros((8, lanes), F32)), 0, keepdims=True)
    mean = total / count

    def spread(start, size, place, crop, carry):
        row = start if which == "all" else place
        gap = (values[pl.ds(row, size), :] - mean) * widen(mask[pl.ds(start, size), :], lanes)
        return carry + rows_down(gap * gap)

    squares = jnp.sum(plan.sweep(spread, jnp.zeros((8, lanes), F32)), 0, keepdims=True)
    return total, squares


GAIN_ONE, SHIFT_ONE, GAIN_TWO, SHIFT_TWO, EXCITE_BIAS, SQUEEZE_BIAS, COUNT = range(7)
MEAN_ONE, INVERSE_ONE, MEAN_TWO, INVERSE_TWO, TOTAL = range(5)


def lane_of(shape):
    return lax.broadcasted_iota(jnp.int32, shape, len(shape) - 1)


def row_of(shape):
    return lax.broadcasted_iota(jnp.int32, shape, len(shape) - 2)


def group_lanes(value, plan):
    lane = lane_of(value.shape)
    moved = pltpu.roll(value, plan.group - plan.width, 1)
    return jnp.where(lane < plan.width, value, jnp.where(lane < plan.group, 0.0, moved))


def fill_mask(plan, mask, base, live_count):
    step = 32
    row = row_of((step, LANE))
    glob = (lax.rem(row, plan.glob_width) < plan.glob_side).astype(F32)
    small = (lax.rem(row, plan.small_width) < plan.small_side).astype(F32)

    def glob_step(tile, carry):
        mask[pl.ds(pl.multiple_of(base + tile * step, step), step), :] = glob
        return carry

    lax.fori_loop(0, plan.glob_own // step, glob_step, 0)
    for slot in range(plan.slots):
        live = jnp.clip(live_count - float(slot), 0.0, 1.0)

        def slot_step(tile, carry, slot=slot, live=live):
            start = base + plan.glob_own + slot * plan.slot_own + tile * step
            mask[pl.ds(pl.multiple_of(start, step), step), :] = small * live
            return carry

        lax.fori_loop(0, plan.slot_own // step, slot_step, 0)


def zero_borders(plan, shifted):
    lanes = shifted.shape[2]
    for side in range(2):
        shifted[side, : plan.glob_base, :] = jnp.zeros((plan.glob_base, lanes), BF16)
        shifted[side, plan.glob_base + plan.glob_all : plan.small_base, :] = jnp.zeros(
            (plan.glob_width, lanes), BF16
        )
        for slot in range(plan.slots):
            low = plan.small_base + slot * plan.slot_conv + plan.slot_all
            shifted[side, low : low + plan.small_width, :] = jnp.zeros(
                (plan.small_width, lanes), BF16
            )


def forward_kernel(
    plan,
    live,
    glob_hbm,
    small_hbm,
    kernel_in_hbm,
    kernel_mid_hbm,
    kernel_out_hbm,
    squeeze_hbm,
    excite_hbm,
    gain_one,
    shift_one,
    gain_two,
    shift_two,
    excite_bias,
    squeeze_bias,
    gain_three,
    shift_three,
    x_out,
    pre_one_out,
    act_one_out,
    pre_two_out,
    act_three_out,
    w_mid_out,
    k_out_both,
    w_in_both,
    vec_three,
    vec_three_other,
    mask_hbm,
    w_squeeze_hbm,
    w_excite_hbm,
    vec,
    stats,
    pooled_out,
    excite_out,
    squeeze_pre_out,
    glob,
    small,
    kernel_in,
    taps,
    kernel_out,
    squeeze,
    excite,
    wide,
    table,
    x_all,
    pre_one,
    shifted,
    w_in,
    w_mid,
    w_turned,
    pre_two,
    act_three,
    k_out,
    pay_one,
    slots_one,
    pay_two,
    slots_two,
    squeeze_send,
    squeeze_recv,
    mask,
    w_squeeze,
    w_excite,
    local_sem,
    send_sem,
    recv_sem,
    spread_send,
    spread_recv,
):
    n, half, group, width = plan.dp, plan.half, plan.group, plan.width
    channels, real = plan.channels, plan.half_real
    me, core = lax.axis_index("dp"), lax.axis_index("rows")

    def local(source, target, index):
        copy = pltpu.make_async_copy(source, target, local_sem.at[index])
        copy.start()
        return copy

    load_glob = local(glob_hbm, glob, 0)
    load_small = local(small_hbm, small, 1)
    load_in = local(kernel_in_hbm, kernel_in, 2)
    entry_barrier(n, me, core)

    def partner(source, target, index):
        copy = to_partner(me, core, source, target, send_sem.at[index], recv_sem.at[index])
        copy.start()
        return copy

    load_glob.wait()

    def glob_row(row, carry):
        rows = plan.rows_of(core, row * plan.glob_width, plan.glob_width)
        wide[: plan.glob_side, :channels] = glob[row].astype(F32)
        for side in range(2):
            x_all[side, rows, :] = wide[: plan.glob_width, side * half : (side + 1) * half].astype(BF16)
        return carry

    def small_row(row, carry):
        rows = plan.rows_of(core, plan.glob_own + row * plan.small_width, plan.small_width)
        wide[: plan.small_side, :channels] = small[row].astype(F32)
        for side in range(2):
            x_all[side, rows, :] = wide[: plan.small_width, side * half : (side + 1) * half].astype(
                BF16
            )
        return carry

    def send_piece(index):
        start = (0, plan.glob_own)[index]
        rows = plan.rows_of(core, start, (plan.glob_own, plan.own - plan.glob_own)[index])
        part = x_all.at[:, rows, :]
        return partner(part, part, index)

    wide[...] = jnp.zeros_like(wide)
    lax.fori_loop(0, plan.glob_height, glob_row, 0)
    x_remote = [send_piece(0)]
    load_small.wait()
    wide[...] = jnp.zeros_like(wide)
    lax.fori_loop(0, plan.slots * plan.small_height, small_row, 0)
    x_remote.append(send_piece(1))

    table[...] = jnp.zeros_like(table)
    load_in.wait()
    load_taps = [local(kernel_mid_hbm.at[tap], taps.at[tap], 3 + tap) for tap in range(3)]
    load_out = local(kernel_out_hbm, kernel_out, 6)
    load_squeeze = local(squeeze_hbm, squeeze, 7)
    load_excite = local(excite_hbm, excite, 8)
    for start in range(0, channels, group):
        length = min(group, channels - start)
        table[:length, :real] = kernel_in[start : start + length, :].astype(F32)
        block = group_lanes(table[:group, :], plan)
        if length < group:
            block = jnp.where(row_of(block.shape) < length, block, 0.0)
        low = start % half
        w_in[start // half, low : low + group, :] = block.astype(BF16)
    base = 2
    send_in = partner(w_in, w_in_both.at[core], base)

    live_count = live[0].astype(F32)
    vec[...] = jnp.zeros_like(vec)
    for index, vector in enumerate(
        (gain_one, shift_one, gain_two, shift_two, excite_bias, squeeze_bias)
    ):
        vec[index : index + 1, : vector.shape[0]] = vector[...].astype(F32).reshape(1, -1)
    vec_three[...] = jnp.zeros_like(vec_three)
    for index, vector in enumerate((gain_three, shift_three)):
        vec_three[index : index + 1, : vector.shape[0]] = vector[...].astype(F32).reshape(1, -1)
    raw = vec[...]
    grouped = group_lanes(raw, plan)
    chip_count = jnp.zeros((1, half), F32) + (plan.glob_area + plan.slot_area * live_count)
    row = row_of(raw.shape)
    vec[...] = jnp.where(row == SQUEEZE_BIAS, raw, jnp.where(row == COUNT, chip_count, grouped))
    send_vec = partner(vec_three, vec_three_other, base + 1)
    for owner in range(2):
        fill_mask(plan, mask, owner * plan.own, live_count)

    def product(owner):
        size = plan.own // 2
        for part in range(2):
            rows = plan.rows_of(owner, part * size, size)
            pre_one[rows, :] = dot(x_all[0, rows, :], w_in[0]) + dot(x_all[1, rows, :], w_in[1])

    def prepare_tap(tap):
        load_taps[tap].wait()
        table[:width, :real] = taps[tap % 3].astype(F32)
        block = group_lanes(table[:group, :], plan)
        block = jnp.where(row_of(block.shape) < width, block, 0.0)
        w_mid[tap // 3, tap % 3 * group : (tap % 3 + 1) * group, :] = block.astype(BF16)
        for side in range(2):
            turned = block[:, side * group : (side + 1) * group].T
            w_turned[side, :, tap * group : (tap + 1) * group] = turned.astype(BF16)
        if tap + 3 < 9:
            load_taps.append(local(kernel_mid_hbm.at[tap + 3], taps.at[tap % 3], 3 + tap % 3))

    product(core)
    zero_borders(plan, shifted)
    for copy in x_remote:
        copy.wait()
    product(1 - core)
    saves = [
        local(x_all, x_out, 9),
        local(pre_one, pre_one_out, 10),
        local(mask, mask_hbm, 19),
    ]

    def local_part(values, which, pay):
        total, squares = local_moments(plan, values, mask, which, vec[COUNT : COUNT + 1, :])
        pay[:, :half] = total
        pay[:, half : 2 * half] = squares
        pay[:, 2 * half :] = vec[COUNT : COUNT + 1, :LANE]

    def spread_of(pay, slots, index):
        spread = Spread(n, me, core, pay, slots, spread_send.at[index], spread_recv.at[index])
        spread.start()
        return spread

    local_part(pre_one, "all", pay_one)
    spread = spread_of(pay_one, slots_one, 0)
    for tap in range(9):
        prepare_tap(tap)
    saves.append(local(w_mid, w_mid_out, 11))
    spread.wait()
    mean, variance, count = merge_moments(slots_one, n, half)
    inverse = lax.rsqrt(variance + EPSILON)
    stats[...] = jnp.zeros_like(stats)
    stats[MEAN_ONE : MEAN_ONE + 1, :] = mean
    stats[INVERSE_ONE : INVERSE_ONE + 1, :] = inverse
    stats[TOTAL : TOTAL + 1, :] = count
    scale = inverse * vec[GAIN_ONE : GAIN_ONE + 1, :]
    shift = vec[SHIFT_ONE : SHIFT_ONE + 1, :]

    def activate_one(start, size, place, crop, carry):
        norm = (pre_one[pl.ds(start, size), :] - mean) * scale + shift
        act = norm * sigmoid(norm) * widen(mask[pl.ds(start, size), :], half)
        before = pltpu.roll(act, 1, 0)
        after = pltpu.roll(act, size - 1, 0)
        for tap, value in enumerate((before, act, after)):
            for side in range(2):
                shifted[side, pl.ds(place, size), tap * group : (tap + 1) * group] = value[
                    :, side * group : (side + 1) * group
                ].astype(BF16)
        return carry

    plan.sweep(activate_one, 0)
    for side in range(2):
        saves.append(
            local(
                shifted.at[side, :, group : 2 * group],
                act_one_out.at[:, side * group : (side + 1) * group],
                12 + side,
            )
        )

    for low, length, wide_row in plan.segments():
        for side in range(2):
            lanes = slice(side * group, (side + 1) * group)
            block = length // 2
            for part in range(2):
                at = low + part * block
                windows = [
                    shifted[side, at + shift_row : at + shift_row + block, :]
                    for shift_row in (-wide_row, 0, wide_row)
                ]
                turned = dot_nt(w_turned[side], jnp.concatenate(windows, 1))
                pre_two[at : at + block, lanes] = turned.T
    saves.append(local(pre_two, pre_two_out, 14))

    local_part(pre_two, "conv", pay_two)
    spread = spread_of(pay_two, slots_two, 1)
    load_out.wait()
    for piece in range(4):
        low = piece * width // 16 * 16
        length = min(table.shape[0], channels - low)
        table[:length, :real] = kernel_out[low : low + length, :].astype(F32)
        off = piece * width - low
        block = table[off : off + group, :]
        block = jnp.where(row_of(block.shape) < width, block, 0.0)
        place = piece % 2 * group
        k_out[piece // 2, place : place + group, :] = block.astype(BF16)
    send_out = partner(k_out, k_out_both.at[core], base + 2)
    load_squeeze.wait()
    for piece in range(2):
        low = piece * width // 16 * 16
        length = min(table.shape[0], 2 * width - low)
        table[:length, :width] = squeeze[low : low + length, :].astype(F32)
        off = piece * width - low
        block = table[off : off + group, :group]
        keep = (row_of(block.shape) < width) & (lane_of(block.shape) < width)
        w_squeeze[piece * group : (piece + 1) * group, :] = jnp.where(keep, block, 0.0).astype(BF16)
    load_excite.wait()
    table[:width, :real] = excite[...].astype(F32)
    block = group_lanes(table[:group, :], plan)
    w_excite[...] = jnp.where(row_of(block.shape) < width, block, 0.0).astype(BF16)
    saves.append(local(w_squeeze, w_squeeze_hbm, 20))
    saves.append(local(w_excite, w_excite_hbm, 21))
    spread.wait()
    mean_two, variance, _ = merge_moments(slots_two, n, half)
    inverse_two = lax.rsqrt(variance + EPSILON)
    stats[MEAN_TWO : MEAN_TWO + 1, :] = mean_two
    stats[INVERSE_TWO : INVERSE_TWO + 1, :] = inverse_two
    scale_two = inverse_two * vec[GAIN_TWO : GAIN_TWO + 1, :]
    shift_two = vec[SHIFT_TWO : SHIFT_TWO + 1, :]
    pooled_out[...] = jnp.zeros_like(pooled_out)
    saves[1].wait()
    act_two = pre_one

    def activate_two(start, size, place, crop, carry):
        norm = (pre_two[pl.ds(place, size), :] - mean_two) * scale_two + shift_two
        act = norm * sigmoid(norm) * widen(mask[pl.ds(start, size), :], half)
        act_two[pl.ds(start, size), :] = act
        pooled_out[pl.ds(crop, 1), :] += jnp.sum(act, 0, keepdims=True)
        return carry

    plan.sweep(activate_two, 0)
    pooled_out[:1, :] = pooled_out[:1, :] * (1.0 / plan.glob_area)
    pooled_out[1:, :] = pooled_out[1:, :] * (1.0 / plan.slot_area)
    part = split_dot(pooled_out[...], w_squeeze[...])
    squeeze_send[...] = part
    swap = partner(squeeze_send, squeeze_recv, base + 3)
    swap.wait()
    squeeze_pre = part + squeeze_recv[...] + vec[SQUEEZE_BIAS : SQUEEZE_BIAS + 1, :group]
    squeeze_pre_out[...] = squeeze_pre
    squeezed = squeeze_pre * sigmoid(squeeze_pre)
    excite_out[...] = sigmoid(
        split_dot(squeezed, w_excite[...]) + vec[EXCITE_BIAS : EXCITE_BIAS + 1, :]
    )
    saves.append(local(w_in, w_in_both.at[core], 15))
    saves.append(local(k_out, k_out_both.at[core], 16))

    def activate_three(start, size, place, crop, carry):
        act_three[core, pl.ds(start, size), :] = (
            act_two[pl.ds(start, size), :] * excite_out[pl.ds(crop, 1), :]
        ).astype(BF16)
        return carry

    plan.sweep(activate_three, 0)
    part = act_three.at[core, plan.rows_of(1 - core), :]
    exchange = partner(part, part, base + 4)
    saves.append(local(act_three.at[core], act_three_out.at[core], 17))
    for copy in (send_in, send_vec, send_out, exchange):
        copy.wait()
    part = act_three.at[1 - core, plan.rows_of(core), :]
    saves.append(local(part, act_three_out.at[1 - core, plan.rows_of(core), :], 18))
    for index, copy in enumerate(saves):
        if index != 1:
            copy.wait()


def forward(
    plan, live, glob, small, kernel_in, kernel_mid, kernel_out, squeeze, excite, vectors
):
    n, half, group = plan.dp, plan.half, plan.group
    shape = jax.ShapeDtypeStruct
    pay = 2 * half + LANE
    smem = pl.BlockSpec(memory_space=pltpu.SMEM)
    return pl.pallas_call(
        functools.partial(forward_kernel, plan),
        out_shape=(
            shape((2, plan.all, half), BF16),
            shape((plan.all, half), F32),
            shape((plan.conv, half), BF16),
            shape((plan.conv, half), F32),
            shape((2, plan.all, half), BF16),
            shape((3, 3 * group, half), BF16),
            shape((2, 2, half, half), BF16),
            shape((2, 2, half, half), BF16),
            shape((8, half), F32),
            shape((8, half), F32),
            shape((plan.all, LANE), F32),
            shape((half, group), BF16),
            shape((group, half), BF16),
            shape((8, half), F32),
            shape((8, half), F32),
            shape((plan.slot_rows, half), F32),
            shape((plan.slot_rows, half), F32),
            shape((plan.slot_rows, group), F32),
        ),
        in_specs=[smem] + [ANY] * 7 + [VMEM] * 8,
        out_specs=(ANY,) * 8 + (VMEM,) * 2 + (ANY,) * 3 + (VMEM,) * 5,
        scratch_shapes=[
            pltpu.VMEM(glob.shape, BF16),
            pltpu.VMEM(small.shape, BF16),
            pltpu.VMEM(kernel_in.shape, BF16),
            pltpu.VMEM((3,) + kernel_mid.shape[1:], BF16),
            pltpu.VMEM(kernel_out.shape, BF16),
            pltpu.VMEM(squeeze.shape, BF16),
            pltpu.VMEM(excite.shape, BF16),
            pltpu.VMEM((32, 2 * half), F32),
            pltpu.VMEM((group + 16, half), F32),
            pltpu.VMEM((2, plan.all, half), BF16),
            pltpu.VMEM((plan.all, half), F32),
            pltpu.VMEM((2, plan.conv, 3 * group), BF16),
            pltpu.VMEM((2, half, half), BF16),
            pltpu.VMEM((3, 3 * group, half), BF16),
            pltpu.VMEM((2, group, 9 * group), BF16),
            pltpu.VMEM((plan.conv, half), F32),
            pltpu.VMEM((2, plan.all, half), BF16),
            pltpu.VMEM((2, half, half), BF16),
            pltpu.VMEM((1, pay), F32),
            pltpu.VMEM((n, 1, pay), F32),
            pltpu.VMEM((1, pay), F32),
            pltpu.VMEM((n, 1, pay), F32),
            pltpu.VMEM((plan.slot_rows, group), F32),
            pltpu.VMEM((plan.slot_rows, group), F32),
            pltpu.VMEM((plan.all, LANE), F32),
            pltpu.VMEM((half, group), BF16),
            pltpu.VMEM((group, half), BF16),
            pltpu.SemaphoreType.DMA((22,)),
            pltpu.SemaphoreType.DMA((7,)),
            pltpu.SemaphoreType.DMA((7,)),
            pltpu.SemaphoreType.DMA((2, n)),
            pltpu.SemaphoreType.DMA((2, n)),
        ],
        compiler_params=pltpu.CompilerParams(
            collective_id=0, has_side_effects=True, vmem_limit_bytes=VMEM_BYTES
        ),
    )(live, glob, small, kernel_in, kernel_mid, kernel_out, squeeze, excite, *vectors)


def own_steps(plan, body, carry):
    step = 32

    def run(tile, state):
        return body(pl.multiple_of(tile * step, step), step, state)

    return lax.fori_loop(0, plan.own // step, run, carry)


def merge_two(first, second, lanes):
    sums = [part[:, :lanes] for part in (first, second)]
    squares = [part[:, lanes : 2 * lanes] for part in (first, second)]
    counts = [widen(part[:, 2 * lanes :], lanes) for part in (first, second)]
    total = sums[0] + sums[1]
    count = counts[0] + counts[1]
    mean = total / count
    spread = squares[0] + squares[1]
    for index in range(2):
        gap = sums[index] / counts[index] - mean
        spread = spread + counts[index] * gap * gap
    return total, spread, count


def split_maps(plan, glob, small, target, base, wide):
    half, real = plan.half, plan.half_real
    low = real // LANE * LANE

    def place(source, row, start, size, real_size):
        wide[:real_size, : plan.channels] = source[row].astype(F32)
        rows = pl.ds(pl.multiple_of(base + start, 16), size)
        first = wide[:size, :half]
        target[0, rows, :] = jnp.where(lane_of(first.shape) < real, first, 0.0).astype(BF16)
        second = wide[:size, low:]
        moved = pltpu.roll(second, second.shape[1] - (real - low), 1)
        target[1, rows, :] = moved[:, :half].astype(BF16)

    def glob_row(row, carry):
        place(glob, row, row * plan.glob_width, plan.glob_width, plan.glob_side)
        return carry

    def small_row(row, carry):
        start = plan.glob_own + row * plan.small_width
        place(small, row, start, plan.small_width, plan.small_side)
        return carry

    if glob is not None:
        wide[...] = jnp.zeros_like(wide)
        lax.fori_loop(0, plan.glob_height, glob_row, 0)
    if small is not None:
        wide[...] = jnp.zeros_like(wide)
        lax.fori_loop(0, plan.slots * plan.small_height, small_row, 0)


def gather_sum(slots, n, lanes):
    def add(step, carry):
        return carry + slots[step]

    return lax.fori_loop(0, n, add, jnp.zeros((1, lanes), F32))


ORDERS = {
    "A": ((0, 1, 2, 3), (1, 0, 2, 3)),
    "B": ((0, 2, 1, 3), (1, 2, 0, 3)),
    "P": ((0, 1, 2, 3), (2, 1, 0, 3)),
    "Q": ((2, 0, 1, 3), (1, 0, 2, 3)),
}
HALVINGS = 3
HANDED = 2


class Steps:
    def __init__(self, n, me, core, order):
        bits = n.bit_length() - 1
        self.halvings = min(bits, HALVINGS)
        self.shards = 2**self.halvings
        self.doublings = bits - self.halvings
        self.bit, self.partner = [], []
        chosen = [[bit for bit in one if bit < bits] for one in ORDERS[order]]
        chosen = [one + list(range(len(one), bits)) for one in chosen]
        for step in range(bits):
            first, second = 2 ** chosen[0][step], 2 ** chosen[1][step]
            distance = first + (second - first) * core
            bit = lax.rem(me // distance, 2)
            self.bit.append(bit)
            self.partner.append((me + distance * (1 - 2 * bit), core))


class Chain:
    def __init__(self, steps, work, land, send, recv, free, begun=0, until=None):
        self.steps, self.work, self.land, self.free = steps, work, land, free
        self.send, self.recv = send, recv
        self.rows = work.shape[0]
        self.shard = self.rows // steps.shards
        self.halvings = steps.halvings
        self.reduce_steps = steps.halvings + steps.doublings
        self.begun, self.until = begun, until
        self.pending = None
        self.step, self.at, self.length = begun, 0, self.rows >> begun
        for step in range(begun):
            self.at = self.at + steps.bit[step] * (self.rows >> (step + 1))
        self.land_base = self.rows - self.length
        self.back = None

    def rows_at(self, row, length):
        return pl.ds(row if isinstance(row, int) else pl.multiple_of(row, 16), length)

    def here(self):
        return self.work.at[self.rows_at(self.at, self.length), :]

    def remote(self, source, target, step, slot):
        self.pending = pltpu.make_async_remote_copy(
            src_ref=source,
            dst_ref=target,
            send_sem=self.send.at[slot],
            recv_sem=self.recv.at[slot],
            device_id=self.steps.partner[step],
            device_id_type=MESH,
        )
        self.pending.start()

    def begin_reduce(self):
        step = self.step
        if step < self.halvings:
            length = self.rows >> (step + 1)
            bit = self.steps.bit[step]
            self.keep = self.at + bit * length
            gone = self.at + (1 - bit) * length
            low = self.rows - 2 * length
        else:
            length = self.shard
            self.keep = gone = self.at
            low = self.rows - self.shard + (step - self.halvings) * self.shard
        self.length = length
        self.landed = self.land.at[pl.ds(low - self.land_base, length), :]
        self.remote(self.work.at[self.rows_at(gone, length), :], self.landed, step, step)

    def end_reduce(self):
        self.pending.wait()
        if self.free is not None and self.step < self.halvings:
            pl.semaphore_signal(
                self.free.at[self.step],
                inc=1,
                device_id=self.steps.partner[self.step],
                device_id_type=MESH,
            )
        size = 48 if self.shard % 48 == 0 else 16

        def add(tile, carry):
            there = self.rows_at(self.keep + tile * size, size)
            here = pl.ds(pl.multiple_of(tile * size, 16), size)
            total = self.work[there, :].astype(F32) + self.landed[here, :].astype(F32)
            self.work[there, :] = total.astype(BF16)
            return carry

        lax.fori_loop(0, self.length // size, add, 0)
        self.at = self.keep
        self.step += 1

    def begin_gather(self):
        if self.back >= self.begun:
            pl.semaphore_wait(self.free.at[self.back], 1)
        part = self.here()
        self.remote(part, part, self.back, self.reduce_steps + self.back)

    def end_gather(self):
        self.pending.wait()
        self.at = self.at - self.steps.bit[self.back] * self.length
        self.length *= 2
        self.back -= 1

    def advance(self):
        if self.pending is not None:
            if self.back is None:
                self.end_reduce()
            else:
                self.end_gather()
            self.pending = None
        if self.step == self.until:
            return
        if self.step < self.reduce_steps:
            self.begin_reduce()
            return
        if self.back is None:
            self.back = self.halvings - 1
        if self.back >= 0:
            self.begin_gather()

    def done(self):
        return self.pending is None and (self.step == self.until or self.back == -1)


def land_rows(n, rows, begun=0, until=None):
    bits = n.bit_length() - 1
    halvings = min(bits, HALVINGS)
    last = halvings if until is None else min(until, halvings)
    extra = bits - halvings if until is None else 0
    return (rows >> begun) - (rows >> last) + extra * (rows >> halvings)


def chain_slots(n):
    bits = n.bit_length() - 1
    return bits + min(bits, HALVINGS)


def silu_slope(value, sigma):
    return sigma * (1.0 + value * (1.0 - sigma))
OUTS = 2
MIDS = 6
INS = 4
CHAINS = (
    tuple("out%d" % i for i in range(OUTS))
    + tuple("mid%d" % i for i in range(MIDS))
    + tuple("in%d" % i for i in range(INS))
)
CHAIN_ORDERS = tuple("AAABPQABPQPQ")

SHIFT_TWO_SUM, GAIN_TWO_SUM = range(2)
SHIFT_ONE_SUM, GAIN_ONE_SUM = range(2)


def middle_kernel(
    plan,
    live,
    act_three_hbm,
    k_out_hbm,
    glob_hbm,
    small_hbm,
    glob_cot_hbm,
    small_cot_hbm,
    pre_two_hbm,
    mask_hbm,
    w_squeeze_hbm,
    w_excite_hbm,
    stats,
    vec,
    vec_three_own,
    vec_three_other,
    pooled,
    excite,
    squeeze_pre,
    result_hbm,
    grad_summed_hbm,
    shard_out,
    grad_norm_out,
    slots_ahead,
    slots_behind,
    sums_three_out,
    sums_out,
    result_out,
    grad_summed_out,
    mask,
    w_squeeze,
    w_excite,
    act_three,
    k_out,
    flat,
    flat_two,
    maps,
    pay,
    pair,
    chip,
    slots,
    finals,
    pay_back,
    pair_back,
    chip_back,
    slots_back,
    finals_back,
    vec_three,
    glob,
    small,
    glob_cot,
    small_cot,
    mask_own,
    wide,
    pre_two,
    work,
    land,
    grad_excite,
    squeeze_send,
    squeeze_recv,
    grad_pooled,
    ahead,
    behind,
    pay_two,
    slots_two,
    local_sem,
    send_sem,
    recv_sem,
    spread_send,
    spread_recv,
    reduce_send,
    reduce_recv,
):
    n, half, group = plan.dp, plan.half, plan.group
    me, core = lax.axis_index("dp"), lax.axis_index("rows")
    own = plan.own
    size = own // 2

    def local(source, target, index):
        copy = pltpu.make_async_copy(source, target, local_sem.at[index])
        copy.start()
        return copy

    def partner(source, target, index):
        copy = to_partner(me, core, source, target, send_sem.at[index], recv_sem.at[index])
        copy.start()
        return copy

    load_act = [local(act_three_hbm.at[core], act_three.at[core], 0)]
    mine = act_three.at[1 - core, plan.rows_of(core), :]
    load_act.append(local(act_three_hbm.at[1 - core, plan.rows_of(core), :], mine, 7 + 1 + OUTS))
    load_k = local(k_out_hbm, k_out, 1)
    entry_barrier(n, me, core)
    vec_three[core] = vec_three_own[...]
    vec_three[1 - core] = vec_three_other[...]
    fill_mask(plan, mask_own, 0, live[0].astype(F32))
    own_count = 0.5 * vec[COUNT : COUNT + 1, :]

    def spread_of(source, target, index):
        spread = Spread(n, me, core, source, target, spread_send.at[index], spread_recv.at[index])
        spread.start()
        return spread

    deep = plan.slot_rows
    before = squeeze_pre[...]
    sigma = sigmoid(before)
    squeezed = before * sigma
    ahead[...] = jnp.zeros_like(ahead)
    ahead[:deep, :] = pooled[...].astype(BF16)
    ahead[deep:, :group] = squeezed.astype(BF16)
    ahead_spread = spread_of(ahead, slots_ahead, 3)

    for copy in load_act:
        copy.wait()
    mine = act_three.at[core, plan.rows_of(core), :]
    act_swap = partner(mine, mine, 5)
    load_k.wait()
    raws = [
        local(source, target, 2 + index)
        for index, (source, target) in enumerate(
            (
                (glob_hbm, glob),
                (small_hbm, small),
                (glob_cot_hbm, glob_cot),
                (small_cot_hbm, small_cot),
            )
        )
    ]
    load_two = [
        local(pre_two_hbm, pre_two, 6),
        local(mask_hbm, mask, 11 + OUTS),
        local(w_squeeze_hbm, w_squeeze, 12 + OUTS),
        local(w_excite_hbm, w_excite, 13 + OUTS),
    ]
    for part in range(2):
        rows = plan.rows_of(core, part * size, size)
        for side in range(2):
            low = side * own + part * size
            flat[low : low + size, :] = dot(act_three[0, rows, :], k_out[side, 0]) + dot(
                act_three[1, rows, :], k_out[side, 1]
            )

    for side in range(2):

        def add(row, step, carry, side=side):
            seen = widen(mask_own[pl.ds(row, step), :], half)
            return carry + rows_down(flat[pl.ds(side * own + row, step), :] * seen)

        total = jnp.sum(own_steps(plan, add, jnp.zeros((8, half), F32)), 0, keepdims=True)
        mean = total / own_count

        def spread_out(row, step, carry, side=side, mean=mean):
            seen = widen(mask_own[pl.ds(row, step), :], half)
            gap = (flat[pl.ds(side * own + row, step), :] - mean) * seen
            return carry + rows_down(gap * gap)

        squares = jnp.sum(own_steps(plan, spread_out, jnp.zeros((8, half), F32)), 0, keepdims=True)
        pay[side, :, :half] = total
        pay[side, :, half : 2 * half] = squares
        pay[side, :, 2 * half :] = own_count[:, :LANE]
    partner(pay.at[1 - core], pair, 0).wait()
    total, squares, count = merge_two(pay[core], pair[...], half)
    chip[:, :half] = total
    chip[:, half : 2 * half] = squares
    chip[:, 2 * half :] = count[:, :LANE]
    exchange = spread_of(chip, slots, 0)
    for copy in raws:
        copy.wait()
    split_maps(plan, glob, small, maps, 0, wide)
    split_maps(plan, glob_cot, None, maps, own, wide)
    exchange.wait()
    mean, variance, full_count = merge_moments(slots, n, half)
    finals[core, :, :half] = mean
    finals[core, :, half:] = lax.rsqrt(variance + EPSILON)
    swap = partner(finals.at[core], finals.at[core], 1)
    split_maps(plan, None, small_cot, maps, own, wide)
    swap.wait()

    for side in range(2):
        mean = finals[side, :, :half]
        inverse = finals[side, :, half:]
        gain = vec_three[side, :1, :]
        shift = vec_three[side, 1:2, :]

        def outer(row, step, carry, side=side, mean=mean, inverse=inverse, gain=gain, shift=shift):
            rows = pl.ds(row, step)
            low = pl.ds(side * own + row, step)
            seen = widen(mask_own[rows, :], half)
            normed = (flat[low, :] - mean) * inverse
            summed = normed * gain + shift + maps[side, rows, :].astype(F32)
            sigma = sigmoid(summed)
            result_out[side, rows, :] = (seen * summed * sigma).astype(BF16)
            slope = sigma * (1.0 + summed * (1.0 - sigma))
            cot = maps[side, pl.ds(pl.multiple_of(own + row, 16), step), :]
            grad = cot.astype(F32) * seen * slope
            flat_two[low, :] = grad
            grad_summed_out[side, rows, :] = grad.astype(BF16)
            return carry[0] + rows_down(grad), carry[1] + rows_down(grad * normed)

        zero = jnp.zeros((8, half), F32)
        shift_sum, gain_sum = own_steps(plan, outer, (zero, zero))
        pay_back[side, :, :half] = jnp.sum(shift_sum, 0, keepdims=True)
        pay_back[side, :, half:] = jnp.sum(gain_sum, 0, keepdims=True)
    saves = [
        local(result_out, result_hbm, 9 + OUTS),
        local(grad_summed_out, grad_summed_hbm, 10 + OUTS),
    ]
    partner(pay_back.at[1 - core], pair_back, 2).wait()
    chip_back[...] = pay_back[core] + pair_back[...]
    spread_of(chip_back, slots_back, 1).wait()
    finals_back[core] = gather_sum(slots_back, n, 2 * half)
    partner(finals_back.at[core], finals_back.at[core], 3).wait()

    grad_pre_three = maps
    swaps = []
    for side in range(2):
        mean = finals[side, :, :half]
        inverse = finals[side, :, half:]
        shift_sum = finals_back[side, :, :half]
        gain_sum = finals_back[side, :, half:]
        sums_three_out[side] = jnp.concatenate([shift_sum, gain_sum, jnp.zeros((6, half), F32)], 0)
        scale = vec_three[side, :1, :] * inverse
        shift_mean = shift_sum / full_count
        gain_mean = gain_sum / full_count * inverse

        def inner(
            row, step, carry, side=side, mean=mean, scale=scale, shift_mean=shift_mean,
            gain_mean=gain_mean
        ):
            low = pl.ds(side * own + row, step)
            seen = widen(mask_own[pl.ds(row, step), :], half)
            centered = flat[low, :] - mean
            grad = scale * (flat_two[low, :] - shift_mean - centered * gain_mean)
            grad_pre_three[side, plan.rows_of(core, row, step), :] = (grad * seen).astype(BF16)
            return carry

        own_steps(plan, inner, 0)
        part = grad_pre_three.at[side, plan.rows_of(core), :]
        swaps.append(partner(part, part, 6 + side))

    grad_act = flat

    def product(owner):
        for part in range(2):
            rows = plan.rows_of(owner, part * size, size)
            grad_act[rows, :] = dot_nt(grad_pre_three[0, rows, :], k_out[0, core]) + dot_nt(
                grad_pre_three[1, rows, :], k_out[1, core]
            )

    product(core)
    for swap in swaps + [act_swap]:
        swap.wait()
    chains, span = [], 2 * half // OUTS
    for side in range(2):
        for part in range(2):
            lanes = slice(part * group, (part + 1) * group)
            low = side * half + part * group
            work[low : low + group, :] = dot_tn(
                act_three[side, :, lanes], grad_pre_three[core]
            ).astype(BF16)
            if (low + group) % span == 0:
                index = low // span
                chain = Chain(
                    Steps(n, me, core, CHAIN_ORDERS[index]), work.at[pl.ds(index * span, span), :],
                    land.at[index], reduce_send.at[index], reduce_recv.at[index], None, until=HANDED
                )
                chain.advance()
                chains.append(chain)
    product(1 - core)
    for copy in load_two:
        copy.wait()

    mean = stats[MEAN_TWO : MEAN_TWO + 1, :]
    inverse = stats[INVERSE_TWO : INVERSE_TWO + 1, :]
    count = stats[TOTAL : TOTAL + 1, :]
    gain = vec[GAIN_TWO : GAIN_TWO + 1, :]
    shift = vec[SHIFT_TWO : SHIFT_TWO + 1, :]
    slopes = flat_two
    grad_excite[...] = jnp.zeros_like(grad_excite)

    def excitation(start, size, place, crop, carry):
        rows = pl.ds(start, size)
        norm = (pre_two[pl.ds(place, size), :] - mean) * (inverse * gain) + shift
        sigma = sigmoid(norm)
        seen = widen(mask[rows, :], half)
        slopes[rows, :] = silu_slope(norm, sigma) * seen
        term = grad_act[rows, :] * (norm * sigma * seen)
        grad_excite[pl.ds(crop, 1), :] += jnp.sum(term, 0, keepdims=True)
        return carry

    plan.sweep(excitation, 0)
    level = excite[...]
    grad_excite_pre = grad_excite[...] * level * (1.0 - level)
    part = split_dot(grad_excite_pre, w_excite[...], nt=True)
    squeeze_send[...] = part
    swap = partner(squeeze_send, squeeze_recv, 4)
    swap.wait()
    grad_squeeze_pre = (part + squeeze_recv[...]) * silu_slope(before, sigma)
    back = split_dot(grad_squeeze_pre, w_squeeze[...], nt=True)
    crop_row = lax.broadcasted_iota(jnp.int32, back.shape, 0)
    area = jnp.where(crop_row == 0, 1.0 / plan.glob_area, 1.0 / plan.slot_area)
    grad_pooled[...] = back * area
    wide_part = plan.packed
    rest = half - wide_part
    behind[...] = jnp.zeros_like(behind)
    behind[:deep, :] = grad_excite_pre[:, :wide_part].astype(BF16)
    behind[deep:, :rest] = grad_excite_pre[:, wide_part:].astype(BF16)
    behind[deep:, rest : rest + group] = grad_squeeze_pre.astype(BF16)

    def gradient(start, size, place, crop, carry):
        rows = pl.ds(start, size)
        incoming = grad_act[rows, :] * excite[pl.ds(crop, 1), :] + grad_pooled[pl.ds(crop, 1), :]
        grad = incoming * slopes[rows, :]
        grad_act[rows, :] = grad
        normed = (pre_two[pl.ds(place, size), :] - mean) * inverse
        return carry[0] + rows_down(grad), carry[1] + rows_down(grad * normed)

    zero = jnp.zeros((8, half), F32)
    shift_sum, gain_sum = plan.sweep(gradient, (zero, zero))
    saves.append(local(grad_act, grad_norm_out, 7))
    pay_two[:, :half] = jnp.sum(shift_sum, 0, keepdims=True)
    pay_two[:, half:] = jnp.sum(gain_sum, 0, keepdims=True)
    spread = spread_of(pay_two, slots_two, 2)
    behind_spread = spread_of(behind, slots_behind, 4)
    for chain in chains:
        chain.advance()
    ahead_spread.wait()
    spread.wait()
    totals = gather_sum(slots_two, n, 2 * half)
    stores = []
    for index, chain in enumerate(chains):
        while not chain.done():
            chain.advance()
        stores.append(local(chain.here(), shard_out.at[index], 8 + index))
    sums_out[...] = jnp.zeros_like(sums_out)
    sums_out[SHIFT_TWO_SUM : SHIFT_TWO_SUM + 1, :] = totals[:, :half]
    sums_out[GAIN_TWO_SUM : GAIN_TWO_SUM + 1, :] = totals[:, half:]
    behind_spread.wait()
    for copy in saves + stores:
        copy.wait()


def middle(
    plan, live, act_three, k_out, glob, small, glob_cot, small_cot, pre_two, stats, vec, vec_three,
    vec_three_other, mask, pooled, excite, squeeze_pre, w_squeeze, w_excite
):
    n, half, group = plan.dp, plan.half, plan.group
    shape = jax.ShapeDtypeStruct
    pay = 2 * half + LANE
    own = (2, plan.own, half)
    rows = 2 * half
    deep = plan.slot_rows
    return pl.pallas_call(
        functools.partial(middle_kernel, plan),
        out_shape=(
            shape(own, BF16),
            shape(own, BF16),
            shape((OUTS, rows // OUTS >> HANDED, half), BF16),
            shape((plan.all, half), F32),
            shape((n, 2 * deep, half), BF16),
            shape((n, 2 * deep, plan.packed), BF16),
            shape((2, 8, half), F32),
            shape((8, half), F32),
        ),
        in_specs=[pl.BlockSpec(memory_space=pltpu.SMEM)] + [ANY] * 10 + [VMEM] * 7,
        out_specs=(ANY, ANY, ANY, ANY, VMEM, VMEM, VMEM, VMEM),
        scratch_shapes=[
            pltpu.VMEM(own, BF16),
            pltpu.VMEM(own, BF16),
            pltpu.VMEM(mask.shape, F32),
            pltpu.VMEM(w_squeeze.shape, BF16),
            pltpu.VMEM(w_excite.shape, BF16),
            pltpu.VMEM((2, plan.all, half), BF16),
            pltpu.VMEM(k_out.shape, BF16),
            pltpu.VMEM((plan.all, half), F32),
            pltpu.VMEM((plan.all, half), F32),
            pltpu.VMEM((2, plan.all, half), BF16),
            pltpu.VMEM((2, 1, pay), F32),
            pltpu.VMEM((1, pay), F32),
            pltpu.VMEM((1, pay), F32),
            pltpu.VMEM((n, 1, pay), F32),
            pltpu.VMEM((2, 1, 2 * half), F32),
            pltpu.VMEM((2, 1, 2 * half), F32),
            pltpu.VMEM((1, 2 * half), F32),
            pltpu.VMEM((1, 2 * half), F32),
            pltpu.VMEM((n, 1, 2 * half), F32),
            pltpu.VMEM((2, 1, 2 * half), F32),
            pltpu.VMEM((2,) + vec_three.shape, F32),
            pltpu.VMEM(glob.shape, BF16),
            pltpu.VMEM(small.shape, BF16),
            pltpu.VMEM(glob.shape, BF16),
            pltpu.VMEM(small.shape, BF16),
            pltpu.VMEM((plan.own, LANE), F32),
            pltpu.VMEM((32, 2 * half), F32),
            pltpu.VMEM((plan.conv, half), F32),
            pltpu.VMEM((rows, half), BF16),
            pltpu.VMEM((OUTS, land_rows(n, rows // OUTS, until=HANDED), half), BF16),
            pltpu.VMEM((deep, half), F32),
            pltpu.VMEM((deep, group), F32),
            pltpu.VMEM((deep, group), F32),
            pltpu.VMEM((deep, half), F32),
            pltpu.VMEM((2 * deep, half), BF16),
            pltpu.VMEM((2 * deep, plan.packed), BF16),
            pltpu.VMEM((1, 2 * half), F32),
            pltpu.VMEM((n, 1, 2 * half), F32),
            pltpu.SemaphoreType.DMA((14 + OUTS,)),
            pltpu.SemaphoreType.DMA((8,)),
            pltpu.SemaphoreType.DMA((8,)),
            pltpu.SemaphoreType.DMA((5, n)),
            pltpu.SemaphoreType.DMA((5, n)),
            pltpu.SemaphoreType.DMA((OUTS, HANDED)),
            pltpu.SemaphoreType.DMA((OUTS, HANDED)),
        ],
        compiler_params=pltpu.CompilerParams(
            collective_id=1, has_side_effects=True, vmem_limit_bytes=VMEM_BYTES
        ),
    )(
        live, act_three, k_out, glob, small, glob_cot, small_cot, pre_two, mask, w_squeeze, w_excite,
        stats, vec, vec_three, vec_three_other, pooled, excite, squeeze_pre
    )


SCHEDULE = (
    "two", "M0", "out1", "M1", "M2", "mid0", "M3", "M4", "C0", "out1", "C1", "mid0", "out0",
    "M5", "mid1", "C2", "C3", "out1", "C4", "out0", "mid0", "mid3", "mid4", "mid2", "mid5",
    "out1", "C5", "C6", "C7", "mid3", "sums", "mid0", "mid4", "out0", "mid2", "mid5", "mid3",
    "mid0", "mid1", "one", "K0", "K1", "mid5", "mid0", "X0", "mid1", "mid2", "in0", "K2",
    "in1", "K3", "mid3", "mid4", "out0", "mid1", "in2", "mid2", "in1", "mid1", "in0", "in3",
    "mid3", "mid2", "in1", "mid4", "mid1", "in2", "mid5", "in0", "in1", "in3", "mid4", "in2",
    "mid2", "in3", "out1", "in1", "in0", "in2", "mid3", "mid4", "mid0", "in3", "in2", "X1",
    "mid5", "mid1", "in0", "out0", "in3", "in1", "in2", "mid5", "mid3", "in0", "in3", "X2",
    "X3", "mid2", "in2", "in1", "mid5", "mid4", "in3", "in0",
)


def first_kernel(
    plan,
    shard_out_hbm,
    grad_norm_hbm,
    pre_two_hbm,
    pre_one_hbm,
    act_one_hbm,
    x_hbm,
    w_mid_hbm,
    w_in_hbm,
    mask_hbm,
    stats,
    vec,
    sums_two,
    gathered_out,
    gathered_mid,
    gathered_in,
    grad_inputs_out,
    sums_out,
    mask,
    flat,
    conv_rows,
    shifted,
    act_one,
    w_mid,
    grad_pre_one,
    grad_other,
    w_in,
    work_out,
    land_out,
    work_mid,
    land_mid,
    work_in,
    land_in,
    pay,
    slots,
    local_sem,
    pair_send,
    pair_recv,
    spread_send,
    spread_recv,
    chain_send,
    chain_recv,
    free,
):
    n, half, group = plan.dp, plan.half, plan.group
    me, core = lax.axis_index("dp"), lax.axis_index("rows")

    def local(source, target, index):
        copy = pltpu.make_async_copy(source, target, local_sem.at[index])
        copy.start()
        return copy

    waits = {
        "norm": local(grad_norm_hbm, flat, 0),
        "two": local(pre_two_hbm, conv_rows, 1),
        "mask": local(mask_hbm, mask, 2),
    }
    chains, targets, saves, state = {}, {}, {}, {}

    def begin(name, work, land, target, begun=0):
        index = CHAINS.index(name)
        steps = Steps(n, me, core, CHAIN_ORDERS[index])
        chains[name] = Chain(
            steps, work, land, chain_send.at[index], chain_recv.at[index], free.at[index], begun
        )
        targets[name] = target
        return chains[name]

    def advance(name):
        chain = chains[name]
        if name in saves:
            return
        chain.advance()
        if chain.done():
            index = CHAINS.index(name)
            saves[name] = local(chain.work, targets[name], 8 + index)

    outs = CHAINS[:OUTS]
    loads = []
    for index, name in enumerate(outs):
        rows = pl.ds(index * (2 * half // OUTS), 2 * half // OUTS)
        out = begin(
            name, work_out.at[rows, :], land_out.at[index], gathered_out.at[rows, :], HANDED
        )
        loads.append(local(shard_out_hbm.at[index], out.here(), 8 + index))
    entry_barrier(n, me, core)
    for name, load in zip(outs, loads):
        load.wait()
        advance(name)
    count = stats[TOTAL : TOTAL + 1, :]

    def norm_two():
        zero_borders(plan, shifted)
        mean = stats[MEAN_TWO : MEAN_TWO + 1, :]
        inverse = stats[INVERSE_TWO : INVERSE_TWO + 1, :]
        scale = vec[GAIN_TWO : GAIN_TWO + 1, :] * inverse
        shift_mean = sums_two[SHIFT_TWO_SUM : SHIFT_TWO_SUM + 1, :] / count
        gain_mean = sums_two[GAIN_TWO_SUM : GAIN_TWO_SUM + 1, :] / count * inverse
        for name in ("norm", "two", "mask"):
            waits[name].wait()
        waits["act"] = local(act_one_hbm, act_one, 3)
        waits["mid"] = local(w_mid_hbm, w_mid, 4)
        waits["in"] = local(w_in_hbm, w_in, 5)

        def into_two(start, size, place, crop, carry):
            rows = pl.ds(start, size)
            centered = conv_rows[pl.ds(place, size), :] - mean
            grad = scale * (flat[rows, :] - shift_mean - centered * gain_mean)
            grad = grad * widen(mask[rows, :], half)
            after = pltpu.roll(grad, size - 1, 0)
            before = pltpu.roll(grad, 1, 0)
            for tap, value in enumerate((after, grad, before)):
                for side in range(2):
                    shifted[side, pl.ds(place, size), tap * group : (tap + 1) * group] = value[
                        :, side * group : (side + 1) * group
                    ].astype(BF16)
            return carry

        plan.sweep(into_two, 0)
        waits["one"] = local(pre_one_hbm, flat, 0)
        waits["act"].wait()

    def mid(index):
        tap = index * 3 // MIDS
        sides = range(2) if MIDS == 3 else (index % 2,)
        for side in sides:
            lanes = slice(side * group, (side + 1) * group)
            total = None
            for low, length, width in plan.segments():
                first = low - (tap - 1) * width
                term = dot_tn(
                    act_one[low : low + length, lanes], shifted[side, first : first + length, :]
                )
                total = term if total is None else total + term
            work_mid[tap, lanes, :] = total.astype(BF16)
        name = CHAINS[OUTS + index]
        rows = pl.ds(sides[0] * group, len(sides) * group)
        begin(name, work_mid.at[tap, rows, :], land_mid.at[index], gathered_mid.at[tap, rows, :])
        advance(name)
        read_shifted()

    def read_shifted():
        state["reads"] = state.get("reads", 0) + 1
        if state["reads"] == MIDS + 8:
            waits["x"] = local(x_hbm, shifted.at[:, pl.ds(0, plan.all), pl.ds(0, half)], 7)

    def conv(index):
        if index == 0:
            waits["mid"].wait()
        low, length, width = plan.segments()[index // 4]
        block = length // 2
        side = index // 2 % 2
        at = low + index % 2 * block
        lanes = slice(side * group, (side + 1) * group)
        weights = [
            w_mid[tap, column * group : (column + 1) * group, lanes]
            for tap in range(3)
            for column in range(3)
        ]
        windows = [
            shifted[side, at + shift_row : at + shift_row + block, :]
            for shift_row in (width, 0, -width)
        ]
        turned = dot_nt(jnp.concatenate(weights, 1), jnp.concatenate(windows, 1))
        conv_rows[at : at + block, lanes] = turned.T
        read_shifted()

    mean = stats[MEAN_ONE : MEAN_ONE + 1, :]
    inverse = stats[INVERSE_ONE : INVERSE_ONE + 1, :]
    gain = vec[GAIN_ONE : GAIN_ONE + 1, :]
    shift = vec[SHIFT_ONE : SHIFT_ONE + 1, :]
    spread = Spread(n, me, core, pay, slots, spread_send, spread_recv)

    def sums_one():
        waits["one"].wait()

        def gradient(start, size, place, crop, carry):
            rows = pl.ds(start, size)
            normed = (flat[rows, :] - mean) * inverse
            norm = normed * gain + shift
            sigma = sigmoid(norm)
            grad = conv_rows[pl.ds(place, size), :] * silu_slope(norm, sigma)
            grad = grad * widen(mask[rows, :], half)
            conv_rows[pl.ds(place, size), :] = grad
            return carry[0] + rows_down(grad), carry[1] + rows_down(grad * normed)

        zero = jnp.zeros((8, half), F32)
        shift_sum, gain_sum = plan.sweep(gradient, (zero, zero))
        pay[:, :half] = jnp.sum(shift_sum, 0, keepdims=True)
        pay[:, half:] = jnp.sum(gain_sum, 0, keepdims=True)
        spread.start()

    def norm_one():
        spread.wait()
        totals = gather_sum(slots, n, 2 * half)
        sums_out[...] = jnp.zeros_like(sums_out)
        sums_out[SHIFT_ONE_SUM : SHIFT_ONE_SUM + 1, :] = totals[:, :half]
        sums_out[GAIN_ONE_SUM : GAIN_ONE_SUM + 1, :] = totals[:, half:]
        scale = gain * inverse
        shift_mean = totals[:, :half] / count
        gain_mean = totals[:, half:] / count * inverse

        def into_one(start, size, place, crop, carry):
            rows = pl.ds(start, size)
            centered = flat[rows, :] - mean
            grad = scale * (conv_rows[pl.ds(place, size), :] - shift_mean - centered * gain_mean)
            grad_pre_one[rows, :] = (grad * widen(mask[rows, :], half)).astype(BF16)
            return carry

        plan.sweep(into_one, 0)
        state["swap"] = to_partner(
            me, core, grad_pre_one.at[plan.rows_of(1 - core), :], grad_other, pair_send, pair_recv
        )
        state["swap"].start()

    def kernel_in(index):
        if index == 0:
            waits["x"].wait()
        size = 2 * half // INS
        side, start = index * size // half, index * size % half
        for low in range(start, start + size, group):
            work_in[side, low : low + group, :] = dot_tn(
                shifted[side, : plan.all, low : low + group], grad_pre_one[...]
            ).astype(BF16)
        name = CHAINS[OUTS + MIDS + index]
        rows = pl.ds(start, size)
        begin(name, work_in.at[side, rows, :], land_in.at[index], gathered_in.at[side, rows, :])
        advance(name)

    def inputs(index):
        if index == 0:
            waits["in"].wait()
            state["swap"].wait()
        part, side = index // 2, index % 2
        size = plan.own // 2
        rows = slice(part * size, (part + 1) * size)
        own = grad_pre_one[plan.rows_of(core, part * size, size), :]
        low = side * plan.own + part * size
        act_one[low : low + size, :] = (
            dot_nt(own, w_in[core, side]) + dot_nt(grad_other[rows, :], w_in[1 - core, side])
        ).astype(BF16)
        if part == 1:
            waits["result%d" % side] = local(
                act_one.at[pl.ds(side * plan.own, plan.own), :],
                grad_inputs_out.at[side],
                8 + len(CHAINS) + side,
            )

    blocks = {
        "two": norm_two,
        "sums": sums_one,
        "one": norm_one,
    }
    for index in range(MIDS):
        blocks["M%d" % index] = functools.partial(mid, index)
    for index in range(8):
        blocks["C%d" % index] = functools.partial(conv, index)
    for index in range(INS):
        blocks["K%d" % index] = functools.partial(kernel_in, index)
    for index in range(4):
        blocks["X%d" % index] = functools.partial(inputs, index)
    for item in SCHEDULE:
        if item in blocks:
            blocks[item]()
        else:
            advance(item)
    while len(saves) < len(CHAINS):
        for name in CHAINS:
            advance(name)
    for name in CHAINS:
        saves[name].wait()
    for side in range(2):
        waits["result%d" % side].wait()


def first(
    plan, shard_out, grad_norm, pre_two, pre_one, act_one, x_all, w_mid, w_in, stats, vec,
    sums_two, mask
):
    n, half, group = plan.dp, plan.half, plan.group
    shape = jax.ShapeDtypeStruct
    return pl.pallas_call(
        functools.partial(first_kernel, plan),
        out_shape=(
            shape((2 * half, half), BF16),
            shape((3, half, 3 * group), BF16),
            shape((2, half, half), BF16),
            shape((2, plan.own, half), BF16),
            shape((8, half), F32),
        ),
        in_specs=[ANY] * 9 + [VMEM] * 3,
        out_specs=(ANY, ANY, ANY, ANY, VMEM),
        scratch_shapes=[
            pltpu.VMEM(mask.shape, F32),
            pltpu.VMEM((plan.all, half), F32),
            pltpu.VMEM((plan.conv, half), F32),
            pltpu.VMEM((2, plan.conv, 3 * group), BF16),
            pltpu.VMEM((plan.conv, half), BF16),
            pltpu.VMEM(w_mid.shape, BF16),
            pltpu.VMEM((plan.all, half), BF16),
            pltpu.VMEM((plan.own, half), BF16),
            pltpu.VMEM(w_in.shape, BF16),
            pltpu.VMEM((2 * half, half), BF16),
            pltpu.VMEM((OUTS, land_rows(n, 2 * half // OUTS, begun=HANDED), half), BF16),
            pltpu.VMEM((3, half, 3 * group), BF16),
            pltpu.VMEM((MIDS, land_rows(n, 3 * half // MIDS), 3 * group), BF16),
            pltpu.VMEM((2, half, half), BF16),
            pltpu.VMEM((INS, land_rows(n, 2 * half // INS), half), BF16),
            pltpu.VMEM((1, 2 * half), F32),
            pltpu.VMEM((n, 1, 2 * half), F32),
            pltpu.SemaphoreType.DMA((10 + len(CHAINS),)),
            pltpu.SemaphoreType.DMA,
            pltpu.SemaphoreType.DMA,
            pltpu.SemaphoreType.DMA((n,)),
            pltpu.SemaphoreType.DMA((n,)),
            pltpu.SemaphoreType.DMA((len(CHAINS), chain_slots(n))),
            pltpu.SemaphoreType.DMA((len(CHAINS), chain_slots(n))),
            pltpu.SemaphoreType.REGULAR((len(CHAINS), HALVINGS)),
        ],
        compiler_params=pltpu.CompilerParams(
            collective_id=2, has_side_effects=True, vmem_limit_bytes=VMEM_BYTES
        ),
    )(
        shard_out, grad_norm, pre_two, pre_one, act_one, x_all, w_mid, w_in, mask, stats, vec,
        sums_two
    )


def join_lanes(low, high, real):
    zeros = jnp.zeros_like(low)
    wide = jnp.concatenate([low, zeros], 1)
    moved = pltpu.roll(jnp.concatenate([high, zeros], 1), real, 1)
    lane = lax.broadcasted_iota(jnp.int32, wide.shape, 1)
    return jnp.where(lane < real, wide, moved)


def finish_kernel(
    plan,
    result_hbm,
    grad_summed_hbm,
    grad_inputs_hbm,
    out_hbm,
    in_hbm,
    mid_hbm,
    slots_ahead,
    slots_behind,
    sums_one,
    sums_two,
    sums_three,
    glob_out_hbm,
    small_out_hbm,
    glob_grad_hbm,
    small_grad_hbm,
    kernel_in_hbm,
    kernel_mid_hbm,
    kernel_out_hbm,
    squeeze_hbm,
    squeeze_bias,
    excite_hbm,
    excite_bias,
    gain_one,
    shift_one,
    gain_two,
    shift_two,
    gain_three,
    shift_three,
    result,
    grad_summed,
    grad_inputs,
    packed_out,
    packed_in,
    packed_mid,
    glob_out,
    small_out,
    glob_grad,
    small_grad,
    kernel_in,
    kernel_mid,
    kernel_out,
    squeeze_out,
    excite_out,
    load_sem,
    store_sem,
):
    half, group, width, real = plan.half, plan.group, plan.width, plan.half_real
    sources = [(mid_hbm.at[tap], packed_mid.at[tap]) for tap in range(3)] + [
        (out_hbm, packed_out),
        (in_hbm, packed_in),
        (result_hbm, result),
        (grad_summed_hbm, grad_summed),
        (grad_inputs_hbm, grad_inputs),
    ]
    loads, stores = [], []

    for source, target in sources:
        copy = pltpu.make_async_copy(source, target, load_sem.at[len(loads)])
        copy.start()
        loads.append(copy)

    def loaded(index):
        loads[index].wait()

    def store(source, target):
        copy = pltpu.make_async_copy(source, target, store_sem.at[len(stores)])
        copy.start()
        stores.append(copy)

    for row_tap in range(3):
        loaded(row_tap)
        for tap in range(3):
            lanes = slice(tap * group, (tap + 1) * group)
            low = packed_mid[row_tap, :group, lanes].astype(F32)
            high = packed_mid[row_tap, group:, lanes].astype(F32)
            kernel_mid[row_tap, tap] = join_lanes(low, high, width)[:width, :real]
        store(kernel_mid.at[row_tap], kernel_mid_hbm.at[row_tap])
    loaded(3)
    for piece in range(4):
        kernel_out[piece * width : (piece + 1) * width, :] = packed_out[
            piece * group : piece * group + width, :real
        ].astype(F32)
    store(kernel_out, kernel_out_hbm)
    loaded(4)
    for side in range(2):
        rows = min(half, plan.channels - side * half)
        low = packed_in[side, :rows, :group].astype(F32)
        high = packed_in[side, :rows, group:].astype(F32)
        kernel_in[side * half : side * half + rows, :] = join_lanes(low, high, width)[:, :real]
    store(kernel_in, kernel_in_hbm)

    def maps(value, glob, small):
        def glob_row(row, carry):
            rows = pl.ds(pl.multiple_of(row * plan.glob_width, 16), plan.glob_width)
            glob[row, :, 0, :] = value(rows)[: plan.glob_side, : plan.channels]
            return carry

        def small_row(row, carry):
            place = plan.glob_own + row * plan.small_width
            rows = pl.ds(pl.multiple_of(place, 16), plan.small_width)
            small[row] = value(rows)[: plan.small_side, : plan.channels]
            return carry

        lax.fori_loop(0, plan.glob_height, glob_row, 0)
        lax.fori_loop(0, plan.slots * plan.small_height, small_row, 0)

    loaded(5)
    def joined(array, rows):
        return join_lanes(array[0, rows, :].astype(F32), array[1, rows, :].astype(F32), real)

    maps(lambda rows: joined(result, rows), glob_out, small_out)
    store(glob_out, glob_out_hbm)
    store(small_out, small_out_hbm)
    n, deep = plan.dp, plan.slot_rows

    def crops(slots, low, lanes, start=0):
        rows = slots[...].astype(F32)[:, low : low + deep, start : start + lanes]
        return rows.reshape(n * deep, lanes)

    rest = half - plan.packed

    wide_pooled, squeezed = crops(slots_ahead, 0, half), crops(slots_ahead, deep, group)
    grad_excite = jnp.concatenate(
        [crops(slots_behind, 0, plan.packed), crops(slots_behind, deep, rest)], 1
    )
    grad_squeeze = crops(slots_behind, deep, group, rest)
    excite = dot_tn(squeezed.astype(BF16), grad_excite.astype(BF16))
    squeeze = dot_tn(wide_pooled.astype(BF16), grad_squeeze.astype(BF16))
    squeeze_out[:width, :] = squeeze[:width, :width]
    squeeze_out[width:, :] = squeeze[group : group + width, :width]
    excite_out[...] = join_lanes(excite[:, :group], excite[:, group:], width)[:width, :real]
    bias = jnp.sum(grad_excite, 0, keepdims=True)
    bias = join_lanes(bias[:, :group], bias[:, group:], width)
    store(squeeze_out, squeeze_hbm)
    store(excite_out, excite_hbm)
    loaded(6)
    loaded(7)
    maps(
        lambda rows: joined(grad_summed, rows)
        + jnp.concatenate([grad_inputs[0, rows, :], grad_inputs[1, rows, :]], 1).astype(F32),
        glob_grad,
        small_grad,
    )
    store(glob_grad, glob_grad_hbm)
    store(small_grad, small_grad_hbm)
    two = join_lanes(sums_two[:, :group], sums_two[:, group:], width)
    one = join_lanes(sums_one[:, :group], sums_one[:, group:], width)
    three = sums_three[lax.axis_index("rows")]
    squeeze_bias[...] = jnp.sum(grad_squeeze, 0)[:width]
    excite_bias[...] = bias[0, :real]
    gain_one[...] = one[GAIN_ONE_SUM, :real]
    shift_one[...] = one[SHIFT_ONE_SUM, :real]
    gain_two[...] = two[GAIN_TWO_SUM, :real]
    shift_two[...] = two[SHIFT_TWO_SUM, :real]
    gain_three[...] = three[1, :real]
    shift_three[...] = three[0, :real]
    for copy in stores:
        copy.wait()


def finish(
    plan, result, grad_summed, grad_inputs, gathered_out, gathered_in, gathered_mid, slots_ahead,
    slots_behind, sums_one, sums_two, sums_three
):
    shape = jax.ShapeDtypeStruct
    width, real, channels = plan.width, plan.half_real, plan.channels
    glob = (plan.glob_height, plan.glob_side, 1, channels)
    small = (plan.slots * plan.small_height, plan.small_side, channels)
    outs = (glob, small, glob, small, (channels, real), (3, 3, width, real), (channels, real))
    ins = (gathered_mid, gathered_out, gathered_in, result, grad_summed, grad_inputs)
    loaded = (result, grad_summed, grad_inputs, gathered_out, gathered_in, gathered_mid)
    return pl.pallas_call(
        functools.partial(finish_kernel, plan),
        out_shape=tuple(shape(out, F32) for out in outs)
        + (shape((real, width), F32), shape((width,), F32), shape((width, real), F32))
        + (shape((real,), F32),) * 7,
        in_specs=[ANY] * 6 + [VMEM] * 5,
        out_specs=(ANY,) * 8 + (VMEM, ANY) + (VMEM,) * 7,
        scratch_shapes=[pltpu.VMEM(array.shape, BF16) for array in loaded]
        + [pltpu.VMEM(out, F32) for out in outs + ((real, width), (width, real))]
        + [pltpu.SemaphoreType.DMA((8,)), pltpu.SemaphoreType.DMA((11,))],
        compiler_params=pltpu.CompilerParams(vmem_limit_bytes=VMEM_BYTES),
    )(
        result, grad_summed, grad_inputs, gathered_out, gathered_in, gathered_mid, slots_ahead,
        slots_behind, sums_one, sums_two, sums_three
    )


def per_device(
    glob_in,
    small_in,
    small_count,
    kernel_in,
    kernel_mid,
    kernel_out,
    squeeze_weight,
    squeeze_bias,
    excite_weight,
    excite_bias,
    gain_first,
    shift_first,
    gain_second,
    shift_second,
    gain_third,
    shift_third,
    glob_cotangent,
    small_cotangent,
):
    plan = Plan(glob_in.shape, small_in.shape, kernel_mid.shape[2], lax.axis_size("dp"))

    def images(maps):
        return maps.reshape((-1,) + maps.shape[2:])

    glob, small = images(glob_in), images(small_in)
    vectors = (
        gain_first, shift_first, gain_second, shift_second, excite_bias, squeeze_bias, gain_third,
        shift_third
    )
    (
        x_all, pre_one, act_one, pre_two, act_three, w_mid, k_out, w_in, vec_three,
        vec_three_other, mask, w_squeeze, w_excite, vec, stats, pooled, excite, squeeze_pre
    ) = forward(
        plan, small_count, glob, small, kernel_in, images(kernel_mid), kernel_out, squeeze_weight,
        excite_weight, vectors
    )
    (
        result, grad_summed, shard_out, grad_norm, slots_ahead, slots_behind, sums_three, sums_two
    ) = middle(
        plan, small_count, act_three, k_out, glob, small, images(glob_cotangent),
        images(small_cotangent), pre_two, stats, vec, vec_three, vec_three_other, mask, pooled,
        excite, squeeze_pre, w_squeeze, w_excite
    )
    gathered_out, gathered_mid, gathered_in, grad_inputs, sums_one = first(
        plan, shard_out, grad_norm, pre_two, pre_one, act_one, x_all, w_mid, w_in, stats, vec,
        sums_two, mask
    )
    outputs = finish(
        plan, result, grad_summed, grad_inputs, gathered_out, gathered_in, gathered_mid,
        slots_ahead, slots_behind, sums_one, sums_two, sums_three
    )
    shapes = (glob_in.shape, small_in.shape) * 2
    return tuple(out.reshape(shape) for out, shape in zip(outputs, shapes)) + outputs[4:]


def solution(mesh):
    maps = P("dp", "rows", None, None)
    vector = P("rows")
    columns = P(None, "rows")
    taps = P(None, None, None, "rows")
    return jax.shard_map(
        per_device,
        mesh=mesh,
        in_specs=(
            maps, maps, P("dp"), columns, taps, columns, P("rows", None), P(), columns,
        )
        + (vector,) * 7
        + (maps, maps),
        out_specs=(maps,) * 4
        + (columns, taps, columns, P("rows", None), P(), columns)
        + (vector,) * 7,
        check_vma=False,
    )
```
